32 devices in a mesh: group: 2 (over x), pw: 16 (over z, y, core).
Axes of the slice: x: 2, y: 2, z: 4, core: 2. Of those that a mesh axis runs over, the one named last changes fastest.
Arguments:
- band_coeffs: bfloat16 [32768, 2048], P('pw', 'group'), parts along dimension 1, may hold values from -6 to 6
- projectors: bfloat16 [32768, 1024], P('pw', 'group'), parts along dimension 1, may hold values from -0.03125 to 0.03125
- counts: int32 [4, 4], P('group'), parts along dimension 0, may hold values from 1 to 64, as said below
- atom_of: int32 [4, 256], P('group'), parts along dimension 0, may hold values from 0 to 15
- owners: int32 [4], P('group'), parts along dimension 0, may hold values from 0 to 15, as said below
- couplings: float32 [16, 512, 256], P('pw', 'group'), parts along dimension 1, may hold values from -6 to 6
Outputs:
- applied: bfloat16 [32768, 2048], P('pw', 'group'), parts along dimension 1
The draws below stay inside these ranges and needn't reach their ends.
There are 2 independent parts, one for each index of `group`. The reference program is written for one: setup_inputs(seed, part) draws one part's arguments, and reference() takes and returns one part's arrays. A program takes and returns all parts, laid end to end along the dimension named above; each array names one. Nothing has to cross between parts.
Inputs may be any that keep to these rules, and one draw needn't show every extreme that they name: `counts`: some entry equals 64 and some entry equals 1. The owners are distinct.
All inputs are finite; a program needn't handle non-finite values.
Results may differ from the reference program's by a relative error of at most 0.005.
Values may be sent and summed in bfloat16 or wider, within the bound.
No kernel may reach another device: no remote copies, remote signals or barrier semaphores. Data moves between devices by JAX's collectives and lax.ppermute only.
A program may use at most 64 MiB of HBM per device.

```python
import jax
import jax.numpy as jnp
from jax import lax

BANDS = 1024
GROUPS = 2
CHANNELS = 4
CH_CAP = 64
ATOMS_G = 16
PCAP = 256
PROJ = 512
NPW = 32768
SLOTS = 16
N_PW = 16


def draw_counts(key, part):
    key = jax.random.fold_in(key, 11)
    first, second = jax.random.split(key)
    total = GROUPS * CHANNELS
    values = jax.random.randint(first, (total,), 1, CH_CAP + 1)
    where_top = jax.random.randint(second, (), 0, total)
    position = jnp.arange(total, dtype=jnp.int32)
    values = jnp.where(position == where_top, CH_CAP, values)
    values = jnp.where(position == (where_top + 1) % total, 1, values)
    return values.reshape(GROUPS, CHANNELS).astype(jnp.int32)


def draw_owners(key, part):
    key = jax.random.fold_in(key, 23)
    order = jax.random.permutation(key, N_PW)
    return order[:GROUPS].astype(jnp.int32)


def place_ends(values, rng, least, high):
    index_at = [jax.random.randint(jax.random.fold_in(rng, axis), (), 0, length) for axis, length in enumerate(values.shape)]
    longest = values.shape.index(max(values.shape))
    next_to = index_at[:longest] + [(index_at[longest] + 1) % values.shape[longest]] + index_at[longest + 1:]
    return values.at[tuple(index_at)].set(least).at[tuple(next_to)].set(high)


def levels(stream_key, extent, cuts, least, top_value):
    gain = 1.0
    for dim, shards_of in cuts:
        draws = jax.random.uniform(jax.random.fold_in(jax.random.fold_in(stream_key, 6), dim), (shards_of,), jnp.float32, least / len(cuts), top_value / len(cuts))
        gain = gain * jnp.repeat(jnp.exp(draws), extent[dim] // shards_of).reshape((-1,) + (1,) * (len(extent) - 1 - dim))
    return gain


def bell_draw(key, dims, spread, bound, pieces=(), kind=jnp.bfloat16):
    entries = jax.random.normal(key, dims, jnp.float32) * spread
    if len(pieces) > 0:
        entries = levels(key, dims, pieces, -0.22, 0.18) * entries
    return jnp.clip(entries, min=-bound, max=bound).astype(kind)


def setup_inputs(seed: int = 0, part: int = 0) -> dict:
    streams_of = jax.random.split(jax.random.key(seed), 7)
    part_splits = jax.random.split(jax.random.fold_in(streams_of[6], part), 7)
    return {
        "band_coeffs": bell_draw(part_splits[0], (NPW, BANDS), 1.0, 6.0, ((0, 16),)),
        "projectors": bell_draw(part_splits[1], (NPW, PROJ), NPW ** -0.5, 0.03125, ((0, 16),)),
        "counts": draw_counts(jax.random.fold_in(jax.random.fold_in(streams_of[6], part), 71), part),
        "atom_of": place_ends(jax.random.randint(part_splits[3], (GROUPS, PCAP), 0, ATOMS_G), jax.random.fold_in(part_splits[3], 1), 0, ATOMS_G - 1).astype(jnp.int32),
        "owners": draw_owners(jax.random.fold_in(jax.random.fold_in(streams_of[6], part), 71), part),
        "couplings": bell_draw(part_splits[5], (SLOTS, PCAP, PCAP), ((NPW // PROJ) ** 0.5 / 4), 6.0, ((0, 16),), jnp.float32),
    }


def alive_mask(counts):
    slot_index = jnp.arange(PCAP, dtype=jnp.int32)
    channel = slot_index // CH_CAP
    within = slot_index % CH_CAP
    onehot = (channel[None, :] == jnp.arange(CHANNELS, dtype=jnp.int32)[:, None]).astype(jnp.int32)
    slot_count = jnp.sum(counts[:, :, None] * onehot[None, :, :], axis=1)
    return (within[None, :] < slot_count).astype(jnp.bfloat16).reshape(PROJ)


def reference(band_coeffs, projectors, counts, atom_of, owners, couplings):
    alive = alive_mask(counts)
    masked = projectors * alive[None, :]
    proj_sums = lax.dot_general(masked, band_coeffs, (((0,), (0,)), ((), ())), preferred_element_type=jnp.float32)
    same_atom = atom_of[:, :, None] == atom_of[:, None, :]
    coupling = jnp.where(same_atom, couplings[owners], jnp.zeros((), jnp.float32))
    grouped = proj_sums.reshape(GROUPS, PCAP, BANDS)
    scaled = jnp.einsum("gij,gjb->gib", coupling, grouped, precision=lax.Precision.HIGHEST)
    scaled = scaled.astype(jnp.bfloat16).reshape(PROJ, BANDS)
    return jnp.dot(masked, scaled, preferred_element_type=jnp.float32).astype(jnp.bfloat16)
```

```python
import jax
import jax.numpy as jnp
from jax import lax
from jax.sharding import PartitionSpec as P

CHANNELS = 4
CH_CAP = 64
PCAP = 256
PROJ = 512


def alive_mask(counts):
    slot = jnp.arange(CH_CAP, dtype=jnp.int32)
    return (slot[None, None, :] < counts[:, :, None]).astype(jnp.bfloat16).reshape(PROJ)


def swap(x, distance):
    count = lax.axis_size("pw")
    return lax.ppermute(x, "pw", [(i, i ^ distance) for i in range(count)])


def gathered_table(own_table, wanted, me, chips):
    sibling_table = swap(own_table, 1)
    part = jnp.where(wanted == me, own_table, jnp.where(wanted == (me ^ 1), sibling_table, 0.0))
    bit = chips // 2
    while bit:
        half = part.shape[0] // 2
        high = (me // 2) & bit != 0
        kept = jnp.where(high, part[half:], part[:half])
        sent = jnp.where(high, part[:half], part[half:])
        part = kept + swap(sent, 2 * bit)
        bit //= 2
    bit = 1
    while bit < chips:
        high = (me // 2) & bit != 0
        other = swap(part, 2 * bit)
        part = jnp.where(high, jnp.concatenate([other, part]), jnp.concatenate([part, other]))
        bit *= 2
    return part


def local(band_coeffs, projectors, counts, atom_of, owners, couplings):
    chips = lax.axis_size("pw") // 2
    me = lax.axis_index("pw")
    chip, core = me // 2, me % 2
    width = band_coeffs.shape[1] // chips

    masked = projectors * alive_mask(counts)[None, :]
    table = gathered_table(couplings[0], owners[core], me, chips)
    atoms = atom_of[core]
    coupling = jnp.where(atoms[:, None] == atoms[None, :], table, 0.0)

    def project(group):
        columns = lax.dynamic_slice_in_dim(masked, group * PCAP, PCAP, 1)
        return lax.dot_general(columns, band_coeffs, (((0,), (0,)), ((), ())), preferred_element_type=jnp.float32)

    theirs = project(1 - core).astype(jnp.bfloat16)
    sums = project(core) + swap(theirs, 1).astype(jnp.float32)

    def chunk(x, at):
        return lax.dynamic_slice_in_dim(x, at * width, width, 1)

    total = chunk(sums, chip)
    for s in range(1, chips):
        total = total + swap(chunk(sums, chip ^ s).astype(jnp.bfloat16), 2 * s).astype(jnp.float32)

    scaled = jnp.dot(coupling, total, precision=lax.Precision.HIGHEST).astype(jnp.bfloat16)
    mine = jnp.zeros((PCAP, band_coeffs.shape[1]), jnp.bfloat16)
    for s in range(chips):
        piece = scaled if s == 0 else swap(scaled, 2 * s)
        mine = lax.dynamic_update_slice_in_dim(mine, piece, (chip ^ s) * width, 1)
    other = swap(mine, 1)
    both = jnp.where(core == 0, jnp.concatenate([mine, other]), jnp.concatenate([other, mine]))
    return jnp.dot(masked, both, preferred_element_type=jnp.float32).astype(jnp.bfloat16)


def solution(mesh):
    placed = (
        P("pw", "group"),
        P("pw", "group"),
        P("group", None),
        P("group", None),
        P("group"),
        P("pw", "group", None),
    )
    return jax.shard_map(
        local, mesh=mesh, in_specs=placed, out_specs=P("pw", "group"), check_vma=False
    )
```

```python
import jax
import jax.numpy as jnp
from jax import lax
from jax.experimental import pallas as pl
from jax.experimental.pallas import tpu as pltpu
from jax.sharding import PartitionSpec as P

CHANNELS = 4
CH_CAP = 64
PCAP = 256
COLUMNS = 256
VMEM_LIMIT = 40 * 1024 * 1024


def swap_cores(x):
    count = lax.axis_size("pw")
    return lax.ppermute(x, "pw", [(i, i ^ 1) for i in range(count)])


def exchange(x):
    count = lax.axis_size("pw")
    same_core = [list(range(core, count, 2)) for core in range(2)]
    return lax.all_to_all(x, "pw", 0, 0, axis_index_groups=same_core)


def project_kernel(where, projectors, bands, out, flipped):
    @pl.when(pl.program_id(0) == 0)
    def _():
        flipped[...] = projectors[...].T

    sums = jnp.dot(flipped[...], bands[...], preferred_element_type=jnp.float32)
    width = out.shape[2]
    for at in range(out.shape[0]):
        out[at] = sums[:, at * width : (at + 1) * width].astype(out.dtype)


def project(group, projectors, band_coeffs, chips, dtype):
    depth, bands = band_coeffs.shape
    width = bands // chips
    return pl.pallas_call(
        project_kernel,
        grid_spec=pltpu.PrefetchScalarGridSpec(
            num_scalar_prefetch=1,
            grid=(bands // COLUMNS,),
            in_specs=[
                pl.BlockSpec((depth, PCAP), lambda j, where: (0, where[0])),
                pl.BlockSpec((depth, COLUMNS), lambda j, where: (0, j)),
            ],
            out_specs=pl.BlockSpec((COLUMNS // width, PCAP, width), lambda j, where: (j, 0, 0)),
            scratch_shapes=[pltpu.VMEM((PCAP, depth), jnp.bfloat16)],
        ),
        out_shape=jax.ShapeDtypeStruct((chips, PCAP, width), dtype),
        compiler_params=pltpu.CompilerParams(vmem_limit_bytes=VMEM_LIMIT),
        cost_estimate=pl.CostEstimate(
            flops=2 * depth * PCAP * bands, bytes_accessed=2 * depth * (bands + PCAP), transcendentals=0
        ),
        name="project",
    )(group, projectors, band_coeffs)


def pack_kernel(where, sums, theirs, table_rows, message, own):
    chips = sums.shape[0]
    for at in range(chips):
        message[at, :PCAP] = (sums[at] + theirs[at].astype(jnp.float32)).astype(jnp.bfloat16)
        message[at, PCAP:] = table_rows[...]
    chip = where[1]
    own[...] = sums[chip] + theirs[chip].astype(jnp.float32)


def pack(where, sums, theirs, table_rows):
    chips, _, width = sums.shape
    vmem = pl.BlockSpec(memory_space=pltpu.VMEM)
    return pl.pallas_call(
        pack_kernel,
        in_specs=[pl.BlockSpec(memory_space=pltpu.SMEM), vmem, vmem, vmem],
        out_specs=[vmem, vmem],
        out_shape=[
            jax.ShapeDtypeStruct((chips, PCAP + table_rows.shape[0], width), jnp.bfloat16),
            jax.ShapeDtypeStruct((PCAP, width), jnp.float32),
        ],
        compiler_params=pltpu.CompilerParams(vmem_limit_bytes=VMEM_LIMIT),
        name="pack",
    )(where, sums, theirs, table_rows)


def couple_kernel(where, counts, atom_of, message, own, out, table):
    chips, _, width = out.shape
    rows = PCAP // chips
    core, chip = where[0], where[1]
    total = own[...]
    for at in range(chips):
        got = message[at, :PCAP].astype(jnp.float32)
        total = total + jnp.where(at == chip, 0.0, got)
        for piece in range(PCAP // width):
            first = PCAP + piece * rows
            table[at * rows : (at + 1) * rows, piece * width : (piece + 1) * width] = message[
                at, first : first + rows
            ].astype(jnp.float32)
    slot = lax.broadcasted_iota(jnp.int32, (1, PCAP), 1)
    limit = jnp.zeros((1, PCAP), jnp.int32)
    for channel in range(CHANNELS):
        limit = jnp.where(slot >= channel * CH_CAP, channel * CH_CAP + counts[core, channel], limit)
    atoms = jnp.where(core == 0, atom_of[0:1], atom_of[1:2])
    code = jnp.broadcast_to(jnp.where(slot < limit, atoms, -1), (PCAP, PCAP))
    coupling = jnp.where((code == code.T) & (code >= 0), table[...], 0.0)
    scaled = jnp.dot(
        coupling, total, precision=lax.Precision.HIGHEST, preferred_element_type=jnp.float32
    ).astype(jnp.bfloat16)
    for at in range(chips):
        out[at] = scaled


def couple(where, counts, atom_of, message, own):
    chips = message.shape[0]
    vmem = pl.BlockSpec(memory_space=pltpu.VMEM)
    smem = pl.BlockSpec(memory_space=pltpu.SMEM)
    return pl.pallas_call(
        couple_kernel,
        in_specs=[smem, smem, vmem, vmem, vmem],
        out_specs=vmem,
        out_shape=jax.ShapeDtypeStruct((chips,) + own.shape, jnp.bfloat16),
        scratch_shapes=[pltpu.VMEM((PCAP, PCAP), jnp.float32)],
        compiler_params=pltpu.CompilerParams(vmem_limit_bytes=VMEM_LIMIT),
        name="couple",
    )(where, counts, atom_of, message, own)


def apply_kernel(where, projectors, mine, other, out, scaled):
    @pl.when(pl.program_id(0) == 0)
    def _():
        chips, _, width = mine.shape
        core = where[0]
        for part, group in ((mine, core), (other, 1 - core)):
            first = pl.multiple_of(group * PCAP, PCAP)
            for at in range(chips):
                scaled[pl.ds(first, PCAP), at * width : (at + 1) * width] = part[at]

    out[...] = jnp.dot(projectors[...], scaled[...], preferred_element_type=jnp.float32).astype(out.dtype)


def apply(where, projectors, mine, other):
    depth, slots = projectors.shape
    chips, _, width = mine.shape
    block = depth // 8
    whole = pl.BlockSpec((chips, PCAP, width), lambda i, where: (0, 0, 0))
    return pl.pallas_call(
        apply_kernel,
        grid_spec=pltpu.PrefetchScalarGridSpec(
            num_scalar_prefetch=1,
            grid=(depth // block,),
            in_specs=[pl.BlockSpec((block, slots), lambda i, where: (i, 0)), whole, whole],
            out_specs=pl.BlockSpec((block, chips * width), lambda i, where: (i, 0)),
            scratch_shapes=[pltpu.VMEM((slots, chips * width), jnp.bfloat16)],
        ),
        out_shape=jax.ShapeDtypeStruct((depth, chips * width), jnp.bfloat16),
        compiler_params=pltpu.CompilerParams(vmem_limit_bytes=VMEM_LIMIT),
        cost_estimate=pl.CostEstimate(
            flops=2 * depth * slots * chips * width,
            bytes_accessed=2 * depth * (slots + chips * width),
            transcendentals=0,
        ),
        name="apply",
    )(where, projectors, mine, other)


def local(band_coeffs, projectors, counts, atom_of, owners, couplings):
    devices = lax.axis_size("pw")
    chips = devices // 2
    me = lax.axis_index("pw")
    chip, core = me // 2, me % 2
    width = band_coeffs.shape[1] // chips
    rows = PCAP // chips
    where = jnp.stack([core, chip])

    slices = couplings[0].astype(jnp.bfloat16).reshape(chips, rows, PCAP // width, width).transpose(0, 2, 1, 3)
    slices = jnp.broadcast_to(slices.reshape(chips, 1, -1, width), (chips, 2, rows * PCAP // width, width))
    slices = lax.all_to_all(slices.reshape(devices, -1, width), "pw", 0, 0)
    table_rows = lax.dynamic_index_in_dim(slices, owners[core], 0, keepdims=False)

    theirs = swap_cores(project((1 - core)[None], projectors, band_coeffs, chips, jnp.bfloat16))
    sums = project(core[None], projectors, band_coeffs, chips, jnp.float32)
    message, own = pack(where, sums, theirs, table_rows)
    message = exchange(message)
    mine = exchange(couple(where, counts, atom_of, message, own))
    return apply(where, projectors, mine, swap_cores(mine))


def solution(mesh):
    placed = (
        P("pw", "group"),
        P("pw", "group"),
        P("group", None),
        P("group", None),
        P("group"),
        P("pw", "group", None),
    )
    return jax.shard_map(
        local, mesh=mesh, in_specs=placed, out_specs=P("pw", "group"), check_vma=False
    )
```

```python
import jax
import jax.numpy as jnp
from jax import lax
from jax.experimental import pallas as pl
from jax.experimental.pallas import tpu as pltpu
from jax.sharding import PartitionSpec as P

CHANNELS = 4
CH_CAP = 64
PCAP = 256
LANES = 128
ROW_BLOCK = 512
PARAMS = pltpu.CompilerParams(vmem_limit_bytes=32 * 1024 * 1024)
VMEM = pl.BlockSpec(memory_space=pltpu.VMEM)
SMEM = pl.BlockSpec(memory_space=pltpu.SMEM)
HBM = pl.BlockSpec(memory_space=pltpu.HBM)


def bit_order(chips, core):
    bits = list(range(chips.bit_length() - 1))
    if core == 1 and len(bits) > 2:
        bits[0], bits[1] = bits[1], bits[0]
    return bits


def offsets(chips, core):
    order = bit_order(chips, core)
    count = len(order)
    return [
        sum(((p >> (count - 1 - i)) & 1) << bit for i, bit in enumerate(order)) for p in range(chips)
    ]


def chunk_of(chips, chip, group, position):
    return chip ^ jnp.where(group == 0, offsets(chips, 0)[position], offsets(chips, 1)[position])


def swap_cores(x):
    count = lax.axis_size("pw")
    return lax.ppermute(x, "pw", [(i, i ^ 1) for i in range(count)])


def swap_bits(x, bits):
    count = lax.axis_size("pw")
    return lax.ppermute(x, "pw", [(i, i ^ (2 << bits[i % 2])) for i in range(count)])


def swap_stage(x, stage):
    chips = lax.axis_size("pw") // 2
    return swap_bits(x, [bit_order(chips, core)[stage] for core in range(2)])


def project_kernel(chips, own, first, where, projectors, bands, *refs):
    fresh = len(refs) == 6
    if fresh:
        out, flipped, columns, slots, column_sems, slot_sem = refs
    else:
        out, columns, column_sems = refs
        flipped = projectors
    core, chip = where[0], where[1]
    group = core if own else 1 - core
    copies = []
    if fresh:
        start = pl.multiple_of(group * PCAP, PCAP)
        slot_copy = pltpu.make_async_copy(projectors.at[:, pl.ds(start, PCAP)], slots, slot_sem)
        slot_copy.start()
    for at in range(out.shape[0]):
        start = pl.multiple_of(chunk_of(chips, chip, group, first + at) * LANES, LANES)
        copies.append(
            pltpu.make_async_copy(
                bands.at[:, pl.ds(start, LANES)],
                columns.at[at // 2, :, (at % 2) * LANES : (at % 2 + 1) * LANES],
                column_sems.at[at],
            )
        )
        copies[-1].start()
    if fresh:
        slot_copy.wait()
        flipped[...] = slots[...].T
    for pair in range(out.shape[0] // 2):
        copies[2 * pair].wait()
        copies[2 * pair + 1].wait()
        sums = jnp.dot(flipped[...], columns[pair], preferred_element_type=jnp.float32)
        out[2 * pair] = sums[:, :LANES].astype(out.dtype)
        out[2 * pair + 1] = sums[:, LANES:].astype(out.dtype)


def project(where, projectors, flipped, band_coeffs, own, first):
    depth, bands = band_coeffs.shape
    chips = lax.axis_size("pw") // 2
    width = bands // chips
    half = chips // 2
    dtype = jnp.float32 if own else jnp.bfloat16
    if width != LANES:
        group = where[0] if own else 1 - where[0]
        chunks = jnp.stack([chunk_of(chips, where[1], group, first + at) for at in range(half)])
        slots = lax.dynamic_slice_in_dim(projectors, group * PCAP, PCAP, 1)
        columns = jnp.take(band_coeffs.reshape(depth, chips, width), chunks, axis=1)
        return jnp.einsum("ds,dhw->hsw", slots, columns, preferred_element_type=jnp.float32).astype(dtype), None
    shape = jax.ShapeDtypeStruct((half, PCAP, width), dtype)
    flipped_shape = jax.ShapeDtypeStruct((PCAP, depth), jnp.bfloat16)
    columns = pltpu.VMEM((half // 2, depth, 2 * LANES), jnp.bfloat16)
    sems = pltpu.SemaphoreType.DMA((half,))
    fresh = flipped is None

    def kernel(*refs):
        project_kernel(chips, own, first, *refs)

    cost = pl.CostEstimate(
        flops=2 * depth * PCAP * half * width, bytes_accessed=2 * depth * half * width, transcendentals=0
    )
    bands_in_hbm = pltpu.with_memory_space_constraint(band_coeffs, pltpu.HBM)
    if fresh:
        return pl.pallas_call(
            kernel,
            in_specs=[SMEM, HBM, HBM],
            out_specs=[VMEM, VMEM],
            out_shape=[shape, flipped_shape],
            scratch_shapes=[
                columns, pltpu.VMEM((depth, PCAP), jnp.bfloat16), sems, pltpu.SemaphoreType.DMA
            ],
            compiler_params=PARAMS,
            cost_estimate=cost,
            name="project_first",
        )(where, pltpu.with_memory_space_constraint(projectors, pltpu.HBM), bands_in_hbm)
    return pl.pallas_call(
        kernel,
        in_specs=[SMEM, VMEM, HBM],
        out_specs=VMEM,
        out_shape=shape,
        scratch_shapes=[columns, sems],
        compiler_params=PARAMS,
        cost_estimate=cost,
        name="project_rest",
    )(where, flipped, bands_in_hbm), None


def fold_kernel(*refs):
    *terms, kept, message = refs
    half = kept.shape[0]
    for at in range(2 * half):
        total = terms[0][at]
        for term in terms[1:]:
            total = total + term[at].astype(jnp.float32)
        if at < half:
            kept[at] = total
        else:
            message[at - half] = total.astype(message.dtype)


def fold(*terms):
    count, rows, width = terms[0].shape
    return pl.pallas_call(
        fold_kernel,
        in_specs=[VMEM] * len(terms),
        out_specs=[VMEM, VMEM],
        out_shape=[
            jax.ShapeDtypeStruct((count // 2, rows, width), jnp.float32),
            jax.ShapeDtypeStruct((count // 2, rows, width), jnp.bfloat16),
        ],
        compiler_params=PARAMS,
        name="fold",
    )(*terms)


def add_kernel(left, right, out):
    for at in range(out.shape[0]):
        out[at] = (left[at] + right[at].astype(jnp.float32)).astype(out.dtype)


def add(left, right):
    return pl.pallas_call(
        add_kernel,
        in_specs=[VMEM, VMEM],
        out_specs=VMEM,
        out_shape=jax.ShapeDtypeStruct(left.shape, jnp.bfloat16),
        compiler_params=PARAMS,
        name="add",
    )(left, right)


def choose_kernel(where, owners, own, sibling, kept, sent):
    core, chip, me = where[0], where[1], where[2]
    owner = jnp.where(core == 0, owners[0], owners[1])
    half = PCAP // 2
    side = chip & 1
    for out, which in ((kept, side), (sent, 1 - side)):
        rows = pl.ds(pl.multiple_of(which * half, half), half)
        part = jnp.where(owner == me, own[rows], jnp.where(owner == (me ^ 1), sibling[rows], 0.0))
        out[...] = part.astype(out.dtype)


def choose(where, owners, own, sibling):
    shape = jax.ShapeDtypeStruct((PCAP // 2, PCAP), jnp.bfloat16)
    return pl.pallas_call(
        choose_kernel,
        in_specs=[SMEM, SMEM, VMEM, VMEM],
        out_specs=[VMEM, VMEM],
        out_shape=[shape, shape],
        compiler_params=PARAMS,
        name="choose",
    )(where, owners, own, sibling)


def couple_kernel(where, counts, atom_of, kept, got, near, far, out, table):
    core, chip = where[0], where[1]
    half = PCAP // 2
    side = chip & 1
    table[pl.ds(pl.multiple_of(side * half, half), half)] = near[...].astype(jnp.float32)
    table[pl.ds(pl.multiple_of((1 - side) * half, half), half)] = far[...].astype(jnp.float32)
    total = kept[0] + got[0].astype(jnp.float32)
    slot = lax.broadcasted_iota(jnp.int32, (1, PCAP), 1)
    limit = jnp.zeros((1, PCAP), jnp.int32)
    for channel in range(CHANNELS):
        limit = jnp.where(slot >= channel * CH_CAP, channel * CH_CAP + counts[core, channel], limit)
    atoms = jnp.where(core == 0, atom_of[0:1], atom_of[1:2])
    code = jnp.broadcast_to(jnp.where(slot < limit, atoms, -1), (PCAP, PCAP))
    coupling = jnp.where((code == code.T) & (code >= 0), table[...], 0.0)
    out[0] = jnp.dot(
        coupling, total, precision=lax.Precision.HIGHEST, preferred_element_type=jnp.float32
    ).astype(out.dtype)


def couple(where, counts, atom_of, kept, got, near, far):
    return pl.pallas_call(
        couple_kernel,
        in_specs=[SMEM, SMEM] + [VMEM] * 5,
        out_specs=VMEM,
        out_shape=jax.ShapeDtypeStruct(kept.shape, jnp.bfloat16),
        scratch_shapes=[pltpu.VMEM((PCAP, PCAP), jnp.float32)],
        compiler_params=PARAMS,
        name="couple",
    )(where, counts, atom_of, kept, got, near, far)


def apply_kernel(chips, where, projectors, *refs):
    *pieces, out, scaled, blocks, sems = refs
    core, chip = where[0], where[1]
    count = len(pieces) // 2
    for own, parts in ((True, pieces[:count]), (False, pieces[count:])):
        group = core if own else 1 - core
        rows = pl.ds(pl.multiple_of(group * PCAP, PCAP), PCAP)
        position = 0
        for part in parts:
            for at in range(part.shape[0]):
                start = pl.multiple_of(chunk_of(chips, chip, group, position) * LANES, LANES)
                scaled[rows, pl.ds(start, LANES)] = part[at]
                position += 1
    copies = []
    for block in range(projectors.shape[0] // ROW_BLOCK):
        rows = slice(block * ROW_BLOCK, (block + 1) * ROW_BLOCK)
        slot = block % 2
        if block >= 2:
            copies[block - 2].wait()
        blocks[slot] = jnp.dot(
            projectors[rows], scaled[...], preferred_element_type=jnp.float32
        ).astype(jnp.bfloat16)
        copies.append(pltpu.make_async_copy(blocks.at[slot], out.at[rows], sems.at[slot]))
        copies[-1].start()
    for copy in copies[-2:]:
        copy.wait()


def apply(where, projectors, pieces):
    depth, slots = projectors.shape
    chips = lax.axis_size("pw") // 2
    width = pieces[0].shape[2]
    bands = chips * width
    if width != LANES:
        count = len(pieces) // 2
        rows = []
        for group in range(2):
            chunks = jnp.stack([chunk_of(chips, where[1], group, at) for at in range(chips)])
            mine = jnp.concatenate(pieces[:count])
            other = jnp.concatenate(pieces[count:])
            blocks = jnp.where(where[0] == group, mine, other)
            rows.append(jnp.zeros_like(blocks).at[chunks].set(blocks).transpose(1, 0, 2).reshape(PCAP, bands))
        return jnp.dot(projectors, jnp.concatenate(rows), preferred_element_type=jnp.float32).astype(jnp.bfloat16)

    def kernel(*refs):
        apply_kernel(chips, *refs)

    return pl.pallas_call(
        kernel,
        in_specs=[SMEM, VMEM] + [VMEM] * len(pieces),
        out_specs=HBM,
        out_shape=jax.ShapeDtypeStruct((depth, bands), jnp.bfloat16),
        scratch_shapes=[
            pltpu.VMEM((slots, bands), jnp.bfloat16),
            pltpu.VMEM((2, ROW_BLOCK, bands), jnp.bfloat16),
            pltpu.SemaphoreType.DMA((2,)),
        ],
        compiler_params=PARAMS,
        cost_estimate=pl.CostEstimate(
            flops=2 * depth * slots * bands, bytes_accessed=2 * depth * (slots + bands), transcendentals=0
        ),
        name="apply",
    )(where, projectors, *pieces)


def local(band_coeffs, projectors, counts, atom_of, owners, couplings):
    chips = lax.axis_size("pw") // 2
    stages = chips.bit_length() - 1
    half = chips // 2
    me = lax.axis_index("pw")
    where = jnp.stack([me % 2, me // 2, me])

    own_table = couplings[0]
    near, far = choose(where, owners, own_table, swap_cores(own_table))
    near = near + swap_bits(far, [0, 0])
    for bit in range(stages - 1, 0, -1):
        near = near + swap_bits(near, [bit, bit])
    far = swap_bits(near, [0, 0])

    theirs, their_flipped = project(where, projectors, None, band_coeffs, False, half)
    theirs = swap_cores(theirs)
    ours, our_flipped = project(where, projectors, None, band_coeffs, True, half)
    got = swap_stage(add(ours, theirs), 0)
    theirs, _ = project(where, projectors, their_flipped, band_coeffs, False, 0)
    theirs = swap_cores(theirs)
    ours, _ = project(where, projectors, our_flipped, band_coeffs, True, 0)
    kept, message = fold(ours, theirs, got)
    for stage in range(1, stages):
        got = swap_stage(message, stage)
        if stage < stages - 1:
            kept, message = fold(kept, got)

    scaled = couple(where, counts, atom_of, kept, got, near, far)
    mine = jnp.concatenate([scaled, swap_stage(scaled, stages - 1)])
    pieces = [mine]
    others = [swap_cores(mine)]
    for stage in range(stages - 2, -1, -1):
        got = swap_stage(mine, stage)
        pieces.append(got)
        others.append(swap_cores(got))
        if stage:
            mine = jnp.concatenate([mine, got])
    return apply(where, projectors, pieces + others)


def solution(mesh):
    placed = (
        P("pw", "group"),
        P("pw", "group"),
        P("group", None),
        P("group", None),
        P("group"),
        P("pw", "group", None),
    )
    return jax.shard_map(
        local, mesh=mesh, in_specs=placed, out_specs=P("pw", "group"), check_vma=False
    )
```

```python
import jax
import jax.numpy as jnp
from jax import lax
from jax.experimental import pallas as pl
from jax.experimental.pallas import tpu as pltpu
from jax.sharding import PartitionSpec as P

CHANNELS = 4
CH_CAP = 64
PCAP = 256
LANES = 128
COLUMNS = 256
PARAMS = pltpu.CompilerParams(vmem_limit_bytes=32 * 1024 * 1024)
VMEM = pl.BlockSpec(memory_space=pltpu.VMEM)
SMEM = pl.BlockSpec(memory_space=pltpu.SMEM)
HBM = pl.BlockSpec(memory_space=pltpu.HBM)
ANY = pl.BlockSpec(memory_space=pl.ANY)


def bit_order(chips, core):
    bits = list(range(chips.bit_length() - 1))
    if core == 1 and len(bits) > 2:
        bits[0], bits[1] = bits[1], bits[0]
    return bits


def offsets(chips, core):
    order = bit_order(chips, core)
    count = len(order)
    return [
        sum(((p >> (count - 1 - i)) & 1) << bit for i, bit in enumerate(order)) for p in range(chips)
    ]


def chunk_of(chips, chip, group, position):
    return chip ^ jnp.where(group == 0, offsets(chips, 0)[position], offsets(chips, 1)[position])


def swap_cores(x):
    count = lax.axis_size("pw")
    return lax.ppermute(x, "pw", [(i, i ^ 1) for i in range(count)])


def swap_bits(x, bits):
    count = lax.axis_size("pw")
    return lax.ppermute(x, "pw", [(i, i ^ (2 << bits[i % 2])) for i in range(count)])


def swap_stage(x, stage):
    chips = lax.axis_size("pw") // 2
    return swap_bits(x, [bit_order(chips, core)[stage] for core in range(2)])


def project_kernel(chips, fresh, where, projectors, bands, *refs):
    if fresh:
        theirs, ours, flipped, columns, slots, slot_sems, column_sems = refs
    else:
        theirs, ours = refs
        flipped, columns = projectors, bands
    core, chip = where[0], where[1]
    half = chips // 2
    first = half if fresh else 0
    if fresh:
        slot_copies, column_copies = [], []
        for copies, source, target, sems in (
            (slot_copies, projectors, slots, slot_sems),
            (column_copies, bands, columns, column_sems),
        ):
            block = source.shape[0] // sems.shape[0]
            for at in range(sems.shape[0]):
                rows = slice(at * block, (at + 1) * block)
                copies.append(pltpu.make_async_copy(source.at[rows], target.at[rows], sems.at[at]))
                copies[-1].start()
        block = slots.shape[0] // len(slot_copies)
        for at, copy in enumerate(slot_copies):
            copy.wait()
            rows = slice(at * block, (at + 1) * block)
            for place, group in enumerate((core, 1 - core)):
                start = pl.multiple_of(group * PCAP, PCAP)
                flipped[place * PCAP : (place + 1) * PCAP, rows] = slots[rows, pl.ds(start, PCAP)].T
        for copy in column_copies:
            copy.wait()

    def pair_of_blocks(group, position):
        starts = [
            pl.multiple_of(chunk_of(chips, chip, group, position + at) * LANES, LANES) for at in range(2)
        ]
        return jnp.concatenate([columns[:, pl.ds(start, LANES)] for start in starts], axis=1)

    def keep(out, at, sums):
        out[at] = sums[:, :LANES].astype(out.dtype)
        out[at + 1] = sums[:, LANES:].astype(out.dtype)

    for at in range(half - 2, -1, -2):
        position = first + at
        if offsets(chips, 0)[position] == offsets(chips, 1)[position]:
            sums = jnp.dot(flipped[...], pair_of_blocks(core, position), preferred_element_type=jnp.float32)
            keep(ours, at, sums[:PCAP])
            keep(theirs, at, sums[PCAP:])
        else:
            for out, rows, group in ((ours, slice(0, PCAP), core), (theirs, slice(PCAP, 2 * PCAP), 1 - core)):
                keep(
                    out,
                    at,
                    jnp.dot(flipped[rows], pair_of_blocks(group, position), preferred_element_type=jnp.float32),
                )


def project_plain(where, projectors, band_coeffs, first):
    depth, bands = band_coeffs.shape
    chips = lax.axis_size("pw") // 2
    half = chips // 2
    outs = []
    for group, dtype in ((1 - where[0], jnp.bfloat16), (where[0], jnp.float32)):
        chunks = jnp.stack([chunk_of(chips, where[1], group, first + at) for at in range(half)])
        slots = lax.dynamic_slice_in_dim(projectors, group * PCAP, PCAP, 1)
        columns = jnp.take(band_coeffs.reshape(depth, chips, bands // chips), chunks, axis=1)
        sums = jnp.einsum("ds,dhw->hsw", slots, columns, preferred_element_type=jnp.float32)
        outs.append(sums.astype(dtype))
    return outs


def project(where, projectors, band_coeffs, fresh):
    depth, bands = band_coeffs.shape
    chips = lax.axis_size("pw") // 2
    half, width = chips // 2, bands // chips

    def kernel(*refs):
        project_kernel(chips, fresh, *refs)

    out_shape = [
        jax.ShapeDtypeStruct((half, PCAP, width), jnp.bfloat16),
        jax.ShapeDtypeStruct((half, PCAP, width), jnp.float32),
    ]
    scratch = []
    if fresh:
        slots = projectors.shape[1]
        out_shape += [
            jax.ShapeDtypeStruct((slots, depth), jnp.bfloat16),
            jax.ShapeDtypeStruct((depth, bands), jnp.bfloat16),
        ]
        scratch = [
            pltpu.VMEM((depth, slots), jnp.bfloat16),
            pltpu.SemaphoreType.DMA((4,)),
            pltpu.SemaphoreType.DMA((8,)),
        ]
        projectors = pltpu.with_memory_space_constraint(projectors, pltpu.HBM)
        band_coeffs = pltpu.with_memory_space_constraint(band_coeffs, pltpu.HBM)
    return pl.pallas_call(
        kernel,
        in_specs=[SMEM, HBM, HBM] if fresh else [SMEM, VMEM, VMEM],
        out_specs=[VMEM] * len(out_shape),
        out_shape=out_shape,
        scratch_shapes=scratch,
        compiler_params=PARAMS,
        cost_estimate=pl.CostEstimate(
            flops=2 * depth * PCAP * bands, bytes_accessed=2 * depth * bands, transcendentals=0
        ),
        name="project_sent" if fresh else "project_kept",
    )(where, projectors, band_coeffs)


def fold_kernel(*refs):
    *terms, kept, message = refs
    half = kept.shape[0]
    for at in range(2 * half):
        total = terms[0][at]
        for term in terms[1:]:
            total = total + term[at].astype(jnp.float32)
        if at < half:
            kept[at] = total
        else:
            message[at - half] = total.astype(message.dtype)


def fold(*terms):
    count, rows, width = terms[0].shape
    return pl.pallas_call(
        fold_kernel,
        in_specs=[VMEM] * len(terms),
        out_specs=[VMEM, VMEM],
        out_shape=[
            jax.ShapeDtypeStruct((count // 2, rows, width), jnp.float32),
            jax.ShapeDtypeStruct((count // 2, rows, width), jnp.bfloat16),
        ],
        compiler_params=PARAMS,
        name="fold",
    )(*terms)


def add_kernel(left, right, out):
    for at in range(out.shape[0]):
        out[at] = (left[at] + right[at].astype(jnp.float32)).astype(out.dtype)


def add(left, right):
    return pl.pallas_call(
        add_kernel,
        in_specs=[VMEM, VMEM],
        out_specs=VMEM,
        out_shape=jax.ShapeDtypeStruct(left.shape, jnp.bfloat16),
        compiler_params=PARAMS,
        name="add",
    )(left, right)


def choose_kernel(where, owners, own, sibling, after, kept, sent):
    del after
    core, chip, me = where[0], where[1], where[2]
    owner = jnp.where(core == 0, owners[0], owners[1])
    half = PCAP // 2
    side = chip & 1
    for out, which in ((kept, side), (sent, 1 - side)):
        rows = pl.ds(pl.multiple_of(which * half, half), half)
        part = jnp.where(owner == me, own[rows], jnp.where(owner == (me ^ 1), sibling[rows], 0.0))
        out[...] = part.astype(out.dtype)


def choose(where, owners, own, sibling, after):
    shape = jax.ShapeDtypeStruct((PCAP // 2, PCAP), jnp.bfloat16)
    return pl.pallas_call(
        choose_kernel,
        in_specs=[SMEM, SMEM, VMEM, VMEM, ANY],
        out_specs=[VMEM, VMEM],
        out_shape=[shape, shape],
        compiler_params=PARAMS,
        name="choose",
    )(where, owners, own, sibling, after)


def merge_kernel(left, right, after, out):
    del after
    out[...] = left[...] + right[...]


def merge(left, right, after):
    return pl.pallas_call(
        merge_kernel,
        in_specs=[VMEM, VMEM, ANY],
        out_specs=VMEM,
        out_shape=jax.ShapeDtypeStruct(left.shape, left.dtype),
        compiler_params=PARAMS,
        name="merge",
    )(left, right, after)


def mask_kernel(where, counts, atom_of, after, out):
    del after
    core = where[0]
    slot = lax.broadcasted_iota(jnp.int32, (1, PCAP), 1)
    limit = jnp.zeros((1, PCAP), jnp.int32)
    for channel in range(CHANNELS):
        limit = jnp.where(slot >= channel * CH_CAP, channel * CH_CAP + counts[core, channel], limit)
    atoms = jnp.where(core == 0, atom_of[0:1], atom_of[1:2])
    code = jnp.broadcast_to(jnp.where(slot < limit, atoms, -1), (PCAP, PCAP))
    out[...] = jnp.where((code == code.T) & (code >= 0), 1.0, 0.0).astype(out.dtype)


def mask(where, counts, atom_of, after):
    return pl.pallas_call(
        mask_kernel,
        in_specs=[SMEM, SMEM, VMEM, ANY],
        out_specs=VMEM,
        out_shape=jax.ShapeDtypeStruct((PCAP, PCAP), jnp.bfloat16),
        compiler_params=PARAMS,
        name="mask",
    )(where, counts, atom_of, after)


def couple_kernel(where, kept, got, allowed, near, far, out, table):
    half = PCAP // 2
    width = out.shape[2]
    side = where[1] & 1
    for part, which in ((near, side), (far, 1 - side)):
        rows = pl.ds(pl.multiple_of(which * half, half), half)
        table[rows] = part[...] * allowed[rows]
    total = kept[0] + got[0].astype(jnp.float32)
    high = total.astype(jnp.bfloat16)
    low = (total - high.astype(jnp.float32)).astype(jnp.bfloat16)
    both = jnp.dot(table[...], jnp.concatenate([high, low], axis=1), preferred_element_type=jnp.float32)
    out[0] = (both[:, :width] + both[:, width:]).astype(out.dtype)


def couple(where, kept, got, allowed, near, far):
    return pl.pallas_call(
        couple_kernel,
        in_specs=[SMEM] + [VMEM] * 5,
        out_specs=VMEM,
        out_shape=jax.ShapeDtypeStruct(kept.shape, jnp.bfloat16),
        scratch_shapes=[pltpu.VMEM((PCAP, PCAP), jnp.bfloat16)],
        compiler_params=PARAMS,
        name="couple",
    )(where, kept, got, allowed, near, far)


def apply_kernel(chips, where, projectors, *refs):
    *pieces, out, scaled, blocks, sems = refs
    core, chip = where[0], where[1]
    count = len(pieces) // 2
    for own, parts in ((True, pieces[:count]), (False, pieces[count:])):
        group = core if own else 1 - core
        rows = pl.ds(pl.multiple_of(group * PCAP, PCAP), PCAP)
        position = 0
        for part in parts:
            for at in range(part.shape[0]):
                start = pl.multiple_of(chunk_of(chips, chip, group, position) * LANES, LANES)
                scaled[rows, pl.ds(start, LANES)] = part[at]
                position += 1
    copies = []
    for block in range(out.shape[1] // COLUMNS):
        columns = slice(block * COLUMNS, (block + 1) * COLUMNS)
        slot = block % 2
        if block >= 2:
            copies[block - 2].wait()
        blocks[slot] = jnp.dot(
            projectors[...], scaled[:, columns], preferred_element_type=jnp.float32
        ).astype(jnp.bfloat16)
        copies.append(pltpu.make_async_copy(blocks.at[slot], out.at[:, columns], sems.at[slot]))
        copies[-1].start()
    for copy in copies[-2:]:
        copy.wait()


def apply(where, projectors, pieces):
    depth, slots = projectors.shape
    chips = lax.axis_size("pw") // 2
    width = pieces[0].shape[2]
    bands = chips * width
    if width != LANES:
        count = len(pieces) // 2
        rows = []
        for group in range(2):
            chunks = jnp.stack([chunk_of(chips, where[1], group, at) for at in range(chips)])
            mine = jnp.concatenate(pieces[:count])
            other = jnp.concatenate(pieces[count:])
            blocks = jnp.where(where[0] == group, mine, other)
            rows.append(jnp.zeros_like(blocks).at[chunks].set(blocks).transpose(1, 0, 2).reshape(PCAP, bands))
        return jnp.dot(projectors, jnp.concatenate(rows), preferred_element_type=jnp.float32).astype(jnp.bfloat16)

    def kernel(*refs):
        apply_kernel(chips, *refs)

    return pl.pallas_call(
        kernel,
        in_specs=[SMEM, VMEM] + [VMEM] * len(pieces),
        out_specs=HBM,
        out_shape=jax.ShapeDtypeStruct((depth, bands), jnp.bfloat16),
        scratch_shapes=[
            pltpu.VMEM((slots, bands), jnp.bfloat16),
            pltpu.VMEM((2, depth, COLUMNS), jnp.bfloat16),
            pltpu.SemaphoreType.DMA((2,)),
        ],
        compiler_params=PARAMS,
        cost_estimate=pl.CostEstimate(
            flops=2 * depth * slots * bands, bytes_accessed=2 * depth * (slots + bands), transcendentals=0
        ),
        name="apply",
    )(where, projectors, *pieces)


def local(band_coeffs, projectors, counts, atom_of, owners, couplings):
    chips = lax.axis_size("pw") // 2
    stages = chips.bit_length() - 1
    half = chips // 2
    width = band_coeffs.shape[1] // chips
    me = lax.axis_index("pw")
    where = jnp.stack([me % 2, me // 2, me])

    own_table = couplings[0]
    sibling_table = swap_cores(own_table)
    if width == LANES:
        theirs, ours, flipped, columns = project(where, projectors, band_coeffs, True)
    else:
        theirs, ours = project_plain(where, projectors, band_coeffs, half)
    near, far = choose(where, owners, own_table, sibling_table, theirs)
    theirs = swap_cores(theirs)
    far = swap_bits(far, [0, 0])
    if width == LANES:
        flipped, far = lax.optimization_barrier((flipped, far))
        low_theirs, low_ours = project(where, flipped, columns, False)
    else:
        low_theirs, low_ours = project_plain(where, projectors, band_coeffs, 0)
    message = add(ours, theirs)
    got = swap_stage(message, 0)
    low_theirs = swap_cores(low_theirs)
    allowed = mask(where, counts, atom_of, message)
    for stage in range(1, stages):
        near = merge(near, far, message)
        far = swap_bits(near, [stages - stage] * 2)
        if stage == 1:
            kept, message = fold(low_ours, low_theirs, got)
        else:
            kept, message = fold(kept, got)
        got = swap_stage(message, stage)
    near = merge(near, far, message)
    far = swap_bits(near, [0, 0])

    scaled = couple(where, kept, got, allowed, near, far)
    mine = jnp.concatenate([scaled, swap_stage(scaled, stages - 1)])
    pieces = [mine]
    others = [swap_cores(mine)]
    for stage in range(stages - 2, -1, -1):
        if stage < stages - 2:
            mine, others[0] = lax.optimization_barrier((mine, others[0]))
        got = swap_stage(mine, stage)
        got, others[-1] = lax.optimization_barrier((got, others[-1]))
        pieces.append(got)
        others.append(swap_cores(got))
        if stage:
            mine = jnp.concatenate([mine, got])
    return apply(where, projectors, pieces + others)


def solution(mesh):
    placed = (
        P("pw", "group"),
        P("pw", "group"),
        P("group", None),
        P("group", None),
        P("group"),
        P("pw", "group", None),
    )
    return jax.shard_map(
        local, mesh=mesh, in_specs=placed, out_specs=P("pw", "group"), check_vma=False
    )
```

```python
import jax
import jax.numpy as jnp
from jax import lax
from jax.experimental import pallas as pl
from jax.experimental.pallas import tpu as pltpu
from jax.sharding import PartitionSpec as P

CHANNELS = 4
CH_CAP = 64
PCAP = 256
LANES = 128
ROW_BLOCK = 512
PARAMS = pltpu.CompilerParams(vmem_limit_bytes=32 * 1024 * 1024)
VMEM = pl.BlockSpec(memory_space=pltpu.VMEM)
SMEM = pl.BlockSpec(memory_space=pltpu.SMEM)
HBM = pl.BlockSpec(memory_space=pltpu.HBM)
ANY = pl.BlockSpec(memory_space=pl.ANY)


def bit_order(chips, core):
    bits = list(range(chips.bit_length() - 1))
    if core == 1 and len(bits) > 2:
        bits[0], bits[1] = bits[1], bits[0]
    return bits


def offsets(chips, core):
    order = bit_order(chips, core)
    count = len(order)
    return [
        sum(((p >> (count - 1 - i)) & 1) << bit for i, bit in enumerate(order)) for p in range(chips)
    ]


def chunk_of(chips, chip, group, position):
    return chip ^ jnp.where(group == 0, offsets(chips, 0)[position], offsets(chips, 1)[position])


def swap_cores(x):
    count = lax.axis_size("pw")
    return lax.ppermute(x, "pw", [(i, i ^ 1) for i in range(count)])


def swap_bits(x, bits):
    count = lax.axis_size("pw")
    return lax.ppermute(x, "pw", [(i, i ^ (2 << bits[i % 2])) for i in range(count)])


def swap_stage(x, stage):
    chips = lax.axis_size("pw") // 2
    return swap_bits(x, [bit_order(chips, core)[stage] for core in range(2)])


def load_kernel(where, projectors, flipped, slots, sems):
    core = where[0]
    count = sems.shape[0]
    block = slots.shape[0] // count
    copies = []
    for at in range(count):
        rows = slice(at * block, (at + 1) * block)
        copies.append(pltpu.make_async_copy(projectors.at[rows], slots.at[rows], sems.at[at]))
        copies[-1].start()
    for at, copy in enumerate(copies):
        copy.wait()
        rows = slice(at * block, (at + 1) * block)
        for place, group in enumerate((core, 1 - core)):
            start = pl.multiple_of(group * PCAP, PCAP)
            flipped[place * PCAP : (place + 1) * PCAP, rows] = slots[rows, pl.ds(start, PCAP)].T


def load(where, projectors):
    depth, slots = projectors.shape
    return pl.pallas_call(
        load_kernel,
        in_specs=[SMEM, HBM],
        out_specs=VMEM,
        out_shape=jax.ShapeDtypeStruct((slots, depth), jnp.bfloat16),
        scratch_shapes=[pltpu.VMEM((depth, slots), jnp.bfloat16), pltpu.SemaphoreType.DMA((4,))],
        compiler_params=PARAMS,
        name="load",
    )(where, pltpu.with_memory_space_constraint(projectors, pltpu.HBM))


def project_kernel(chips, first, where, flipped, columns, theirs, ours):
    core, chip = where[0], where[1]
    half = chips // 2

    def pair_of_blocks(group, position):
        starts = [
            pl.multiple_of(chunk_of(chips, chip, group, position + at) * LANES, LANES) for at in range(2)
        ]
        return jnp.concatenate([columns[:, pl.ds(start, LANES)] for start in starts], axis=1)

    def keep(out, at, sums):
        out[at] = sums[:, :LANES].astype(out.dtype)
        out[at + 1] = sums[:, LANES:].astype(out.dtype)

    for at in range(half - 2, -1, -2):
        position = first + at
        if offsets(chips, 0)[position] == offsets(chips, 1)[position]:
            sums = jnp.dot(flipped[...], pair_of_blocks(core, position), preferred_element_type=jnp.float32)
            keep(ours, at, sums[:PCAP])
            keep(theirs, at, sums[PCAP:])
        else:
            for out, rows, group in ((ours, slice(0, PCAP), core), (theirs, slice(PCAP, 2 * PCAP), 1 - core)):
                keep(
                    out,
                    at,
                    jnp.dot(flipped[rows], pair_of_blocks(group, position), preferred_element_type=jnp.float32),
                )


def project(where, flipped, band_coeffs, first):
    depth, bands = band_coeffs.shape
    chips = lax.axis_size("pw") // 2
    half, width = chips // 2, bands // chips

    def kernel(*refs):
        project_kernel(chips, first, *refs)

    return pl.pallas_call(
        kernel,
        in_specs=[SMEM, VMEM, VMEM],
        out_specs=[VMEM, VMEM],
        out_shape=[
            jax.ShapeDtypeStruct((half, PCAP, width), jnp.bfloat16),
            jax.ShapeDtypeStruct((half, PCAP, width), jnp.float32),
        ],
        compiler_params=PARAMS,
        cost_estimate=pl.CostEstimate(
            flops=2 * depth * PCAP * bands, bytes_accessed=2 * depth * bands, transcendentals=0
        ),
        name="project",
    )(where, flipped, pltpu.with_memory_space_constraint(band_coeffs, pltpu.VMEM))


def project_plain(where, projectors, band_coeffs, first):
    depth, bands = band_coeffs.shape
    chips = lax.axis_size("pw") // 2
    half = chips // 2
    outs = []
    for group, dtype in ((1 - where[0], jnp.bfloat16), (where[0], jnp.float32)):
        chunks = jnp.stack([chunk_of(chips, where[1], group, first + at) for at in range(half)])
        slots = lax.dynamic_slice_in_dim(projectors, group * PCAP, PCAP, 1)
        columns = jnp.take(band_coeffs.reshape(depth, chips, bands // chips), chunks, axis=1)
        sums = jnp.einsum("ds,dhw->hsw", slots, columns, preferred_element_type=jnp.float32)
        outs.append(sums.astype(dtype))
    return outs


def fold_kernel(*refs):
    *terms, kept, message = refs
    half = kept.shape[0]
    for at in range(2 * half):
        total = terms[0][at]
        for term in terms[1:]:
            total = total + term[at].astype(jnp.float32)
        if at < half:
            kept[at] = total
        else:
            message[at - half] = total.astype(message.dtype)


def fold(*terms):
    count, rows, width = terms[0].shape
    return pl.pallas_call(
        fold_kernel,
        in_specs=[VMEM] * len(terms),
        out_specs=[VMEM, VMEM],
        out_shape=[
            jax.ShapeDtypeStruct((count // 2, rows, width), jnp.float32),
            jax.ShapeDtypeStruct((count // 2, rows, width), jnp.bfloat16),
        ],
        compiler_params=PARAMS,
        name="fold",
    )(*terms)


def add_kernel(left, right, out):
    for at in range(out.shape[0]):
        out[at] = (left[at] + right[at].astype(jnp.float32)).astype(out.dtype)


def add(left, right):
    return pl.pallas_call(
        add_kernel,
        in_specs=[VMEM, VMEM],
        out_specs=VMEM,
        out_shape=jax.ShapeDtypeStruct(left.shape, jnp.bfloat16),
        compiler_params=PARAMS,
        name="add",
    )(left, right)


def choose_kernel(where, owners, own, sibling, after, kept, sent):
    del after
    core, chip, me = where[0], where[1], where[2]
    owner = jnp.where(core == 0, owners[0], owners[1])
    half = PCAP // 2
    side = chip & 1
    for out, which in ((kept, side), (sent, 1 - side)):
        rows = pl.ds(pl.multiple_of(which * half, half), half)
        part = jnp.where(owner == me, own[rows], jnp.where(owner == (me ^ 1), sibling[rows], 0.0))
        out[...] = part.astype(out.dtype)


def choose(where, owners, own, sibling, after):
    shape = jax.ShapeDtypeStruct((PCAP // 2, PCAP), jnp.bfloat16)
    return pl.pallas_call(
        choose_kernel,
        in_specs=[SMEM, SMEM, VMEM, VMEM, ANY],
        out_specs=[VMEM, VMEM],
        out_shape=[shape, shape],
        compiler_params=PARAMS,
        name="choose",
    )(where, owners, own, sibling, after)


def merge_kernel(left, right, after, out):
    del after
    out[...] = left[...] + right[...]


def merge(left, right, after):
    return pl.pallas_call(
        merge_kernel,
        in_specs=[VMEM, VMEM, ANY],
        out_specs=VMEM,
        out_shape=jax.ShapeDtypeStruct(left.shape, left.dtype),
        compiler_params=PARAMS,
        name="merge",
    )(left, right, after)


def mask_kernel(where, counts, atom_of, after, out):
    del after
    core = where[0]
    slot = lax.broadcasted_iota(jnp.int32, (1, PCAP), 1)
    limit = jnp.zeros((1, PCAP), jnp.int32)
    for channel in range(CHANNELS):
        limit = jnp.where(slot >= channel * CH_CAP, channel * CH_CAP + counts[core, channel], limit)
    atoms = jnp.where(core == 0, atom_of[0:1], atom_of[1:2])
    code = jnp.broadcast_to(jnp.where(slot < limit, atoms, -1), (PCAP, PCAP))
    out[...] = jnp.where((code == code.T) & (code >= 0), 1.0, 0.0).astype(out.dtype)


def mask(where, counts, atom_of, after):
    return pl.pallas_call(
        mask_kernel,
        in_specs=[SMEM, SMEM, VMEM, ANY],
        out_specs=VMEM,
        out_shape=jax.ShapeDtypeStruct((PCAP, PCAP), jnp.bfloat16),
        compiler_params=PARAMS,
        name="mask",
    )(where, counts, atom_of, after)


def couple_kernel(where, kept, got, allowed, near, far, out, table):
    half = PCAP // 2
    width = out.shape[2]
    side = where[1] & 1
    for part, which in ((near, side), (far, 1 - side)):
        rows = pl.ds(pl.multiple_of(which * half, half), half)
        table[rows] = part[...] * allowed[rows]
    total = kept[0] + got[0].astype(jnp.float32)
    high = total.astype(jnp.bfloat16)
    low = (total - high.astype(jnp.float32)).astype(jnp.bfloat16)
    both = jnp.dot(table[...], jnp.concatenate([high, low], axis=1), preferred_element_type=jnp.float32)
    out[0] = (both[:, :width] + both[:, width:]).astype(out.dtype)


def couple(where, kept, got, allowed, near, far):
    return pl.pallas_call(
        couple_kernel,
        in_specs=[SMEM] + [VMEM] * 5,
        out_specs=VMEM,
        out_shape=jax.ShapeDtypeStruct(kept.shape, jnp.bfloat16),
        scratch_shapes=[pltpu.VMEM((PCAP, PCAP), jnp.bfloat16)],
        compiler_params=PARAMS,
        name="couple",
    )(where, kept, got, allowed, near, far)


def place(scaled, core, own, other):
    for part, group in ((own, core), (other, 1 - core)):
        rows = pl.ds(pl.multiple_of(group * PCAP, PCAP), PCAP)
        scaled[rows, :LANES] = part[0]
        scaled[rows, LANES:] = part[1]


def begin_kernel(where, projectors, own_first, own_second, other_first, other_second, done, own, other, scaled):
    core = where[0]
    place(scaled, core, own_first[...], other_first[...])
    for block in range(projectors.shape[0] // ROW_BLOCK):
        rows = slice(block * ROW_BLOCK, (block + 1) * ROW_BLOCK)
        done[rows] = jnp.dot(projectors[rows], scaled[...], preferred_element_type=jnp.float32).astype(done.dtype)
        for out, part, group in ((own, own_second, core), (other, other_second, 1 - core)):
            slots = pl.ds(pl.multiple_of(group * PCAP, PCAP), PCAP)
            weights = jnp.concatenate([part[0], part[1]], axis=1)
            out[rows] = jnp.dot(projectors[rows, slots], weights, preferred_element_type=jnp.float32)


def begin(where, projectors, own_first, own_second, other_first, other_second):
    depth, slots = projectors.shape
    pair = 2 * LANES
    return pl.pallas_call(
        begin_kernel,
        in_specs=[SMEM] + [VMEM] * 5,
        out_specs=[VMEM] * 3,
        out_shape=[
            jax.ShapeDtypeStruct((depth, pair), jnp.bfloat16),
            jax.ShapeDtypeStruct((depth, pair), jnp.float32),
            jax.ShapeDtypeStruct((depth, pair), jnp.float32),
        ],
        scratch_shapes=[pltpu.VMEM((slots, pair), jnp.bfloat16)],
        compiler_params=PARAMS,
        cost_estimate=pl.CostEstimate(
            flops=4 * depth * slots * pair, bytes_accessed=2 * depth * slots, transcendentals=0
        ),
        name="begin",
    )(where, projectors, own_first, own_second, other_first, other_second)


def finish_kernel(chips, where, projectors, done, own, other, own_rest, other_rest, out, scaled, blocks, sems):
    core, chip = where[0], where[1]
    place(scaled, core, own_rest[2:], other_rest[2:])
    copies = []
    for block in range(projectors.shape[0] // ROW_BLOCK):
        rows = slice(block * ROW_BLOCK, (block + 1) * ROW_BLOCK)
        slot = block % 2
        if block >= 2:
            copies[block - 2].wait()

        def put(group, position, sums):
            for at in range(2):
                start = pl.multiple_of(chunk_of(chips, chip, group, position + at) * LANES, LANES)
                blocks[slot, :, pl.ds(start, LANES)] = sums[:, at * LANES : (at + 1) * LANES].astype(blocks.dtype)

        put(core, 0, done[rows])
        put(core, 6, jnp.dot(projectors[rows], scaled[...], preferred_element_type=jnp.float32))
        for partial, part, group in ((own, other_rest, 1 - core), (other, own_rest, core)):
            slots = pl.ds(pl.multiple_of(group * PCAP, PCAP), PCAP)
            weights = jnp.concatenate([part[0], part[1]], axis=1)
            put(
                group,
                4,
                partial[rows] + jnp.dot(projectors[rows, slots], weights, preferred_element_type=jnp.float32),
            )
        copies.append(pltpu.make_async_copy(blocks.at[slot], out.at[rows], sems.at[slot]))
        copies[-1].start()
    for copy in copies[-2:]:
        copy.wait()


def finish(where, projectors, done, own, other, own_rest, other_rest):
    depth, slots = projectors.shape
    chips = lax.axis_size("pw") // 2
    bands = chips * LANES

    def kernel(*refs):
        finish_kernel(chips, *refs)

    return pl.pallas_call(
        kernel,
        in_specs=[SMEM] + [VMEM] * 6,
        out_specs=HBM,
        out_shape=jax.ShapeDtypeStruct((depth, bands), jnp.bfloat16),
        scratch_shapes=[
            pltpu.VMEM((slots, 2 * LANES), jnp.bfloat16),
            pltpu.VMEM((2, ROW_BLOCK, bands), jnp.bfloat16),
            pltpu.SemaphoreType.DMA((2,)),
        ],
        compiler_params=PARAMS,
        cost_estimate=pl.CostEstimate(
            flops=depth * slots * bands, bytes_accessed=2 * depth * (slots + bands), transcendentals=0
        ),
        name="finish",
    )(where, projectors, done, own, other, own_rest, other_rest)


def apply_plain(where, projectors, mine, other):
    chips, _, width = mine.shape
    rows = []
    for group in range(2):
        chunks = jnp.stack([chunk_of(chips, where[1], group, at) for at in range(chips)])
        blocks = jnp.where(where[0] == group, mine, other)
        blocks = jnp.zeros_like(blocks).at[chunks].set(blocks)
        rows.append(blocks.transpose(1, 0, 2).reshape(PCAP, chips * width))
    return jnp.dot(projectors, jnp.concatenate(rows), preferred_element_type=jnp.float32).astype(jnp.bfloat16)


def local(band_coeffs, projectors, counts, atom_of, owners, couplings):
    chips = lax.axis_size("pw") // 2
    stages = chips.bit_length() - 1
    half = chips // 2
    width = band_coeffs.shape[1] // chips
    me = lax.axis_index("pw")
    where = jnp.stack([me % 2, me // 2, me])

    fast = width == LANES and stages == 3
    own_table = couplings[0]
    sibling_table = swap_cores(own_table)
    if fast:
        flipped = load(where, projectors)
    else:
        flipped = projectors
    near, far = choose(where, owners, own_table, sibling_table, flipped)
    far = swap_bits(far, [0, 0])
    if fast:
        flipped, near = lax.optimization_barrier((flipped, near))
        theirs, ours = project(where, flipped, band_coeffs, half)
    else:
        theirs, ours = project_plain(where, projectors, band_coeffs, half)
    theirs = swap_cores(theirs)
    near = merge(near, far, ours)
    theirs, near = lax.optimization_barrier((theirs, near))
    far = swap_bits(near, [stages - 1] * 2)
    message = add(ours, theirs)
    got = swap_stage(message, 0)
    if fast:
        low_theirs, low_ours = project(where, flipped, band_coeffs, 0)
    else:
        low_theirs, low_ours = project_plain(where, projectors, band_coeffs, 0)
    low_theirs = swap_cores(low_theirs)
    allowed = mask(where, counts, atom_of, message)
    for stage in range(1, stages):
        near = merge(near, far, message)
        got, near = lax.optimization_barrier((got, near))
        far = swap_bits(near, [stages - 1 - stage] * 2)
        if stage == 1:
            kept, message = fold(low_ours, low_theirs, got)
        else:
            kept, message = fold(kept, got)
        got = swap_stage(message, stage)

    scaled = couple(where, kept, got, allowed, near, far)
    mine = jnp.concatenate([scaled, swap_stage(scaled, stages - 1)])
    pieces = [mine]
    others = [swap_cores(mine)]
    for stage in range(stages - 2, -1, -1):
        if stage < stages - 2:
            mine, others[0] = lax.optimization_barrier((mine, others[0]))
        got = swap_stage(mine, stage)
        got, others[-1] = lax.optimization_barrier((got, others[-1]))
        pieces.append(got)
        others.append(swap_cores(got))
        if stage:
            mine = jnp.concatenate([mine, got])
    if not fast:
        return apply_plain(where, projectors, jnp.concatenate(pieces), jnp.concatenate(others))
    begun = begin(where, projectors, *pieces[:2], *others[:2])
    return finish(where, projectors, *begun, pieces[2], others[2])


def solution(mesh):
    placed = (
        P("pw", "group"),
        P("pw", "group"),
        P("group", None),
        P("group", None),
        P("group"),
        P("pw", "group", None),
    )
    return jax.shard_map(
        local, mesh=mesh, in_specs=placed, out_specs=P("pw", "group"), check_vma=False
    )
```

```python
import jax
import jax.numpy as jnp
from jax import lax
from jax.experimental import pallas as pl
from jax.experimental.pallas import tpu as pltpu
from jax.sharding import PartitionSpec as P

CHANNELS = 4
CH_CAP = 64
PCAP = 256
LANES = 128
ROW_BLOCK = 512
COPY_ROWS = 128
PARAMS = pltpu.CompilerParams(vmem_limit_bytes=32 * 1024 * 1024)
VMEM = pl.BlockSpec(memory_space=pltpu.VMEM)
SMEM = pl.BlockSpec(memory_space=pltpu.SMEM)
HBM = pl.BlockSpec(memory_space=pltpu.HBM)
ANY = pl.BlockSpec(memory_space=pl.ANY)


def bit_order(chips, core):
    bits = list(range(chips.bit_length() - 1))
    if core == 1 and len(bits) > 2:
        bits[0], bits[1] = bits[1], bits[0]
    return bits


def offsets(chips, core):
    order = bit_order(chips, core)
    count = len(order)
    return [
        sum(((p >> (count - 1 - i)) & 1) << bit for i, bit in enumerate(order)) for p in range(chips)
    ]


def chunk_of(chips, chip, group, position):
    return chip ^ jnp.where(group == 0, offsets(chips, 0)[position], offsets(chips, 1)[position])


def swap_cores(x):
    count = lax.axis_size("pw")
    return lax.ppermute(x, "pw", [(i, i ^ 1) for i in range(count)])


def swap_bits(x, bits):
    count = lax.axis_size("pw")
    return lax.ppermute(x, "pw", [(i, i ^ (2 << bits[i % 2])) for i in range(count)])


def swap_stage(x, stage):
    chips = lax.axis_size("pw") // 2
    return swap_bits(x, [bit_order(chips, core)[stage] for core in range(2)])


def load_kernel(where, projectors, flipped, slots, sems):
    core = where[0]
    count = sems.shape[0]
    block = slots.shape[0] // count
    copies = []
    for at in range(count):
        rows = slice(at * block, (at + 1) * block)
        copies.append(pltpu.make_async_copy(projectors.at[rows], slots.at[rows], sems.at[at]))
        copies[-1].start()
    for at, copy in enumerate(copies):
        copy.wait()
        rows = slice(at * block, (at + 1) * block)
        for place, group in enumerate((core, 1 - core)):
            start = pl.multiple_of(group * PCAP, PCAP)
            flipped[place * PCAP : (place + 1) * PCAP, rows] = slots[rows, pl.ds(start, PCAP)].T


def load(where, projectors):
    depth, slots = projectors.shape
    return pl.pallas_call(
        load_kernel,
        in_specs=[SMEM, HBM],
        out_specs=VMEM,
        out_shape=jax.ShapeDtypeStruct((slots, depth), jnp.bfloat16),
        scratch_shapes=[pltpu.VMEM((depth, slots), jnp.bfloat16), pltpu.SemaphoreType.DMA((4,))],
        compiler_params=PARAMS,
        name="load",
    )(where, pltpu.with_memory_space_constraint(projectors, pltpu.HBM))


def project_kernel(chips, first, where, flipped, columns, theirs, ours):
    core, chip = where[0], where[1]
    half = chips // 2

    def pair_of_blocks(group, position):
        starts = [
            pl.multiple_of(chunk_of(chips, chip, group, position + at) * LANES, LANES) for at in range(2)
        ]
        return jnp.concatenate([columns[:, pl.ds(start, LANES)] for start in starts], axis=1)

    def keep(out, at, sums):
        out[at] = sums[:, :LANES].astype(out.dtype)
        out[at + 1] = sums[:, LANES:].astype(out.dtype)

    for at in range(half - 2, -1, -2):
        position = first + at
        if offsets(chips, 0)[position] == offsets(chips, 1)[position]:
            sums = jnp.dot(flipped[...], pair_of_blocks(core, position), preferred_element_type=jnp.float32)
            keep(ours, at, sums[:PCAP])
            keep(theirs, at, sums[PCAP:])
        else:
            for out, rows, group in ((ours, slice(0, PCAP), core), (theirs, slice(PCAP, 2 * PCAP), 1 - core)):
                keep(
                    out,
                    at,
                    jnp.dot(flipped[rows], pair_of_blocks(group, position), preferred_element_type=jnp.float32),
                )


def project(where, flipped, band_coeffs, first):
    depth, bands = band_coeffs.shape
    chips = lax.axis_size("pw") // 2
    half, width = chips // 2, bands // chips

    def kernel(*refs):
        project_kernel(chips, first, *refs)

    return pl.pallas_call(
        kernel,
        in_specs=[SMEM, VMEM, VMEM],
        out_specs=[VMEM, VMEM],
        out_shape=[
            jax.ShapeDtypeStruct((half, PCAP, width), jnp.bfloat16),
            jax.ShapeDtypeStruct((half, PCAP, width), jnp.float32),
        ],
        compiler_params=PARAMS,
        cost_estimate=pl.CostEstimate(
            flops=2 * depth * PCAP * bands, bytes_accessed=2 * depth * bands, transcendentals=0
        ),
        name="project",
    )(where, flipped, pltpu.with_memory_space_constraint(band_coeffs, pltpu.VMEM))


def project_plain(where, projectors, band_coeffs, first):
    depth, bands = band_coeffs.shape
    chips = lax.axis_size("pw") // 2
    half = chips // 2
    outs = []
    for group, dtype in ((1 - where[0], jnp.bfloat16), (where[0], jnp.float32)):
        chunks = jnp.stack([chunk_of(chips, where[1], group, first + at) for at in range(half)])
        slots = lax.dynamic_slice_in_dim(projectors, group * PCAP, PCAP, 1)
        columns = jnp.take(band_coeffs.reshape(depth, chips, bands // chips), chunks, axis=1)
        sums = jnp.einsum("ds,dhw->hsw", slots, columns, preferred_element_type=jnp.float32)
        outs.append(sums.astype(dtype))
    return outs


def fold_kernel(*refs):
    *terms, kept, message = refs
    half = kept.shape[0]
    for at in range(2 * half):
        total = terms[0][at]
        for term in terms[1:]:
            total = total + term[at].astype(jnp.float32)
        if at < half:
            kept[at] = total
        else:
            message[at - half] = total.astype(message.dtype)


def fold(*terms):
    count, rows, width = terms[0].shape
    return pl.pallas_call(
        fold_kernel,
        in_specs=[VMEM] * len(terms),
        out_specs=[VMEM, VMEM],
        out_shape=[
            jax.ShapeDtypeStruct((count // 2, rows, width), jnp.float32),
            jax.ShapeDtypeStruct((count // 2, rows, width), jnp.bfloat16),
        ],
        compiler_params=PARAMS,
        name="fold",
    )(*terms)


def add_kernel(left, right, out):
    for at in range(out.shape[0]):
        out[at] = (left[at] + right[at].astype(jnp.float32)).astype(out.dtype)


def add(left, right):
    return pl.pallas_call(
        add_kernel,
        in_specs=[VMEM, VMEM],
        out_specs=VMEM,
        out_shape=jax.ShapeDtypeStruct(left.shape, jnp.bfloat16),
        compiler_params=PARAMS,
        name="add",
    )(left, right)


def halve_kernel(where, table, kept, sent, rows, sems):
    half = PCAP // 2
    side = where[1] & 1
    copies = []
    for at, which in enumerate((1 - side, side)):
        start = pl.multiple_of(which * half, half)
        copies.append(pltpu.make_async_copy(table.at[0, pl.ds(start, half)], rows.at[at], sems.at[at]))
        copies[-1].start()
    for at, out in enumerate((sent, kept)):
        copies[at].wait()
        out[...] = rows[at].astype(out.dtype)


def halve(where, couplings):
    half = PCAP // 2
    shape = jax.ShapeDtypeStruct((half, PCAP), jnp.bfloat16)
    return pl.pallas_call(
        halve_kernel,
        in_specs=[SMEM, HBM],
        out_specs=[VMEM, VMEM],
        out_shape=[shape, shape],
        scratch_shapes=[pltpu.VMEM((2, half, PCAP), jnp.float32), pltpu.SemaphoreType.DMA((2,))],
        compiler_params=PARAMS,
        name="halve",
    )(where, pltpu.with_memory_space_constraint(couplings, pltpu.HBM))


def choose_kernel(where, owners, kept, got, after, near, sent):
    del after
    core, me = where[0], where[2]
    for out, group in ((near, core), (sent, 1 - core)):
        owner = jnp.where(group == 0, owners[0], owners[1])
        out[...] = jnp.where(owner == me, kept[...], jnp.where(owner == (me ^ 2), got[...], jnp.zeros_like(got)))


def choose(where, owners, kept, got, after):
    shape = jax.ShapeDtypeStruct(kept.shape, kept.dtype)
    return pl.pallas_call(
        choose_kernel,
        in_specs=[SMEM, SMEM, VMEM, VMEM, ANY],
        out_specs=[VMEM, VMEM],
        out_shape=[shape, shape],
        compiler_params=PARAMS,
        name="choose",
    )(where, owners, kept, got, after)


def merge_kernel(left, right, after, out):
    del after
    out[...] = left[...] + right[...]


def merge(left, right, after):
    return pl.pallas_call(
        merge_kernel,
        in_specs=[VMEM, VMEM, ANY],
        out_specs=VMEM,
        out_shape=jax.ShapeDtypeStruct(left.shape, left.dtype),
        compiler_params=PARAMS,
        name="merge",
    )(left, right, after)


def mask_kernel(where, counts, atom_of, after, out):
    del after
    core = where[0]
    slot = lax.broadcasted_iota(jnp.int32, (1, PCAP), 1)
    limit = jnp.zeros((1, PCAP), jnp.int32)
    for channel in range(CHANNELS):
        limit = jnp.where(slot >= channel * CH_CAP, channel * CH_CAP + counts[core, channel], limit)
    atoms = jnp.where(core == 0, atom_of[0:1], atom_of[1:2])
    code = jnp.broadcast_to(jnp.where(slot < limit, atoms, -1), (PCAP, PCAP))
    out[...] = jnp.where((code == code.T) & (code >= 0), 1.0, 0.0).astype(out.dtype)


def mask(where, counts, atom_of, after):
    return pl.pallas_call(
        mask_kernel,
        in_specs=[SMEM, SMEM, VMEM, ANY],
        out_specs=VMEM,
        out_shape=jax.ShapeDtypeStruct((PCAP, PCAP), jnp.bfloat16),
        compiler_params=PARAMS,
        name="mask",
    )(where, counts, atom_of, after)


def couple_kernel(where, kept, got, allowed, near, far, out, table):
    half = PCAP // 2
    width = out.shape[2]
    side = where[1] & 1
    for part, which in ((near, side), (far, 1 - side)):
        rows = pl.ds(pl.multiple_of(which * half, half), half)
        table[rows] = part[...] * allowed[rows]
    total = kept[0] + got[0].astype(jnp.float32)
    high = total.astype(jnp.bfloat16)
    low = (total - high.astype(jnp.float32)).astype(jnp.bfloat16)
    both = jnp.dot(table[...], jnp.concatenate([high, low], axis=1), preferred_element_type=jnp.float32)
    out[0] = (both[:, :width] + both[:, width:]).astype(out.dtype)


def couple(where, kept, got, allowed, near, far):
    return pl.pallas_call(
        couple_kernel,
        in_specs=[SMEM] + [VMEM] * 5,
        out_specs=VMEM,
        out_shape=jax.ShapeDtypeStruct(kept.shape, jnp.bfloat16),
        scratch_shapes=[pltpu.VMEM((PCAP, PCAP), jnp.bfloat16)],
        compiler_params=PARAMS,
        name="couple",
    )(where, kept, got, allowed, near, far)


def place(scaled, core, own, other):
    for part, group in ((own, core), (other, 1 - core)):
        rows = pl.ds(pl.multiple_of(group * PCAP, PCAP), PCAP)
        scaled[rows, :LANES] = part[0]
        scaled[rows, LANES:] = part[1]


def begin_kernel(where, projectors, own, first, second, held):
    slots = pl.ds(pl.multiple_of(where[0] * PCAP, PCAP), PCAP)
    held[...] = own[...]
    for out, at in ((first, 0), (second, 2)):
        weights = jnp.concatenate([own[at], own[at + 1]], axis=1)
        for block in range(projectors.shape[0] // ROW_BLOCK):
            rows = slice(block * ROW_BLOCK, (block + 1) * ROW_BLOCK)
            out[rows] = jnp.dot(projectors[rows, slots], weights, preferred_element_type=jnp.float32)


def begin(where, projectors, own):
    depth, slots = projectors.shape
    shape = jax.ShapeDtypeStruct((depth, 2 * LANES), jnp.float32)

    return pl.pallas_call(
        begin_kernel,
        in_specs=[SMEM, VMEM, VMEM],
        out_specs=[VMEM] * 3,
        out_shape=[shape, shape, jax.ShapeDtypeStruct(own.shape, own.dtype)],
        compiler_params=PARAMS,
        cost_estimate=pl.CostEstimate(
            flops=4 * depth * slots * LANES, bytes_accessed=2 * depth * slots, transcendentals=0
        ),
        name="begin",
    )(where, projectors, own)


def extend_kernel(where, projectors, partial, other, done, second):
    slots = pl.ds(pl.multiple_of((1 - where[0]) * PCAP, PCAP), PCAP)
    for out, at in ((done, 0), (second, 2)):
        weights = jnp.concatenate([other[at], other[at + 1]], axis=1)
        for block in range(projectors.shape[0] // ROW_BLOCK):
            rows = slice(block * ROW_BLOCK, (block + 1) * ROW_BLOCK)
            sums = jnp.dot(projectors[rows, slots], weights, preferred_element_type=jnp.float32)
            if at == 0:
                sums = sums + partial[rows]
            out[rows] = sums.astype(out.dtype)


def extend(where, projectors, partial, other):
    depth, slots = projectors.shape
    pair = 2 * LANES
    return pl.pallas_call(
        extend_kernel,
        in_specs=[SMEM, VMEM, VMEM, VMEM],
        out_specs=[VMEM] * 2,
        out_shape=[
            jax.ShapeDtypeStruct((depth, pair), jnp.bfloat16),
            jax.ShapeDtypeStruct((depth, pair), jnp.float32),
        ],
        compiler_params=PARAMS,
        cost_estimate=pl.CostEstimate(
            flops=4 * depth * slots * LANES, bytes_accessed=2 * depth * slots, transcendentals=0
        ),
        name="extend",
    )(where, projectors, partial, other)


def finish_kernel(chips, where, projectors, done, own, other, own_rest, other_rest, out, scaled, blocks, sems):
    core, chip = where[0], where[1]
    place(scaled, core, own_rest[2:], other_rest[2:])
    copies = []

    def put(rows, group, position, sums):
        for at in range(2):
            start = pl.multiple_of(chunk_of(chips, chip, group, position + at) * LANES, LANES)
            blocks[rows, pl.ds(start, LANES)] = sums[:, at * LANES : (at + 1) * LANES].astype(blocks.dtype)

    for block in range(projectors.shape[0] // ROW_BLOCK):
        rows = slice(block * ROW_BLOCK, (block + 1) * ROW_BLOCK)
        put(rows, core, 0, done[rows])
        put(rows, core, 6, jnp.dot(projectors[rows], scaled[...], preferred_element_type=jnp.float32))
        for partial, part, group in ((own, other_rest, 1 - core), (other, own_rest, core)):
            slots = pl.ds(pl.multiple_of(group * PCAP, PCAP), PCAP)
            weights = jnp.concatenate([part[0], part[1]], axis=1)
            sums = jnp.dot(projectors[rows, slots], weights, preferred_element_type=jnp.float32)
            put(rows, group, 4, partial[rows] + sums)
        for piece in range(ROW_BLOCK // COPY_ROWS):
            start = block * ROW_BLOCK + piece * COPY_ROWS
            written = slice(start, start + COPY_ROWS)
            copies.append(pltpu.make_async_copy(blocks.at[written], out.at[written], sems.at[len(copies)]))
            copies[-1].start()
    for copy in copies:
        copy.wait()


def finish(where, projectors, done, own, other, own_rest, other_rest):
    depth, slots = projectors.shape
    chips = lax.axis_size("pw") // 2
    bands = chips * LANES

    def kernel(*refs):
        finish_kernel(chips, *refs)

    return pl.pallas_call(
        kernel,
        in_specs=[SMEM] + [VMEM] * 6,
        out_specs=HBM,
        out_shape=jax.ShapeDtypeStruct((depth, bands), jnp.bfloat16),
        scratch_shapes=[
            pltpu.VMEM((slots, 2 * LANES), jnp.bfloat16),
            pltpu.VMEM((depth, bands), jnp.bfloat16),
            pltpu.SemaphoreType.DMA((depth // COPY_ROWS,)),
        ],
        compiler_params=PARAMS,
        cost_estimate=pl.CostEstimate(
            flops=depth * slots * bands, bytes_accessed=2 * depth * (slots + bands), transcendentals=0
        ),
        name="finish",
    )(where, projectors, done, own, other, own_rest, other_rest)


def apply_plain(where, projectors, mine, other):
    chips, _, width = mine.shape
    rows = []
    for group in range(2):
        chunks = jnp.stack([chunk_of(chips, where[1], group, at) for at in range(chips)])
        blocks = jnp.where(where[0] == group, mine, other)
        blocks = jnp.zeros_like(blocks).at[chunks].set(blocks)
        rows.append(blocks.transpose(1, 0, 2).reshape(PCAP, chips * width))
    return jnp.dot(projectors, jnp.concatenate(rows), preferred_element_type=jnp.float32).astype(jnp.bfloat16)


def local(band_coeffs, projectors, counts, atom_of, owners, couplings):
    chips = lax.axis_size("pw") // 2
    stages = chips.bit_length() - 1
    half = chips // 2
    width = band_coeffs.shape[1] // chips
    me = lax.axis_index("pw")
    where = jnp.stack([me % 2, me // 2, me])

    fast = width == LANES and stages == 3
    kept, sent = halve(where, couplings)
    early, sent = lax.optimization_barrier((projectors, sent))
    got = swap_bits(sent, [0, 0])
    if fast:
        flipped = load(where, early)
        flipped, got = lax.optimization_barrier((flipped, got))
        theirs, ours = project(where, flipped, band_coeffs, half)
    else:
        theirs, ours = project_plain(where, projectors, band_coeffs, half)
    near, far = choose(where, owners, kept, got, ours)
    theirs = swap_cores(theirs)
    far = swap_cores(far)
    message = add(ours, theirs)
    near = merge(near, far, message)
    got = swap_stage(message, 0)
    far = swap_bits(near, [stages - 1] * 2)
    if fast:
        flipped, near = lax.optimization_barrier((flipped, near))
        low_theirs, low_ours = project(where, flipped, band_coeffs, 0)
    else:
        low_theirs, low_ours = project_plain(where, projectors, band_coeffs, 0)
    near = merge(near, far, message)
    low_theirs, near = lax.optimization_barrier((low_theirs, near))
    low_theirs = swap_cores(low_theirs)
    allowed = mask(where, counts, atom_of, message)
    for stage in range(1, stages):
        far = swap_bits(near, [stages - 1 - stage] * 2)
        if stage == 1:
            kept, message = fold(low_ours, low_theirs, got)
        else:
            kept, message = fold(kept, got)
        got = swap_stage(message, stage)
        if stage < stages - 1:
            near = merge(near, far, message)
            got, near = lax.optimization_barrier((got, near))

    scaled = couple(where, kept, got, allowed, near, far)
    mine = jnp.concatenate([scaled, swap_stage(scaled, stages - 1)])
    for stage in range(stages - 2, 0, -1):
        mine = jnp.concatenate([mine, swap_stage(mine, stage)])
    got = swap_stage(mine, 0)
    if not fast:
        mine = jnp.concatenate([mine, got])
        return apply_plain(where, projectors, mine, swap_cores(mine))
    first, own, held = begin(where, projectors, mine)
    done, other = extend(where, projectors, first, swap_cores(held))
    got, done = lax.optimization_barrier((got, done))
    return finish(where, projectors, done, own, other, got, swap_cores(got))


def solution(mesh):
    placed = (
        P("pw", "group"),
        P("pw", "group"),
        P("group", None),
        P("group", None),
        P("group"),
        P("pw", "group", None),
    )
    return jax.shard_map(
        local, mesh=mesh, in_specs=placed, out_specs=P("pw", "group"), check_vma=False
    )
```

```python
import jax
import jax.numpy as jnp
from jax import lax
from jax.experimental import pallas as pl
from jax.experimental.pallas import tpu as pltpu
from jax.sharding import PartitionSpec as P

CHANNELS = 4
CH_CAP = 64
PCAP = 256
LANES = 128
ROW_BLOCK = 512
COPY_ROWS = 128
PARAMS = pltpu.CompilerParams(vmem_limit_bytes=32 * 1024 * 1024)
VMEM = pl.BlockSpec(memory_space=pltpu.VMEM)
SMEM = pl.BlockSpec(memory_space=pltpu.SMEM)
HBM = pl.BlockSpec(memory_space=pltpu.HBM)
ANY = pl.BlockSpec(memory_space=pl.ANY)


def bit_order(chips, core):
    bits = list(range(chips.bit_length() - 1))
    if core == 1 and len(bits) > 2:
        bits[0], bits[1] = bits[1], bits[0]
    return bits


def offsets(chips, core):
    order = bit_order(chips, core)
    count = len(order)
    return [
        sum(((p >> (count - 1 - i)) & 1) << bit for i, bit in enumerate(order)) for p in range(chips)
    ]


def chunk_of(chips, chip, group, position):
    return chip ^ jnp.where(group == 0, offsets(chips, 0)[position], offsets(chips, 1)[position])


def swap_cores(x):
    count = lax.axis_size("pw")
    return lax.ppermute(x, "pw", [(i, i ^ 1) for i in range(count)])


def swap_bits(x, bits):
    count = lax.axis_size("pw")
    return lax.ppermute(x, "pw", [(i, i ^ (2 << bits[i % 2])) for i in range(count)])


def swap_stage(x, stage):
    chips = lax.axis_size("pw") // 2
    return swap_bits(x, [bit_order(chips, core)[stage] for core in range(2)])


def load_kernel(where, projectors, flipped, slots, sems):
    core = where[0]
    count = sems.shape[0]
    block = slots.shape[0] // count
    copies = []
    for at in range(count):
        rows = slice(at * block, (at + 1) * block)
        copies.append(pltpu.make_async_copy(projectors.at[rows], slots.at[rows], sems.at[at]))
        copies[-1].start()
    for at, copy in enumerate(copies):
        copy.wait()
        rows = slice(at * block, (at + 1) * block)
        for place, group in enumerate((core, 1 - core)):
            start = pl.multiple_of(group * PCAP, PCAP)
            flipped[place * PCAP : (place + 1) * PCAP, rows] = slots[rows, pl.ds(start, PCAP)].T


def load(where, projectors):
    depth, slots = projectors.shape
    return pl.pallas_call(
        load_kernel,
        in_specs=[SMEM, HBM],
        out_specs=VMEM,
        out_shape=jax.ShapeDtypeStruct((slots, depth), jnp.bfloat16),
        scratch_shapes=[pltpu.VMEM((depth, slots), jnp.bfloat16), pltpu.SemaphoreType.DMA((4,))],
        compiler_params=PARAMS,
        name="load",
    )(where, pltpu.with_memory_space_constraint(projectors, pltpu.HBM))


def project_kernel(chips, first, where, flipped, columns, theirs, ours):
    core, chip = where[0], where[1]
    half = chips // 2

    def pair_of_blocks(group, position):
        starts = [
            pl.multiple_of(chunk_of(chips, chip, group, position + at) * LANES, LANES) for at in range(2)
        ]
        return jnp.concatenate([columns[:, pl.ds(start, LANES)] for start in starts], axis=1)

    def keep(out, at, sums):
        out[at] = sums[:, :LANES].astype(out.dtype)
        out[at + 1] = sums[:, LANES:].astype(out.dtype)

    for at in range(half - 2, -1, -2):
        position = first + at
        if offsets(chips, 0)[position] == offsets(chips, 1)[position]:
            sums = jnp.dot(flipped[...], pair_of_blocks(core, position), preferred_element_type=jnp.float32)
            keep(ours, at, sums[:PCAP])
            keep(theirs, at, sums[PCAP:])
        else:
            for out, rows, group in ((ours, slice(0, PCAP), core), (theirs, slice(PCAP, 2 * PCAP), 1 - core)):
                keep(
                    out,
                    at,
                    jnp.dot(flipped[rows], pair_of_blocks(group, position), preferred_element_type=jnp.float32),
                )


def project(where, flipped, band_coeffs, first):
    depth, bands = band_coeffs.shape
    chips = lax.axis_size("pw") // 2
    half, width = chips // 2, bands // chips

    def kernel(*refs):
        project_kernel(chips, first, *refs)

    return pl.pallas_call(
        kernel,
        in_specs=[SMEM, VMEM, VMEM],
        out_specs=[VMEM, VMEM],
        out_shape=[
            jax.ShapeDtypeStruct((half, PCAP, width), jnp.bfloat16),
            jax.ShapeDtypeStruct((half, PCAP, width), jnp.float32),
        ],
        compiler_params=PARAMS,
        cost_estimate=pl.CostEstimate(
            flops=2 * depth * PCAP * bands, bytes_accessed=2 * depth * bands, transcendentals=0
        ),
        name="project",
    )(where, flipped, pltpu.with_memory_space_constraint(band_coeffs, pltpu.VMEM))


def project_plain(where, projectors, band_coeffs, first):
    depth, bands = band_coeffs.shape
    chips = lax.axis_size("pw") // 2
    half = chips // 2
    outs = []
    for group, dtype in ((1 - where[0], jnp.bfloat16), (where[0], jnp.float32)):
        chunks = jnp.stack([chunk_of(chips, where[1], group, first + at) for at in range(half)])
        slots = lax.dynamic_slice_in_dim(projectors, group * PCAP, PCAP, 1)
        columns = jnp.take(band_coeffs.reshape(depth, chips, bands // chips), chunks, axis=1)
        sums = jnp.einsum("ds,dhw->hsw", slots, columns, preferred_element_type=jnp.float32)
        outs.append(sums.astype(dtype))
    return outs


def fold_kernel(*refs):
    *terms, kept, message = refs
    half = kept.shape[0]
    for at in range(2 * half):
        total = terms[0][at]
        for term in terms[1:]:
            total = total + term[at].astype(jnp.float32)
        if at < half:
            kept[at] = total
        else:
            message[at - half] = total.astype(message.dtype)


def fold(*terms):
    count, rows, width = terms[0].shape
    return pl.pallas_call(
        fold_kernel,
        in_specs=[VMEM] * len(terms),
        out_specs=[VMEM, VMEM],
        out_shape=[
            jax.ShapeDtypeStruct((count // 2, rows, width), jnp.float32),
            jax.ShapeDtypeStruct((count // 2, rows, width), jnp.bfloat16),
        ],
        compiler_params=PARAMS,
        name="fold",
    )(*terms)


def total_kernel(left, right, kept, message):
    for at in range(kept.shape[0]):
        total = left[at] + right[at].astype(jnp.float32)
        kept[at] = total
        message[at ^ 1] = total.astype(message.dtype)


def total_of(left, right):
    return pl.pallas_call(
        total_kernel,
        in_specs=[VMEM, VMEM],
        out_specs=[VMEM, VMEM],
        out_shape=[
            jax.ShapeDtypeStruct(left.shape, jnp.float32),
            jax.ShapeDtypeStruct(left.shape, jnp.bfloat16),
        ],
        compiler_params=PARAMS,
        name="total",
    )(left, right)


def add_kernel(left, right, out):
    for at in range(out.shape[0]):
        out[at] = (left[at] + right[at].astype(jnp.float32)).astype(out.dtype)


def add(left, right):
    return pl.pallas_call(
        add_kernel,
        in_specs=[VMEM, VMEM],
        out_specs=VMEM,
        out_shape=jax.ShapeDtypeStruct(left.shape, jnp.bfloat16),
        compiler_params=PARAMS,
        name="add",
    )(left, right)


def choose_kernel(where, owners, own, sibling, after, kept, sent):
    del after
    core, chip, me = where[0], where[1], where[2]
    owner = jnp.where(core == 0, owners[0], owners[1])
    half = PCAP // 2
    side = chip & 1
    for out, which in ((kept, side), (sent, 1 - side)):
        rows = pl.ds(pl.multiple_of(which * half, half), half)
        part = jnp.where(owner == me, own[rows], jnp.where(owner == (me ^ 1), sibling[rows], 0.0))
        out[...] = part.astype(out.dtype)


def choose(where, owners, own, sibling, after):
    shape = jax.ShapeDtypeStruct((PCAP // 2, PCAP), jnp.bfloat16)
    return pl.pallas_call(
        choose_kernel,
        in_specs=[SMEM, SMEM, VMEM, VMEM, ANY],
        out_specs=[VMEM, VMEM],
        out_shape=[shape, shape],
        compiler_params=PARAMS,
        name="choose",
    )(where, owners, own, sibling, after)


def merge_kernel(left, right, after, out):
    del after
    out[...] = left[...] + right[...]


def merge(left, right, after):
    return pl.pallas_call(
        merge_kernel,
        in_specs=[VMEM, VMEM, ANY],
        out_specs=VMEM,
        out_shape=jax.ShapeDtypeStruct(left.shape, left.dtype),
        compiler_params=PARAMS,
        name="merge",
    )(left, right, after)


def mask_kernel(where, counts, atom_of, after, out):
    del after
    core = where[0]
    slot = lax.broadcasted_iota(jnp.int32, (1, PCAP), 1)
    limit = jnp.zeros((1, PCAP), jnp.int32)
    for channel in range(CHANNELS):
        limit = jnp.where(slot >= channel * CH_CAP, channel * CH_CAP + counts[core, channel], limit)
    atoms = jnp.where(core == 0, atom_of[0:1], atom_of[1:2])
    code = jnp.broadcast_to(jnp.where(slot < limit, atoms, -1), (PCAP, PCAP))
    out[...] = jnp.where((code == code.T) & (code >= 0), 1.0, 0.0).astype(out.dtype)


def mask(where, counts, atom_of, after):
    return pl.pallas_call(
        mask_kernel,
        in_specs=[SMEM, SMEM, VMEM, ANY],
        out_specs=VMEM,
        out_shape=jax.ShapeDtypeStruct((PCAP, PCAP), jnp.bfloat16),
        compiler_params=PARAMS,
        name="mask",
    )(where, counts, atom_of, after)


def coupling_kernel(where, allowed, near, far, out):
    half = PCAP // 2
    side = where[1] & 1
    for part, which in ((near, side), (far, 1 - side)):
        rows = pl.ds(pl.multiple_of(which * half, half), half)
        out[rows] = part[...] * allowed[rows]


def coupling_of(where, allowed, near, far):
    return pl.pallas_call(
        coupling_kernel,
        in_specs=[SMEM] + [VMEM] * 3,
        out_specs=VMEM,
        out_shape=jax.ShapeDtypeStruct((PCAP, PCAP), jnp.bfloat16),
        compiler_params=PARAMS,
        name="coupling",
    )(where, allowed, near, far)


def scale(coupling, sums, out):
    width = out.shape[2]
    wide = jnp.concatenate([sums[at] for at in range(out.shape[0])], axis=1)
    scaled = jnp.dot(coupling[...], wide, preferred_element_type=jnp.float32).astype(out.dtype)
    for at in range(out.shape[0]):
        out[at] = scaled[:, at * width : (at + 1) * width]


def couple(coupling, sums):
    return pl.pallas_call(
        scale,
        in_specs=[VMEM, VMEM],
        out_specs=VMEM,
        out_shape=jax.ShapeDtypeStruct(sums.shape, jnp.bfloat16),
        compiler_params=PARAMS,
        name="couple",
    )(coupling, sums)


def place(scaled, core, own, other):
    for part, group in ((own, core), (other, 1 - core)):
        rows = pl.ds(pl.multiple_of(group * PCAP, PCAP), PCAP)
        scaled[rows, :LANES] = part[0]
        scaled[rows, LANES:] = part[1]


def begin_kernel(where, projectors, coupling, sums, first, second, scaled):
    slots = pl.ds(pl.multiple_of(where[0] * PCAP, PCAP), PCAP)
    scale(coupling, sums, scaled)
    for out, at in ((first, 0), (second, 2)):
        weights = jnp.concatenate([scaled[at], scaled[at + 1]], axis=1)
        for block in range(projectors.shape[0] // ROW_BLOCK):
            rows = slice(block * ROW_BLOCK, (block + 1) * ROW_BLOCK)
            out[rows] = jnp.dot(projectors[rows, slots], weights, preferred_element_type=jnp.float32)


def begin(where, projectors, coupling, sums):
    depth, slots = projectors.shape
    shape = jax.ShapeDtypeStruct((depth, 2 * LANES), jnp.float32)
    return pl.pallas_call(
        begin_kernel,
        in_specs=[SMEM, VMEM, VMEM, VMEM],
        out_specs=[VMEM] * 3,
        out_shape=[shape, shape, jax.ShapeDtypeStruct(sums.shape, sums.dtype)],
        compiler_params=PARAMS,
        cost_estimate=pl.CostEstimate(
            flops=4 * depth * slots * LANES, bytes_accessed=2 * depth * slots, transcendentals=0
        ),
        name="begin",
    )(where, projectors, coupling, sums)


def extend_kernel(where, projectors, partial, other, done, second):
    slots = pl.ds(pl.multiple_of((1 - where[0]) * PCAP, PCAP), PCAP)
    for out, at in ((done, 0), (second, 2)):
        weights = jnp.concatenate([other[at], other[at + 1]], axis=1)
        for block in range(projectors.shape[0] // ROW_BLOCK):
            rows = slice(block * ROW_BLOCK, (block + 1) * ROW_BLOCK)
            sums = jnp.dot(projectors[rows, slots], weights, preferred_element_type=jnp.float32)
            if at == 0:
                sums = sums + partial[rows]
            out[rows] = sums.astype(out.dtype)


def extend(where, projectors, partial, other):
    depth, slots = projectors.shape
    pair = 2 * LANES
    return pl.pallas_call(
        extend_kernel,
        in_specs=[SMEM, VMEM, VMEM, VMEM],
        out_specs=[VMEM] * 2,
        out_shape=[
            jax.ShapeDtypeStruct((depth, pair), jnp.bfloat16),
            jax.ShapeDtypeStruct((depth, pair), jnp.float32),
        ],
        compiler_params=PARAMS,
        cost_estimate=pl.CostEstimate(
            flops=4 * depth * slots * LANES, bytes_accessed=2 * depth * slots, transcendentals=0
        ),
        name="extend",
    )(where, projectors, partial, other)


def finish_kernel(chips, where, projectors, done, own, other, own_rest, other_rest, out, scaled, blocks, sems):
    core, chip = where[0], where[1]
    place(scaled, core, own_rest[2:], other_rest[2:])
    copies = []

    def put(rows, group, position, sums):
        for at in range(2):
            start = pl.multiple_of(chunk_of(chips, chip, group, position + at) * LANES, LANES)
            blocks[rows, pl.ds(start, LANES)] = sums[:, at * LANES : (at + 1) * LANES].astype(blocks.dtype)

    for block in range(projectors.shape[0] // ROW_BLOCK):
        rows = slice(block * ROW_BLOCK, (block + 1) * ROW_BLOCK)
        put(rows, core, 0, done[rows])
        put(rows, core, 6, jnp.dot(projectors[rows], scaled[...], preferred_element_type=jnp.float32))
        for partial, part, group in ((own, other_rest, 1 - core), (other, own_rest, core)):
            slots = pl.ds(pl.multiple_of(group * PCAP, PCAP), PCAP)
            weights = jnp.concatenate([part[0], part[1]], axis=1)
            sums = jnp.dot(projectors[rows, slots], weights, preferred_element_type=jnp.float32)
            put(rows, group, 4, partial[rows] + sums)
        for piece in range(ROW_BLOCK // COPY_ROWS):
            start = block * ROW_BLOCK + piece * COPY_ROWS
            written = slice(start, start + COPY_ROWS)
            copies.append(pltpu.make_async_copy(blocks.at[written], out.at[written], sems.at[len(copies)]))
            copies[-1].start()
    for copy in copies:
        copy.wait()


def finish(where, projectors, done, own, other, own_rest, other_rest):
    depth, slots = projectors.shape
    chips = lax.axis_size("pw") // 2
    bands = chips * LANES

    def kernel(*refs):
        finish_kernel(chips, *refs)

    return pl.pallas_call(
        kernel,
        in_specs=[SMEM] + [VMEM] * 6,
        out_specs=HBM,
        out_shape=jax.ShapeDtypeStruct((depth, bands), jnp.bfloat16),
        scratch_shapes=[
            pltpu.VMEM((slots, 2 * LANES), jnp.bfloat16),
            pltpu.VMEM((depth, bands), jnp.bfloat16),
            pltpu.SemaphoreType.DMA((depth // COPY_ROWS,)),
        ],
        compiler_params=PARAMS,
        cost_estimate=pl.CostEstimate(
            flops=depth * slots * bands, bytes_accessed=2 * depth * (slots + bands), transcendentals=0
        ),
        name="finish",
    )(where, projectors, done, own, other, own_rest, other_rest)


def apply_plain(where, projectors, mine, other):
    chips, _, width = mine.shape
    rows = []
    for group in range(2):
        chunks = jnp.stack([chunk_of(chips, where[1], group, at) for at in range(chips)])
        blocks = jnp.where(where[0] == group, mine, other)
        blocks = jnp.zeros_like(blocks).at[chunks].set(blocks)
        rows.append(blocks.transpose(1, 0, 2).reshape(PCAP, chips * width))
    return jnp.dot(projectors, jnp.concatenate(rows), preferred_element_type=jnp.float32).astype(jnp.bfloat16)


def local(band_coeffs, projectors, counts, atom_of, owners, couplings):
    chips = lax.axis_size("pw") // 2
    stages = chips.bit_length() - 1
    half = chips // 2
    width = band_coeffs.shape[1] // chips
    me = lax.axis_index("pw")
    where = jnp.stack([me % 2, me // 2, me])

    fast = width == LANES and stages == 3
    own_table = couplings[0]
    sibling_table = swap_cores(own_table)
    if fast:
        flipped = load(where, projectors)
        theirs, ours = project(where, flipped, band_coeffs, half)
    else:
        theirs, ours = project_plain(where, projectors, band_coeffs, half)
    if fast:
        low_theirs, low_ours = project(where, flipped, band_coeffs, 0)
    else:
        low_theirs, low_ours = project_plain(where, projectors, band_coeffs, 0)
    theirs, low_ours = lax.optimization_barrier((swap_cores(theirs), low_ours))
    message = add(ours, theirs)
    got = swap_stage(message, 0)
    low_theirs = swap_cores(low_theirs)
    near, far = choose(where, owners, own_table, sibling_table, message)
    far = swap_bits(far, [0, 0])
    allowed = mask(where, counts, atom_of, message)
    near = merge(near, far, message)
    got, near = lax.optimization_barrier((got, near))
    kept, message = fold(low_ours, low_theirs, got)
    for stage in range(1, stages):
        got = swap_stage(message, stage)
        far = swap_bits(near, [stages - stage] * 2)
        near = merge(near, far, message)
        got, near = lax.optimization_barrier((got, near))
        if stage < stages - 2:
            kept, message = fold(kept, got)
        elif stage == stages - 2:
            kept, message = total_of(kept, got)
    mine = add(kept, got)
    far = swap_bits(near, [0, 0])
    for stage in range(stages - 2, 0, -1):
        got = swap_stage(mine, stage)
        if stage == 1:
            got, far = lax.optimization_barrier((got, far))
        mine = jnp.concatenate([mine, got])
    coupling = coupling_of(where, allowed, near, far)
    got = swap_stage(mine, 0)
    if not fast:
        mine = couple(coupling, jnp.concatenate([mine, got]))
        return apply_plain(where, projectors, mine, swap_cores(mine))
    first, own, scaled = begin(where, projectors, coupling, mine)
    done, other = extend(where, projectors, first, swap_cores(scaled))
    got = couple(coupling, got)
    return finish(where, projectors, done, own, other, got, swap_cores(got))


def solution(mesh):
    placed = (
        P("pw", "group"),
        P("pw", "group"),
        P("group", None),
        P("group", None),
        P("group"),
        P("pw", "group", None),
    )
    return jax.shard_map(
        local, mesh=mesh, in_specs=placed, out_specs=P("pw", "group"), check_vma=False
    )
```

```python
import jax
import jax.numpy as jnp
from jax import lax
from jax.experimental import pallas as pl
from jax.experimental.pallas import tpu as pltpu
from jax.sharding import PartitionSpec as P

CHANNELS = 4
CH_CAP = 64
PCAP = 256
LANES = 128
SQUARE = 4
QUARTER = PCAP // SQUARE
ROW_BLOCK = 512
COPY_ROWS = 128
PARAMS = pltpu.CompilerParams(vmem_limit_bytes=40 * 1024 * 1024)
VMEM = pl.BlockSpec(memory_space=pltpu.VMEM)
SMEM = pl.BlockSpec(memory_space=pltpu.SMEM)
HBM = pl.BlockSpec(memory_space=pltpu.HBM)
ANY = pl.BlockSpec(memory_space=pl.ANY)


def block_of(chip, part, entry):
    return chip ^ (part + SQUARE * entry)


def swap(x, distance):
    count = lax.axis_size("pw")
    return lax.ppermute(x, "pw", [(i, i ^ distance) for i in range(count)])


def swap_cores(x):
    return swap(x, 1)


def swap_square(x, part):
    return swap(x, 2 * part)


def load_kernel(where, projectors, flipped, slots, sems):
    core = where[0]
    count = sems.shape[0]
    block = slots.shape[0] // count
    copies = []
    for at in range(count):
        rows = slice(at * block, (at + 1) * block)
        copies.append(pltpu.make_async_copy(projectors.at[rows], slots.at[rows], sems.at[at]))
        copies[-1].start()
    for at, copy in enumerate(copies):
        copy.wait()
        rows = slice(at * block, (at + 1) * block)
        for place, group in enumerate((core, 1 - core)):
            start = pl.multiple_of(group * PCAP, PCAP)
            flipped[place * PCAP : (place + 1) * PCAP, rows] = slots[rows, pl.ds(start, PCAP)].T


def load(where, projectors):
    depth, slots = projectors.shape
    return pl.pallas_call(
        load_kernel,
        in_specs=[SMEM, HBM],
        out_specs=VMEM,
        out_shape=jax.ShapeDtypeStruct((slots, depth), jnp.bfloat16),
        scratch_shapes=[pltpu.VMEM((depth, slots), jnp.bfloat16), pltpu.SemaphoreType.DMA((4,))],
        compiler_params=PARAMS,
        name="load",
    )(where, pltpu.with_memory_space_constraint(projectors, pltpu.HBM))


def project_kernel(parts, where, flipped, columns, theirs, ours):
    chip = where[1]
    for at, part in enumerate(parts):
        starts = [pl.multiple_of(block_of(chip, part, entry) * LANES, LANES) for entry in range(2)]
        pair = jnp.concatenate([columns[:, pl.ds(start, LANES)] for start in starts], axis=1)
        sums = jnp.dot(flipped[...], pair, preferred_element_type=jnp.float32)
        for entry in range(2):
            lanes = slice(entry * LANES, (entry + 1) * LANES)
            ours[2 * at + entry] = sums[:PCAP, lanes]
            theirs[2 * at + entry] = sums[PCAP:, lanes].astype(theirs.dtype)


def project(where, flipped, band_coeffs, parts):
    depth, bands = band_coeffs.shape
    count = 2 * len(parts)

    def kernel(*refs):
        project_kernel(parts, *refs)

    return pl.pallas_call(
        kernel,
        in_specs=[SMEM, VMEM, VMEM],
        out_specs=[VMEM, VMEM],
        out_shape=[
            jax.ShapeDtypeStruct((count, PCAP, LANES), jnp.bfloat16),
            jax.ShapeDtypeStruct((count, PCAP, LANES), jnp.float32),
        ],
        compiler_params=PARAMS,
        cost_estimate=pl.CostEstimate(
            flops=4 * depth * PCAP * count * LANES, bytes_accessed=2 * depth * count * LANES, transcendentals=0
        ),
        name="project",
    )(where, flipped, pltpu.with_memory_space_constraint(band_coeffs, pltpu.VMEM))


def project_plain(where, projectors, band_coeffs, parts):
    depth, bands = band_coeffs.shape
    chips = lax.axis_size("pw") // 2
    blocks = jnp.stack([block_of(where[1], q, r) for q in parts for r in range(chips // SQUARE)])
    columns = jnp.take(band_coeffs.reshape(depth, chips, bands // chips), blocks, axis=1)
    outs = []
    for group, dtype in ((1 - where[0], jnp.bfloat16), (where[0], jnp.float32)):
        slots = lax.dynamic_slice_in_dim(projectors, group * PCAP, PCAP, 1)
        sums = jnp.einsum("ds,dhw->hsw", slots, columns, preferred_element_type=jnp.float32)
        outs.append(sums.astype(dtype))
    return outs


def choose_kernel(where, owners, own, sibling, after, out):
    del after
    core, chip, me = where[0], where[1], where[2]
    owner = jnp.where(core == 0, owners[0], owners[1])
    width = out.shape[2]
    for part in range(SQUARE):
        rows = pl.ds(pl.multiple_of(((chip & 3) ^ part) * QUARTER, QUARTER), QUARTER)
        piece = jnp.where(owner == me, own[rows], jnp.where(owner == (me ^ 1), sibling[rows], 0.0))
        for cut in range(PCAP // width):
            out[part, cut * QUARTER : (cut + 1) * QUARTER] = piece[:, cut * width : (cut + 1) * width].astype(
                out.dtype
            )


def choose(where, owners, own, sibling, width, after):
    return pl.pallas_call(
        choose_kernel,
        in_specs=[SMEM, SMEM, VMEM, VMEM, ANY],
        out_specs=VMEM,
        out_shape=jax.ShapeDtypeStruct((SQUARE, QUARTER * PCAP // width, width), jnp.bfloat16),
        compiler_params=PARAMS,
        name="choose",
    )(where, owners, own, sibling, after)


def pack_kernel(ours, theirs, quarters, *messages):
    entries = ours.shape[0] // len(messages)
    for at, message in enumerate(messages):
        for entry in range(entries):
            place = at * entries + entry
            total = ours[place] + theirs[place].astype(jnp.float32)
            message[entry * PCAP : (entry + 1) * PCAP] = total.astype(message.dtype)
        message[entries * PCAP :] = quarters[at + 1]


def pack(ours, theirs, quarters):
    entries, _, width = ours.shape
    entries //= SQUARE - 1
    shape = jax.ShapeDtypeStruct((entries * PCAP + quarters.shape[1], width), jnp.bfloat16)
    return pl.pallas_call(
        pack_kernel,
        in_specs=[VMEM] * 3,
        out_specs=[VMEM] * (SQUARE - 1),
        out_shape=[shape] * (SQUARE - 1),
        compiler_params=PARAMS,
        name="pack",
    )(ours, theirs, quarters)


def fold_kernel(ours, theirs, quarters, *refs):
    *gots, kept, message = refs
    entries = ours.shape[0]
    for entry in range(entries):
        rows = slice(entry * PCAP, (entry + 1) * PCAP)
        total = ours[entry] + theirs[entry].astype(jnp.float32)
        for got in gots:
            total = total + got[rows].astype(jnp.float32)
        kept[rows] = total
        away = entry ^ 1
        message[away * PCAP : (away + 1) * PCAP] = total.astype(message.dtype)
    table = quarters[0]
    for got in gots:
        table = table + got[entries * PCAP :]
    kept[entries * PCAP :] = table.astype(kept.dtype)
    message[entries * PCAP :] = table


def fold(ours, theirs, quarters, gots):
    shape = gots[0].shape
    return pl.pallas_call(
        fold_kernel,
        in_specs=[VMEM] * (3 + len(gots)),
        out_specs=[VMEM, VMEM],
        out_shape=[jax.ShapeDtypeStruct(shape, jnp.float32), jax.ShapeDtypeStruct(shape, jnp.bfloat16)],
        compiler_params=PARAMS,
        name="fold",
    )(ours, theirs, quarters, *gots)


def add_kernel(left, right, out):
    out[...] = (left[...] + right[...].astype(jnp.float32)).astype(out.dtype)


def add(left, right):
    return pl.pallas_call(
        add_kernel,
        in_specs=[VMEM, VMEM],
        out_specs=VMEM,
        out_shape=jax.ShapeDtypeStruct(left.shape, jnp.bfloat16),
        compiler_params=PARAMS,
        name="add",
    )(left, right)


def mask_kernel(where, counts, atom_of, after, out):
    del after
    core = where[0]
    slot = lax.broadcasted_iota(jnp.int32, (1, PCAP), 1)
    limit = jnp.zeros((1, PCAP), jnp.int32)
    for channel in range(CHANNELS):
        limit = jnp.where(slot >= channel * CH_CAP, channel * CH_CAP + counts[core, channel], limit)
    atoms = jnp.where(core == 0, atom_of[0:1], atom_of[1:2])
    code = jnp.broadcast_to(jnp.where(slot < limit, atoms, -1), (PCAP, PCAP))
    out[...] = jnp.where((code == code.T) & (code >= 0), 1.0, 0.0).astype(out.dtype)


def mask(where, counts, atom_of, after):
    return pl.pallas_call(
        mask_kernel,
        in_specs=[SMEM, SMEM, VMEM, ANY],
        out_specs=VMEM,
        out_shape=jax.ShapeDtypeStruct((PCAP, PCAP), jnp.bfloat16),
        compiler_params=PARAMS,
        name="mask",
    )(where, counts, atom_of, after)


def couple_kernel(where, allowed, *refs):
    *messages, out, coupling = refs
    width = out.shape[2]
    entries = out.shape[0] // SQUARE
    for part, message in enumerate(messages):
        start = pl.multiple_of(((where[1] & 3) ^ part) * QUARTER, QUARTER)
        for cut in range(PCAP // width):
            lanes = slice(cut * width, (cut + 1) * width)
            first = entries * PCAP + cut * QUARTER
            coupling[pl.ds(start, QUARTER), lanes] = (
                message[first : first + QUARTER] * allowed[pl.ds(start, QUARTER), lanes]
            )
    for part, message in enumerate(messages):
        wide = jnp.concatenate([message[e * PCAP : (e + 1) * PCAP] for e in range(entries)], axis=1)
        scaled = jnp.dot(coupling[...], wide, preferred_element_type=jnp.float32).astype(out.dtype)
        for entry in range(entries):
            out[part * entries + entry] = scaled[:, entry * width : (entry + 1) * width]


def couple(where, allowed, messages):
    rows, width = messages[0].shape
    entries = (rows - QUARTER * PCAP // width) // PCAP
    return pl.pallas_call(
        couple_kernel,
        in_specs=[SMEM] + [VMEM] * (1 + SQUARE),
        out_specs=VMEM,
        out_shape=jax.ShapeDtypeStruct((SQUARE * entries, PCAP, width), jnp.bfloat16),
        scratch_shapes=[pltpu.VMEM((PCAP, PCAP), jnp.bfloat16)],
        compiler_params=PARAMS,
        name="couple",
    )(where, allowed, *messages)


def begin_kernel(where, projectors, scaled, *outs):
    slots = pl.ds(pl.multiple_of(where[0] * PCAP, PCAP), PCAP)
    for part, out in enumerate(outs):
        weights = jnp.concatenate([scaled[2 * part], scaled[2 * part + 1]], axis=1)
        for block in range(projectors.shape[0] // ROW_BLOCK):
            rows = slice(block * ROW_BLOCK, (block + 1) * ROW_BLOCK)
            out[rows] = jnp.dot(projectors[rows, slots], weights, preferred_element_type=jnp.float32)


def begin(where, projectors, scaled):
    depth, slots = projectors.shape
    count = SQUARE - 1
    return pl.pallas_call(
        begin_kernel,
        in_specs=[SMEM, VMEM, VMEM],
        out_specs=[VMEM] * count,
        out_shape=[jax.ShapeDtypeStruct((depth, 2 * LANES), jnp.float32)] * count,
        compiler_params=PARAMS,
        cost_estimate=pl.CostEstimate(
            flops=2 * depth * slots * LANES * count, bytes_accessed=2 * depth * slots, transcendentals=0
        ),
        name="begin",
    )(where, projectors, scaled)


def finish_kernel(where, projectors, mine, other, *refs):
    *begun, out, weights, blocks, sems = refs
    core, chip = where[0], where[1]
    last = 2 * len(begun)
    for part, group in ((mine, core), (other, 1 - core)):
        rows = pl.ds(pl.multiple_of(group * PCAP, PCAP), PCAP)
        weights[rows, :LANES] = part[last]
        weights[rows, LANES:] = part[last + 1]
    slots = pl.ds(pl.multiple_of((1 - core) * PCAP, PCAP), PCAP)
    copies = []

    def put(rows, part, sums):
        for entry in range(2):
            start = pl.multiple_of(block_of(chip, part, entry) * LANES, LANES)
            blocks[rows, pl.ds(start, LANES)] = sums[:, entry * LANES : (entry + 1) * LANES].astype(blocks.dtype)

    for block in range(projectors.shape[0] // ROW_BLOCK):
        rows = slice(block * ROW_BLOCK, (block + 1) * ROW_BLOCK)
        put(rows, len(begun), jnp.dot(projectors[rows], weights[...], preferred_element_type=jnp.float32))
        for part, partial in enumerate(begun):
            pair = jnp.concatenate([other[2 * part], other[2 * part + 1]], axis=1)
            sums = jnp.dot(projectors[rows, slots], pair, preferred_element_type=jnp.float32)
            put(rows, part, partial[rows] + sums)
        for piece in range(ROW_BLOCK // COPY_ROWS):
            start = block * ROW_BLOCK + piece * COPY_ROWS
            written = slice(start, start + COPY_ROWS)
            copies.append(pltpu.make_async_copy(blocks.at[written], out.at[written], sems.at[len(copies)]))
            copies[-1].start()
    for copy in copies:
        copy.wait()


def finish(where, projectors, mine, other, begun):
    depth, slots = projectors.shape
    bands = mine.shape[0] * LANES
    return pl.pallas_call(
        finish_kernel,
        in_specs=[SMEM] + [VMEM] * (3 + len(begun)),
        out_specs=HBM,
        out_shape=jax.ShapeDtypeStruct((depth, bands), jnp.bfloat16),
        scratch_shapes=[
            pltpu.VMEM((slots, 2 * LANES), jnp.bfloat16),
            pltpu.VMEM((depth, bands), jnp.bfloat16),
            pltpu.SemaphoreType.DMA((depth // COPY_ROWS,)),
        ],
        compiler_params=PARAMS,
        cost_estimate=pl.CostEstimate(
            flops=depth * slots * bands, bytes_accessed=2 * depth * (slots + bands), transcendentals=0
        ),
        name="finish",
    )(where, projectors, mine, other, *begun)


def apply_plain(where, projectors, mine, other):
    chips, _, width = mine.shape
    blocks = jnp.stack([block_of(where[1], q, r) for q in range(SQUARE) for r in range(chips // SQUARE)])
    rows = []
    for group in range(2):
        part = jnp.where(where[0] == group, mine, other)
        part = jnp.zeros_like(part).at[blocks].set(part)
        rows.append(part.transpose(1, 0, 2).reshape(PCAP, chips * width))
    return jnp.dot(projectors, jnp.concatenate(rows), preferred_element_type=jnp.float32).astype(jnp.bfloat16)


def local(band_coeffs, projectors, counts, atom_of, owners, couplings):
    chips = lax.axis_size("pw") // 2
    entries = chips // SQUARE
    width = band_coeffs.shape[1] // chips
    fast = width == LANES and entries == 2
    me = lax.axis_index("pw")
    where = jnp.stack([me % 2, me // 2, me])

    own_table = couplings[0]
    sibling_table = swap_cores(own_table)
    sent, kept = tuple(range(1, SQUARE)), (0,)
    if fast:
        flipped = load(where, projectors)
        theirs, ours = project(where, flipped, band_coeffs, sent)
        low_theirs, low_ours = project(where, flipped, band_coeffs, kept)
    else:
        theirs, ours = project_plain(where, projectors, band_coeffs, sent)
        low_theirs, low_ours = project_plain(where, projectors, band_coeffs, kept)
    quarters = choose(where, owners, own_table, sibling_table, width, ours)
    theirs, low_ours = lax.optimization_barrier((swap_cores(theirs), low_ours))
    messages = pack(ours, theirs, quarters)
    low_theirs = swap_cores(low_theirs)
    gots = [swap_square(message, part) for message, part in zip(messages, sent)]
    allowed = mask(where, counts, atom_of, messages[0])

    total, message = fold(low_ours, low_theirs, quarters, gots)
    mine = add(total, swap_square(message, SQUARE))
    distance = 2 * SQUARE
    while distance < chips:
        body = mine[: entries * PCAP].reshape(entries, PCAP, width)
        order = [entry ^ (distance // SQUARE) for entry in range(entries)]
        message = jnp.concatenate([body[jnp.array(order)].reshape(-1, width), mine[entries * PCAP :]])
        mine = add(mine.astype(jnp.float32), swap_square(message, distance))
        distance *= 2

    gathered = [mine] + [swap_square(mine, part) for part in sent]
    scaled = couple(where, allowed, gathered)
    other = swap_cores(scaled)
    if not fast:
        return apply_plain(where, projectors, scaled, other)
    return finish(where, projectors, scaled, other, begin(where, projectors, scaled))


def solution(mesh):
    placed = (
        P("pw", "group"),
        P("pw", "group"),
        P("group", None),
        P("group", None),
        P("group"),
        P("pw", "group", None),
    )
    return jax.shard_map(
        local, mesh=mesh, in_specs=placed, out_specs=P("pw", "group"), check_vma=False
    )
```

```python
import jax
import jax.numpy as jnp
from jax import lax
from jax.experimental import pallas as pl
from jax.experimental.pallas import tpu as pltpu
from jax.sharding import PartitionSpec as P

CHANNELS = 4
CH_CAP = 64
PCAP = 256
LANES = 128
SQUARE = 4
QUARTER = PCAP // SQUARE
ROW_BLOCK = 512
COPY_ROWS = 128
PARAMS = pltpu.CompilerParams(vmem_limit_bytes=40 * 1024 * 1024)
VMEM = pl.BlockSpec(memory_space=pltpu.VMEM)
SMEM = pl.BlockSpec(memory_space=pltpu.SMEM)
HBM = pl.BlockSpec(memory_space=pltpu.HBM)
ANY = pl.BlockSpec(memory_space=pl.ANY)


def block_of(chip, part, entry):
    return chip ^ (part + SQUARE * entry)


def swap(x, distance):
    count = lax.axis_size("pw")
    return lax.ppermute(x, "pw", [(i, i ^ distance) for i in range(count)])


def swap_cores(x):
    return swap(x, 1)


def swap_square(x, part):
    return swap(x, 2 * part)


def load_kernel(where, projectors, flipped, slots, sems):
    core = where[0]
    count = sems.shape[0]
    block = slots.shape[0] // count
    copies = []
    for at in range(count):
        rows = slice(at * block, (at + 1) * block)
        copies.append(pltpu.make_async_copy(projectors.at[rows], slots.at[rows], sems.at[at]))
        copies[-1].start()
    for at, copy in enumerate(copies):
        copy.wait()
        rows = slice(at * block, (at + 1) * block)
        for place, group in enumerate((core, 1 - core)):
            start = pl.multiple_of(group * PCAP, PCAP)
            flipped[place * PCAP : (place + 1) * PCAP, rows] = slots[rows, pl.ds(start, PCAP)].T


def load(where, projectors):
    depth, slots = projectors.shape
    return pl.pallas_call(
        load_kernel,
        in_specs=[SMEM, HBM],
        out_specs=VMEM,
        out_shape=jax.ShapeDtypeStruct((slots, depth), jnp.bfloat16),
        scratch_shapes=[pltpu.VMEM((depth, slots), jnp.bfloat16), pltpu.SemaphoreType.DMA((4,))],
        compiler_params=PARAMS,
        name="load",
    )(where, pltpu.with_memory_space_constraint(projectors, pltpu.HBM))


def project_kernel(parts, where, flipped, columns, theirs, ours):
    chip = where[1]
    for at, part in enumerate(parts):
        starts = [pl.multiple_of(block_of(chip, part, entry) * LANES, LANES) for entry in range(2)]
        pair = jnp.concatenate([columns[:, pl.ds(start, LANES)] for start in starts], axis=1)
        sums = jnp.dot(flipped[...], pair, preferred_element_type=jnp.float32)
        for entry in range(2):
            lanes = slice(entry * LANES, (entry + 1) * LANES)
            ours[2 * at + entry] = sums[:PCAP, lanes]
            theirs[2 * at + entry] = sums[PCAP:, lanes].astype(theirs.dtype)


def project(where, flipped, band_coeffs, parts):
    depth, bands = band_coeffs.shape
    count = 2 * len(parts)

    def kernel(*refs):
        project_kernel(parts, *refs)

    return pl.pallas_call(
        kernel,
        in_specs=[SMEM, VMEM, VMEM],
        out_specs=[VMEM, VMEM],
        out_shape=[
            jax.ShapeDtypeStruct((count, PCAP, LANES), jnp.bfloat16),
            jax.ShapeDtypeStruct((count, PCAP, LANES), jnp.float32),
        ],
        compiler_params=PARAMS,
        cost_estimate=pl.CostEstimate(
            flops=4 * depth * PCAP * count * LANES, bytes_accessed=2 * depth * count * LANES, transcendentals=0
        ),
        name="project",
    )(where, flipped, pltpu.with_memory_space_constraint(band_coeffs, pltpu.VMEM))


def project_plain(where, projectors, band_coeffs, parts):
    depth, bands = band_coeffs.shape
    chips = lax.axis_size("pw") // 2
    blocks = jnp.stack([block_of(where[1], q, r) for q in parts for r in range(chips // SQUARE)])
    columns = jnp.take(band_coeffs.reshape(depth, chips, bands // chips), blocks, axis=1)
    outs = []
    for group, dtype in ((1 - where[0], jnp.bfloat16), (where[0], jnp.float32)):
        slots = lax.dynamic_slice_in_dim(projectors, group * PCAP, PCAP, 1)
        sums = jnp.einsum("ds,dhw->hsw", slots, columns, preferred_element_type=jnp.float32)
        outs.append(sums.astype(dtype))
    return outs


def chosen(where, owners, group, own, across):
    me = where[2]
    owner = jnp.where(group == 0, owners[0], owners[1])
    part = jnp.where(owner == me, own, jnp.where(owner == (me ^ (2 * SQUARE)), across, 0.0))
    return part.astype(jnp.bfloat16)


def cuts(table, width):
    return jnp.concatenate([table[:, cut : cut + width] for cut in range(0, PCAP, width)], axis=0)


def choose_kernel(where, owners, own, across, theirs, near, message):
    core = where[0]
    entries, _, width = theirs.shape
    near[...] = chosen(where, owners, core, own[...], across[...])
    for entry in range(entries):
        message[entry * PCAP : (entry + 1) * PCAP] = theirs[entry]
    message[entries * PCAP :] = cuts(chosen(where, owners, 1 - core, own[...], across[...]), width)


def choose(where, owners, own, across, theirs):
    entries, _, width = theirs.shape
    return pl.pallas_call(
        choose_kernel,
        in_specs=[SMEM, SMEM, VMEM, VMEM, VMEM],
        out_specs=[VMEM, VMEM],
        out_shape=[
            jax.ShapeDtypeStruct(own.shape, jnp.bfloat16),
            jax.ShapeDtypeStruct((entries * PCAP + PCAP * PCAP // width, width), jnp.bfloat16),
        ],
        compiler_params=PARAMS,
        name="choose",
    )(where, owners, own, across, theirs)


def choose_plain(where, owners, own, across, theirs, chips):
    entries, _, width = theirs.shape
    tables = [chosen(where, owners, group, own, across) for group in (where[0], 1 - where[0])]
    distance = 2 * SQUARE
    while distance < chips:
        tables = [table + swap_square(table, distance) for table in tables]
        distance *= 2
    return tables[0], jnp.concatenate([theirs.reshape(entries * PCAP, width), cuts(tables[1], width)])


def quarter_kernel(where, near, got, *quarters):
    width = got.shape[1]
    first = got.shape[0] - PCAP * PCAP // width
    for part, quarter in enumerate(quarters):
        start = pl.multiple_of(((where[1] & 3) ^ part) * QUARTER, QUARTER)
        for cut in range(PCAP // width):
            piece = near[pl.ds(start, QUARTER), cut * width : (cut + 1) * width]
            quarter[cut * QUARTER : (cut + 1) * QUARTER] = piece + got[pl.ds(first + cut * PCAP + start, QUARTER)]


def quarters_of(where, near, got):
    width = got.shape[1]
    shape = jax.ShapeDtypeStruct((QUARTER * PCAP // width, width), jnp.bfloat16)
    return pl.pallas_call(
        quarter_kernel,
        in_specs=[SMEM, VMEM, VMEM],
        out_specs=[VMEM] * SQUARE,
        out_shape=[shape] * SQUARE,
        compiler_params=PARAMS,
        name="quarter",
    )(where, near, got)


def pack_kernel(ours, theirs, *messages):
    entries = messages[0].shape[0]
    for at, message in enumerate(messages):
        for entry in range(entries):
            place = at * entries + entry
            message[entry] = (ours[place] + theirs[place].astype(jnp.float32)).astype(message.dtype)


def pack(ours, theirs):
    count, _, width = ours.shape
    shape = jax.ShapeDtypeStruct((count // (SQUARE - 1), PCAP, width), jnp.bfloat16)
    return pl.pallas_call(
        pack_kernel,
        in_specs=[VMEM, VMEM],
        out_specs=[VMEM] * (SQUARE - 1),
        out_shape=[shape] * (SQUARE - 1),
        compiler_params=PARAMS,
        name="pack",
    )(ours, theirs)


def fold_kernel(ours, theirs, *refs):
    gots, quarters, (kept, message, quarter) = refs[: SQUARE - 1], refs[SQUARE - 1 : -3], refs[-3:]
    for entry in range(ours.shape[0]):
        total = ours[entry] + theirs[entry * PCAP : (entry + 1) * PCAP].astype(jnp.float32)
        for got in gots:
            total = total + got[entry].astype(jnp.float32)
        kept[entry] = total
        message[entry ^ 1] = total.astype(message.dtype)
    table = quarters[0][...]
    for got in quarters[1:]:
        table = table + got[...]
    quarter[...] = table


def fold(ours, theirs, gots, quarters):
    return pl.pallas_call(
        fold_kernel,
        in_specs=[VMEM] * (1 + 2 * SQUARE),
        out_specs=[VMEM] * 3,
        out_shape=[
            jax.ShapeDtypeStruct(ours.shape, jnp.float32),
            jax.ShapeDtypeStruct(ours.shape, jnp.bfloat16),
            jax.ShapeDtypeStruct(quarters[0].shape, jnp.bfloat16),
        ],
        compiler_params=PARAMS,
        name="fold",
    )(ours, theirs, *gots, *quarters)


def mask_kernel(where, counts, atom_of, after, out):
    del after
    core = where[0]
    slot = lax.broadcasted_iota(jnp.int32, (1, PCAP), 1)
    limit = jnp.zeros((1, PCAP), jnp.int32)
    for channel in range(CHANNELS):
        limit = jnp.where(slot >= channel * CH_CAP, channel * CH_CAP + counts[core, channel], limit)
    atoms = jnp.where(core == 0, atom_of[0:1], atom_of[1:2])
    code = jnp.broadcast_to(jnp.where(slot < limit, atoms, -1), (PCAP, PCAP))
    out[...] = jnp.where((code == code.T) & (code >= 0), 1.0, 0.0).astype(out.dtype)


def mask(where, counts, atom_of, after):
    return pl.pallas_call(
        mask_kernel,
        in_specs=[SMEM, SMEM, VMEM, ANY],
        out_specs=VMEM,
        out_shape=jax.ShapeDtypeStruct((PCAP, PCAP), jnp.bfloat16),
        compiler_params=PARAMS,
        name="mask",
    )(where, counts, atom_of, after)


def coupling_kernel(where, allowed, *refs):
    *quarters, out = refs
    width = quarters[0].shape[1]
    for part, quarter in enumerate(quarters):
        rows = pl.ds(pl.multiple_of(((where[1] & 3) ^ part) * QUARTER, QUARTER), QUARTER)
        for cut in range(PCAP // width):
            lanes = slice(cut * width, (cut + 1) * width)
            out[rows, lanes] = quarter[cut * QUARTER : (cut + 1) * QUARTER] * allowed[rows, lanes]


def coupling_of(where, allowed, quarters):
    return pl.pallas_call(
        coupling_kernel,
        in_specs=[SMEM] + [VMEM] * (1 + SQUARE),
        out_specs=VMEM,
        out_shape=jax.ShapeDtypeStruct((PCAP, PCAP), jnp.bfloat16),
        compiler_params=PARAMS,
        name="coupling",
    )(where, allowed, *quarters)


def couple_kernel(coupling, kept, got, out):
    entries, _, width = out.shape
    totals = [kept[e] + got[e].astype(jnp.float32) for e in range(entries)]
    high = [total.astype(jnp.bfloat16) for total in totals]
    low = [(total - part.astype(jnp.float32)).astype(jnp.bfloat16) for total, part in zip(totals, high)]
    both = jnp.dot(coupling[...], jnp.concatenate(high + low, axis=1), preferred_element_type=jnp.float32)
    for e in range(entries):
        first, second = e * width, (entries + e) * width
        out[e] = (both[:, first : first + width] + both[:, second : second + width]).astype(out.dtype)


def couple(coupling, kept, got):
    return pl.pallas_call(
        couple_kernel,
        in_specs=[VMEM] * 3,
        out_specs=VMEM,
        out_shape=jax.ShapeDtypeStruct(kept.shape, jnp.bfloat16),
        compiler_params=PARAMS,
        name="couple",
    )(coupling, kept, got)


def apply_kernel(part, where, projectors, mine, other, *refs):
    out, weights, blocks, sems = refs[-4:]
    core, chip = where[0], where[1]
    for scaled, group in ((mine, core), (other, 1 - core)):
        rows = pl.ds(pl.multiple_of(group * PCAP, PCAP), PCAP)
        weights[rows, :LANES] = scaled[0]
        weights[rows, LANES:] = scaled[1]
    copies = []
    for block in range(projectors.shape[0] // ROW_BLOCK):
        rows = slice(block * ROW_BLOCK, (block + 1) * ROW_BLOCK)
        blocks[rows] = jnp.dot(
            projectors[rows], weights[...], preferred_element_type=jnp.float32
        ).astype(blocks.dtype)
        for entry in range(2):
            start = pl.multiple_of(block_of(chip, part, entry) * LANES, LANES)
            copies.append(
                pltpu.make_async_copy(
                    blocks.at[rows, entry * LANES : (entry + 1) * LANES],
                    out.at[rows, pl.ds(start, LANES)],
                    sems.at[len(copies)],
                )
            )
            copies[-1].start()
    for copy in copies:
        copy.wait()


def apply(where, projectors, mine, other, part, out):
    depth, slots = projectors.shape
    pair = 2 * LANES

    def kernel(*refs):
        apply_kernel(part, *refs)

    operands = [where, projectors, mine, other] + ([] if out is None else [out])
    return pl.pallas_call(
        kernel,
        in_specs=[SMEM, VMEM, VMEM, VMEM] + ([] if out is None else [HBM]),
        out_specs=HBM,
        out_shape=jax.ShapeDtypeStruct((depth, SQUARE * pair), jnp.bfloat16),
        input_output_aliases={} if out is None else {4: 0},
        scratch_shapes=[
            pltpu.VMEM((slots, pair), jnp.bfloat16),
            pltpu.VMEM((depth, pair), jnp.bfloat16),
            pltpu.SemaphoreType.DMA((2 * depth // ROW_BLOCK,)),
        ],
        compiler_params=PARAMS,
        cost_estimate=pl.CostEstimate(
            flops=2 * depth * slots * pair, bytes_accessed=2 * depth * (slots + pair), transcendentals=0
        ),
        name="apply",
    )(*operands)


def apply_plain(where, projectors, mine, other):
    chips, _, width = mine.shape
    blocks = jnp.stack([block_of(where[1], q, r) for q in range(SQUARE) for r in range(chips // SQUARE)])
    rows = []
    for group in range(2):
        part = jnp.where(where[0] == group, mine, other)
        part = jnp.zeros_like(part).at[blocks].set(part)
        rows.append(part.transpose(1, 0, 2).reshape(PCAP, chips * width))
    return jnp.dot(projectors, jnp.concatenate(rows), preferred_element_type=jnp.float32).astype(jnp.bfloat16)


def local(band_coeffs, projectors, counts, atom_of, owners, couplings):
    chips = lax.axis_size("pw") // 2
    entries = chips // SQUARE
    width = band_coeffs.shape[1] // chips
    fast = width == LANES and entries == 2
    me = lax.axis_index("pw")
    where = jnp.stack([me % 2, me // 2, me])

    own_table = couplings[0]
    across = swap_square(own_table, SQUARE)
    sent, kept = tuple(range(1, SQUARE)), (0,)
    if fast:
        flipped = load(where, projectors)
        theirs, ours = project(where, flipped, band_coeffs, sent)
        low_theirs, low_ours = project(where, flipped, band_coeffs, kept)
        near, low_theirs = choose(where, owners, own_table, across, low_theirs)
    else:
        theirs, ours = project_plain(where, projectors, band_coeffs, sent)
        low_theirs, low_ours = project_plain(where, projectors, band_coeffs, kept)
        near, low_theirs = choose_plain(where, owners, own_table, across, low_theirs, chips)
    theirs, near = lax.optimization_barrier((swap_cores(theirs), near))
    messages = pack(ours, theirs)
    low_theirs = swap_cores(low_theirs)
    gots = [swap_square(message, part) for message, part in zip(messages, sent)]
    quarters = quarters_of(where, near, low_theirs)
    quarters = [quarters[0]] + [swap_square(quarters[part], part) for part in sent]
    allowed = mask(where, counts, atom_of, messages[0])

    total, message, quarter = fold(low_ours, low_theirs, gots, quarters)
    got = swap_square(message, SQUARE)
    coupling = coupling_of(where, allowed, [quarter] + [swap_square(quarter, part) for part in sent])
    distance = SQUARE
    while 2 * distance < chips:
        distance *= 2
        total = total + got.astype(jnp.float32)
        order = jnp.array([entry ^ (distance // SQUARE) for entry in range(entries)])
        got = swap_square(total[order].astype(jnp.bfloat16), distance)

    scaled = couple(coupling, total, got)
    gathered = [scaled] + [swap_square(scaled, part) for part in sent]
    if not fast:
        mine = jnp.concatenate(gathered)
        return apply_plain(where, projectors, mine, swap_cores(mine))
    first, second, third = gathered[3], gathered[1], gathered[2]
    out = apply(where, projectors, scaled, swap_cores(scaled), 0, None)
    first, out = lax.optimization_barrier((first, out))
    others = swap_cores(first), swap_cores(second)
    out = apply(where, projectors, first, others[0], 3, out)
    third, out = lax.optimization_barrier((third, out))
    last = swap_cores(third)
    out = apply(where, projectors, second, others[1], 1, out)
    return apply(where, projectors, third, last, 2, out)


def solution(mesh):
    placed = (
        P("pw", "group"),
        P("pw", "group"),
        P("group", None),
        P("group", None),
        P("group"),
        P("pw", "group", None),
    )
    return jax.shard_map(
        local, mesh=mesh, in_specs=placed, out_specs=P("pw", "group"), check_vma=False
    )
```

```python
import jax
import jax.numpy as jnp
from jax import lax
from jax.experimental import pallas as pl
from jax.experimental.pallas import tpu as pltpu
from jax.sharding import PartitionSpec as P

CHANNELS = 4
CH_CAP = 64
PCAP = 256
LANES = 128
SQUARE = 4
QUARTER = PCAP // SQUARE
ROW_BLOCK = 512
COPY_ROWS = 128
PARAMS = pltpu.CompilerParams(vmem_limit_bytes=40 * 1024 * 1024)
VMEM = pl.BlockSpec(memory_space=pltpu.VMEM)
SMEM = pl.BlockSpec(memory_space=pltpu.SMEM)
HBM = pl.BlockSpec(memory_space=pltpu.HBM)
ANY = pl.BlockSpec(memory_space=pl.ANY)


def swap(x, distance):
    count = lax.axis_size("pw")
    return lax.ppermute(x, "pw", [(i, i ^ distance) for i in range(count)])


def swap_cores(x):
    return swap(x, 1)


def swap_square(x, part):
    return swap(x, 2 * part)


def load_kernel(where, projectors, flipped, slots, sems):
    core = where[0]
    count = sems.shape[0]
    block = slots.shape[0] // count
    copies = []
    for at in range(count):
        rows = slice(at * block, (at + 1) * block)
        copies.append(pltpu.make_async_copy(projectors.at[rows], slots.at[rows], sems.at[at]))
        copies[-1].start()
    for at, copy in enumerate(copies):
        copy.wait()
        rows = slice(at * block, (at + 1) * block)
        for place, group in enumerate((core, 1 - core)):
            start = pl.multiple_of(group * PCAP, PCAP)
            flipped[place * PCAP : (place + 1) * PCAP, rows] = slots[rows, pl.ds(start, PCAP)].T


def load(where, projectors):
    depth, slots = projectors.shape
    return pl.pallas_call(
        load_kernel,
        in_specs=[SMEM, HBM],
        out_specs=VMEM,
        out_shape=jax.ShapeDtypeStruct((slots, depth), jnp.bfloat16),
        scratch_shapes=[pltpu.VMEM((depth, slots), jnp.bfloat16), pltpu.SemaphoreType.DMA((4,))],
        compiler_params=PARAMS,
        name="load",
    )(where, pltpu.with_memory_space_constraint(projectors, pltpu.HBM))


def project_kernel(where, flipped, columns, theirs, ours):
    corner = where[1] & 3
    for first in range(0, SQUARE, 2):
        lanes = slice(first * LANES, (first + 2) * LANES)
        sums = jnp.dot(flipped[...], columns[:, lanes], preferred_element_type=jnp.float32)
        for at in range(2):
            part = corner ^ (first + at)
            block = sums[:, at * LANES : (at + 1) * LANES]
            ours[part] = block[:PCAP]
            theirs[part] = block[PCAP:].astype(theirs.dtype)


def project(where, flipped, band_coeffs, half):
    depth, bands = band_coeffs.shape
    wide = bands // 2
    return pl.pallas_call(
        project_kernel,
        grid=(1,),
        in_specs=[
            SMEM,
            pl.BlockSpec(flipped.shape, lambda i: (0, 0)),
            pl.BlockSpec((depth, wide), lambda i: (0, half)),
        ],
        out_specs=[pl.BlockSpec((SQUARE, PCAP, LANES), lambda i: (0, 0, 0))] * 2,
        out_shape=[
            jax.ShapeDtypeStruct((SQUARE, PCAP, LANES), jnp.bfloat16),
            jax.ShapeDtypeStruct((SQUARE, PCAP, LANES), jnp.float32),
        ],
        compiler_params=PARAMS,
        cost_estimate=pl.CostEstimate(
            flops=4 * depth * PCAP * wide, bytes_accessed=2 * depth * wide, transcendentals=0
        ),
        name="project",
    )(where, flipped, pltpu.with_memory_space_constraint(band_coeffs, pltpu.VMEM))


def parts_plain(where, blocks):
    order = jnp.arange(SQUARE) ^ (where[1] & 3)
    return jnp.take(blocks, order, axis=1)


def project_plain(where, projectors, band_coeffs, half):
    depth, bands = band_coeffs.shape
    width = 2 * bands // lax.axis_size("pw")
    columns = band_coeffs[:, half * bands // 2 : (half + 1) * bands // 2]
    outs = []
    for group, dtype in ((1 - where[0], jnp.bfloat16), (where[0], jnp.float32)):
        slots = lax.dynamic_slice_in_dim(projectors, group * PCAP, PCAP, 1)
        sums = lax.dot_general(slots, columns, (((0,), (0,)), ((), ())), preferred_element_type=jnp.float32)
        blocks = sums.reshape(PCAP, -1, SQUARE, width).transpose(1, 2, 0, 3)
        blocks = parts_plain(where, blocks).transpose(1, 0, 2, 3)
        outs.append(blocks.reshape(SQUARE, -1, width).astype(dtype))
    return outs


def quarter_of(where, owners, own, sibling, part, width):
    core, chip, me = where[0], where[1], where[2]
    owner = jnp.where(core == 0, owners[0], owners[1])
    rows = pl.ds(pl.multiple_of(((chip & 3) ^ part) * QUARTER, QUARTER), QUARTER)
    piece = jnp.where(owner == me, own[rows], jnp.where(owner == (me ^ 1), sibling[rows], 0.0))
    piece = piece.astype(jnp.bfloat16)
    return jnp.concatenate([piece[:, cut : cut + width] for cut in range(0, PCAP, width)], axis=0)


def pack_kernel(ours, theirs, *messages):
    for at, message in enumerate(messages):
        message[...] = (ours[at + 1] + theirs[at + 1].astype(jnp.float32)).astype(message.dtype)


def pack_table_kernel(where, owners, ours, theirs, own, sibling, quarter, *messages):
    _, rows, width = ours.shape
    for at, message in enumerate(messages):
        message[:rows] = (ours[at + 1] + theirs[at + 1].astype(jnp.float32)).astype(message.dtype)
        message[rows:] = quarter_of(where, owners, own, sibling, at + 1, width)
    quarter[...] = quarter_of(where, owners, own, sibling, 0, width)


def pack(where, owners, ours, theirs, tables):
    _, rows, width = ours.shape
    kernel, in_specs, operands, out_shape = pack_kernel, [VMEM, VMEM], (ours, theirs), []
    if tables is not None:
        kernel = pack_table_kernel
        in_specs = [SMEM, SMEM] + [VMEM] * 4
        operands = (where, owners, ours, theirs) + tables
        extra = QUARTER * PCAP // width
        out_shape = [jax.ShapeDtypeStruct((extra, width), jnp.bfloat16)]
        rows += extra
    out_shape = out_shape + [jax.ShapeDtypeStruct((rows, width), jnp.bfloat16)] * (SQUARE - 1)
    return pl.pallas_call(
        kernel,
        in_specs=in_specs,
        out_specs=[VMEM] * len(out_shape),
        out_shape=out_shape,
        compiler_params=PARAMS,
        name="pack",
    )(*operands)


def fold_kernel(ours, theirs, *refs):
    gots, quarters, (kept, message) = refs[: SQUARE - 1], refs[SQUARE - 1 : -2], refs[-2:]
    rows = ours.shape[1]
    total = ours[0] + theirs[0].astype(jnp.float32)
    for got in gots:
        total = total + got[:rows].astype(jnp.float32)
    kept[:rows] = total
    message[:rows] = total.astype(message.dtype)
    for quarter in quarters:
        table = quarter[...]
        for got in gots:
            table = table + got[rows:]
        kept[rows:] = table.astype(kept.dtype)
        message[rows:] = table


def fold(ours, theirs, gots, quarters):
    shape = gots[0].shape
    return pl.pallas_call(
        fold_kernel,
        in_specs=[VMEM] * (1 + SQUARE + len(quarters)),
        out_specs=[VMEM, VMEM],
        out_shape=[jax.ShapeDtypeStruct(shape, jnp.float32), jax.ShapeDtypeStruct(shape, jnp.bfloat16)],
        compiler_params=PARAMS,
        name="fold",
    )(ours, theirs, *gots, *quarters)


def add_kernel(left, right, out):
    out[...] = (left[...] + right[...].astype(jnp.float32)).astype(out.dtype)


def add(left, right):
    return pl.pallas_call(
        add_kernel,
        in_specs=[VMEM, VMEM],
        out_specs=VMEM,
        out_shape=jax.ShapeDtypeStruct(left.shape, jnp.bfloat16),
        compiler_params=PARAMS,
        name="add",
    )(left, right)


def mask_kernel(where, counts, atom_of, after, out):
    del after
    core = where[0]
    slot = lax.broadcasted_iota(jnp.int32, (1, PCAP), 1)
    limit = jnp.zeros((1, PCAP), jnp.int32)
    for channel in range(CHANNELS):
        limit = jnp.where(slot >= channel * CH_CAP, channel * CH_CAP + counts[core, channel], limit)
    atoms = jnp.where(core == 0, atom_of[0:1], atom_of[1:2])
    code = jnp.broadcast_to(jnp.where(slot < limit, atoms, -1), (PCAP, PCAP))
    out[...] = jnp.where((code == code.T) & (code >= 0), 1.0, 0.0).astype(out.dtype)


def mask(where, counts, atom_of, after):
    return pl.pallas_call(
        mask_kernel,
        in_specs=[SMEM, SMEM, VMEM, ANY],
        out_specs=VMEM,
        out_shape=jax.ShapeDtypeStruct((PCAP, PCAP), jnp.bfloat16),
        compiler_params=PARAMS,
        name="mask",
    )(where, counts, atom_of, after)


def scale(coupling, messages, rows, out):
    width = out.shape[2]
    wide = [message[at : at + PCAP] for message in messages for at in range(0, rows, PCAP)]
    scaled = jnp.dot(coupling[...], jnp.concatenate(wide, axis=1), preferred_element_type=jnp.float32)
    scaled = scaled.astype(out.dtype)
    for at in range(len(wide)):
        part, first = at * PCAP // rows, at * PCAP % rows
        out[part, first : first + PCAP] = scaled[:, at * width : (at + 1) * width]


def couple_first_kernel(where, allowed, *refs):
    *messages, out, coupling = refs
    _, rows, width = out.shape
    for part, message in enumerate(messages):
        start = pl.multiple_of(((where[1] & 3) ^ part) * QUARTER, QUARTER)
        for cut in range(PCAP // width):
            lanes = slice(cut * width, (cut + 1) * width)
            first = rows + cut * QUARTER
            coupling[pl.ds(start, QUARTER), lanes] = (
                message[first : first + QUARTER] * allowed[pl.ds(start, QUARTER), lanes]
            )
    scale(coupling, messages, rows, out)


def couple_first(where, allowed, messages, rows):
    width = messages[0].shape[1]
    return pl.pallas_call(
        couple_first_kernel,
        in_specs=[SMEM] + [VMEM] * (1 + SQUARE),
        out_specs=[VMEM, VMEM],
        out_shape=[
            jax.ShapeDtypeStruct((SQUARE, rows, width), jnp.bfloat16),
            jax.ShapeDtypeStruct((PCAP, PCAP), jnp.bfloat16),
        ],
        compiler_params=PARAMS,
        name="couple_first",
    )(where, allowed, *messages)


def couple_kernel(coupling, *refs):
    *messages, out = refs
    scale(coupling, messages, out.shape[1], out)


def couple(coupling, messages):
    rows, width = messages[0].shape
    return pl.pallas_call(
        couple_kernel,
        in_specs=[VMEM] * (1 + SQUARE),
        out_specs=VMEM,
        out_shape=jax.ShapeDtypeStruct((SQUARE, rows, width), jnp.bfloat16),
        compiler_params=PARAMS,
        name="couple",
    )(coupling, *messages)


def apply_kernel(half, where, projectors, mine, other, *refs):
    out, weights, blocks, sems = refs[-4:]
    core, corner = where[0], where[1] & 3
    for scaled, group in ((mine, core), (other, 1 - core)):
        rows = pl.ds(pl.multiple_of(group * PCAP, PCAP), PCAP)
        for part in range(SQUARE):
            start = pl.multiple_of((corner ^ part) * LANES, LANES)
            weights[rows, pl.ds(start, LANES)] = scaled[part]
    wide = weights.shape[1]
    copies = []
    for block in range(projectors.shape[0] // ROW_BLOCK):
        rows = slice(block * ROW_BLOCK, (block + 1) * ROW_BLOCK)
        blocks[rows] = jnp.dot(
            projectors[rows], weights[...], preferred_element_type=jnp.float32
        ).astype(blocks.dtype)
        for start in range(block * ROW_BLOCK, (block + 1) * ROW_BLOCK, COPY_ROWS):
            written = slice(start, start + COPY_ROWS)
            copies.append(
                pltpu.make_async_copy(
                    blocks.at[written],
                    out.at[written, half * wide : (half + 1) * wide],
                    sems.at[len(copies)],
                )
            )
            copies[-1].start()
    for copy in copies:
        copy.wait()


def apply(where, projectors, mine, other, half, out):
    depth, slots = projectors.shape
    wide = SQUARE * LANES

    def kernel(*refs):
        apply_kernel(half, *refs)

    operands = [where, projectors, mine, other] + ([] if out is None else [out])
    return pl.pallas_call(
        kernel,
        in_specs=[SMEM, VMEM, VMEM, VMEM] + ([] if out is None else [HBM]),
        out_specs=HBM,
        out_shape=jax.ShapeDtypeStruct((depth, 2 * wide), jnp.bfloat16),
        input_output_aliases={} if out is None else {4: 0},
        scratch_shapes=[
            pltpu.VMEM((slots, wide), jnp.bfloat16),
            pltpu.VMEM((depth, wide), jnp.bfloat16),
            pltpu.SemaphoreType.DMA((depth // COPY_ROWS,)),
        ],
        compiler_params=PARAMS,
        cost_estimate=pl.CostEstimate(
            flops=2 * depth * slots * wide, bytes_accessed=2 * depth * (slots + wide), transcendentals=0
        ),
        name="apply",
    )(*operands)


def apply_plain(where, projectors, halves):
    columns = []
    for mine, other in halves:
        rows = []
        for group in range(2):
            blocks = jnp.where(where[0] == group, mine, other)
            width = blocks.shape[2]
            blocks = blocks.reshape(SQUARE, -1, PCAP, width).transpose(1, 0, 2, 3)
            blocks = parts_plain(where, blocks).transpose(2, 0, 1, 3)
            rows.append(blocks.reshape(PCAP, -1))
        columns.append(jnp.concatenate(rows))
    scaled = jnp.concatenate(columns, axis=1)
    return jnp.dot(projectors, scaled, preferred_element_type=jnp.float32).astype(jnp.bfloat16)


def local(band_coeffs, projectors, counts, atom_of, owners, couplings):
    chips = lax.axis_size("pw") // 2
    width = band_coeffs.shape[1] // chips
    rows = chips // (2 * SQUARE) * PCAP
    fast = width == LANES and rows == PCAP
    me = lax.axis_index("pw")
    where = jnp.stack([me % 2, me // 2, me])
    sent = range(1, SQUARE)

    def partial(half):
        if fast:
            return project(where, flipped, band_coeffs, half)
        return project_plain(where, projectors, band_coeffs, half)

    def scatter(messages):
        return [swap_square(message, part) for message, part in zip(messages, sent)]

    def across(total, got):
        distance = 2 * SQUARE
        while distance < chips:
            mine = add(total, got)
            total, got = mine.astype(jnp.float32), swap_square(mine, distance)
            distance *= 2
        return add(total, got)

    def gather(mine):
        return [mine] + [swap_square(mine, part) for part in sent]

    own_table = couplings[0]
    sibling_table = swap_cores(own_table)
    flipped = load(where, projectors) if fast else None
    theirs, ours = partial(0)
    late_theirs, late_ours = partial(1)
    theirs, late_ours = lax.optimization_barrier((swap_cores(theirs), late_ours))
    late_theirs = swap_cores(late_theirs)
    quarter, *messages = pack(where, owners, ours, theirs, (own_table, sibling_table))
    allowed = mask(where, counts, atom_of, quarter)
    gots = scatter(messages)
    late_messages = pack(where, owners, late_ours, late_theirs, None)
    gots[0], late_messages = lax.optimization_barrier((gots[0], late_messages))
    late_gots = scatter(late_messages)
    total, message = fold(ours, theirs, gots, [quarter])
    got = swap_square(message, SQUARE)
    late_total, message = fold(late_ours, late_theirs, late_gots, [])
    got, message = lax.optimization_barrier((got, message))
    late_got = swap_square(message, SQUARE)
    gathered = gather(across(total, got))
    late_mine = across(late_total, late_got)
    gathered[1], late_mine = lax.optimization_barrier((gathered[1], late_mine))
    late_gathered = gather(late_mine)

    scaled, coupling = couple_first(where, allowed, gathered, rows)
    halves = [(scaled, swap_cores(scaled))]
    if fast:
        out = apply(where, projectors, *halves[0], 0, None)
        late_gathered[1], out = lax.optimization_barrier((late_gathered[1], out))
    scaled = couple(coupling, late_gathered)
    halves.append((scaled, swap_cores(scaled)))
    if not fast:
        return apply_plain(where, projectors, halves)
    return apply(where, projectors, *halves[1], 1, out)


def solution(mesh):
    placed = (
        P("pw", "group"),
        P("pw", "group"),
        P("group", None),
        P("group", None),
        P("group"),
        P("pw", "group", None),
    )
    return jax.shard_map(
        local, mesh=mesh, in_specs=placed, out_specs=P("pw", "group"), check_vma=False
    )
```

```python
import jax
import jax.numpy as jnp
from jax import lax
from jax.experimental import pallas as pl
from jax.experimental.pallas import tpu as pltpu
from jax.sharding import PartitionSpec as P

CHANNELS = 4
CH_CAP = 64
PCAP = 256
LANES = 128
SQUARE = 4
QUARTER = PCAP // SQUARE
ROW_BLOCK = 512
COPY_ROWS = 128
PARAMS = pltpu.CompilerParams(vmem_limit_bytes=40 * 1024 * 1024)
VMEM = pl.BlockSpec(memory_space=pltpu.VMEM)
SMEM = pl.BlockSpec(memory_space=pltpu.SMEM)
HBM = pl.BlockSpec(memory_space=pltpu.HBM)
ANY = pl.BlockSpec(memory_space=pl.ANY)


def block_of(chip, part, entry):
    return chip ^ (part + SQUARE * entry)


def swap(x, distance):
    count = lax.axis_size("pw")
    return lax.ppermute(x, "pw", [(i, i ^ distance) for i in range(count)])


def swap_cores(x):
    return swap(x, 1)


def swap_chips(x, distance):
    return swap(x, 2 * distance)


def swap_first(x):
    count = lax.axis_size("pw")
    return lax.ppermute(x, "pw", [(i, i ^ (2, 4)[i % 2]) for i in range(count)])


def swap_second(x):
    count = lax.axis_size("pw")
    return lax.ppermute(x, "pw", [(i, i ^ (4, 2)[i % 2]) for i in range(count)])


def load_kernel(where, projectors, flipped, slots, sems):
    core = where[0]
    count = sems.shape[0]
    block = slots.shape[0] // count
    copies = []
    for at in range(count):
        rows = slice(at * block, (at + 1) * block)
        copies.append(pltpu.make_async_copy(projectors.at[rows], slots.at[rows], sems.at[at]))
        copies[-1].start()
    for at, copy in enumerate(copies):
        copy.wait()
        rows = slice(at * block, (at + 1) * block)
        for place, group in enumerate((core, 1 - core)):
            start = pl.multiple_of(group * PCAP, PCAP)
            flipped[place * PCAP : (place + 1) * PCAP, rows] = slots[rows, pl.ds(start, PCAP)].T


def load(where, projectors):
    depth, slots = projectors.shape
    return pl.pallas_call(
        load_kernel,
        in_specs=[SMEM, HBM],
        out_specs=VMEM,
        out_shape=jax.ShapeDtypeStruct((slots, depth), jnp.bfloat16),
        scratch_shapes=[pltpu.VMEM((depth, slots), jnp.bfloat16), pltpu.SemaphoreType.DMA((4,))],
        compiler_params=PARAMS,
        name="load",
    )(where, pltpu.with_memory_space_constraint(projectors, pltpu.HBM))


def project_kernel(parts, where, flipped, columns, theirs, ours):
    chip = where[1]
    for at, part in enumerate(parts):
        starts = [pl.multiple_of(block_of(chip, part, entry) * LANES, LANES) for entry in range(2)]
        pair = jnp.concatenate([columns[:, pl.ds(start, LANES)] for start in starts], axis=1)
        sums = jnp.dot(flipped[...], pair, preferred_element_type=jnp.float32)
        for entry in range(2):
            lanes = slice(entry * LANES, (entry + 1) * LANES)
            ours[2 * at + entry] = sums[:PCAP, lanes]
            theirs[2 * at + entry] = sums[PCAP:, lanes].astype(theirs.dtype)


def project(where, flipped, band_coeffs, parts):
    depth, bands = band_coeffs.shape
    count = 2 * len(parts)

    def kernel(*refs):
        project_kernel(parts, *refs)

    return pl.pallas_call(
        kernel,
        in_specs=[SMEM, VMEM, VMEM],
        out_specs=[VMEM, VMEM],
        out_shape=[
            jax.ShapeDtypeStruct((count, PCAP, LANES), jnp.bfloat16),
            jax.ShapeDtypeStruct((count, PCAP, LANES), jnp.float32),
        ],
        compiler_params=PARAMS,
        cost_estimate=pl.CostEstimate(
            flops=4 * depth * PCAP * count * LANES, bytes_accessed=2 * depth * count * LANES, transcendentals=0
        ),
        name="project",
    )(where, flipped, pltpu.with_memory_space_constraint(band_coeffs, pltpu.VMEM))


def project_plain(where, projectors, band_coeffs, parts):
    depth, bands = band_coeffs.shape
    chips = lax.axis_size("pw") // 2
    blocks = jnp.stack([block_of(where[1], q, r) for q in parts for r in range(chips // SQUARE)])
    columns = jnp.take(band_coeffs.reshape(depth, chips, bands // chips), blocks, axis=1)
    outs = []
    for group, dtype in ((1 - where[0], jnp.bfloat16), (where[0], jnp.float32)):
        slots = lax.dynamic_slice_in_dim(projectors, group * PCAP, PCAP, 1)
        sums = jnp.einsum("ds,dhw->hsw", slots, columns, preferred_element_type=jnp.float32)
        outs.append(sums.astype(dtype))
    return outs


def choose_kernel(where, owners, own, sibling, after, out):
    del after
    core, chip, me = where[0], where[1], where[2]
    owner = jnp.where(core == 0, owners[0], owners[1])
    width = out.shape[2]
    for part in range(SQUARE):
        rows = pl.ds(pl.multiple_of(((chip & 3) ^ part) * QUARTER, QUARTER), QUARTER)
        piece = jnp.where(owner == me, own[rows], jnp.where(owner == (me ^ 1), sibling[rows], 0.0))
        for cut in range(PCAP // width):
            out[part, cut * QUARTER : (cut + 1) * QUARTER] = piece[:, cut * width : (cut + 1) * width].astype(
                out.dtype
            )


def choose(where, owners, own, sibling, width, after):
    return pl.pallas_call(
        choose_kernel,
        in_specs=[SMEM, SMEM, VMEM, VMEM, ANY],
        out_specs=VMEM,
        out_shape=jax.ShapeDtypeStruct((SQUARE, QUARTER * PCAP // width, width), jnp.bfloat16),
        compiler_params=PARAMS,
        name="choose",
    )(where, owners, own, sibling, after)


def send_kernel(first, second, where, ours, theirs, quarters, message):
    entries = ours.shape[0] // (1 if first == second else 2)
    start, part = (0, first) if first == second else (where[0] * entries, 1 + where[0])
    for entry in range(entries):
        total = ours[start + entry] + theirs[start + entry].astype(jnp.float32)
        message[entry * PCAP : (entry + 1) * PCAP] = total.astype(message.dtype)
    message[entries * PCAP :] = quarters[part]


def send(where, ours, theirs, quarters, parts):
    count, _, width = ours.shape
    rows = count // len(parts) * PCAP + quarters.shape[1]

    def kernel(*refs):
        send_kernel(parts[0], parts[-1], *refs)

    return pl.pallas_call(
        kernel,
        in_specs=[SMEM] + [VMEM] * 3,
        out_specs=VMEM,
        out_shape=jax.ShapeDtypeStruct((rows, width), jnp.bfloat16),
        compiler_params=PARAMS,
        name="send",
    )(where, ours, theirs, quarters)


def forward_kernel(where, ours, theirs, quarters, got, message):
    entries = ours.shape[0] // 2
    start = (1 - where[0]) * entries
    for entry in range(entries):
        rows = slice(entry * PCAP, (entry + 1) * PCAP)
        total = ours[start + entry] + theirs[start + entry].astype(jnp.float32)
        message[rows] = (total + got[rows].astype(jnp.float32)).astype(message.dtype)
    message[entries * PCAP :] = quarters[2 - where[0]] + got[entries * PCAP :]


def forward(where, ours, theirs, quarters, got):
    return pl.pallas_call(
        forward_kernel,
        in_specs=[SMEM] + [VMEM] * 4,
        out_specs=VMEM,
        out_shape=jax.ShapeDtypeStruct(got.shape, got.dtype),
        compiler_params=PARAMS,
        name="forward",
    )(where, ours, theirs, quarters, got)


def fold_kernel(ours, theirs, quarters, *refs):
    *gots, kept, message = refs
    entries = ours.shape[0]
    for entry in range(entries):
        rows = slice(entry * PCAP, (entry + 1) * PCAP)
        total = ours[entry] + theirs[entry].astype(jnp.float32)
        for got in gots:
            total = total + got[rows].astype(jnp.float32)
        kept[rows] = total
        away = entry ^ 1
        message[away * PCAP : (away + 1) * PCAP] = total.astype(message.dtype)
    table = quarters[0]
    for got in gots:
        table = table + got[entries * PCAP :]
    kept[entries * PCAP :] = table.astype(kept.dtype)
    message[entries * PCAP :] = table


def fold(ours, theirs, quarters, gots):
    shape = gots[0].shape
    return pl.pallas_call(
        fold_kernel,
        in_specs=[VMEM] * (3 + len(gots)),
        out_specs=[VMEM, VMEM],
        out_shape=[jax.ShapeDtypeStruct(shape, jnp.float32), jax.ShapeDtypeStruct(shape, jnp.bfloat16)],
        compiler_params=PARAMS,
        name="fold",
    )(ours, theirs, quarters, *gots)


def add_kernel(left, right, out):
    out[...] = (left[...] + right[...].astype(jnp.float32)).astype(out.dtype)


def add(left, right):
    return pl.pallas_call(
        add_kernel,
        in_specs=[VMEM, VMEM],
        out_specs=VMEM,
        out_shape=jax.ShapeDtypeStruct(left.shape, jnp.bfloat16),
        compiler_params=PARAMS,
        name="add",
    )(left, right)


def mask_kernel(where, counts, atom_of, after, out):
    del after
    core = where[0]
    slot = lax.broadcasted_iota(jnp.int32, (1, PCAP), 1)
    limit = jnp.zeros((1, PCAP), jnp.int32)
    for channel in range(CHANNELS):
        limit = jnp.where(slot >= channel * CH_CAP, channel * CH_CAP + counts[core, channel], limit)
    atoms = jnp.where(core == 0, atom_of[0:1], atom_of[1:2])
    code = jnp.broadcast_to(jnp.where(slot < limit, atoms, -1), (PCAP, PCAP))
    out[...] = jnp.where((code == code.T) & (code >= 0), 1.0, 0.0).astype(out.dtype)


def mask(where, counts, atom_of, after):
    return pl.pallas_call(
        mask_kernel,
        in_specs=[SMEM, SMEM, VMEM, ANY],
        out_specs=VMEM,
        out_shape=jax.ShapeDtypeStruct((PCAP, PCAP), jnp.bfloat16),
        compiler_params=PARAMS,
        name="mask",
    )(where, counts, atom_of, after)


def couple_kernel(where, allowed, *refs):
    *messages, out, coupling = refs
    width = out.shape[2]
    entries = out.shape[0] // SQUARE
    parts = (0, 1 + where[0], 2 - where[0], 3)
    for part, message in zip(parts, messages):
        start = pl.multiple_of(((where[1] & 3) ^ part) * QUARTER, QUARTER)
        for cut in range(PCAP // width):
            lanes = slice(cut * width, (cut + 1) * width)
            first = entries * PCAP + cut * QUARTER
            coupling[pl.ds(start, QUARTER), lanes] = (
                message[first : first + QUARTER] * allowed[pl.ds(start, QUARTER), lanes]
            )
    for part, message in zip(parts, messages):
        wide = jnp.concatenate([message[e * PCAP : (e + 1) * PCAP] for e in range(entries)], axis=1)
        scaled = jnp.dot(coupling[...], wide, preferred_element_type=jnp.float32).astype(out.dtype)
        for entry in range(entries):
            out[part * entries + entry] = scaled[:, entry * width : (entry + 1) * width]


def couple(where, allowed, messages):
    rows, width = messages[0].shape
    entries = (rows - QUARTER * PCAP // width) // PCAP
    return pl.pallas_call(
        couple_kernel,
        in_specs=[SMEM] + [VMEM] * (1 + SQUARE),
        out_specs=VMEM,
        out_shape=jax.ShapeDtypeStruct((SQUARE * entries, PCAP, width), jnp.bfloat16),
        scratch_shapes=[pltpu.VMEM((PCAP, PCAP), jnp.bfloat16)],
        compiler_params=PARAMS,
        name="couple",
    )(where, allowed, *messages)


def begin_kernel(where, projectors, scaled, *outs):
    slots = pl.ds(pl.multiple_of(where[0] * PCAP, PCAP), PCAP)
    for part, out in enumerate(outs):
        weights = jnp.concatenate([scaled[2 * part], scaled[2 * part + 1]], axis=1)
        for block in range(projectors.shape[0] // ROW_BLOCK):
            rows = slice(block * ROW_BLOCK, (block + 1) * ROW_BLOCK)
            out[rows] = jnp.dot(projectors[rows, slots], weights, preferred_element_type=jnp.float32)


def begin(where, projectors, scaled):
    depth, slots = projectors.shape
    count = SQUARE - 1
    return pl.pallas_call(
        begin_kernel,
        in_specs=[SMEM, VMEM, VMEM],
        out_specs=[VMEM] * count,
        out_shape=[jax.ShapeDtypeStruct((depth, 2 * LANES), jnp.float32)] * count,
        compiler_params=PARAMS,
        cost_estimate=pl.CostEstimate(
            flops=2 * depth * slots * LANES * count, bytes_accessed=2 * depth * slots, transcendentals=0
        ),
        name="begin",
    )(where, projectors, scaled)


def finish_kernel(where, projectors, mine, other, *refs):
    *begun, out, weights, blocks, sems = refs
    core, chip = where[0], where[1]
    last = 2 * len(begun)
    for part, group in ((mine, core), (other, 1 - core)):
        rows = pl.ds(pl.multiple_of(group * PCAP, PCAP), PCAP)
        weights[rows, :LANES] = part[last]
        weights[rows, LANES:] = part[last + 1]
    slots = pl.ds(pl.multiple_of((1 - core) * PCAP, PCAP), PCAP)
    copies = []

    def put(rows, part, sums):
        for entry in range(2):
            start = pl.multiple_of(block_of(chip, part, entry) * LANES, LANES)
            blocks[rows, pl.ds(start, LANES)] = sums[:, entry * LANES : (entry + 1) * LANES].astype(blocks.dtype)

    for block in range(projectors.shape[0] // ROW_BLOCK):
        rows = slice(block * ROW_BLOCK, (block + 1) * ROW_BLOCK)
        put(rows, len(begun), jnp.dot(projectors[rows], weights[...], preferred_element_type=jnp.float32))
        for part, partial in enumerate(begun):
            pair = jnp.concatenate([other[2 * part], other[2 * part + 1]], axis=1)
            sums = jnp.dot(projectors[rows, slots], pair, preferred_element_type=jnp.float32)
            put(rows, part, partial[rows] + sums)
        for piece in range(ROW_BLOCK // COPY_ROWS):
            start = block * ROW_BLOCK + piece * COPY_ROWS
            written = slice(start, start + COPY_ROWS)
            copies.append(pltpu.make_async_copy(blocks.at[written], out.at[written], sems.at[len(copies)]))
            copies[-1].start()
    for copy in copies:
        copy.wait()


def finish(where, projectors, mine, other, begun):
    depth, slots = projectors.shape
    bands = mine.shape[0] * LANES
    return pl.pallas_call(
        finish_kernel,
        in_specs=[SMEM] + [VMEM] * (3 + len(begun)),
        out_specs=HBM,
        out_shape=jax.ShapeDtypeStruct((depth, bands), jnp.bfloat16),
        scratch_shapes=[
            pltpu.VMEM((slots, 2 * LANES), jnp.bfloat16),
            pltpu.VMEM((depth, bands), jnp.bfloat16),
            pltpu.SemaphoreType.DMA((depth // COPY_ROWS,)),
        ],
        compiler_params=PARAMS,
        cost_estimate=pl.CostEstimate(
            flops=depth * slots * bands, bytes_accessed=2 * depth * (slots + bands), transcendentals=0
        ),
        name="finish",
    )(where, projectors, mine, other, *begun)


def apply_plain(where, projectors, mine, other):
    chips, _, width = mine.shape
    blocks = jnp.stack([block_of(where[1], q, r) for q in range(SQUARE) for r in range(chips // SQUARE)])
    rows = []
    for group in range(2):
        part = jnp.where(where[0] == group, mine, other)
        part = jnp.zeros_like(part).at[blocks].set(part)
        rows.append(part.transpose(1, 0, 2).reshape(PCAP, chips * width))
    return jnp.dot(projectors, jnp.concatenate(rows), preferred_element_type=jnp.float32).astype(jnp.bfloat16)


def local(band_coeffs, projectors, counts, atom_of, owners, couplings):
    chips = lax.axis_size("pw") // 2
    entries = chips // SQUARE
    width = band_coeffs.shape[1] // chips
    fast = width == LANES and entries == 2
    me = lax.axis_index("pw")
    where = jnp.stack([me % 2, me // 2, me])

    own_table = couplings[0]
    sibling_table = swap_cores(own_table)
    pair = (1, 2)
    if fast:
        flipped = load(where, projectors)

        def partial(parts):
            return project(where, flipped, band_coeffs, parts)
    else:

        def partial(parts):
            return project_plain(where, projectors, band_coeffs, parts)

    theirs, ours = partial((3,))
    theirs = swap_cores(theirs)
    pair_theirs, pair_ours = partial(pair)
    quarters = choose(where, owners, own_table, sibling_table, width, ours)
    got = swap_first(send(where, ours, theirs, quarters, (3,)))
    pair_theirs = swap_cores(pair_theirs)
    low_theirs, low_ours = partial((0,))
    low_theirs = swap_cores(low_theirs)
    got_first = swap_first(send(where, pair_ours, pair_theirs, quarters, pair))
    message = forward(where, pair_ours, pair_theirs, quarters, got)
    got_second = swap_second(message)
    allowed = mask(where, counts, atom_of, message)

    total, message = fold(low_ours, low_theirs, quarters, [got_first, got_second])
    mine = add(total, swap_chips(message, SQUARE))
    distance = 2 * SQUARE
    while distance < chips:
        body = mine[: entries * PCAP].reshape(entries, PCAP, width)
        order = [entry ^ (distance // SQUARE) for entry in range(entries)]
        message = jnp.concatenate([body[jnp.array(order)].reshape(-1, width), mine[entries * PCAP :]])
        mine = add(mine.astype(jnp.float32), swap_chips(message, distance))
        distance *= 2

    second = swap_second(mine)
    first = swap_first(mine)
    scaled = couple(where, allowed, [mine, first, second, swap_first(second)])
    other = swap_cores(scaled)
    if not fast:
        return apply_plain(where, projectors, scaled, other)
    return finish(where, projectors, scaled, other, begin(where, projectors, scaled))


def solution(mesh):
    placed = (
        P("pw", "group"),
        P("pw", "group"),
        P("group", None),
        P("group", None),
        P("group"),
        P("pw", "group", None),
    )
    return jax.shard_map(
        local, mesh=mesh, in_specs=placed, out_specs=P("pw", "group"), check_vma=False
    )
```

```python
import jax
import jax.numpy as jnp
from jax import lax
from jax.experimental import pallas as pl
from jax.experimental.pallas import tpu as pltpu
from jax.sharding import PartitionSpec as P

CHANNELS = 4
CH_CAP = 64
PCAP = 256
LANES = 128
SQUARE = 4
QUARTER = PCAP // SQUARE
ROW_BLOCK = 512
ROW_BLOCKS = (512, 512, 512, 256, 256)
COPY_ROWS = 128
PARAMS = pltpu.CompilerParams(vmem_limit_bytes=40 * 1024 * 1024)
VMEM = pl.BlockSpec(memory_space=pltpu.VMEM)
SMEM = pl.BlockSpec(memory_space=pltpu.SMEM)
HBM = pl.BlockSpec(memory_space=pltpu.HBM)
ANY = pl.BlockSpec(memory_space=pl.ANY)


def place():
    me = lax.axis_index("pw")
    return lax.rem(me, 2), lax.div(me, 2)


def block_of(chip, part, entry):
    return chip ^ (part + SQUARE * entry)


def swap(x, distance):
    count = lax.axis_size("pw")
    return lax.ppermute(x, "pw", [(i, i ^ distance) for i in range(count)])


def swap_cores(x):
    return swap(x, 1)


def swap_square(x, part):
    return swap(x, 2 * part)


def pair_at(columns, rows, part):
    chip = place()[1]
    starts = [pl.multiple_of(block_of(chip, part, entry) * LANES, LANES) for entry in range(2)]
    return jnp.concatenate([columns[rows, pl.ds(start, LANES)] for start in starts], axis=1)


def keep_sums(ours, theirs, at, sums):
    for entry in range(2):
        lanes = slice(entry * LANES, (entry + 1) * LANES)
        ours[2 * at + entry] = sums[:PCAP, lanes]
        theirs[2 * at + entry] = sums[PCAP:, lanes].astype(theirs.dtype)


def project_sent_kernel(projectors, bands, theirs, ours, flipped, columns, slots, totals, slot_sems, column_sems):
    core = place()[0]
    count = slot_sems.shape[0]
    depth = slots.shape[0] // count
    copies = []
    for at in range(count):
        rows = slice(at * depth, (at + 1) * depth)
        copies.append(
            (
                pltpu.make_async_copy(projectors.at[rows], slots.at[rows], slot_sems.at[at]),
                pltpu.make_async_copy(bands.at[rows], columns.at[rows], column_sems.at[at]),
            )
        )
        for copy in copies[-1]:
            copy.start()
    for at in range(count):
        rows = slice(at * depth, (at + 1) * depth)
        copies[at][0].wait()
        for side, group in enumerate((core, 1 - core)):
            start = pl.multiple_of(group * PCAP, PCAP)
            flipped[side * PCAP : (side + 1) * PCAP, rows] = slots[rows, pl.ds(start, PCAP)].T
        copies[at][1].wait()
        for part in range(1, SQUARE):
            sums = jnp.dot(
                flipped[:, rows], pair_at(columns, rows, part), preferred_element_type=jnp.float32
            )
            if at:
                sums = totals[part - 1] + sums
            if at < count - 1:
                totals[part - 1] = sums
            else:
                keep_sums(ours, theirs, part - 1, sums)


def sums_shape(parts):
    shape = (2 * parts, PCAP, LANES)
    return [jax.ShapeDtypeStruct(shape, jnp.bfloat16), jax.ShapeDtypeStruct(shape, jnp.float32)]


def project_sent(projectors, band_coeffs):
    depth, slots = projectors.shape
    bands = band_coeffs.shape[1]
    blocks = 4
    return pl.pallas_call(
        project_sent_kernel,
        in_specs=[HBM, HBM],
        out_specs=[VMEM] * 4,
        out_shape=sums_shape(SQUARE - 1)
        + [
            jax.ShapeDtypeStruct((slots, depth), jnp.bfloat16),
            jax.ShapeDtypeStruct((depth, bands), jnp.bfloat16),
        ],
        scratch_shapes=[
            pltpu.VMEM((depth, slots), jnp.bfloat16),
            pltpu.VMEM((SQUARE - 1, slots, 2 * LANES), jnp.float32),
            pltpu.SemaphoreType.DMA((blocks,)),
            pltpu.SemaphoreType.DMA((blocks,)),
        ],
        compiler_params=PARAMS,
        cost_estimate=pl.CostEstimate(
            flops=2 * depth * slots * bands, bytes_accessed=2 * depth * (bands + slots), transcendentals=0
        ),
        name="project_sent",
    )(
        pltpu.with_memory_space_constraint(projectors, pltpu.HBM),
        pltpu.with_memory_space_constraint(band_coeffs, pltpu.HBM),
    )


def project_kept_kernel(flipped, columns, theirs, ours):
    rows = slice(0, columns.shape[0])
    sums = jnp.dot(flipped[...], pair_at(columns, rows, 0), preferred_element_type=jnp.float32)
    keep_sums(ours, theirs, 0, sums)


def project_kept(flipped, columns):
    slots, depth = flipped.shape
    return pl.pallas_call(
        project_kept_kernel,
        in_specs=[VMEM, VMEM],
        out_specs=[VMEM, VMEM],
        out_shape=sums_shape(1),
        compiler_params=PARAMS,
        cost_estimate=pl.CostEstimate(
            flops=4 * depth * slots * LANES, bytes_accessed=2 * depth * slots, transcendentals=0
        ),
        name="project_kept",
    )(flipped, columns)


def project_plain(projectors, band_coeffs, parts):
    depth, bands = band_coeffs.shape
    chips = lax.axis_size("pw") // 2
    blocks = jnp.stack([block_of(place()[1], q, r) for q in parts for r in range(chips // SQUARE)])
    columns = jnp.take(band_coeffs.reshape(depth, chips, bands // chips), blocks, axis=1)
    outs = []
    core = place()[0]
    for group, dtype in ((1 - core, jnp.bfloat16), (core, jnp.float32)):
        slots = lax.dynamic_slice_in_dim(projectors, group * PCAP, PCAP, 1)
        sums = jnp.einsum("ds,dhw->hsw", slots, columns, preferred_element_type=jnp.float32)
        outs.append(sums.astype(dtype))
    return outs


def choose_kernel(owners, own, sibling, after, out):
    del after
    core, chip = place()
    me = 2 * chip + core
    owner = jnp.where(core == 0, owners[0], owners[1])
    width = out.shape[2]
    for part in range(SQUARE):
        rows = pl.ds(pl.multiple_of(((chip & 3) ^ part) * QUARTER, QUARTER), QUARTER)
        piece = jnp.where(owner == me, own[rows], jnp.where(owner == (me ^ 1), sibling[rows], 0.0))
        for cut in range(PCAP // width):
            out[part, cut * QUARTER : (cut + 1) * QUARTER] = piece[:, cut * width : (cut + 1) * width].astype(
                out.dtype
            )


def choose(owners, own, sibling, width, after):
    return pl.pallas_call(
        choose_kernel,
        in_specs=[SMEM, VMEM, VMEM, ANY],
        out_specs=VMEM,
        out_shape=jax.ShapeDtypeStruct((SQUARE, QUARTER * PCAP // width, width), jnp.bfloat16),
        compiler_params=PARAMS,
        name="choose",
    )(owners, own, sibling, after)


def pack_kernel(ours, theirs, quarters, *messages):
    entries = ours.shape[0] // len(messages)
    for at, message in enumerate(messages):
        for entry in range(entries):
            place = at * entries + entry
            total = ours[place] + theirs[place].astype(jnp.float32)
            message[entry * PCAP : (entry + 1) * PCAP] = total.astype(message.dtype)
        message[entries * PCAP :] = quarters[at + 1]


def pack(ours, theirs, quarters):
    entries, _, width = ours.shape
    entries //= SQUARE - 1
    shape = jax.ShapeDtypeStruct((entries * PCAP + quarters.shape[1], width), jnp.bfloat16)
    return pl.pallas_call(
        pack_kernel,
        in_specs=[VMEM] * 3,
        out_specs=[VMEM] * (SQUARE - 1),
        out_shape=[shape] * (SQUARE - 1),
        compiler_params=PARAMS,
        name="pack",
    )(ours, theirs, quarters)


def fold_kernel(ours, theirs, quarters, *refs):
    *gots, kept, message = refs
    entries = ours.shape[0]
    for entry in range(entries):
        rows = slice(entry * PCAP, (entry + 1) * PCAP)
        total = ours[entry] + theirs[entry].astype(jnp.float32)
        for got in gots:
            total = total + got[rows].astype(jnp.float32)
        kept[rows] = total
        away = entry ^ 1
        message[away * PCAP : (away + 1) * PCAP] = total.astype(message.dtype)
    table = quarters[0]
    for got in gots:
        table = table + got[entries * PCAP :]
    kept[entries * PCAP :] = table.astype(kept.dtype)
    message[entries * PCAP :] = table


def fold(ours, theirs, quarters, gots):
    shape = gots[0].shape
    return pl.pallas_call(
        fold_kernel,
        in_specs=[VMEM] * (3 + len(gots)),
        out_specs=[VMEM, VMEM],
        out_shape=[jax.ShapeDtypeStruct(shape, jnp.float32), jax.ShapeDtypeStruct(shape, jnp.bfloat16)],
        compiler_params=PARAMS,
        name="fold",
    )(ours, theirs, quarters, *gots)


def add_kernel(left, right, out):
    out[...] = (left[...] + right[...].astype(jnp.float32)).astype(out.dtype)


def add(left, right):
    return pl.pallas_call(
        add_kernel,
        in_specs=[VMEM, VMEM],
        out_specs=VMEM,
        out_shape=jax.ShapeDtypeStruct(left.shape, jnp.bfloat16),
        compiler_params=PARAMS,
        name="add",
    )(left, right)


def mask_kernel(counts, atom_of, after, out):
    del after
    core = place()[0]
    slot = lax.broadcasted_iota(jnp.int32, (1, PCAP), 1)
    limit = jnp.zeros((1, PCAP), jnp.int32)
    for channel in range(CHANNELS):
        limit = jnp.where(slot >= channel * CH_CAP, channel * CH_CAP + counts[core, channel], limit)
    atoms = jnp.where(core == 0, atom_of[0:1], atom_of[1:2])
    code = jnp.broadcast_to(jnp.where(slot < limit, atoms, -1), (PCAP, PCAP))
    out[...] = jnp.where((code == code.T) & (code >= 0), 1.0, 0.0).astype(out.dtype)


def mask(counts, atom_of, after):
    return pl.pallas_call(
        mask_kernel,
        in_specs=[SMEM, VMEM, ANY],
        out_specs=VMEM,
        out_shape=jax.ShapeDtypeStruct((PCAP, PCAP), jnp.bfloat16),
        compiler_params=PARAMS,
        name="mask",
    )(counts, atom_of, after)


def couple_kernel(allowed, *refs):
    *messages, out, coupling = refs
    width = out.shape[2]
    entries = out.shape[0] // SQUARE
    corner = place()[1] & 3
    for part, message in enumerate(messages):
        start = pl.multiple_of((corner ^ part) * QUARTER, QUARTER)
        for cut in range(PCAP // width):
            lanes = slice(cut * width, (cut + 1) * width)
            first = entries * PCAP + cut * QUARTER
            coupling[pl.ds(start, QUARTER), lanes] = (
                message[first : first + QUARTER] * allowed[pl.ds(start, QUARTER), lanes]
            )
    for part, message in enumerate(messages):
        wide = jnp.concatenate([message[e * PCAP : (e + 1) * PCAP] for e in range(entries)], axis=1)
        scaled = jnp.dot(coupling[...], wide, preferred_element_type=jnp.float32).astype(out.dtype)
        for entry in range(entries):
            out[part * entries + entry] = scaled[:, entry * width : (entry + 1) * width]


def couple(allowed, messages):
    rows, width = messages[0].shape
    entries = (rows - QUARTER * PCAP // width) // PCAP
    return pl.pallas_call(
        couple_kernel,
        in_specs=[VMEM] * (1 + SQUARE),
        out_specs=VMEM,
        out_shape=jax.ShapeDtypeStruct((SQUARE * entries, PCAP, width), jnp.bfloat16),
        scratch_shapes=[pltpu.VMEM((PCAP, PCAP), jnp.bfloat16)],
        compiler_params=PARAMS,
        name="couple",
    )(allowed, *messages)


def group_slots(group):
    return pl.ds(pl.multiple_of(group * PCAP, PCAP), PCAP)


def wide_pair(scaled, part):
    return jnp.concatenate([scaled[2 * part], scaled[2 * part + 1]], axis=1)


def begin_kernel(projectors, scaled, out):
    slots = group_slots(place()[0])
    for part in range(SQUARE):
        for block in range(projectors.shape[0] // ROW_BLOCK):
            rows = slice(block * ROW_BLOCK, (block + 1) * ROW_BLOCK)
            out[part, rows] = jnp.dot(
                projectors[rows, slots], wide_pair(scaled, part), preferred_element_type=jnp.float32
            )


def begin(projectors, scaled):
    depth, slots = projectors.shape
    return pl.pallas_call(
        begin_kernel,
        in_specs=[VMEM, VMEM],
        out_specs=VMEM,
        out_shape=jax.ShapeDtypeStruct((SQUARE, depth, 2 * LANES), jnp.float32),
        compiler_params=PARAMS,
        cost_estimate=pl.CostEstimate(
            flops=2 * depth * slots * LANES * SQUARE, bytes_accessed=2 * depth * slots, transcendentals=0
        ),
        name="begin",
    )(projectors, scaled)


def finish_kernel(projectors, begun, other, out, blocks, sems):
    core, chip = place()
    slots = group_slots(1 - core)
    copies = []
    first = 0
    for size in ROW_BLOCKS:
        rows = slice(first, first + size)
        first += size
        for part in range(SQUARE):
            sums = begun[part, rows] + jnp.dot(
                projectors[rows, slots], wide_pair(other, part), preferred_element_type=jnp.float32
            )
            for entry in range(2):
                start = pl.multiple_of(block_of(chip, part, entry) * LANES, LANES)
                lanes = slice(entry * LANES, (entry + 1) * LANES)
                blocks[rows, pl.ds(start, LANES)] = sums[:, lanes].astype(blocks.dtype)
        for start in range(rows.start, rows.stop, COPY_ROWS):
            written = slice(start, start + COPY_ROWS)
            copies.append(pltpu.make_async_copy(blocks.at[written], out.at[written], sems.at[len(copies)]))
            copies[-1].start()
    for copy in copies:
        copy.wait()


def finish(projectors, begun, other):
    depth, slots = projectors.shape
    bands = other.shape[0] * LANES
    return pl.pallas_call(
        finish_kernel,
        in_specs=[VMEM] * 3,
        out_specs=HBM,
        out_shape=jax.ShapeDtypeStruct((depth, bands), jnp.bfloat16),
        scratch_shapes=[
            pltpu.VMEM((depth, bands), jnp.bfloat16),
            pltpu.SemaphoreType.DMA((depth // COPY_ROWS,)),
        ],
        compiler_params=PARAMS,
        cost_estimate=pl.CostEstimate(
            flops=depth * slots * bands, bytes_accessed=2 * depth * (slots + bands), transcendentals=0
        ),
        name="finish",
    )(projectors, begun, other)


def apply_plain(projectors, mine, other):
    chips, _, width = mine.shape
    blocks = jnp.stack([block_of(place()[1], q, r) for q in range(SQUARE) for r in range(chips // SQUARE)])
    rows = []
    for group in range(2):
        part = jnp.where(place()[0] == group, mine, other)
        part = jnp.zeros_like(part).at[blocks].set(part)
        rows.append(part.transpose(1, 0, 2).reshape(PCAP, chips * width))
    return jnp.dot(projectors, jnp.concatenate(rows), preferred_element_type=jnp.float32).astype(jnp.bfloat16)


def local(band_coeffs, projectors, counts, atom_of, owners, couplings):
    chips = lax.axis_size("pw") // 2
    entries = chips // SQUARE
    width = band_coeffs.shape[1] // chips
    fast = width == LANES and entries == 2
    own_table = couplings[0]
    sibling_table = swap_cores(own_table)
    sent, kept = tuple(range(1, SQUARE)), (0,)
    if fast:
        theirs, ours, flipped, columns = project_sent(projectors, band_coeffs)
        low_theirs, low_ours = project_kept(flipped, columns)
    else:
        theirs, ours = project_plain(projectors, band_coeffs, sent)
        low_theirs, low_ours = project_plain(projectors, band_coeffs, kept)
    quarters = choose(owners, own_table, sibling_table, width, ours)
    theirs, low_ours = lax.optimization_barrier((swap_cores(theirs), low_ours))
    messages = pack(ours, theirs, quarters)
    low_theirs = swap_cores(low_theirs)
    gots = [swap_square(message, part) for message, part in zip(messages, sent)]
    allowed = mask(counts, atom_of, messages[0])

    total, message = fold(low_ours, low_theirs, quarters, gots)
    mine = add(total, swap_square(message, SQUARE))
    distance = 2 * SQUARE
    while distance < chips:
        body = mine[: entries * PCAP].reshape(entries, PCAP, width)
        order = [entry ^ (distance // SQUARE) for entry in range(entries)]
        message = jnp.concatenate([body[jnp.array(order)].reshape(-1, width), mine[entries * PCAP :]])
        mine = add(mine.astype(jnp.float32), swap_square(message, distance))
        distance *= 2

    gathered = [mine] + [swap_square(mine, part) for part in sent]
    scaled = couple(allowed, gathered)
    other = swap_cores(scaled)
    if not fast:
        return apply_plain(projectors, scaled, other)
    return finish(projectors, begin(projectors, scaled), other)


def solution(mesh):
    placed = (
        P("pw", "group"),
        P("pw", "group"),
        P("group", None),
        P("group", None),
        P("group"),
        P("pw", "group", None),
    )
    return jax.shard_map(
        local, mesh=mesh, in_specs=placed, out_specs=P("pw", "group"), check_vma=False
    )
```

```python
import jax
import jax.numpy as jnp
from jax import lax
from jax.experimental import pallas as pl
from jax.experimental.pallas import tpu as pltpu
from jax.sharding import PartitionSpec as P

CHANNELS = 4
CH_CAP = 64
PCAP = 256
LANES = 128
SQUARE = 4
QUARTER = PCAP // SQUARE
ROW_BLOCK = 512
ROW_BLOCKS = (512, 512, 512, 256, 256)
COPY_ROWS = 128
GATHERED = (0, 2, 3, 1)
PARAMS = pltpu.CompilerParams(vmem_limit_bytes=40 * 1024 * 1024)
VMEM = pl.BlockSpec(memory_space=pltpu.VMEM)
SMEM = pl.BlockSpec(memory_space=pltpu.SMEM)
HBM = pl.BlockSpec(memory_space=pltpu.HBM)
ANY = pl.BlockSpec(memory_space=pl.ANY)


def place():
    me = lax.axis_index("pw")
    return lax.rem(me, 2), lax.div(me, 2)


def block_of(chip, part, entry):
    return chip ^ (part + SQUARE * entry)


def swap(x, distance):
    count = lax.axis_size("pw")
    return lax.ppermute(x, "pw", [(i, i ^ distance) for i in range(count)])


def swap_cores(x):
    return swap(x, 1)


def swap_square(x, part):
    return swap(x, 2 * part)


def pair_at(columns, rows, part):
    chip = place()[1]
    starts = [pl.multiple_of(block_of(chip, part, entry) * LANES, LANES) for entry in range(2)]
    return jnp.concatenate([columns[rows, pl.ds(start, LANES)] for start in starts], axis=1)


def keep_sums(ours, theirs, at, sums):
    for entry in range(2):
        lanes = slice(entry * LANES, (entry + 1) * LANES)
        ours[2 * at + entry] = sums[:PCAP, lanes]
        theirs[2 * at + entry] = sums[PCAP:, lanes].astype(theirs.dtype)


def project_sent_kernel(projectors, bands, theirs, ours, flipped, columns, slots, totals, slot_sems, column_sems):
    core = place()[0]
    count = slot_sems.shape[0]
    depth = slots.shape[0] // count
    copies = []
    for at in range(count):
        rows = slice(at * depth, (at + 1) * depth)
        copies.append(
            (
                pltpu.make_async_copy(projectors.at[rows], slots.at[rows], slot_sems.at[at]),
                pltpu.make_async_copy(bands.at[rows], columns.at[rows], column_sems.at[at]),
            )
        )
    for pair in copies[:2]:
        for copy in pair:
            copy.start()
    for at in range(count):
        rows = slice(at * depth, (at + 1) * depth)
        copies[at][0].wait()
        if at + 2 < count:
            copies[at + 2][0].start()
        for side, group in enumerate((core, 1 - core)):
            start = pl.multiple_of(group * PCAP, PCAP)
            flipped[side * PCAP : (side + 1) * PCAP, rows] = slots[rows, pl.ds(start, PCAP)].T
        copies[at][1].wait()
        if at + 2 < count:
            copies[at + 2][1].start()
        for part in range(1, SQUARE):
            sums = jnp.dot(
                flipped[:, rows], pair_at(columns, rows, part), preferred_element_type=jnp.float32
            )
            if at:
                sums = totals[part - 1] + sums
            if at < count - 1:
                totals[part - 1] = sums
            else:
                keep_sums(ours, theirs, part - 1, sums)


def sums_shape(parts):
    shape = (2 * parts, PCAP, LANES)
    return [jax.ShapeDtypeStruct(shape, jnp.bfloat16), jax.ShapeDtypeStruct(shape, jnp.float32)]


def project_sent(projectors, band_coeffs):
    depth, slots = projectors.shape
    bands = band_coeffs.shape[1]
    blocks = 4
    return pl.pallas_call(
        project_sent_kernel,
        in_specs=[HBM, HBM],
        out_specs=[VMEM] * 4,
        out_shape=sums_shape(SQUARE - 1)
        + [
            jax.ShapeDtypeStruct((slots, depth), jnp.bfloat16),
            jax.ShapeDtypeStruct((depth, bands), jnp.bfloat16),
        ],
        scratch_shapes=[
            pltpu.VMEM((depth, slots), jnp.bfloat16),
            pltpu.VMEM((SQUARE - 1, slots, 2 * LANES), jnp.float32),
            pltpu.SemaphoreType.DMA((blocks,)),
            pltpu.SemaphoreType.DMA((blocks,)),
        ],
        compiler_params=PARAMS,
        cost_estimate=pl.CostEstimate(
            flops=2 * depth * slots * bands, bytes_accessed=2 * depth * (bands + slots), transcendentals=0
        ),
        name="project_sent",
    )(
        pltpu.with_memory_space_constraint(projectors, pltpu.HBM),
        pltpu.with_memory_space_constraint(band_coeffs, pltpu.HBM),
    )


def project_kept_kernel(flipped, columns, theirs, ours):
    rows = slice(0, columns.shape[0])
    sums = jnp.dot(flipped[...], pair_at(columns, rows, 0), preferred_element_type=jnp.float32)
    keep_sums(ours, theirs, 0, sums)


def project_kept(flipped, columns):
    slots, depth = flipped.shape
    return pl.pallas_call(
        project_kept_kernel,
        in_specs=[VMEM, VMEM],
        out_specs=[VMEM, VMEM],
        out_shape=sums_shape(1),
        compiler_params=PARAMS,
        cost_estimate=pl.CostEstimate(
            flops=4 * depth * slots * LANES, bytes_accessed=2 * depth * slots, transcendentals=0
        ),
        name="project_kept",
    )(flipped, columns)


def project_plain(projectors, band_coeffs, parts):
    depth, bands = band_coeffs.shape
    chips = lax.axis_size("pw") // 2
    blocks = jnp.stack([block_of(place()[1], q, r) for q in parts for r in range(chips // SQUARE)])
    columns = jnp.take(band_coeffs.reshape(depth, chips, bands // chips), blocks, axis=1)
    outs = []
    core = place()[0]
    for group, dtype in ((1 - core, jnp.bfloat16), (core, jnp.float32)):
        slots = lax.dynamic_slice_in_dim(projectors, group * PCAP, PCAP, 1)
        sums = jnp.einsum("ds,dhw->hsw", slots, columns, preferred_element_type=jnp.float32)
        outs.append(sums.astype(dtype))
    return outs


def choose_kernel(owners, own, sibling, after, out):
    del after
    core, chip = place()
    me = 2 * chip + core
    owner = jnp.where(core == 0, owners[0:1, :], owners[1:2, :])
    width = out.shape[2]
    for part in range(SQUARE):
        rows = pl.ds(pl.multiple_of(((chip & 3) ^ part) * QUARTER, QUARTER), QUARTER)
        piece = jnp.where(owner == me, own[rows], jnp.where(owner == (me ^ 1), sibling[rows], 0.0))
        for cut in range(PCAP // width):
            out[part, cut * QUARTER : (cut + 1) * QUARTER] = piece[:, cut * width : (cut + 1) * width].astype(
                out.dtype
            )


def choose(owners, own, sibling, width, after):
    return pl.pallas_call(
        choose_kernel,
        in_specs=[VMEM, VMEM, VMEM, ANY],
        out_specs=VMEM,
        out_shape=jax.ShapeDtypeStruct((SQUARE, QUARTER * PCAP // width, width), jnp.bfloat16),
        compiler_params=PARAMS,
        name="choose",
    )(jnp.broadcast_to(owners[:, None], (owners.shape[0], PCAP)), own, sibling, after)


def pack_kernel(ours, theirs, quarters, *messages):
    entries = ours.shape[0] // len(messages)
    for at, message in enumerate(messages):
        for entry in range(entries):
            place = at * entries + entry
            total = ours[place] + theirs[place].astype(jnp.float32)
            message[entry * PCAP : (entry + 1) * PCAP] = total.astype(message.dtype)
        message[entries * PCAP :] = quarters[at + 1]


def pack(ours, theirs, quarters):
    entries, _, width = ours.shape
    entries //= SQUARE - 1
    shape = jax.ShapeDtypeStruct((entries * PCAP + quarters.shape[1], width), jnp.bfloat16)
    return pl.pallas_call(
        pack_kernel,
        in_specs=[VMEM] * 3,
        out_specs=[VMEM] * (SQUARE - 1),
        out_shape=[shape] * (SQUARE - 1),
        compiler_params=PARAMS,
        name="pack",
    )(ours, theirs, quarters)


def fold_kernel(ours, theirs, quarters, *refs):
    *gots, kept, message = refs
    entries = ours.shape[0]
    for entry in range(entries):
        rows = slice(entry * PCAP, (entry + 1) * PCAP)
        total = ours[entry] + theirs[entry].astype(jnp.float32)
        for got in gots:
            total = total + got[rows].astype(jnp.float32)
        kept[rows] = total
        away = entry ^ 1
        message[away * PCAP : (away + 1) * PCAP] = total.astype(message.dtype)
    table = quarters[0]
    for got in gots:
        table = table + got[entries * PCAP :]
    kept[entries * PCAP :] = table.astype(kept.dtype)
    message[entries * PCAP :] = table


def fold(ours, theirs, quarters, gots):
    shape = gots[0].shape
    return pl.pallas_call(
        fold_kernel,
        in_specs=[VMEM] * (3 + len(gots)),
        out_specs=[VMEM, VMEM],
        out_shape=[jax.ShapeDtypeStruct(shape, jnp.float32), jax.ShapeDtypeStruct(shape, jnp.bfloat16)],
        compiler_params=PARAMS,
        name="fold",
    )(ours, theirs, quarters, *gots)


def add_kernel(left, right, out):
    out[...] = (left[...] + right[...].astype(jnp.float32)).astype(out.dtype)


def add(left, right):
    return pl.pallas_call(
        add_kernel,
        in_specs=[VMEM, VMEM],
        out_specs=VMEM,
        out_shape=jax.ShapeDtypeStruct(left.shape, jnp.bfloat16),
        compiler_params=PARAMS,
        name="add",
    )(left, right)


def mask_kernel(counts, atom_of, after, out):
    del after
    core = place()[0]
    slot = lax.broadcasted_iota(jnp.int32, (1, PCAP), 1)
    limit = jnp.zeros((1, PCAP), jnp.int32)
    for channel in range(CHANNELS):
        limit = jnp.where(slot >= channel * CH_CAP, channel * CH_CAP + counts[core, channel], limit)
    atoms = jnp.where(core == 0, atom_of[0:1], atom_of[1:2])
    code = jnp.broadcast_to(jnp.where(slot < limit, atoms, -1), (PCAP, PCAP))
    out[...] = jnp.where((code == code.T) & (code >= 0), 1.0, 0.0).astype(out.dtype)


def mask(counts, atom_of, after):
    return pl.pallas_call(
        mask_kernel,
        in_specs=[SMEM, VMEM, ANY],
        out_specs=VMEM,
        out_shape=jax.ShapeDtypeStruct((PCAP, PCAP), jnp.bfloat16),
        compiler_params=PARAMS,
        name="mask",
    )(counts, atom_of, after)


def couple_kernel(allowed, *refs):
    *messages, out, coupling = refs
    width = out.shape[2]
    entries = out.shape[0] // SQUARE
    corner = place()[1] & 3
    for part, message in zip(GATHERED, messages):
        start = pl.multiple_of((corner ^ part) * QUARTER, QUARTER)
        for cut in range(PCAP // width):
            lanes = slice(cut * width, (cut + 1) * width)
            first = entries * PCAP + cut * QUARTER
            coupling[pl.ds(start, QUARTER), lanes] = (
                message[first : first + QUARTER] * allowed[pl.ds(start, QUARTER), lanes]
            )
    for part, message in zip(GATHERED, messages):
        wide = jnp.concatenate([message[e * PCAP : (e + 1) * PCAP] for e in range(entries)], axis=1)
        scaled = jnp.dot(coupling[...], wide, preferred_element_type=jnp.float32).astype(out.dtype)
        for entry in range(entries):
            out[part * entries + entry] = scaled[:, entry * width : (entry + 1) * width]


def couple(allowed, messages):
    rows, width = messages[0].shape
    entries = (rows - QUARTER * PCAP // width) // PCAP
    return pl.pallas_call(
        couple_kernel,
        in_specs=[VMEM] * (1 + SQUARE),
        out_specs=VMEM,
        out_shape=jax.ShapeDtypeStruct((SQUARE * entries, PCAP, width), jnp.bfloat16),
        scratch_shapes=[pltpu.VMEM((PCAP, PCAP), jnp.bfloat16)],
        compiler_params=PARAMS,
        name="couple",
    )(allowed, *messages)


def group_slots(group):
    return pl.ds(pl.multiple_of(group * PCAP, PCAP), PCAP)


def wide_pair(scaled, part):
    return jnp.concatenate([scaled[2 * part], scaled[2 * part + 1]], axis=1)


def begin_kernel(projectors, scaled, out):
    slots = group_slots(place()[0])
    for part in range(SQUARE):
        for block in range(projectors.shape[0] // ROW_BLOCK):
            rows = slice(block * ROW_BLOCK, (block + 1) * ROW_BLOCK)
            out[part, rows] = jnp.dot(
                projectors[rows, slots], wide_pair(scaled, part), preferred_element_type=jnp.float32
            )


def begin(projectors, scaled):
    depth, slots = projectors.shape
    return pl.pallas_call(
        begin_kernel,
        in_specs=[VMEM, VMEM],
        out_specs=VMEM,
        out_shape=jax.ShapeDtypeStruct((SQUARE, depth, 2 * LANES), jnp.float32),
        compiler_params=PARAMS,
        cost_estimate=pl.CostEstimate(
            flops=2 * depth * slots * LANES * SQUARE, bytes_accessed=2 * depth * slots, transcendentals=0
        ),
        name="begin",
    )(projectors, scaled)


def finish_kernel(projectors, begun, other, out, blocks, sems):
    core, chip = place()
    slots = group_slots(1 - core)
    copies = []
    first = 0
    for size in ROW_BLOCKS:
        rows = slice(first, first + size)
        first += size
        for part in range(SQUARE):
            sums = begun[part, rows] + jnp.dot(
                projectors[rows, slots], wide_pair(other, part), preferred_element_type=jnp.float32
            )
            for entry in range(2):
                start = pl.multiple_of(block_of(chip, part, entry) * LANES, LANES)
                lanes = slice(entry * LANES, (entry + 1) * LANES)
                blocks[rows, pl.ds(start, LANES)] = sums[:, lanes].astype(blocks.dtype)
        for start in range(rows.start, rows.stop, COPY_ROWS):
            written = slice(start, start + COPY_ROWS)
            copies.append(pltpu.make_async_copy(blocks.at[written], out.at[written], sems.at[len(copies)]))
            copies[-1].start()
    for copy in copies:
        copy.wait()


def finish(projectors, begun, other):
    depth, slots = projectors.shape
    bands = other.shape[0] * LANES
    return pl.pallas_call(
        finish_kernel,
        in_specs=[VMEM] * 3,
        out_specs=HBM,
        out_shape=jax.ShapeDtypeStruct((depth, bands), jnp.bfloat16),
        scratch_shapes=[
            pltpu.VMEM((depth, bands), jnp.bfloat16),
            pltpu.SemaphoreType.DMA((depth // COPY_ROWS,)),
        ],
        compiler_params=PARAMS,
        cost_estimate=pl.CostEstimate(
            flops=depth * slots * bands, bytes_accessed=2 * depth * (slots + bands), transcendentals=0
        ),
        name="finish",
    )(projectors, begun, other)


def apply_plain(projectors, mine, other):
    chips, _, width = mine.shape
    blocks = jnp.stack([block_of(place()[1], q, r) for q in range(SQUARE) for r in range(chips // SQUARE)])
    rows = []
    for group in range(2):
        part = jnp.where(place()[0] == group, mine, other)
        part = jnp.zeros_like(part).at[blocks].set(part)
        rows.append(part.transpose(1, 0, 2).reshape(PCAP, chips * width))
    return jnp.dot(projectors, jnp.concatenate(rows), preferred_element_type=jnp.float32).astype(jnp.bfloat16)


def local(band_coeffs, projectors, counts, atom_of, owners, couplings):
    chips = lax.axis_size("pw") // 2
    entries = chips // SQUARE
    width = band_coeffs.shape[1] // chips
    fast = width == LANES and entries == 2
    own_table = couplings[0]
    sibling_table = swap_cores(own_table)
    sent, kept = tuple(range(1, SQUARE)), (0,)
    if fast:
        theirs, ours, flipped, columns = project_sent(projectors, band_coeffs)
        theirs, sibling_table = lax.optimization_barrier((theirs, sibling_table))
        low_theirs, low_ours = project_kept(flipped, columns)
    else:
        theirs, ours = project_plain(projectors, band_coeffs, sent)
        low_theirs, low_ours = project_plain(projectors, band_coeffs, kept)
    quarters = choose(owners, own_table, sibling_table, width, ours)
    theirs, low_ours = lax.optimization_barrier((swap_cores(theirs), low_ours))
    messages = pack(ours, theirs, quarters)
    low_theirs = swap_cores(low_theirs)
    gots = [swap_square(messages[part - 1], part) for part in (2, 1, 3)]
    allowed = mask(counts, atom_of, messages[0])

    total, message = fold(low_ours, low_theirs, quarters, gots)
    mine = add(total, swap_square(message, SQUARE))
    distance = 2 * SQUARE
    while distance < chips:
        body = mine[: entries * PCAP].reshape(entries, PCAP, width)
        order = [entry ^ (distance // SQUARE) for entry in range(entries)]
        message = jnp.concatenate([body[jnp.array(order)].reshape(-1, width), mine[entries * PCAP :]])
        mine = add(mine.astype(jnp.float32), swap_square(message, distance))
        distance *= 2

    scaled = couple(allowed, [swap_square(mine, part) if part else mine for part in GATHERED])
    other = swap_cores(scaled)
    if not fast:
        return apply_plain(projectors, scaled, other)
    return finish(projectors, begin(projectors, scaled), other)


def solution(mesh):
    placed = (
        P("pw", "group"),
        P("pw", "group"),
        P("group", None),
        P("group", None),
        P("group"),
        P("pw", "group", None),
    )
    return jax.shard_map(
        local, mesh=mesh, in_specs=placed, out_specs=P("pw", "group"), check_vma=False
    )
```

```python
import jax
import jax.numpy as jnp
from jax import lax
from jax.experimental import pallas as pl
from jax.experimental.pallas import tpu as pltpu
from jax.sharding import PartitionSpec as P

CHANNELS = 4
CH_CAP = 64
PCAP = 256
LANES = 128
SQUARE = 4
QUARTER = PCAP // SQUARE
ROW_BLOCK = 512
ROW_BLOCKS = (512, 512, 512, 256, 256)
COPY_ROWS = 128
GATHERED = (0, 1, 2, 3)
PARAMS = pltpu.CompilerParams(vmem_limit_bytes=40 * 1024 * 1024)
VMEM = pl.BlockSpec(memory_space=pltpu.VMEM)
SMEM = pl.BlockSpec(memory_space=pltpu.SMEM)
HBM = pl.BlockSpec(memory_space=pltpu.HBM)
ANY = pl.BlockSpec(memory_space=pl.ANY)


def place():
    me = lax.axis_index("pw")
    return lax.rem(me, 2), lax.div(me, 2)


def block_of(chip, part, entry):
    return chip ^ (part + SQUARE * entry)


def swap(x, distance):
    count = lax.axis_size("pw")
    return lax.ppermute(x, "pw", [(i, i ^ distance) for i in range(count)])


def swap_cores(x):
    return swap(x, 1)


def swap_chips(x, distance):
    return swap(x, 2 * distance)


def swap_first(x):
    count = lax.axis_size("pw")
    return lax.ppermute(x, "pw", [(i, i ^ (2, 4)[i % 2]) for i in range(count)])


def swap_second(x):
    count = lax.axis_size("pw")
    return lax.ppermute(x, "pw", [(i, i ^ (4, 2)[i % 2]) for i in range(count)])


def pair_at(columns, rows, part):
    chip = place()[1]
    starts = [pl.multiple_of(block_of(chip, part, entry) * LANES, LANES) for entry in range(2)]
    return jnp.concatenate([columns[rows, pl.ds(start, LANES)] for start in starts], axis=1)


def keep_sums(ours, theirs, at, sums):
    for entry in range(2):
        lanes = slice(entry * LANES, (entry + 1) * LANES)
        ours[2 * at + entry] = sums[:PCAP, lanes]
        theirs[2 * at + entry] = sums[PCAP:, lanes].astype(theirs.dtype)


def load_kernel(projectors, flipped, slots, sems):
    core = place()[0]
    count = sems.shape[0]
    block = slots.shape[0] // count
    copies = []
    for at in range(count):
        rows = slice(at * block, (at + 1) * block)
        copies.append(pltpu.make_async_copy(projectors.at[rows], slots.at[rows], sems.at[at]))
        copies[-1].start()
    for at, copy in enumerate(copies):
        copy.wait()
        rows = slice(at * block, (at + 1) * block)
        for side, group in enumerate((core, 1 - core)):
            start = pl.multiple_of(group * PCAP, PCAP)
            flipped[side * PCAP : (side + 1) * PCAP, rows] = slots[rows, pl.ds(start, PCAP)].T


def load(projectors):
    depth, slots = projectors.shape
    return pl.pallas_call(
        load_kernel,
        in_specs=[HBM],
        out_specs=VMEM,
        out_shape=jax.ShapeDtypeStruct((slots, depth), jnp.bfloat16),
        scratch_shapes=[pltpu.VMEM((depth, slots), jnp.bfloat16), pltpu.SemaphoreType.DMA((4,))],
        compiler_params=PARAMS,
        name="load",
    )(pltpu.with_memory_space_constraint(projectors, pltpu.HBM))


def project_kernel(parts, flipped, columns, theirs, ours):
    rows = slice(0, columns.shape[0])
    for at, part in enumerate(parts):
        sums = jnp.dot(flipped[...], pair_at(columns, rows, part), preferred_element_type=jnp.float32)
        keep_sums(ours, theirs, at, sums)


def project(flipped, band_coeffs, parts):
    slots, depth = flipped.shape
    shape = (2 * len(parts), PCAP, LANES)

    def kernel(*refs):
        project_kernel(parts, *refs)

    return pl.pallas_call(
        kernel,
        in_specs=[VMEM, VMEM],
        out_specs=[VMEM, VMEM],
        out_shape=[jax.ShapeDtypeStruct(shape, jnp.bfloat16), jax.ShapeDtypeStruct(shape, jnp.float32)],
        compiler_params=PARAMS,
        cost_estimate=pl.CostEstimate(
            flops=4 * depth * slots * len(parts) * LANES, bytes_accessed=2 * depth * slots, transcendentals=0
        ),
        name="project",
    )(flipped, pltpu.with_memory_space_constraint(band_coeffs, pltpu.VMEM))


def project_plain(projectors, band_coeffs, parts):
    depth, bands = band_coeffs.shape
    chips = lax.axis_size("pw") // 2
    blocks = jnp.stack([block_of(place()[1], q, r) for q in parts for r in range(chips // SQUARE)])
    columns = jnp.take(band_coeffs.reshape(depth, chips, bands // chips), blocks, axis=1)
    outs = []
    core = place()[0]
    for group, dtype in ((1 - core, jnp.bfloat16), (core, jnp.float32)):
        slots = lax.dynamic_slice_in_dim(projectors, group * PCAP, PCAP, 1)
        sums = jnp.einsum("ds,dhw->hsw", slots, columns, preferred_element_type=jnp.float32)
        outs.append(sums.astype(dtype))
    return outs


def choose_kernel(owners, own, sibling, after, out):
    del after
    core, chip = place()
    me = 2 * chip + core
    owner = jnp.where(core == 0, owners[0:1, :], owners[1:2, :])
    width = out.shape[2]
    for part in range(SQUARE):
        rows = pl.ds(pl.multiple_of(((chip & 3) ^ part) * QUARTER, QUARTER), QUARTER)
        piece = jnp.where(owner == me, own[rows], jnp.where(owner == (me ^ 1), sibling[rows], 0.0))
        for cut in range(PCAP // width):
            out[part, cut * QUARTER : (cut + 1) * QUARTER] = piece[:, cut * width : (cut + 1) * width].astype(
                out.dtype
            )


def choose(owners, own, sibling, width, after):
    return pl.pallas_call(
        choose_kernel,
        in_specs=[VMEM, VMEM, VMEM, ANY],
        out_specs=VMEM,
        out_shape=jax.ShapeDtypeStruct((SQUARE, QUARTER * PCAP // width, width), jnp.bfloat16),
        compiler_params=PARAMS,
        name="choose",
    )(jnp.broadcast_to(owners[:, None], (owners.shape[0], PCAP)), own, sibling, after)


def send_kernel(first, second, ours, theirs, quarters, message):
    entries = ours.shape[0] // (1 if first == second else 2)
    core = place()[0]
    start, part = (0, first) if first == second else (core * entries, 1 + core)
    for entry in range(entries):
        total = ours[start + entry] + theirs[start + entry].astype(jnp.float32)
        message[entry * PCAP : (entry + 1) * PCAP] = total.astype(message.dtype)
    message[entries * PCAP :] = quarters[part]


def send(ours, theirs, quarters, parts):
    count, _, width = ours.shape
    rows = count // len(parts) * PCAP + quarters.shape[1]

    def kernel(*refs):
        send_kernel(parts[0], parts[-1], *refs)

    return pl.pallas_call(
        kernel,
        in_specs=[VMEM] * 3,
        out_specs=VMEM,
        out_shape=jax.ShapeDtypeStruct((rows, width), jnp.bfloat16),
        compiler_params=PARAMS,
        name="send",
    )(ours, theirs, quarters)


def forward_kernel(ours, theirs, quarters, got, message):
    core = place()[0]
    entries = ours.shape[0] // 2
    start = (1 - core) * entries
    for entry in range(entries):
        rows = slice(entry * PCAP, (entry + 1) * PCAP)
        total = ours[start + entry] + theirs[start + entry].astype(jnp.float32)
        message[rows] = (total + got[rows].astype(jnp.float32)).astype(message.dtype)
    message[entries * PCAP :] = quarters[2 - core] + got[entries * PCAP :]


def forward(ours, theirs, quarters, got):
    return pl.pallas_call(
        forward_kernel,
        in_specs=[VMEM] * 4,
        out_specs=VMEM,
        out_shape=jax.ShapeDtypeStruct(got.shape, got.dtype),
        compiler_params=PARAMS,
        name="forward",
    )(ours, theirs, quarters, got)


def fold_kernel(ours, theirs, quarters, *refs):
    *gots, kept, message = refs
    entries = ours.shape[0]
    for entry in range(entries):
        rows = slice(entry * PCAP, (entry + 1) * PCAP)
        total = ours[entry] + theirs[entry].astype(jnp.float32)
        for got in gots:
            total = total + got[rows].astype(jnp.float32)
        kept[rows] = total
        away = entry ^ 1
        message[away * PCAP : (away + 1) * PCAP] = total.astype(message.dtype)
    table = quarters[0]
    for got in gots:
        table = table + got[entries * PCAP :]
    kept[entries * PCAP :] = table.astype(kept.dtype)
    message[entries * PCAP :] = table


def fold(ours, theirs, quarters, gots):
    shape = gots[0].shape
    return pl.pallas_call(
        fold_kernel,
        in_specs=[VMEM] * (3 + len(gots)),
        out_specs=[VMEM, VMEM],
        out_shape=[jax.ShapeDtypeStruct(shape, jnp.float32), jax.ShapeDtypeStruct(shape, jnp.bfloat16)],
        compiler_params=PARAMS,
        name="fold",
    )(ours, theirs, quarters, *gots)


def add_kernel(left, right, out):
    out[...] = (left[...] + right[...].astype(jnp.float32)).astype(out.dtype)


def add(left, right):
    return pl.pallas_call(
        add_kernel,
        in_specs=[VMEM, VMEM],
        out_specs=VMEM,
        out_shape=jax.ShapeDtypeStruct(left.shape, jnp.bfloat16),
        compiler_params=PARAMS,
        name="add",
    )(left, right)


def mask_kernel(counts, atom_of, after, out):
    del after
    core = place()[0]
    slot = lax.broadcasted_iota(jnp.int32, (1, PCAP), 1)
    limit = jnp.zeros((1, PCAP), jnp.int32)
    for channel in range(CHANNELS):
        limit = jnp.where(slot >= channel * CH_CAP, channel * CH_CAP + counts[core, channel], limit)
    atoms = jnp.where(core == 0, atom_of[0:1], atom_of[1:2])
    code = jnp.broadcast_to(jnp.where(slot < limit, atoms, -1), (PCAP, PCAP))
    out[...] = jnp.where((code == code.T) & (code >= 0), 1.0, 0.0).astype(out.dtype)


def mask(counts, atom_of, after):
    return pl.pallas_call(
        mask_kernel,
        in_specs=[SMEM, VMEM, ANY],
        out_specs=VMEM,
        out_shape=jax.ShapeDtypeStruct((PCAP, PCAP), jnp.bfloat16),
        compiler_params=PARAMS,
        name="mask",
    )(counts, atom_of, after)


def couple_kernel(allowed, *refs):
    *messages, out, coupling = refs
    width = out.shape[2]
    entries = out.shape[0] // SQUARE
    corner = place()[1] & 3
    for part, message in zip(GATHERED, messages):
        start = pl.multiple_of((corner ^ part) * QUARTER, QUARTER)
        for cut in range(PCAP // width):
            lanes = slice(cut * width, (cut + 1) * width)
            first = entries * PCAP + cut * QUARTER
            coupling[pl.ds(start, QUARTER), lanes] = (
                message[first : first + QUARTER] * allowed[pl.ds(start, QUARTER), lanes]
            )
    for part, message in zip(GATHERED, messages):
        wide = jnp.concatenate([message[e * PCAP : (e + 1) * PCAP] for e in range(entries)], axis=1)
        scaled = jnp.dot(coupling[...], wide, preferred_element_type=jnp.float32).astype(out.dtype)
        for entry in range(entries):
            out[part * entries + entry] = scaled[:, entry * width : (entry + 1) * width]


def couple(allowed, messages):
    rows, width = messages[0].shape
    entries = (rows - QUARTER * PCAP // width) // PCAP
    return pl.pallas_call(
        couple_kernel,
        in_specs=[VMEM] * (1 + SQUARE),
        out_specs=VMEM,
        out_shape=jax.ShapeDtypeStruct((SQUARE * entries, PCAP, width), jnp.bfloat16),
        scratch_shapes=[pltpu.VMEM((PCAP, PCAP), jnp.bfloat16)],
        compiler_params=PARAMS,
        name="couple",
    )(allowed, *messages)


def group_slots(group):
    return pl.ds(pl.multiple_of(group * PCAP, PCAP), PCAP)


def wide_pair(scaled, part):
    return jnp.concatenate([scaled[2 * part], scaled[2 * part + 1]], axis=1)


def begin_kernel(projectors, scaled, out):
    slots = group_slots(place()[0])
    for part in range(SQUARE):
        for block in range(projectors.shape[0] // ROW_BLOCK):
            rows = slice(block * ROW_BLOCK, (block + 1) * ROW_BLOCK)
            out[part, rows] = jnp.dot(
                projectors[rows, slots], wide_pair(scaled, part), preferred_element_type=jnp.float32
            )


def begin(projectors, scaled):
    depth, slots = projectors.shape
    return pl.pallas_call(
        begin_kernel,
        in_specs=[VMEM, VMEM],
        out_specs=VMEM,
        out_shape=jax.ShapeDtypeStruct((SQUARE, depth, 2 * LANES), jnp.float32),
        compiler_params=PARAMS,
        cost_estimate=pl.CostEstimate(
            flops=2 * depth * slots * LANES * SQUARE, bytes_accessed=2 * depth * slots, transcendentals=0
        ),
        name="begin",
    )(projectors, scaled)


def finish_kernel(projectors, begun, other, out, blocks, sems):
    core, chip = place()
    slots = group_slots(1 - core)
    copies = []
    first = 0
    for size in ROW_BLOCKS:
        rows = slice(first, first + size)
        first += size
        for part in range(SQUARE):
            sums = begun[part, rows] + jnp.dot(
                projectors[rows, slots], wide_pair(other, part), preferred_element_type=jnp.float32
            )
            for entry in range(2):
                start = pl.multiple_of(block_of(chip, part, entry) * LANES, LANES)
                lanes = slice(entry * LANES, (entry + 1) * LANES)
                blocks[rows, pl.ds(start, LANES)] = sums[:, lanes].astype(blocks.dtype)
        for start in range(rows.start, rows.stop, COPY_ROWS):
            written = slice(start, start + COPY_ROWS)
            copies.append(pltpu.make_async_copy(blocks.at[written], out.at[written], sems.at[len(copies)]))
            copies[-1].start()
    for copy in copies:
        copy.wait()


def finish(projectors, begun, other):
    depth, slots = projectors.shape
    bands = other.shape[0] * LANES
    return pl.pallas_call(
        finish_kernel,
        in_specs=[VMEM] * 3,
        out_specs=HBM,
        out_shape=jax.ShapeDtypeStruct((depth, bands), jnp.bfloat16),
        scratch_shapes=[
            pltpu.VMEM((depth, bands), jnp.bfloat16),
            pltpu.SemaphoreType.DMA((depth // COPY_ROWS,)),
        ],
        compiler_params=PARAMS,
        cost_estimate=pl.CostEstimate(
            flops=depth * slots * bands, bytes_accessed=2 * depth * (slots + bands), transcendentals=0
        ),
        name="finish",
    )(projectors, begun, other)


def apply_plain(projectors, mine, other):
    chips, _, width = mine.shape
    blocks = jnp.stack([block_of(place()[1], q, r) for q in range(SQUARE) for r in range(chips // SQUARE)])
    rows = []
    for group in range(2):
        part = jnp.where(place()[0] == group, mine, other)
        part = jnp.zeros_like(part).at[blocks].set(part)
        rows.append(part.transpose(1, 0, 2).reshape(PCAP, chips * width))
    return jnp.dot(projectors, jnp.concatenate(rows), preferred_element_type=jnp.float32).astype(jnp.bfloat16)


def local(band_coeffs, projectors, counts, atom_of, owners, couplings):
    chips = lax.axis_size("pw") // 2
    entries = chips // SQUARE
    width = band_coeffs.shape[1] // chips
    fast = width == LANES and entries == 2
    own_table = couplings[0]
    sibling_table = swap_cores(own_table)
    if fast:
        flipped = load(projectors)

        def partial(parts):
            return project(flipped, band_coeffs, parts)
    else:

        def partial(parts):
            return project_plain(projectors, band_coeffs, parts)

    theirs, ours = partial((3,))
    theirs, sibling_table = lax.optimization_barrier((theirs, sibling_table))
    theirs = swap_cores(theirs)
    pair_theirs, pair_ours = partial((1, 2))
    quarters = choose(owners, own_table, sibling_table, width, ours)
    got = swap_first(send(ours, theirs, quarters, (3,)))
    pair_theirs = swap_cores(pair_theirs)
    low_theirs, low_ours = partial((0,))
    low_theirs = swap_cores(low_theirs)
    got_first = swap_first(send(pair_ours, pair_theirs, quarters, (1, 2)))
    message = forward(pair_ours, pair_theirs, quarters, got)
    got_second = swap_second(message)
    allowed = mask(counts, atom_of, message)

    total, message = fold(low_ours, low_theirs, quarters, [got_first, got_second])
    mine = add(total, swap_chips(message, SQUARE))
    distance = 2 * SQUARE
    while distance < chips:
        body = mine[: entries * PCAP].reshape(entries, PCAP, width)
        order = [entry ^ (distance // SQUARE) for entry in range(entries)]
        message = jnp.concatenate([body[jnp.array(order)].reshape(-1, width), mine[entries * PCAP :]])
        mine = add(mine.astype(jnp.float32), swap_chips(message, distance))
        distance *= 2

    scaled = couple(allowed, [swap_chips(mine, part) if part else mine for part in GATHERED])
    other = swap_cores(scaled)
    if not fast:
        return apply_plain(projectors, scaled, other)
    return finish(projectors, begin(projectors, scaled), other)


def solution(mesh):
    placed = (
        P("pw", "group"),
        P("pw", "group"),
        P("group", None),
        P("group", None),
        P("group"),
        P("pw", "group", None),
    )
    return jax.shard_map(
        local, mesh=mesh, in_specs=placed, out_specs=P("pw", "group"), check_vma=False
    )
```

```python
import jax
import jax.numpy as jnp
from jax import lax
from jax.experimental import pallas as pl
from jax.experimental.pallas import tpu as pltpu
from jax.sharding import PartitionSpec as P

CHANNELS = 4
CH_CAP = 64
PCAP = 256
LANES = 128
SQUARE = 4
QUARTER = PCAP // SQUARE
ROW_BLOCK = 512
ROW_BLOCKS = (256, 512, 512, 512, 256)
COPY_ROWS = 128
GATHERED = (0, 1, 2, 3)
PARAMS = pltpu.CompilerParams(vmem_limit_bytes=40 * 1024 * 1024)
VMEM = pl.BlockSpec(memory_space=pltpu.VMEM)
SMEM = pl.BlockSpec(memory_space=pltpu.SMEM)
HBM = pl.BlockSpec(memory_space=pltpu.HBM)
ANY = pl.BlockSpec(memory_space=pl.ANY)


def place():
    me = lax.axis_index("pw")
    return lax.rem(me, 2), lax.div(me, 2)


def block_of(chip, part, entry):
    return chip ^ (part + SQUARE * entry)


def swap(x, distance):
    count = lax.axis_size("pw")
    return lax.ppermute(x, "pw", [(i, i ^ distance) for i in range(count)])


def swap_cores(x):
    return swap(x, 1)


def swap_chips(x, distance):
    return swap(x, 2 * distance)


def swap_first(x):
    count = lax.axis_size("pw")
    return lax.ppermute(x, "pw", [(i, i ^ (2, 4)[i % 2]) for i in range(count)])


def swap_second(x):
    count = lax.axis_size("pw")
    return lax.ppermute(x, "pw", [(i, i ^ (4, 2)[i % 2]) for i in range(count)])


def pair_at(columns, rows, part):
    chip = place()[1]
    starts = [pl.multiple_of(block_of(chip, part, entry) * LANES, LANES) for entry in range(2)]
    return jnp.concatenate([columns[rows, pl.ds(start, LANES)] for start in starts], axis=1)


def load_kernel(projectors, flipped, slots, sems):
    core = place()[0]
    count = sems.shape[0]
    block = slots.shape[0] // count
    copies = []
    for at in range(count):
        rows = slice(at * block, (at + 1) * block)
        copies.append(pltpu.make_async_copy(projectors.at[rows], slots.at[rows], sems.at[at]))
        copies[-1].start()
    for at, copy in enumerate(copies):
        copy.wait()
        rows = slice(at * block, (at + 1) * block)
        for side, group in enumerate((core, 1 - core)):
            start = pl.multiple_of(group * PCAP, PCAP)
            flipped[side * PCAP : (side + 1) * PCAP, rows] = slots[rows, pl.ds(start, PCAP)].T


def load(projectors):
    depth, slots = projectors.shape
    return pl.pallas_call(
        load_kernel,
        in_specs=[HBM],
        out_specs=VMEM,
        out_shape=jax.ShapeDtypeStruct((slots, depth), jnp.bfloat16),
        scratch_shapes=[pltpu.VMEM((depth, slots), jnp.bfloat16), pltpu.SemaphoreType.DMA((4,))],
        compiler_params=PARAMS,
        name="load",
    )(pltpu.with_memory_space_constraint(projectors, pltpu.HBM))


def project_kernel(part, flipped, columns, theirs, ours):
    rows = slice(0, columns.shape[0])
    sums = jnp.dot(flipped[...], pair_at(columns, rows, part), preferred_element_type=jnp.float32)
    for entry in range(2):
        lanes = slice(entry * LANES, (entry + 1) * LANES)
        ours[entry] = sums[:PCAP, lanes]
        theirs[entry] = sums[PCAP:, lanes].astype(theirs.dtype)


def project(flipped, band_coeffs, part):
    slots, depth = flipped.shape

    def kernel(*refs):
        project_kernel(part, *refs)

    return pl.pallas_call(
        kernel,
        in_specs=[VMEM, VMEM],
        out_specs=[VMEM, VMEM],
        out_shape=[
            jax.ShapeDtypeStruct((2, PCAP, LANES), jnp.bfloat16),
            jax.ShapeDtypeStruct((2, PCAP, LANES), jnp.float32),
        ],
        compiler_params=PARAMS,
        cost_estimate=pl.CostEstimate(
            flops=4 * depth * slots * LANES, bytes_accessed=2 * depth * slots, transcendentals=0
        ),
        name="project",
    )(flipped, pltpu.with_memory_space_constraint(band_coeffs, pltpu.VMEM))


def project_plain(projectors, band_coeffs, part):
    depth, bands = band_coeffs.shape
    chips = lax.axis_size("pw") // 2
    blocks = jnp.stack([block_of(place()[1], part, r) for r in range(chips // SQUARE)])
    columns = jnp.take(band_coeffs.reshape(depth, chips, bands // chips), blocks, axis=1)
    core = place()[0]
    outs = []
    for group, dtype in ((1 - core, jnp.bfloat16), (core, jnp.float32)):
        slots = lax.dynamic_slice_in_dim(projectors, group * PCAP, PCAP, 1)
        sums = jnp.einsum("ds,dhw->hsw", slots, columns, preferred_element_type=jnp.float32)
        outs.append(sums.astype(dtype))
    return outs


def choose_kernel(owners, own, sibling, after, out):
    del after
    core, chip = place()
    me = 2 * chip + core
    owner = jnp.where(core == 0, owners[0:1, :], owners[1:2, :])
    width = out.shape[2]
    for part in range(SQUARE):
        rows = pl.ds(pl.multiple_of(((chip & 3) ^ part) * QUARTER, QUARTER), QUARTER)
        piece = jnp.where(owner == me, own[rows], jnp.where(owner == (me ^ 1), sibling[rows], 0.0))
        for cut in range(PCAP // width):
            out[part, cut * QUARTER : (cut + 1) * QUARTER] = piece[:, cut * width : (cut + 1) * width].astype(
                out.dtype
            )


def choose(owners, own, sibling, width, after):
    return pl.pallas_call(
        choose_kernel,
        in_specs=[VMEM, VMEM, VMEM, ANY],
        out_specs=VMEM,
        out_shape=jax.ShapeDtypeStruct((SQUARE, QUARTER * PCAP // width, width), jnp.bfloat16),
        compiler_params=PARAMS,
        name="choose",
    )(jnp.broadcast_to(owners[:, None], (owners.shape[0], PCAP)), own, sibling, after)


def send_kernel(ours, theirs, quarters, message):
    entries = ours.shape[0]
    for entry in range(entries):
        total = ours[entry] + theirs[entry].astype(jnp.float32)
        message[entry * PCAP : (entry + 1) * PCAP] = total.astype(message.dtype)
    message[entries * PCAP :] = quarters[3]


def send(ours, theirs, quarters):
    entries, _, width = ours.shape
    return pl.pallas_call(
        send_kernel,
        in_specs=[VMEM] * 3,
        out_specs=VMEM,
        out_shape=jax.ShapeDtypeStruct((entries * PCAP + quarters.shape[1], width), jnp.bfloat16),
        compiler_params=PARAMS,
        name="send",
    )(ours, theirs, quarters)


def put_sums(part, sums, message, got=None):
    one, two, their_one, their_two = sums
    entries = one.shape[0]
    for entry in range(entries):
        rows = slice(entry * PCAP, (entry + 1) * PCAP)
        total = jnp.where(part == 1, one[entry], two[entry])
        total = total + jnp.where(part == 1, their_one[entry], their_two[entry]).astype(jnp.float32)
        if got is not None:
            total = total + got[rows].astype(jnp.float32)
        message[rows] = total.astype(message.dtype)
    return slice(entries * PCAP, message.shape[0])


def send_first_kernel(*refs):
    *sums, quarters, message = refs
    part = 1 + place()[0]
    rows = put_sums(part, sums, message)
    message[rows] = quarters[part]


def forward_kernel(*refs):
    *sums, quarters, got, message = refs
    part = 2 - place()[0]
    rows = put_sums(part, sums, message, got)
    message[rows] = quarters[part] + got[rows]


def send_pair(sums, quarters, got=None):
    entries, _, width = sums[0].shape
    operands = sums + (quarters,) + (() if got is None else (got,))
    return pl.pallas_call(
        send_first_kernel if got is None else forward_kernel,
        in_specs=[VMEM] * len(operands),
        out_specs=VMEM,
        out_shape=jax.ShapeDtypeStruct((entries * PCAP + quarters.shape[1], width), jnp.bfloat16),
        compiler_params=PARAMS,
        name="send_first" if got is None else "forward",
    )(*operands)


def fold_kernel(ours, theirs, quarters, *refs):
    *gots, kept, message = refs
    entries = ours.shape[0]
    for entry in range(entries):
        rows = slice(entry * PCAP, (entry + 1) * PCAP)
        total = ours[entry] + theirs[entry].astype(jnp.float32)
        for got in gots:
            total = total + got[rows].astype(jnp.float32)
        kept[rows] = total
        away = entry ^ 1
        message[away * PCAP : (away + 1) * PCAP] = total.astype(message.dtype)
    table = quarters[0]
    for got in gots:
        table = table + got[entries * PCAP :]
    kept[entries * PCAP :] = table.astype(kept.dtype)
    message[entries * PCAP :] = table


def fold(ours, theirs, quarters, gots):
    shape = gots[0].shape
    return pl.pallas_call(
        fold_kernel,
        in_specs=[VMEM] * (3 + len(gots)),
        out_specs=[VMEM, VMEM],
        out_shape=[jax.ShapeDtypeStruct(shape, jnp.float32), jax.ShapeDtypeStruct(shape, jnp.bfloat16)],
        compiler_params=PARAMS,
        name="fold",
    )(ours, theirs, quarters, *gots)


def add_kernel(left, right, out):
    out[...] = (left[...] + right[...].astype(jnp.float32)).astype(out.dtype)


def add(left, right):
    return pl.pallas_call(
        add_kernel,
        in_specs=[VMEM, VMEM],
        out_specs=VMEM,
        out_shape=jax.ShapeDtypeStruct(left.shape, jnp.bfloat16),
        compiler_params=PARAMS,
        name="add",
    )(left, right)


def mask_kernel(counts, atom_of, after, out):
    del after
    core = place()[0]
    slot = lax.broadcasted_iota(jnp.int32, (1, PCAP), 1)
    limit = jnp.zeros((1, PCAP), jnp.int32)
    for channel in range(CHANNELS):
        limit = jnp.where(slot >= channel * CH_CAP, channel * CH_CAP + counts[core, channel], limit)
    atoms = jnp.where(core == 0, atom_of[0:1], atom_of[1:2])
    code = jnp.broadcast_to(jnp.where(slot < limit, atoms, -1), (PCAP, PCAP))
    out[...] = jnp.where((code == code.T) & (code >= 0), 1.0, 0.0).astype(out.dtype)


def mask(counts, atom_of, after):
    return pl.pallas_call(
        mask_kernel,
        in_specs=[SMEM, VMEM, ANY],
        out_specs=VMEM,
        out_shape=jax.ShapeDtypeStruct((PCAP, PCAP), jnp.bfloat16),
        compiler_params=PARAMS,
        name="mask",
    )(counts, atom_of, after)


def couple_kernel(allowed, *refs):
    *messages, out, coupling = refs
    width = out.shape[2]
    entries = out.shape[0] // SQUARE
    corner = place()[1] & 3
    for part, message in zip(GATHERED, messages):
        start = pl.multiple_of((corner ^ part) * QUARTER, QUARTER)
        for cut in range(PCAP // width):
            lanes = slice(cut * width, (cut + 1) * width)
            first = entries * PCAP + cut * QUARTER
            coupling[pl.ds(start, QUARTER), lanes] = (
                message[first : first + QUARTER] * allowed[pl.ds(start, QUARTER), lanes]
            )
    for part, message in zip(GATHERED, messages):
        wide = jnp.concatenate([message[e * PCAP : (e + 1) * PCAP] for e in range(entries)], axis=1)
        scaled = jnp.dot(coupling[...], wide, preferred_element_type=jnp.float32).astype(out.dtype)
        for entry in range(entries):
            out[part * entries + entry] = scaled[:, entry * width : (entry + 1) * width]


def couple(allowed, messages):
    rows, width = messages[0].shape
    entries = (rows - QUARTER * PCAP // width) // PCAP
    return pl.pallas_call(
        couple_kernel,
        in_specs=[VMEM] * (1 + SQUARE),
        out_specs=VMEM,
        out_shape=jax.ShapeDtypeStruct((SQUARE * entries, PCAP, width), jnp.bfloat16),
        scratch_shapes=[pltpu.VMEM((PCAP, PCAP), jnp.bfloat16)],
        compiler_params=PARAMS,
        name="couple",
    )(allowed, *messages)


def group_slots(group):
    return pl.ds(pl.multiple_of(group * PCAP, PCAP), PCAP)


def wide_pair(scaled, part):
    return jnp.concatenate([scaled[2 * part], scaled[2 * part + 1]], axis=1)


def begin_kernel(projectors, scaled, out):
    slots = group_slots(place()[0])
    for part in range(SQUARE):
        for block in range(projectors.shape[0] // ROW_BLOCK):
            rows = slice(block * ROW_BLOCK, (block + 1) * ROW_BLOCK)
            out[part, rows] = jnp.dot(
                projectors[rows, slots], wide_pair(scaled, part), preferred_element_type=jnp.float32
            )


def begin(projectors, scaled):
    depth, slots = projectors.shape
    return pl.pallas_call(
        begin_kernel,
        in_specs=[VMEM, VMEM],
        out_specs=VMEM,
        out_shape=jax.ShapeDtypeStruct((SQUARE, depth, 2 * LANES), jnp.float32),
        compiler_params=PARAMS,
        cost_estimate=pl.CostEstimate(
            flops=2 * depth * slots * LANES * SQUARE, bytes_accessed=2 * depth * slots, transcendentals=0
        ),
        name="begin",
    )(projectors, scaled)


def finish_kernel(projectors, begun, other, out, blocks, sems):
    core, chip = place()
    slots = group_slots(1 - core)
    copies = []
    first = 0
    for size in ROW_BLOCKS:
        rows = slice(first, first + size)
        first += size
        for part in range(SQUARE):
            sums = begun[part, rows] + jnp.dot(
                projectors[rows, slots], wide_pair(other, part), preferred_element_type=jnp.float32
            )
            for entry in range(2):
                start = pl.multiple_of(block_of(chip, part, entry) * LANES, LANES)
                lanes = slice(entry * LANES, (entry + 1) * LANES)
                blocks[rows, pl.ds(start, LANES)] = sums[:, lanes].astype(blocks.dtype)
        for start in range(rows.start, rows.stop, COPY_ROWS):
            written = slice(start, start + COPY_ROWS)
            copies.append(pltpu.make_async_copy(blocks.at[written], out.at[written], sems.at[len(copies)]))
            copies[-1].start()
    for copy in copies:
        copy.wait()


def finish(projectors, begun, other):
    depth, slots = projectors.shape
    bands = other.shape[0] * LANES
    return pl.pallas_call(
        finish_kernel,
        in_specs=[VMEM] * 3,
        out_specs=HBM,
        out_shape=jax.ShapeDtypeStruct((depth, bands), jnp.bfloat16),
        scratch_shapes=[
            pltpu.VMEM((depth, bands), jnp.bfloat16),
            pltpu.SemaphoreType.DMA((depth // COPY_ROWS,)),
        ],
        compiler_params=PARAMS,
        cost_estimate=pl.CostEstimate(
            flops=depth * slots * bands, bytes_accessed=2 * depth * (slots + bands), transcendentals=0
        ),
        name="finish",
    )(projectors, begun, other)


def apply_plain(projectors, mine, other):
    chips, _, width = mine.shape
    blocks = jnp.stack([block_of(place()[1], q, r) for q in range(SQUARE) for r in range(chips // SQUARE)])
    rows = []
    for group in range(2):
        part = jnp.where(place()[0] == group, mine, other)
        part = jnp.zeros_like(part).at[blocks].set(part)
        rows.append(part.transpose(1, 0, 2).reshape(PCAP, chips * width))
    return jnp.dot(projectors, jnp.concatenate(rows), preferred_element_type=jnp.float32).astype(jnp.bfloat16)


def local(band_coeffs, projectors, counts, atom_of, owners, couplings):
    chips = lax.axis_size("pw") // 2
    entries = chips // SQUARE
    width = band_coeffs.shape[1] // chips
    fast = width == LANES and entries == 2
    own_table = couplings[0]
    sibling_table = swap_cores(own_table)
    if fast:
        flipped = load(projectors)

        def partial(part):
            return project(flipped, band_coeffs, part)
    else:

        def partial(part):
            return project_plain(projectors, band_coeffs, part)

    theirs, ours = partial(3)
    theirs, sibling_table = lax.optimization_barrier((theirs, sibling_table))
    theirs = swap_cores(theirs)
    their_one, one = partial(1)
    quarters = choose(owners, own_table, sibling_table, width, ours)
    theirs, their_one = lax.optimization_barrier((theirs, their_one))
    message = send(ours, theirs, quarters)
    got = swap_first(message)
    if fast:
        flipped, message = lax.optimization_barrier((flipped, message))
    their_two, two = partial(2)
    sums = (one, two, swap_cores(their_one), swap_cores(their_two))
    low_theirs, low_ours = partial(0)
    low_theirs = swap_cores(low_theirs)
    got_first = swap_first(send_pair(sums, quarters))
    message = send_pair(sums, quarters, got)
    got_second = swap_second(message)
    allowed = mask(counts, atom_of, message)

    total, message = fold(low_ours, low_theirs, quarters, [got_first, got_second])
    mine = add(total, swap_chips(message, SQUARE))
    distance = 2 * SQUARE
    while distance < chips:
        body = mine[: entries * PCAP].reshape(entries, PCAP, width)
        order = [entry ^ (distance // SQUARE) for entry in range(entries)]
        message = jnp.concatenate([body[jnp.array(order)].reshape(-1, width), mine[entries * PCAP :]])
        mine = add(mine.astype(jnp.float32), swap_chips(message, distance))
        distance *= 2

    scaled = couple(allowed, [swap_chips(mine, part) if part else mine for part in GATHERED])
    other = swap_cores(scaled)
    if not fast:
        return apply_plain(projectors, scaled, other)
    return finish(projectors, begin(projectors, scaled), other)


def solution(mesh):
    placed = (
        P("pw", "group"),
        P("pw", "group"),
        P("group", None),
        P("group", None),
        P("group"),
        P("pw", "group", None),
    )
    return jax.shard_map(
        local, mesh=mesh, in_specs=placed, out_specs=P("pw", "group"), check_vma=False
    )
```

```python
import jax
import jax.numpy as jnp
from jax import lax
from jax.experimental import pallas as pl
from jax.experimental.pallas import tpu as pltpu
from jax.sharding import PartitionSpec as P

CHANNELS = 4
CH_CAP = 64
PCAP = 256
LANES = 128
SQUARE = 4
QUARTER = PCAP // SQUARE
ROW_BLOCK = 512
ROW_BLOCKS = (512, 512, 512, 256, 256)
COPY_ROWS = 128
PARAMS = pltpu.CompilerParams(vmem_limit_bytes=40 * 1024 * 1024)
VMEM = pl.BlockSpec(memory_space=pltpu.VMEM)
SMEM = pl.BlockSpec(memory_space=pltpu.SMEM)
HBM = pl.BlockSpec(memory_space=pltpu.HBM)
ANY = pl.BlockSpec(memory_space=pl.ANY)


def place():
    me = lax.axis_index("pw")
    return lax.rem(me, 2), lax.div(me, 2)


def block_of(chip, part, entry):
    return chip ^ (part + SQUARE * entry)


def swap(x, distance):
    count = lax.axis_size("pw")
    return lax.ppermute(x, "pw", [(i, i ^ distance) for i in range(count)])


def swap_cores(x):
    return swap(x, 1)


def swap_chips(x, distance):
    return swap(x, 2 * distance)


def swap_first(x):
    count = lax.axis_size("pw")
    return lax.ppermute(x, "pw", [(i, i ^ (2, 4)[i % 2]) for i in range(count)])


def swap_second(x):
    count = lax.axis_size("pw")
    return lax.ppermute(x, "pw", [(i, i ^ (4, 2)[i % 2]) for i in range(count)])


def pair_at(columns, rows, part):
    chip = place()[1]
    starts = [pl.multiple_of(block_of(chip, part, entry) * LANES, LANES) for entry in range(2)]
    return jnp.concatenate([columns[rows, pl.ds(start, LANES)] for start in starts], axis=1)


def keep_sums(ours, theirs, at, sums):
    for entry in range(2):
        lanes = slice(entry * LANES, (entry + 1) * LANES)
        ours[2 * at + entry] = sums[:PCAP, lanes]
        theirs[2 * at + entry] = sums[PCAP:, lanes].astype(theirs.dtype)


def load_kernel(projectors, flipped, slots, sems):
    core = place()[0]
    count = sems.shape[0]
    block = slots.shape[0] // count
    copies = []
    for at in range(count):
        rows = slice(at * block, (at + 1) * block)
        copies.append(pltpu.make_async_copy(projectors.at[rows], slots.at[rows], sems.at[at]))
        copies[-1].start()
    for at, copy in enumerate(copies):
        copy.wait()
        rows = slice(at * block, (at + 1) * block)
        for side, group in enumerate((core, 1 - core)):
            start = pl.multiple_of(group * PCAP, PCAP)
            flipped[side * PCAP : (side + 1) * PCAP, rows] = slots[rows, pl.ds(start, PCAP)].T


def load(projectors):
    depth, slots = projectors.shape
    return pl.pallas_call(
        load_kernel,
        in_specs=[HBM],
        out_specs=VMEM,
        out_shape=jax.ShapeDtypeStruct((slots, depth), jnp.bfloat16),
        scratch_shapes=[pltpu.VMEM((depth, slots), jnp.bfloat16), pltpu.SemaphoreType.DMA((4,))],
        compiler_params=PARAMS,
        name="load",
    )(pltpu.with_memory_space_constraint(projectors, pltpu.HBM))


def project_kernel(parts, flipped, columns, theirs, ours):
    rows = slice(0, columns.shape[0])
    for at, part in enumerate(parts):
        sums = jnp.dot(flipped[...], pair_at(columns, rows, part), preferred_element_type=jnp.float32)
        keep_sums(ours, theirs, at, sums)


def project(flipped, band_coeffs, parts):
    slots, depth = flipped.shape
    shape = (2 * len(parts), PCAP, LANES)

    def kernel(*refs):
        project_kernel(parts, *refs)

    return pl.pallas_call(
        kernel,
        in_specs=[VMEM, VMEM],
        out_specs=[VMEM, VMEM],
        out_shape=[jax.ShapeDtypeStruct(shape, jnp.bfloat16), jax.ShapeDtypeStruct(shape, jnp.float32)],
        compiler_params=PARAMS,
        cost_estimate=pl.CostEstimate(
            flops=4 * depth * slots * len(parts) * LANES, bytes_accessed=2 * depth * slots, transcendentals=0
        ),
        name="project",
    )(flipped, pltpu.with_memory_space_constraint(band_coeffs, pltpu.VMEM))


def project_plain(projectors, band_coeffs, parts):
    depth, bands = band_coeffs.shape
    chips = lax.axis_size("pw") // 2
    blocks = jnp.stack([block_of(place()[1], q, r) for q in parts for r in range(chips // SQUARE)])
    columns = jnp.take(band_coeffs.reshape(depth, chips, bands // chips), blocks, axis=1)
    outs = []
    core = place()[0]
    for group, dtype in ((1 - core, jnp.bfloat16), (core, jnp.float32)):
        slots = lax.dynamic_slice_in_dim(projectors, group * PCAP, PCAP, 1)
        sums = jnp.einsum("ds,dhw->hsw", slots, columns, preferred_element_type=jnp.float32)
        outs.append(sums.astype(dtype))
    return outs


def choose_kernel(owners, own, sibling, after, out):
    del after
    core, chip = place()
    me = 2 * chip + core
    owner = jnp.where(core == 0, owners[0:1, :], owners[1:2, :])
    width = out.shape[2]
    for part in range(SQUARE):
        rows = pl.ds(pl.multiple_of(((chip & 3) ^ part) * QUARTER, QUARTER), QUARTER)
        piece = jnp.where(owner == me, own[rows], jnp.where(owner == (me ^ 1), sibling[rows], 0.0))
        for cut in range(PCAP // width):
            out[part, cut * QUARTER : (cut + 1) * QUARTER] = piece[:, cut * width : (cut + 1) * width].astype(
                out.dtype
            )


def choose(owners, own, sibling, width, after):
    return pl.pallas_call(
        choose_kernel,
        in_specs=[VMEM, VMEM, VMEM, ANY],
        out_specs=VMEM,
        out_shape=jax.ShapeDtypeStruct((SQUARE, QUARTER * PCAP // width, width), jnp.bfloat16),
        compiler_params=PARAMS,
        name="choose",
    )(jnp.broadcast_to(owners[:, None], (owners.shape[0], PCAP)), own, sibling, after)


def send_kernel(first, second, ours, theirs, quarters, message):
    entries = ours.shape[0] // (1 if first == second else 2)
    core = place()[0]
    start, part = (0, first) if first == second else (core * entries, 1 + core)
    for entry in range(entries):
        total = ours[start + entry] + theirs[start + entry].astype(jnp.float32)
        message[entry * PCAP : (entry + 1) * PCAP] = total.astype(message.dtype)
    message[entries * PCAP :] = quarters[part]


def send(ours, theirs, quarters, parts):
    count, _, width = ours.shape
    rows = count // len(parts) * PCAP + quarters.shape[1]

    def kernel(*refs):
        send_kernel(parts[0], parts[-1], *refs)

    return pl.pallas_call(
        kernel,
        in_specs=[VMEM] * 3,
        out_specs=VMEM,
        out_shape=jax.ShapeDtypeStruct((rows, width), jnp.bfloat16),
        compiler_params=PARAMS,
        name="send",
    )(ours, theirs, quarters)


def forward_kernel(ours, theirs, quarters, got, message):
    core = place()[0]
    entries = ours.shape[0] // 2
    start = (1 - core) * entries
    for entry in range(entries):
        rows = slice(entry * PCAP, (entry + 1) * PCAP)
        total = ours[start + entry] + theirs[start + entry].astype(jnp.float32)
        message[rows] = (total + got[rows].astype(jnp.float32)).astype(message.dtype)
    message[entries * PCAP :] = quarters[2 - core] + got[entries * PCAP :]


def forward(ours, theirs, quarters, got):
    return pl.pallas_call(
        forward_kernel,
        in_specs=[VMEM] * 4,
        out_specs=VMEM,
        out_shape=jax.ShapeDtypeStruct(got.shape, got.dtype),
        compiler_params=PARAMS,
        name="forward",
    )(ours, theirs, quarters, got)


def fold_kernel(ours, theirs, quarters, *refs):
    *gots, kept, message = refs
    entries = ours.shape[0]
    for entry in range(entries):
        rows = slice(entry * PCAP, (entry + 1) * PCAP)
        total = ours[entry] + theirs[entry].astype(jnp.float32)
        for got in gots:
            total = total + got[rows].astype(jnp.float32)
        kept[rows] = total
        away = entry ^ 1
        message[away * PCAP : (away + 1) * PCAP] = total.astype(message.dtype)
    table = quarters[0]
    for got in gots:
        table = table + got[entries * PCAP :]
    kept[entries * PCAP :] = table.astype(kept.dtype)
    message[entries * PCAP :] = table


def fold(ours, theirs, quarters, gots):
    shape = gots[0].shape
    return pl.pallas_call(
        fold_kernel,
        in_specs=[VMEM] * (3 + len(gots)),
        out_specs=[VMEM, VMEM],
        out_shape=[jax.ShapeDtypeStruct(shape, jnp.float32), jax.ShapeDtypeStruct(shape, jnp.bfloat16)],
        compiler_params=PARAMS,
        name="fold",
    )(ours, theirs, quarters, *gots)


def add_kernel(left, right, out):
    out[...] = (left[...] + right[...].astype(jnp.float32)).astype(out.dtype)


def add(left, right):
    return pl.pallas_call(
        add_kernel,
        in_specs=[VMEM, VMEM],
        out_specs=VMEM,
        out_shape=jax.ShapeDtypeStruct(left.shape, jnp.bfloat16),
        compiler_params=PARAMS,
        name="add",
    )(left, right)


def mask_kernel(counts, atom_of, after, out):
    del after
    core = place()[0]
    slot = lax.broadcasted_iota(jnp.int32, (1, PCAP), 1)
    limit = jnp.zeros((1, PCAP), jnp.int32)
    for channel in range(CHANNELS):
        limit = jnp.where(slot >= channel * CH_CAP, channel * CH_CAP + counts[core, channel], limit)
    atoms = jnp.where(core == 0, atom_of[0:1], atom_of[1:2])
    code = jnp.broadcast_to(jnp.where(slot < limit, atoms, -1), (PCAP, PCAP))
    out[...] = jnp.where((code == code.T) & (code >= 0), 1.0, 0.0).astype(out.dtype)


def mask(counts, atom_of, after):
    return pl.pallas_call(
        mask_kernel,
        in_specs=[SMEM, VMEM, ANY],
        out_specs=VMEM,
        out_shape=jax.ShapeDtypeStruct((PCAP, PCAP), jnp.bfloat16),
        compiler_params=PARAMS,
        name="mask",
    )(counts, atom_of, after)


def couple_kernel(allowed, *refs):
    *messages, out, coupling = refs
    width = out.shape[2]
    entries = out.shape[0] // SQUARE
    core, chip = place()
    corner = chip & 3
    parts = (0, 1 + core, 2 - core, 3)
    for part, message in zip(parts, messages):
        start = pl.multiple_of((corner ^ part) * QUARTER, QUARTER)
        for cut in range(PCAP // width):
            lanes = slice(cut * width, (cut + 1) * width)
            first = entries * PCAP + cut * QUARTER
            coupling[pl.ds(start, QUARTER), lanes] = (
                message[first : first + QUARTER] * allowed[pl.ds(start, QUARTER), lanes]
            )
    for part, message in zip(parts, messages):
        wide = jnp.concatenate([message[e * PCAP : (e + 1) * PCAP] for e in range(entries)], axis=1)
        scaled = jnp.dot(coupling[...], wide, preferred_element_type=jnp.float32).astype(out.dtype)
        for entry in range(entries):
            out[part * entries + entry] = scaled[:, entry * width : (entry + 1) * width]


def couple(allowed, messages):
    rows, width = messages[0].shape
    entries = (rows - QUARTER * PCAP // width) // PCAP
    return pl.pallas_call(
        couple_kernel,
        in_specs=[VMEM] * (1 + SQUARE),
        out_specs=VMEM,
        out_shape=jax.ShapeDtypeStruct((SQUARE * entries, PCAP, width), jnp.bfloat16),
        scratch_shapes=[pltpu.VMEM((PCAP, PCAP), jnp.bfloat16)],
        compiler_params=PARAMS,
        name="couple",
    )(allowed, *messages)


def group_slots(group):
    return pl.ds(pl.multiple_of(group * PCAP, PCAP), PCAP)


def wide_pair(scaled, part):
    return jnp.concatenate([scaled[2 * part], scaled[2 * part + 1]], axis=1)


def begin_kernel(projectors, scaled, out):
    slots = group_slots(place()[0])
    for part in range(SQUARE):
        for block in range(projectors.shape[0] // ROW_BLOCK):
            rows = slice(block * ROW_BLOCK, (block + 1) * ROW_BLOCK)
            out[part, rows] = jnp.dot(
                projectors[rows, slots], wide_pair(scaled, part), preferred_element_type=jnp.float32
            )


def begin(projectors, scaled):
    depth, slots = projectors.shape
    return pl.pallas_call(
        begin_kernel,
        in_specs=[VMEM, VMEM],
        out_specs=VMEM,
        out_shape=jax.ShapeDtypeStruct((SQUARE, depth, 2 * LANES), jnp.float32),
        compiler_params=PARAMS,
        cost_estimate=pl.CostEstimate(
            flops=2 * depth * slots * LANES * SQUARE, bytes_accessed=2 * depth * slots, transcendentals=0
        ),
        name="begin",
    )(projectors, scaled)


def finish_kernel(projectors, begun, other, out, blocks, sems):
    core, chip = place()
    slots = group_slots(1 - core)
    copies = []
    first = 0
    for size in ROW_BLOCKS:
        rows = slice(first, first + size)
        first += size
        for part in range(SQUARE):
            sums = begun[part, rows] + jnp.dot(
                projectors[rows, slots], wide_pair(other, part), preferred_element_type=jnp.float32
            )
            for entry in range(2):
                start = pl.multiple_of(block_of(chip, part, entry) * LANES, LANES)
                lanes = slice(entry * LANES, (entry + 1) * LANES)
                blocks[rows, pl.ds(start, LANES)] = sums[:, lanes].astype(blocks.dtype)
        for start in range(rows.start, rows.stop, COPY_ROWS):
            written = slice(start, start + COPY_ROWS)
            copies.append(pltpu.make_async_copy(blocks.at[written], out.at[written], sems.at[len(copies)]))
            copies[-1].start()
    for copy in copies:
        copy.wait()


def finish(projectors, begun, other):
    depth, slots = projectors.shape
    bands = other.shape[0] * LANES
    return pl.pallas_call(
        finish_kernel,
        in_specs=[VMEM] * 3,
        out_specs=HBM,
        out_shape=jax.ShapeDtypeStruct((depth, bands), jnp.bfloat16),
        scratch_shapes=[
            pltpu.VMEM((depth, bands), jnp.bfloat16),
            pltpu.SemaphoreType.DMA((depth // COPY_ROWS,)),
        ],
        compiler_params=PARAMS,
        cost_estimate=pl.CostEstimate(
            flops=depth * slots * bands, bytes_accessed=2 * depth * (slots + bands), transcendentals=0
        ),
        name="finish",
    )(projectors, begun, other)


def apply_plain(projectors, mine, other):
    chips, _, width = mine.shape
    blocks = jnp.stack([block_of(place()[1], q, r) for q in range(SQUARE) for r in range(chips // SQUARE)])
    rows = []
    for group in range(2):
        part = jnp.where(place()[0] == group, mine, other)
        part = jnp.zeros_like(part).at[blocks].set(part)
        rows.append(part.transpose(1, 0, 2).reshape(PCAP, chips * width))
    return jnp.dot(projectors, jnp.concatenate(rows), preferred_element_type=jnp.float32).astype(jnp.bfloat16)


def local(band_coeffs, projectors, counts, atom_of, owners, couplings):
    chips = lax.axis_size("pw") // 2
    entries = chips // SQUARE
    width = band_coeffs.shape[1] // chips
    fast = width == LANES and entries == 2
    own_table = couplings[0]
    sibling_table = swap_cores(own_table)
    if fast:
        flipped = load(projectors)

        def partial(parts):
            return project(flipped, band_coeffs, parts)
    else:

        def partial(parts):
            return project_plain(projectors, band_coeffs, parts)

    theirs, ours = partial((3,))
    theirs, sibling_table = lax.optimization_barrier((theirs, sibling_table))
    theirs = swap_cores(theirs)
    pair_theirs, pair_ours = partial((1, 2))
    quarters = choose(owners, own_table, sibling_table, width, ours)
    got = swap_first(send(ours, theirs, quarters, (3,)))
    pair_theirs = swap_cores(pair_theirs)
    low_theirs, low_ours = partial((0,))
    low_theirs = swap_cores(low_theirs)
    got_first = swap_first(send(pair_ours, pair_theirs, quarters, (1, 2)))
    message = forward(pair_ours, pair_theirs, quarters, got)
    got_second = swap_second(message)
    allowed = mask(counts, atom_of, message)

    total, message = fold(low_ours, low_theirs, quarters, [got_first, got_second])
    mine = add(total, swap_chips(message, SQUARE))
    distance = 2 * SQUARE
    while distance < chips:
        body = mine[: entries * PCAP].reshape(entries, PCAP, width)
        order = [entry ^ (distance // SQUARE) for entry in range(entries)]
        message = jnp.concatenate([body[jnp.array(order)].reshape(-1, width), mine[entries * PCAP :]])
        mine = add(mine.astype(jnp.float32), swap_chips(message, distance))
        distance *= 2

    scaled = couple(allowed, [mine, swap_first(mine), swap_second(mine), swap_chips(mine, 3)])
    other = swap_cores(scaled)
    if not fast:
        return apply_plain(projectors, scaled, other)
    return finish(projectors, begin(projectors, scaled), other)


def solution(mesh):
    placed = (
        P("pw", "group"),
        P("pw", "group"),
        P("group", None),
        P("group", None),
        P("group"),
        P("pw", "group", None),
    )
    return jax.shard_map(
        local, mesh=mesh, in_specs=placed, out_specs=P("pw", "group"), check_vma=False
    )
```

```python
import jax
import jax.numpy as jnp
from jax import lax
from jax.experimental import pallas as pl
from jax.experimental.pallas import tpu as pltpu
from jax.sharding import PartitionSpec as P

CHANNELS = 4
CH_CAP = 64
PCAP = 256
LANES = 128
SQUARE = 4
QUARTER = PCAP // SQUARE
ROW_BLOCK = 512
ROW_BLOCKS = (512, 512, 512, 256, 256)
COPY_ROWS = 128
PARAMS = pltpu.CompilerParams(vmem_limit_bytes=40 * 1024 * 1024)
VMEM = pl.BlockSpec(memory_space=pltpu.VMEM)
SMEM = pl.BlockSpec(memory_space=pltpu.SMEM)
HBM = pl.BlockSpec(memory_space=pltpu.HBM)
ANY = pl.BlockSpec(memory_space=pl.ANY)


def place():
    me = lax.axis_index("pw")
    return lax.rem(me, 2), lax.div(me, 2)


def block_of(chip, part, entry):
    return chip ^ (part + SQUARE * entry)


def swap(x, distance):
    count = lax.axis_size("pw")
    return lax.ppermute(x, "pw", [(i, i ^ distance) for i in range(count)])


def swap_cores(x):
    return swap(x, 1)


def swap_chips(x, distance):
    return swap(x, 2 * distance)


def swap_first(x):
    count = lax.axis_size("pw")
    return lax.ppermute(x, "pw", [(i, i ^ (2, 4)[i % 2]) for i in range(count)])


def swap_second(x):
    count = lax.axis_size("pw")
    return lax.ppermute(x, "pw", [(i, i ^ (4, 2)[i % 2]) for i in range(count)])


def pair_at(columns, rows, part):
    chip = place()[1]
    starts = [pl.multiple_of(block_of(chip, part, entry) * LANES, LANES) for entry in range(2)]
    return jnp.concatenate([columns[rows, pl.ds(start, LANES)] for start in starts], axis=1)


def keep_sums(ours, theirs, at, sums):
    for entry in range(2):
        lanes = slice(entry * LANES, (entry + 1) * LANES)
        ours[2 * at + entry] = sums[:PCAP, lanes]
        theirs[2 * at + entry] = sums[PCAP:, lanes].astype(theirs.dtype)


def exchange_square(x):
    count = lax.axis_size("pw")
    groups = [
        list(range(base + core, base + 2 * SQUARE, 2)) for base in range(0, count, 2 * SQUARE) for core in range(2)
    ]
    return lax.all_to_all(x, "pw", 0, 0, axis_index_groups=groups)


def load_kernel(projectors, flipped, slots, sems):
    core = place()[0]
    count = sems.shape[0]
    block = slots.shape[0] // count
    copies = []
    for at in range(count):
        rows = slice(at * block, (at + 1) * block)
        copies.append(pltpu.make_async_copy(projectors.at[rows], slots.at[rows], sems.at[at]))
        copies[-1].start()
    for at, copy in enumerate(copies):
        copy.wait()
        rows = slice(at * block, (at + 1) * block)
        for side, group in enumerate((core, 1 - core)):
            start = pl.multiple_of(group * PCAP, PCAP)
            flipped[side * PCAP : (side + 1) * PCAP, rows] = slots[rows, pl.ds(start, PCAP)].T


def load(projectors):
    depth, slots = projectors.shape
    return pl.pallas_call(
        load_kernel,
        in_specs=[HBM],
        out_specs=VMEM,
        out_shape=jax.ShapeDtypeStruct((slots, depth), jnp.bfloat16),
        scratch_shapes=[pltpu.VMEM((depth, slots), jnp.bfloat16), pltpu.SemaphoreType.DMA((4,))],
        compiler_params=PARAMS,
        name="load",
    )(pltpu.with_memory_space_constraint(projectors, pltpu.HBM))


def project_kernel(parts, flipped, columns, theirs, ours):
    rows = slice(0, columns.shape[0])
    for at, part in enumerate(parts):
        sums = jnp.dot(flipped[...], pair_at(columns, rows, part), preferred_element_type=jnp.float32)
        keep_sums(ours, theirs, at, sums)


def project(flipped, band_coeffs, parts):
    slots, depth = flipped.shape
    shape = (2 * len(parts), PCAP, LANES)

    def kernel(*refs):
        project_kernel(parts, *refs)

    return pl.pallas_call(
        kernel,
        in_specs=[VMEM, VMEM],
        out_specs=[VMEM, VMEM],
        out_shape=[jax.ShapeDtypeStruct(shape, jnp.bfloat16), jax.ShapeDtypeStruct(shape, jnp.float32)],
        compiler_params=PARAMS,
        cost_estimate=pl.CostEstimate(
            flops=4 * depth * slots * len(parts) * LANES, bytes_accessed=2 * depth * slots, transcendentals=0
        ),
        name="project",
    )(flipped, pltpu.with_memory_space_constraint(band_coeffs, pltpu.VMEM))


def project_plain(projectors, band_coeffs, parts):
    depth, bands = band_coeffs.shape
    chips = lax.axis_size("pw") // 2
    blocks = jnp.stack([block_of(place()[1], q, r) for q in parts for r in range(chips // SQUARE)])
    columns = jnp.take(band_coeffs.reshape(depth, chips, bands // chips), blocks, axis=1)
    outs = []
    core = place()[0]
    for group, dtype in ((1 - core, jnp.bfloat16), (core, jnp.float32)):
        slots = lax.dynamic_slice_in_dim(projectors, group * PCAP, PCAP, 1)
        sums = jnp.einsum("ds,dhw->hsw", slots, columns, preferred_element_type=jnp.float32)
        outs.append(sums.astype(dtype))
    return outs


def choose_kernel(owners, own, sibling, after, out):
    del after
    core, chip = place()
    me = 2 * chip + core
    owner = jnp.where(core == 0, owners[0:1, :], owners[1:2, :])
    width = out.shape[2]
    for part in range(SQUARE):
        rows = pl.ds(pl.multiple_of(((chip & 3) ^ part) * QUARTER, QUARTER), QUARTER)
        piece = jnp.where(owner == me, own[rows], jnp.where(owner == (me ^ 1), sibling[rows], 0.0))
        for cut in range(PCAP // width):
            out[part, cut * QUARTER : (cut + 1) * QUARTER] = piece[:, cut * width : (cut + 1) * width].astype(
                out.dtype
            )


def choose(owners, own, sibling, width, after):
    return pl.pallas_call(
        choose_kernel,
        in_specs=[VMEM, VMEM, VMEM, ANY],
        out_specs=VMEM,
        out_shape=jax.ShapeDtypeStruct((SQUARE, QUARTER * PCAP // width, width), jnp.bfloat16),
        compiler_params=PARAMS,
        name="choose",
    )(jnp.broadcast_to(owners[:, None], (owners.shape[0], PCAP)), own, sibling, after)


def send_kernel(first, second, ours, theirs, quarters, message):
    entries = ours.shape[0] // (1 if first == second else 2)
    core = place()[0]
    start, part = (0, first) if first == second else (core * entries, 1 + core)
    for entry in range(entries):
        total = ours[start + entry] + theirs[start + entry].astype(jnp.float32)
        message[entry * PCAP : (entry + 1) * PCAP] = total.astype(message.dtype)
    message[entries * PCAP :] = quarters[part]


def send(ours, theirs, quarters, parts):
    count, _, width = ours.shape
    rows = count // len(parts) * PCAP + quarters.shape[1]

    def kernel(*refs):
        send_kernel(parts[0], parts[-1], *refs)

    return pl.pallas_call(
        kernel,
        in_specs=[VMEM] * 3,
        out_specs=VMEM,
        out_shape=jax.ShapeDtypeStruct((rows, width), jnp.bfloat16),
        compiler_params=PARAMS,
        name="send",
    )(ours, theirs, quarters)


def forward_kernel(ours, theirs, quarters, got, message):
    core = place()[0]
    entries = ours.shape[0] // 2
    start = (1 - core) * entries
    for entry in range(entries):
        rows = slice(entry * PCAP, (entry + 1) * PCAP)
        total = ours[start + entry] + theirs[start + entry].astype(jnp.float32)
        message[rows] = (total + got[rows].astype(jnp.float32)).astype(message.dtype)
    message[entries * PCAP :] = quarters[2 - core] + got[entries * PCAP :]


def forward(ours, theirs, quarters, got):
    return pl.pallas_call(
        forward_kernel,
        in_specs=[VMEM] * 4,
        out_specs=VMEM,
        out_shape=jax.ShapeDtypeStruct(got.shape, got.dtype),
        compiler_params=PARAMS,
        name="forward",
    )(ours, theirs, quarters, got)


def fold_kernel(ours, theirs, quarters, *refs):
    *gots, kept, message = refs
    entries = ours.shape[0]
    for entry in range(entries):
        rows = slice(entry * PCAP, (entry + 1) * PCAP)
        total = ours[entry] + theirs[entry].astype(jnp.float32)
        for got in gots:
            total = total + got[rows].astype(jnp.float32)
        kept[rows] = total
        away = entry ^ 1
        message[away * PCAP : (away + 1) * PCAP] = total.astype(message.dtype)
    table = quarters[0]
    for got in gots:
        table = table + got[entries * PCAP :]
    kept[entries * PCAP :] = table.astype(kept.dtype)
    message[entries * PCAP :] = table


def fold(ours, theirs, quarters, gots):
    shape = gots[0].shape
    return pl.pallas_call(
        fold_kernel,
        in_specs=[VMEM] * (3 + len(gots)),
        out_specs=[VMEM, VMEM],
        out_shape=[jax.ShapeDtypeStruct(shape, jnp.float32), jax.ShapeDtypeStruct(shape, jnp.bfloat16)],
        compiler_params=PARAMS,
        name="fold",
    )(ours, theirs, quarters, *gots)


def add_kernel(left, right, out):
    out[...] = (left[...] + right[...].astype(jnp.float32)).astype(out.dtype)


def add(left, right):
    return pl.pallas_call(
        add_kernel,
        in_specs=[VMEM, VMEM],
        out_specs=VMEM,
        out_shape=jax.ShapeDtypeStruct(left.shape, jnp.bfloat16),
        compiler_params=PARAMS,
        name="add",
    )(left, right)


def add_copies_kernel(left, right, out):
    total = (left[...] + right[...].astype(jnp.float32)).astype(out.dtype)
    for at in range(out.shape[0]):
        out[at] = total


def add_copies(left, right):
    return pl.pallas_call(
        add_copies_kernel,
        in_specs=[VMEM, VMEM],
        out_specs=VMEM,
        out_shape=jax.ShapeDtypeStruct((SQUARE,) + left.shape, jnp.bfloat16),
        compiler_params=PARAMS,
        name="add_copies",
    )(left, right)


def mask_kernel(counts, atom_of, after, out):
    del after
    core = place()[0]
    slot = lax.broadcasted_iota(jnp.int32, (1, PCAP), 1)
    limit = jnp.zeros((1, PCAP), jnp.int32)
    for channel in range(CHANNELS):
        limit = jnp.where(slot >= channel * CH_CAP, channel * CH_CAP + counts[core, channel], limit)
    atoms = jnp.where(core == 0, atom_of[0:1], atom_of[1:2])
    code = jnp.broadcast_to(jnp.where(slot < limit, atoms, -1), (PCAP, PCAP))
    out[...] = jnp.where((code == code.T) & (code >= 0), 1.0, 0.0).astype(out.dtype)


def mask(counts, atom_of, after):
    return pl.pallas_call(
        mask_kernel,
        in_specs=[SMEM, VMEM, ANY],
        out_specs=VMEM,
        out_shape=jax.ShapeDtypeStruct((PCAP, PCAP), jnp.bfloat16),
        compiler_params=PARAMS,
        name="mask",
    )(counts, atom_of, after)


def couple_kernel(allowed, messages, out, coupling):
    corner = place()[1] & 3
    width = out.shape[2]
    entries = out.shape[0] // SQUARE
    for at in range(SQUARE):
        for cut in range(PCAP // width):
            rows = slice(at * QUARTER, (at + 1) * QUARTER)
            lanes = slice(cut * width, (cut + 1) * width)
            first = entries * PCAP + cut * QUARTER
            coupling[rows, lanes] = messages[at, first : first + QUARTER] * allowed[rows, lanes]
    for at in range(SQUARE):
        wide = jnp.concatenate([messages[at, e * PCAP : (e + 1) * PCAP] for e in range(entries)], axis=1)
        scaled = jnp.dot(coupling[...], wide, preferred_element_type=jnp.float32).astype(out.dtype)
        part = corner ^ at
        for entry in range(entries):
            out[part * entries + entry] = scaled[:, entry * width : (entry + 1) * width]


def couple(allowed, messages):
    _, rows, width = messages.shape
    entries = (rows - QUARTER * PCAP // width) // PCAP
    return pl.pallas_call(
        couple_kernel,
        in_specs=[VMEM, VMEM],
        out_specs=VMEM,
        out_shape=jax.ShapeDtypeStruct((SQUARE * entries, PCAP, width), jnp.bfloat16),
        scratch_shapes=[pltpu.VMEM((PCAP, PCAP), jnp.bfloat16)],
        compiler_params=PARAMS,
        name="couple",
    )(allowed, messages)


def group_slots(group):
    return pl.ds(pl.multiple_of(group * PCAP, PCAP), PCAP)


def wide_pair(scaled, part):
    return jnp.concatenate([scaled[2 * part], scaled[2 * part + 1]], axis=1)


def begin_kernel(projectors, scaled, out):
    slots = group_slots(place()[0])
    for part in range(SQUARE):
        for block in range(projectors.shape[0] // ROW_BLOCK):
            rows = slice(block * ROW_BLOCK, (block + 1) * ROW_BLOCK)
            out[part, rows] = jnp.dot(
                projectors[rows, slots], wide_pair(scaled, part), preferred_element_type=jnp.float32
            )


def begin(projectors, scaled):
    depth, slots = projectors.shape
    return pl.pallas_call(
        begin_kernel,
        in_specs=[VMEM, VMEM],
        out_specs=VMEM,
        out_shape=jax.ShapeDtypeStruct((SQUARE, depth, 2 * LANES), jnp.float32),
        compiler_params=PARAMS,
        cost_estimate=pl.CostEstimate(
            flops=2 * depth * slots * LANES * SQUARE, bytes_accessed=2 * depth * slots, transcendentals=0
        ),
        name="begin",
    )(projectors, scaled)


def finish_kernel(projectors, begun, other, out, blocks, sems):
    core, chip = place()
    slots = group_slots(1 - core)
    copies = []
    first = 0
    for size in ROW_BLOCKS:
        rows = slice(first, first + size)
        first += size
        for part in range(SQUARE):
            sums = begun[part, rows] + jnp.dot(
                projectors[rows, slots], wide_pair(other, part), preferred_element_type=jnp.float32
            )
            for entry in range(2):
                start = pl.multiple_of(block_of(chip, part, entry) * LANES, LANES)
                lanes = slice(entry * LANES, (entry + 1) * LANES)
                blocks[rows, pl.ds(start, LANES)] = sums[:, lanes].astype(blocks.dtype)
        for start in range(rows.start, rows.stop, COPY_ROWS):
            written = slice(start, start + COPY_ROWS)
            copies.append(pltpu.make_async_copy(blocks.at[written], out.at[written], sems.at[len(copies)]))
            copies[-1].start()
    for copy in copies:
        copy.wait()


def finish(projectors, begun, other):
    depth, slots = projectors.shape
    bands = other.shape[0] * LANES
    return pl.pallas_call(
        finish_kernel,
        in_specs=[VMEM] * 3,
        out_specs=HBM,
        out_shape=jax.ShapeDtypeStruct((depth, bands), jnp.bfloat16),
        scratch_shapes=[
            pltpu.VMEM((depth, bands), jnp.bfloat16),
            pltpu.SemaphoreType.DMA((depth // COPY_ROWS,)),
        ],
        compiler_params=PARAMS,
        cost_estimate=pl.CostEstimate(
            flops=depth * slots * bands, bytes_accessed=2 * depth * (slots + bands), transcendentals=0
        ),
        name="finish",
    )(projectors, begun, other)


def apply_plain(projectors, mine, other):
    chips, _, width = mine.shape
    blocks = jnp.stack([block_of(place()[1], q, r) for q in range(SQUARE) for r in range(chips // SQUARE)])
    rows = []
    for group in range(2):
        part = jnp.where(place()[0] == group, mine, other)
        part = jnp.zeros_like(part).at[blocks].set(part)
        rows.append(part.transpose(1, 0, 2).reshape(PCAP, chips * width))
    return jnp.dot(projectors, jnp.concatenate(rows), preferred_element_type=jnp.float32).astype(jnp.bfloat16)


def local(band_coeffs, projectors, counts, atom_of, owners, couplings):
    chips = lax.axis_size("pw") // 2
    entries = chips // SQUARE
    width = band_coeffs.shape[1] // chips
    fast = width == LANES and entries == 2
    own_table = couplings[0]
    sibling_table = swap_cores(own_table)
    if fast:
        flipped = load(projectors)

        def partial(parts):
            return project(flipped, band_coeffs, parts)
    else:

        def partial(parts):
            return project_plain(projectors, band_coeffs, parts)

    theirs, ours = partial((3,))
    theirs, sibling_table = lax.optimization_barrier((theirs, sibling_table))
    theirs = swap_cores(theirs)
    pair_theirs, pair_ours = partial((1, 2))
    quarters = choose(owners, own_table, sibling_table, width, ours)
    got = swap_first(send(ours, theirs, quarters, (3,)))
    pair_theirs = swap_cores(pair_theirs)
    low_theirs, low_ours = partial((0,))
    low_theirs = swap_cores(low_theirs)
    got_first = swap_first(send(pair_ours, pair_theirs, quarters, (1, 2)))
    message = forward(pair_ours, pair_theirs, quarters, got)
    got_second = swap_second(message)
    allowed = mask(counts, atom_of, message)

    total, message = fold(low_ours, low_theirs, quarters, [got_first, got_second])
    got = swap_chips(message, SQUARE)
    distance = 2 * SQUARE
    while distance < chips:
        total = add(total, got).astype(jnp.float32)
        body = total[: entries * PCAP].reshape(entries, PCAP, width)
        order = [entry ^ (distance // SQUARE) for entry in range(entries)]
        message = jnp.concatenate([body[jnp.array(order)].reshape(-1, width), total[entries * PCAP :]])
        got = swap_chips(message.astype(jnp.bfloat16), distance)
        distance *= 2

    scaled = couple(allowed, exchange_square(add_copies(total, got)))
    other = swap_cores(scaled)
    if not fast:
        return apply_plain(projectors, scaled, other)
    return finish(projectors, begin(projectors, scaled), other)


def solution(mesh):
    placed = (
        P("pw", "group"),
        P("pw", "group"),
        P("group", None),
        P("group", None),
        P("group"),
        P("pw", "group", None),
    )
    return jax.shard_map(
        local, mesh=mesh, in_specs=placed, out_specs=P("pw", "group"), check_vma=False
    )
```

```python
import jax
import jax.numpy as jnp
from jax import lax
from jax.experimental import pallas as pl
from jax.experimental.pallas import tpu as pltpu
from jax.sharding import PartitionSpec as P

CHANNELS = 4
CH_CAP = 64
PCAP = 256
LANES = 128
SQUARE = 4
QUARTER = PCAP // SQUARE
ROW_BLOCK = 512
ROW_BLOCKS = (512, 512, 512, 256, 256)
COPY_ROWS = 128
PARAMS = pltpu.CompilerParams(vmem_limit_bytes=40 * 1024 * 1024)
VMEM = pl.BlockSpec(memory_space=pltpu.VMEM)
SMEM = pl.BlockSpec(memory_space=pltpu.SMEM)
HBM = pl.BlockSpec(memory_space=pltpu.HBM)
ANY = pl.BlockSpec(memory_space=pl.ANY)


def place():
    me = lax.axis_index("pw")
    return lax.rem(me, 2), lax.div(me, 2)


def block_of(chip, part, entry):
    return chip ^ (part + SQUARE * entry)


def swap(x, distance):
    count = lax.axis_size("pw")
    return lax.ppermute(x, "pw", [(i, i ^ distance) for i in range(count)])


def swap_cores(x):
    return swap(x, 1)


def swap_chips(x, distance):
    return swap(x, 2 * distance)


def swap_first(x):
    count = lax.axis_size("pw")
    return lax.ppermute(x, "pw", [(i, i ^ (4, 2)[i % 2]) for i in range(count)])


def swap_second(x):
    count = lax.axis_size("pw")
    return lax.ppermute(x, "pw", [(i, i ^ (2, 4)[i % 2]) for i in range(count)])


def pair_at(columns, rows, part):
    chip = place()[1]
    starts = [pl.multiple_of(block_of(chip, part, entry) * LANES, LANES) for entry in range(2)]
    return jnp.concatenate([columns[rows, pl.ds(start, LANES)] for start in starts], axis=1)


def keep_sums(ours, theirs, at, sums):
    for entry in range(2):
        lanes = slice(entry * LANES, (entry + 1) * LANES)
        ours[2 * at + entry] = sums[:PCAP, lanes]
        theirs[2 * at + entry] = sums[PCAP:, lanes].astype(theirs.dtype)


def load_kernel(projectors, flipped, slots, sems):
    core = place()[0]
    count = sems.shape[0]
    block = slots.shape[0] // count
    copies = []
    for at in range(count):
        rows = slice(at * block, (at + 1) * block)
        copies.append(pltpu.make_async_copy(projectors.at[rows], slots.at[rows], sems.at[at]))
        copies[-1].start()
    for at, copy in enumerate(copies):
        copy.wait()
        rows = slice(at * block, (at + 1) * block)
        for side, group in enumerate((core, 1 - core)):
            start = pl.multiple_of(group * PCAP, PCAP)
            flipped[side * PCAP : (side + 1) * PCAP, rows] = slots[rows, pl.ds(start, PCAP)].T


def load(projectors):
    depth, slots = projectors.shape
    return pl.pallas_call(
        load_kernel,
        in_specs=[HBM],
        out_specs=VMEM,
        out_shape=jax.ShapeDtypeStruct((slots, depth), jnp.bfloat16),
        scratch_shapes=[pltpu.VMEM((depth, slots), jnp.bfloat16), pltpu.SemaphoreType.DMA((4,))],
        compiler_params=PARAMS,
        name="load",
    )(pltpu.with_memory_space_constraint(projectors, pltpu.HBM))


def project_kernel(parts, flipped, columns, theirs, ours):
    rows = slice(0, columns.shape[0])
    for at, part in enumerate(parts):
        sums = jnp.dot(flipped[...], pair_at(columns, rows, part), preferred_element_type=jnp.float32)
        keep_sums(ours, theirs, at, sums)


def project(flipped, band_coeffs, parts):
    slots, depth = flipped.shape
    shape = (2 * len(parts), PCAP, LANES)

    def kernel(*refs):
        project_kernel(parts, *refs)

    return pl.pallas_call(
        kernel,
        in_specs=[VMEM, VMEM],
        out_specs=[VMEM, VMEM],
        out_shape=[jax.ShapeDtypeStruct(shape, jnp.bfloat16), jax.ShapeDtypeStruct(shape, jnp.float32)],
        compiler_params=PARAMS,
        cost_estimate=pl.CostEstimate(
            flops=4 * depth * slots * len(parts) * LANES, bytes_accessed=2 * depth * slots, transcendentals=0
        ),
        name="project",
    )(flipped, pltpu.with_memory_space_constraint(band_coeffs, pltpu.VMEM))


def project_plain(projectors, band_coeffs, parts):
    depth, bands = band_coeffs.shape
    chips = lax.axis_size("pw") // 2
    blocks = jnp.stack([block_of(place()[1], q, r) for q in parts for r in range(chips // SQUARE)])
    columns = jnp.take(band_coeffs.reshape(depth, chips, bands // chips), blocks, axis=1)
    outs = []
    core = place()[0]
    for group, dtype in ((1 - core, jnp.bfloat16), (core, jnp.float32)):
        slots = lax.dynamic_slice_in_dim(projectors, group * PCAP, PCAP, 1)
        sums = jnp.einsum("ds,dhw->hsw", slots, columns, preferred_element_type=jnp.float32)
        outs.append(sums.astype(dtype))
    return outs


def choose_kernel(owners, own, sibling, after, out):
    del after
    core, chip = place()
    me = 2 * chip + core
    owner = jnp.where(core == 0, owners[0:1, :], owners[1:2, :])
    width = out.shape[2]
    for part in range(SQUARE):
        rows = pl.ds(pl.multiple_of(((chip & 3) ^ part) * QUARTER, QUARTER), QUARTER)
        piece = jnp.where(owner == me, own[rows], jnp.where(owner == (me ^ 1), sibling[rows], 0.0))
        for cut in range(PCAP // width):
            out[part, cut * QUARTER : (cut + 1) * QUARTER] = piece[:, cut * width : (cut + 1) * width].astype(
                out.dtype
            )


def choose(owners, own, sibling, width, after):
    return pl.pallas_call(
        choose_kernel,
        in_specs=[VMEM, VMEM, VMEM, ANY],
        out_specs=VMEM,
        out_shape=jax.ShapeDtypeStruct((SQUARE, QUARTER * PCAP // width, width), jnp.bfloat16),
        compiler_params=PARAMS,
        name="choose",
    )(jnp.broadcast_to(owners[:, None], (owners.shape[0], PCAP)), own, sibling, after)


def send_kernel(first, second, ours, theirs, quarters, message):
    entries = ours.shape[0] // (1 if first == second else 2)
    core = place()[0]
    start, part = (0, first) if first == second else ((1 - core) * entries, 2 - core)
    for entry in range(entries):
        total = ours[start + entry] + theirs[start + entry].astype(jnp.float32)
        message[entry * PCAP : (entry + 1) * PCAP] = total.astype(message.dtype)
    message[entries * PCAP :] = quarters[part]


def send(ours, theirs, quarters, parts):
    count, _, width = ours.shape
    rows = count // len(parts) * PCAP + quarters.shape[1]

    def kernel(*refs):
        send_kernel(parts[0], parts[-1], *refs)

    return pl.pallas_call(
        kernel,
        in_specs=[VMEM] * 3,
        out_specs=VMEM,
        out_shape=jax.ShapeDtypeStruct((rows, width), jnp.bfloat16),
        compiler_params=PARAMS,
        name="send",
    )(ours, theirs, quarters)


def forward_kernel(ours, theirs, quarters, got, message):
    core = place()[0]
    entries = ours.shape[0] // 2
    start = core * entries
    for entry in range(entries):
        rows = slice(entry * PCAP, (entry + 1) * PCAP)
        total = ours[start + entry] + theirs[start + entry].astype(jnp.float32)
        message[rows] = (total + got[rows].astype(jnp.float32)).astype(message.dtype)
    message[entries * PCAP :] = quarters[1 + core] + got[entries * PCAP :]


def forward(ours, theirs, quarters, got):
    return pl.pallas_call(
        forward_kernel,
        in_specs=[VMEM] * 4,
        out_specs=VMEM,
        out_shape=jax.ShapeDtypeStruct(got.shape, got.dtype),
        compiler_params=PARAMS,
        name="forward",
    )(ours, theirs, quarters, got)


def fold_kernel(ours, theirs, quarters, *refs):
    *gots, kept, message = refs
    entries = ours.shape[0]
    for entry in range(entries):
        rows = slice(entry * PCAP, (entry + 1) * PCAP)
        total = ours[entry] + theirs[entry].astype(jnp.float32)
        for got in gots:
            total = total + got[rows].astype(jnp.float32)
        kept[rows] = total
        away = entry ^ 1
        message[away * PCAP : (away + 1) * PCAP] = total.astype(message.dtype)
    table = quarters[0]
    for got in gots:
        table = table + got[entries * PCAP :]
    kept[entries * PCAP :] = table.astype(kept.dtype)
    message[entries * PCAP :] = table


def fold(ours, theirs, quarters, gots):
    shape = gots[0].shape
    return pl.pallas_call(
        fold_kernel,
        in_specs=[VMEM] * (3 + len(gots)),
        out_specs=[VMEM, VMEM],
        out_shape=[jax.ShapeDtypeStruct(shape, jnp.float32), jax.ShapeDtypeStruct(shape, jnp.bfloat16)],
        compiler_params=PARAMS,
        name="fold",
    )(ours, theirs, quarters, *gots)


def add_kernel(left, right, out):
    out[...] = (left[...] + right[...].astype(jnp.float32)).astype(out.dtype)


def add(left, right):
    return pl.pallas_call(
        add_kernel,
        in_specs=[VMEM, VMEM],
        out_specs=VMEM,
        out_shape=jax.ShapeDtypeStruct(left.shape, jnp.bfloat16),
        compiler_params=PARAMS,
        name="add",
    )(left, right)


def mask_kernel(counts, atom_of, after, out):
    del after
    core = place()[0]
    slot = lax.broadcasted_iota(jnp.int32, (1, PCAP), 1)
    limit = jnp.zeros((1, PCAP), jnp.int32)
    for channel in range(CHANNELS):
        limit = jnp.where(slot >= channel * CH_CAP, channel * CH_CAP + counts[core, channel], limit)
    atoms = jnp.where(core == 0, atom_of[0:1], atom_of[1:2])
    code = jnp.broadcast_to(jnp.where(slot < limit, atoms, -1), (PCAP, PCAP))
    out[...] = jnp.where((code == code.T) & (code >= 0), 1.0, 0.0).astype(out.dtype)


def mask(counts, atom_of, after):
    return pl.pallas_call(
        mask_kernel,
        in_specs=[SMEM, VMEM, ANY],
        out_specs=VMEM,
        out_shape=jax.ShapeDtypeStruct((PCAP, PCAP), jnp.bfloat16),
        compiler_params=PARAMS,
        name="mask",
    )(counts, atom_of, after)


def couple_kernel(allowed, *refs):
    *messages, out, coupling = refs
    width = out.shape[2]
    entries = out.shape[0] // SQUARE
    core, chip = place()
    corner = chip & 3
    parts = (0, 2 - core, 1 + core, 3)
    for part, message in zip(parts, messages):
        start = pl.multiple_of((corner ^ part) * QUARTER, QUARTER)
        for cut in range(PCAP // width):
            lanes = slice(cut * width, (cut + 1) * width)
            first = entries * PCAP + cut * QUARTER
            coupling[pl.ds(start, QUARTER), lanes] = (
                message[first : first + QUARTER] * allowed[pl.ds(start, QUARTER), lanes]
            )
    for part, message in zip(parts, messages):
        wide = jnp.concatenate([message[e * PCAP : (e + 1) * PCAP] for e in range(entries)], axis=1)
        scaled = jnp.dot(coupling[...], wide, preferred_element_type=jnp.float32).astype(out.dtype)
        for entry in range(entries):
            out[part * entries + entry] = scaled[:, entry * width : (entry + 1) * width]


def couple(allowed, messages):
    rows, width = messages[0].shape
    entries = (rows - QUARTER * PCAP // width) // PCAP
    return pl.pallas_call(
        couple_kernel,
        in_specs=[VMEM] * (1 + SQUARE),
        out_specs=VMEM,
        out_shape=jax.ShapeDtypeStruct((SQUARE * entries, PCAP, width), jnp.bfloat16),
        scratch_shapes=[pltpu.VMEM((PCAP, PCAP), jnp.bfloat16)],
        compiler_params=PARAMS,
        name="couple",
    )(allowed, *messages)


def group_slots(group):
    return pl.ds(pl.multiple_of(group * PCAP, PCAP), PCAP)


def wide_pair(scaled, part):
    return jnp.concatenate([scaled[2 * part], scaled[2 * part + 1]], axis=1)


def begin_kernel(projectors, scaled, out):
    slots = group_slots(place()[0])
    for part in range(SQUARE):
        for block in range(projectors.shape[0] // ROW_BLOCK):
            rows = slice(block * ROW_BLOCK, (block + 1) * ROW_BLOCK)
            out[part, rows] = jnp.dot(
                projectors[rows, slots], wide_pair(scaled, part), preferred_element_type=jnp.float32
            )


def begin(projectors, scaled):
    depth, slots = projectors.shape
    return pl.pallas_call(
        begin_kernel,
        in_specs=[VMEM, VMEM],
        out_specs=VMEM,
        out_shape=jax.ShapeDtypeStruct((SQUARE, depth, 2 * LANES), jnp.float32),
        compiler_params=PARAMS,
        cost_estimate=pl.CostEstimate(
            flops=2 * depth * slots * LANES * SQUARE, bytes_accessed=2 * depth * slots, transcendentals=0
        ),
        name="begin",
    )(projectors, scaled)


def finish_kernel(projectors, begun, other, out, blocks, sems):
    core, chip = place()
    slots = group_slots(1 - core)
    copies = []
    first = 0
    for size in ROW_BLOCKS:
        rows = slice(first, first + size)
        first += size
        for part in range(SQUARE):
            sums = begun[part, rows] + jnp.dot(
                projectors[rows, slots], wide_pair(other, part), preferred_element_type=jnp.float32
            )
            for entry in range(2):
                start = pl.multiple_of(block_of(chip, part, entry) * LANES, LANES)
                lanes = slice(entry * LANES, (entry + 1) * LANES)
                blocks[rows, pl.ds(start, LANES)] = sums[:, lanes].astype(blocks.dtype)
        for start in range(rows.start, rows.stop, COPY_ROWS):
            written = slice(start, start + COPY_ROWS)
            copies.append(pltpu.make_async_copy(blocks.at[written], out.at[written], sems.at[len(copies)]))
            copies[-1].start()
    for copy in copies:
        copy.wait()


def finish(projectors, begun, other):
    depth, slots = projectors.shape
    bands = other.shape[0] * LANES
    return pl.pallas_call(
        finish_kernel,
        in_specs=[VMEM] * 3,
        out_specs=HBM,
        out_shape=jax.ShapeDtypeStruct((depth, bands), jnp.bfloat16),
        scratch_shapes=[
            pltpu.VMEM((depth, bands), jnp.bfloat16),
            pltpu.SemaphoreType.DMA((depth // COPY_ROWS,)),
        ],
        compiler_params=PARAMS,
        cost_estimate=pl.CostEstimate(
            flops=depth * slots * bands, bytes_accessed=2 * depth * (slots + bands), transcendentals=0
        ),
        name="finish",
    )(projectors, begun, other)


def apply_plain(projectors, mine, other):
    chips, _, width = mine.shape
    blocks = jnp.stack([block_of(place()[1], q, r) for q in range(SQUARE) for r in range(chips // SQUARE)])
    rows = []
    for group in range(2):
        part = jnp.where(place()[0] == group, mine, other)
        part = jnp.zeros_like(part).at[blocks].set(part)
        rows.append(part.transpose(1, 0, 2).reshape(PCAP, chips * width))
    return jnp.dot(projectors, jnp.concatenate(rows), preferred_element_type=jnp.float32).astype(jnp.bfloat16)


def local(band_coeffs, projectors, counts, atom_of, owners, couplings):
    chips = lax.axis_size("pw") // 2
    entries = chips // SQUARE
    width = band_coeffs.shape[1] // chips
    fast = width == LANES and entries == 2
    own_table = couplings[0]
    sibling_table = swap_cores(own_table)
    if fast:
        flipped = load(projectors)

        def partial(parts):
            return project(flipped, band_coeffs, parts)
    else:

        def partial(parts):
            return project_plain(projectors, band_coeffs, parts)

    theirs, ours = partial((3,))
    theirs, sibling_table = lax.optimization_barrier((theirs, sibling_table))
    theirs = swap_cores(theirs)
    pair_theirs, pair_ours = partial((1, 2))
    quarters = choose(owners, own_table, sibling_table, width, ours)
    got = swap_first(send(ours, theirs, quarters, (3,)))
    pair_theirs = swap_cores(pair_theirs)
    low_theirs, low_ours = partial((0,))
    low_theirs = swap_cores(low_theirs)
    got_first = swap_first(send(pair_ours, pair_theirs, quarters, (1, 2)))
    message = forward(pair_ours, pair_theirs, quarters, got)
    got_second = swap_second(message)
    allowed = mask(counts, atom_of, message)

    total, message = fold(low_ours, low_theirs, quarters, [got_first, got_second])
    mine = add(total, swap_chips(message, SQUARE))
    distance = 2 * SQUARE
    while distance < chips:
        body = mine[: entries * PCAP].reshape(entries, PCAP, width)
        order = [entry ^ (distance // SQUARE) for entry in range(entries)]
        message = jnp.concatenate([body[jnp.array(order)].reshape(-1, width), mine[entries * PCAP :]])
        mine = add(mine.astype(jnp.float32), swap_chips(message, distance))
        distance *= 2

    scaled = couple(allowed, [mine, swap_first(mine), swap_second(mine), swap_chips(mine, 3)])
    other = swap_cores(scaled)
    if not fast:
        return apply_plain(projectors, scaled, other)
    return finish(projectors, begin(projectors, scaled), other)


def solution(mesh):
    placed = (
        P("pw", "group"),
        P("pw", "group"),
        P("group", None),
        P("group", None),
        P("group"),
        P("pw", "group", None),
    )
    return jax.shard_map(
        local, mesh=mesh, in_specs=placed, out_specs=P("pw", "group"), check_vma=False
    )
```

```python
import jax
import jax.numpy as jnp
from jax import lax
from jax.experimental import pallas as pl
from jax.experimental.pallas import tpu as pltpu
from jax.sharding import PartitionSpec as P

CHANNELS = 4
CH_CAP = 64
PCAP = 256
LANES = 128
SQUARE = 4
QUARTER = PCAP // SQUARE
ROW_BLOCK = 512
ROW_BLOCKS = (512, 512, 512, 256, 256)
COPY_ROWS = 128
PARAMS = pltpu.CompilerParams(vmem_limit_bytes=40 * 1024 * 1024)
VMEM = pl.BlockSpec(memory_space=pltpu.VMEM)
SMEM = pl.BlockSpec(memory_space=pltpu.SMEM)
HBM = pl.BlockSpec(memory_space=pltpu.HBM)
ANY = pl.BlockSpec(memory_space=pl.ANY)


def place():
    me = lax.axis_index("pw")
    return lax.rem(me, 2), lax.div(me, 2)


def block_of(chip, part, entry):
    return chip ^ (part + SQUARE * entry)


def swap(x, distance):
    count = lax.axis_size("pw")
    return lax.ppermute(x, "pw", [(i, i ^ distance) for i in range(count)])


def swap_cores(x):
    return swap(x, 1)


def swap_chips(x, distance):
    return swap(x, 2 * distance)


def swap_first(x):
    count = lax.axis_size("pw")
    return lax.ppermute(x, "pw", [(i, i ^ (4, 2)[i % 2]) for i in range(count)])


def swap_second(x):
    count = lax.axis_size("pw")
    return lax.ppermute(x, "pw", [(i, i ^ (2, 4)[i % 2]) for i in range(count)])


def pair_at(columns, rows, part):
    chip = place()[1]
    starts = [pl.multiple_of(block_of(chip, part, entry) * LANES, LANES) for entry in range(2)]
    return jnp.concatenate([columns[rows, pl.ds(start, LANES)] for start in starts], axis=1)


def keep_sums(ours, theirs, at, sums):
    for entry in range(2):
        lanes = slice(entry * LANES, (entry + 1) * LANES)
        ours[2 * at + entry] = sums[:PCAP, lanes]
        theirs[2 * at + entry] = sums[PCAP:, lanes].astype(theirs.dtype)


def load_kernel(projectors, flipped, slots, sems):
    core = place()[0]
    count = sems.shape[0]
    block = slots.shape[0] // count
    copies = []
    for at in range(count):
        rows = slice(at * block, (at + 1) * block)
        copies.append(pltpu.make_async_copy(projectors.at[rows], slots.at[rows], sems.at[at]))
        copies[-1].start(priority=at % 2)
    for at, copy in enumerate(copies):
        copy.wait()
        rows = slice(at * block, (at + 1) * block)
        for side, group in enumerate((core, 1 - core)):
            start = pl.multiple_of(group * PCAP, PCAP)
            flipped[side * PCAP : (side + 1) * PCAP, rows] = slots[rows, pl.ds(start, PCAP)].T


def load(projectors):
    depth, slots = projectors.shape
    return pl.pallas_call(
        load_kernel,
        in_specs=[HBM],
        out_specs=VMEM,
        out_shape=jax.ShapeDtypeStruct((slots, depth), jnp.bfloat16),
        scratch_shapes=[pltpu.VMEM((depth, slots), jnp.bfloat16), pltpu.SemaphoreType.DMA((4,))],
        compiler_params=PARAMS,
        name="load",
    )(pltpu.with_memory_space_constraint(projectors, pltpu.HBM))


def project_kernel(parts, flipped, columns, theirs, ours):
    rows = slice(0, columns.shape[0])
    for at, part in enumerate(parts):
        sums = jnp.dot(flipped[...], pair_at(columns, rows, part), preferred_element_type=jnp.float32)
        keep_sums(ours, theirs, at, sums)


def project(flipped, band_coeffs, parts):
    slots, depth = flipped.shape
    shape = (2 * len(parts), PCAP, LANES)

    def kernel(*refs):
        project_kernel(parts, *refs)

    return pl.pallas_call(
        kernel,
        in_specs=[VMEM, VMEM],
        out_specs=[VMEM, VMEM],
        out_shape=[jax.ShapeDtypeStruct(shape, jnp.bfloat16), jax.ShapeDtypeStruct(shape, jnp.float32)],
        compiler_params=PARAMS,
        cost_estimate=pl.CostEstimate(
            flops=4 * depth * slots * len(parts) * LANES, bytes_accessed=2 * depth * slots, transcendentals=0
        ),
        name="project",
    )(flipped, pltpu.with_memory_space_constraint(band_coeffs, pltpu.VMEM))


def project_plain(projectors, band_coeffs, parts):
    depth, bands = band_coeffs.shape
    chips = lax.axis_size("pw") // 2
    blocks = jnp.stack([block_of(place()[1], q, r) for q in parts for r in range(chips // SQUARE)])
    columns = jnp.take(band_coeffs.reshape(depth, chips, bands // chips), blocks, axis=1)
    outs = []
    core = place()[0]
    for group, dtype in ((1 - core, jnp.bfloat16), (core, jnp.float32)):
        slots = lax.dynamic_slice_in_dim(projectors, group * PCAP, PCAP, 1)
        sums = jnp.einsum("ds,dhw->hsw", slots, columns, preferred_element_type=jnp.float32)
        outs.append(sums.astype(dtype))
    return outs


def choose_kernel(owners, own, sibling, after, out):
    del after
    core, chip = place()
    me = 2 * chip + core
    owner = jnp.where(core == 0, owners[0:1, :], owners[1:2, :])
    width = out.shape[2]
    for part in range(SQUARE):
        rows = pl.ds(pl.multiple_of(((chip & 3) ^ part) * QUARTER, QUARTER), QUARTER)
        piece = jnp.where(owner == me, own[rows], jnp.where(owner == (me ^ 1), sibling[rows], 0.0))
        for cut in range(PCAP // width):
            out[part, cut * QUARTER : (cut + 1) * QUARTER] = piece[:, cut * width : (cut + 1) * width].astype(
                out.dtype
            )


def choose(owners, own, sibling, width, after):
    return pl.pallas_call(
        choose_kernel,
        in_specs=[VMEM, VMEM, VMEM, ANY],
        out_specs=VMEM,
        out_shape=jax.ShapeDtypeStruct((SQUARE, QUARTER * PCAP // width, width), jnp.bfloat16),
        compiler_params=PARAMS,
        name="choose",
    )(jnp.broadcast_to(owners[:, None], (owners.shape[0], PCAP)), own, sibling, after)


def send_kernel(first, second, ours, theirs, quarters, message):
    entries = ours.shape[0] // (1 if first == second else 2)
    core = place()[0]
    start, part = (0, first) if first == second else ((1 - core) * entries, 2 - core)
    for entry in range(entries):
        total = ours[start + entry] + theirs[start + entry].astype(jnp.float32)
        message[entry * PCAP : (entry + 1) * PCAP] = total.astype(message.dtype)
    message[entries * PCAP :] = quarters[part]


def send(ours, theirs, quarters, parts):
    count, _, width = ours.shape
    rows = count // len(parts) * PCAP + quarters.shape[1]

    def kernel(*refs):
        send_kernel(parts[0], parts[-1], *refs)

    return pl.pallas_call(
        kernel,
        in_specs=[VMEM] * 3,
        out_specs=VMEM,
        out_shape=jax.ShapeDtypeStruct((rows, width), jnp.bfloat16),
        compiler_params=PARAMS,
        name="send",
    )(ours, theirs, quarters)


def forward_kernel(ours, theirs, quarters, got, message):
    core = place()[0]
    entries = ours.shape[0] // 2
    start = core * entries
    for entry in range(entries):
        rows = slice(entry * PCAP, (entry + 1) * PCAP)
        total = ours[start + entry] + theirs[start + entry].astype(jnp.float32)
        message[rows] = (total + got[rows].astype(jnp.float32)).astype(message.dtype)
    message[entries * PCAP :] = quarters[1 + core] + got[entries * PCAP :]


def forward(ours, theirs, quarters, got):
    return pl.pallas_call(
        forward_kernel,
        in_specs=[VMEM] * 4,
        out_specs=VMEM,
        out_shape=jax.ShapeDtypeStruct(got.shape, got.dtype),
        compiler_params=PARAMS,
        name="forward",
    )(ours, theirs, quarters, got)


def fold_kernel(ours, theirs, quarters, *refs):
    *gots, kept, message = refs
    entries = ours.shape[0]
    for entry in range(entries):
        rows = slice(entry * PCAP, (entry + 1) * PCAP)
        total = ours[entry] + theirs[entry].astype(jnp.float32)
        for got in gots:
            total = total + got[rows].astype(jnp.float32)
        kept[rows] = total
        away = entry ^ 1
        message[away * PCAP : (away + 1) * PCAP] = total.astype(message.dtype)
    table = quarters[0]
    for got in gots:
        table = table + got[entries * PCAP :]
    kept[entries * PCAP :] = table.astype(kept.dtype)
    message[entries * PCAP :] = table


def fold(ours, theirs, quarters, gots):
    shape = gots[0].shape
    return pl.pallas_call(
        fold_kernel,
        in_specs=[VMEM] * (3 + len(gots)),
        out_specs=[VMEM, VMEM],
        out_shape=[jax.ShapeDtypeStruct(shape, jnp.float32), jax.ShapeDtypeStruct(shape, jnp.bfloat16)],
        compiler_params=PARAMS,
        name="fold",
    )(ours, theirs, quarters, *gots)


def add_kernel(left, right, out):
    out[...] = (left[...] + right[...].astype(jnp.float32)).astype(out.dtype)


def add(left, right):
    return pl.pallas_call(
        add_kernel,
        in_specs=[VMEM, VMEM],
        out_specs=VMEM,
        out_shape=jax.ShapeDtypeStruct(left.shape, jnp.bfloat16),
        compiler_params=PARAMS,
        name="add",
    )(left, right)


def mask_kernel(counts, atom_of, after, out):
    del after
    core = place()[0]
    slot = lax.broadcasted_iota(jnp.int32, (1, PCAP), 1)
    limit = jnp.zeros((1, PCAP), jnp.int32)
    for channel in range(CHANNELS):
        limit = jnp.where(slot >= channel * CH_CAP, channel * CH_CAP + counts[core, channel], limit)
    atoms = jnp.where(core == 0, atom_of[0:1], atom_of[1:2])
    code = jnp.broadcast_to(jnp.where(slot < limit, atoms, -1), (PCAP, PCAP))
    out[...] = jnp.where((code == code.T) & (code >= 0), 1.0, 0.0).astype(out.dtype)


def mask(counts, atom_of, after):
    return pl.pallas_call(
        mask_kernel,
        in_specs=[SMEM, VMEM, ANY],
        out_specs=VMEM,
        out_shape=jax.ShapeDtypeStruct((PCAP, PCAP), jnp.bfloat16),
        compiler_params=PARAMS,
        name="mask",
    )(counts, atom_of, after)


def couple_kernel(allowed, *refs):
    *messages, out, coupling = refs
    width = out.shape[2]
    entries = out.shape[0] // SQUARE
    core, chip = place()
    corner = chip & 3
    parts = (0, 2 - core, 1 + core, 3)
    for part, message in zip(parts, messages):
        start = pl.multiple_of((corner ^ part) * QUARTER, QUARTER)
        for cut in range(PCAP // width):
            lanes = slice(cut * width, (cut + 1) * width)
            first = entries * PCAP + cut * QUARTER
            coupling[pl.ds(start, QUARTER), lanes] = (
                message[first : first + QUARTER] * allowed[pl.ds(start, QUARTER), lanes]
            )
    for part, message in zip(parts, messages):
        wide = jnp.concatenate([message[e * PCAP : (e + 1) * PCAP] for e in range(entries)], axis=1)
        scaled = jnp.dot(coupling[...], wide, preferred_element_type=jnp.float32).astype(out.dtype)
        for entry in range(entries):
            out[part * entries + entry] = scaled[:, entry * width : (entry + 1) * width]


def couple(allowed, messages):
    rows, width = messages[0].shape
    entries = (rows - QUARTER * PCAP // width) // PCAP
    return pl.pallas_call(
        couple_kernel,
        in_specs=[VMEM] * (1 + SQUARE),
        out_specs=VMEM,
        out_shape=jax.ShapeDtypeStruct((SQUARE * entries, PCAP, width), jnp.bfloat16),
        scratch_shapes=[pltpu.VMEM((PCAP, PCAP), jnp.bfloat16)],
        compiler_params=PARAMS,
        name="couple",
    )(allowed, *messages)


def group_slots(group):
    return pl.ds(pl.multiple_of(group * PCAP, PCAP), PCAP)


def wide_pair(scaled, part):
    return jnp.concatenate([scaled[2 * part], scaled[2 * part + 1]], axis=1)


def begin_kernel(projectors, scaled, out):
    slots = group_slots(place()[0])
    for part in range(SQUARE):
        for block in range(projectors.shape[0] // ROW_BLOCK):
            rows = slice(block * ROW_BLOCK, (block + 1) * ROW_BLOCK)
            out[part, rows] = jnp.dot(
                projectors[rows, slots], wide_pair(scaled, part), preferred_element_type=jnp.float32
            )


def begin(projectors, scaled):
    depth, slots = projectors.shape
    return pl.pallas_call(
        begin_kernel,
        in_specs=[VMEM, VMEM],
        out_specs=VMEM,
        out_shape=jax.ShapeDtypeStruct((SQUARE, depth, 2 * LANES), jnp.float32),
        compiler_params=PARAMS,
        cost_estimate=pl.CostEstimate(
            flops=2 * depth * slots * LANES * SQUARE, bytes_accessed=2 * depth * slots, transcendentals=0
        ),
        name="begin",
    )(projectors, scaled)


def finish_kernel(projectors, begun, other, out, blocks, sems):
    core, chip = place()
    slots = group_slots(1 - core)
    copies = []
    first = 0
    for size in ROW_BLOCKS:
        rows = slice(first, first + size)
        first += size
        for part in range(SQUARE):
            sums = begun[part, rows] + jnp.dot(
                projectors[rows, slots], wide_pair(other, part), preferred_element_type=jnp.float32
            )
            for entry in range(2):
                start = pl.multiple_of(block_of(chip, part, entry) * LANES, LANES)
                lanes = slice(entry * LANES, (entry + 1) * LANES)
                blocks[rows, pl.ds(start, LANES)] = sums[:, lanes].astype(blocks.dtype)
        for start in range(rows.start, rows.stop, COPY_ROWS):
            written = slice(start, start + COPY_ROWS)
            copies.append(pltpu.make_async_copy(blocks.at[written], out.at[written], sems.at[len(copies)]))
            copies[-1].start(priority=len(copies) % 2)
    for copy in copies:
        copy.wait()


def finish(projectors, begun, other):
    depth, slots = projectors.shape
    bands = other.shape[0] * LANES
    return pl.pallas_call(
        finish_kernel,
        in_specs=[VMEM] * 3,
        out_specs=HBM,
        out_shape=jax.ShapeDtypeStruct((depth, bands), jnp.bfloat16),
        scratch_shapes=[
            pltpu.VMEM((depth, bands), jnp.bfloat16),
            pltpu.SemaphoreType.DMA((depth // COPY_ROWS,)),
        ],
        compiler_params=PARAMS,
        cost_estimate=pl.CostEstimate(
            flops=depth * slots * bands, bytes_accessed=2 * depth * (slots + bands), transcendentals=0
        ),
        name="finish",
    )(projectors, begun, other)


def apply_plain(projectors, mine, other):
    chips, _, width = mine.shape
    blocks = jnp.stack([block_of(place()[1], q, r) for q in range(SQUARE) for r in range(chips // SQUARE)])
    rows = []
    for group in range(2):
        part = jnp.where(place()[0] == group, mine, other)
        part = jnp.zeros_like(part).at[blocks].set(part)
        rows.append(part.transpose(1, 0, 2).reshape(PCAP, chips * width))
    return jnp.dot(projectors, jnp.concatenate(rows), preferred_element_type=jnp.float32).astype(jnp.bfloat16)


def local(band_coeffs, projectors, counts, atom_of, owners, couplings):
    chips = lax.axis_size("pw") // 2
    entries = chips // SQUARE
    width = band_coeffs.shape[1] // chips
    fast = width == LANES and entries == 2
    own_table = couplings[0]
    sibling_table = swap_cores(own_table)
    if fast:
        flipped = load(projectors)

        def partial(parts):
            return project(flipped, band_coeffs, parts)
    else:

        def partial(parts):
            return project_plain(projectors, band_coeffs, parts)

    theirs, ours = partial((3,))
    theirs, sibling_table = lax.optimization_barrier((theirs, sibling_table))
    theirs = swap_cores(theirs)
    pair_theirs, pair_ours = partial((1, 2))
    quarters = choose(owners, own_table, sibling_table, width, ours)
    got = swap_first(send(ours, theirs, quarters, (3,)))
    pair_theirs = swap_cores(pair_theirs)
    low_theirs, low_ours = partial((0,))
    low_theirs = swap_cores(low_theirs)
    got_first = swap_first(send(pair_ours, pair_theirs, quarters, (1, 2)))
    message = forward(pair_ours, pair_theirs, quarters, got)
    got_second = swap_second(message)
    allowed = mask(counts, atom_of, message)

    total, message = fold(low_ours, low_theirs, quarters, [got_first, got_second])
    mine = add(total, swap_chips(message, SQUARE))
    distance = 2 * SQUARE
    while distance < chips:
        body = mine[: entries * PCAP].reshape(entries, PCAP, width)
        order = [entry ^ (distance // SQUARE) for entry in range(entries)]
        message = jnp.concatenate([body[jnp.array(order)].reshape(-1, width), mine[entries * PCAP :]])
        mine = add(mine.astype(jnp.float32), swap_chips(message, distance))
        distance *= 2

    scaled = couple(allowed, [mine, swap_first(mine), swap_second(mine), swap_chips(mine, 3)])
    other = swap_cores(scaled)
    if not fast:
        return apply_plain(projectors, scaled, other)
    return finish(projectors, begin(projectors, scaled), other)


def solution(mesh):
    placed = (
        P("pw", "group"),
        P("pw", "group"),
        P("group", None),
        P("group", None),
        P("group"),
        P("pw", "group", None),
    )
    return jax.shard_map(
        local, mesh=mesh, in_specs=placed, out_specs=P("pw", "group"), check_vma=False
    )
```

```python
import jax
import jax.numpy as jnp
from jax import lax
from jax.experimental import pallas as pl
from jax.experimental.pallas import tpu as pltpu
from jax.sharding import PartitionSpec as P

CHANNELS = 4
CH_CAP = 64
PCAP = 256
LANES = 128
SQUARE = 4
QUARTER = PCAP // SQUARE
ROW_BLOCK = 512
ROW_BLOCKS = (512, 512, 512, 256, 256)
COPY_ROWS = 128
PARAMS = pltpu.CompilerParams(vmem_limit_bytes=40 * 1024 * 1024)
VMEM = pl.BlockSpec(memory_space=pltpu.VMEM)
SMEM = pl.BlockSpec(memory_space=pltpu.SMEM)
HBM = pl.BlockSpec(memory_space=pltpu.HBM)
ANY = pl.BlockSpec(memory_space=pl.ANY)


def place():
    me = lax.axis_index("pw")
    return lax.rem(me, 2), lax.div(me, 2)


def block_of(chip, part, entry):
    return chip ^ (part + SQUARE * entry)


def swap(x, distance):
    count = lax.axis_size("pw")
    return lax.ppermute(x, "pw", [(i, i ^ distance) for i in range(count)])


def swap_cores(x):
    return swap(x, 1)


def swap_chips(x, distance):
    return swap(x, 2 * distance)


def swap_first(x):
    count = lax.axis_size("pw")
    return lax.ppermute(x, "pw", [(i, i ^ (4, 2)[i % 2]) for i in range(count)])


def swap_second(x):
    count = lax.axis_size("pw")
    return lax.ppermute(x, "pw", [(i, i ^ (2, 4)[i % 2]) for i in range(count)])


def pair_at(columns, rows, part):
    chip = place()[1]
    starts = [pl.multiple_of(block_of(chip, part, entry) * LANES, LANES) for entry in range(2)]
    return jnp.concatenate([columns[rows, pl.ds(start, LANES)] for start in starts], axis=1)


def keep_sums(ours, theirs, at, sums):
    for entry in range(2):
        lanes = slice(entry * LANES, (entry + 1) * LANES)
        ours[2 * at + entry] = sums[:PCAP, lanes]
        theirs[2 * at + entry] = sums[PCAP:, lanes].astype(theirs.dtype)


def load_kernel(projectors, flipped, slots, sems):
    core = place()[0]
    count = sems.shape[0]
    block = slots.shape[0] // count
    copies = []
    for at in range(count):
        rows = slice(at * block, (at + 1) * block)
        copies.append(pltpu.make_async_copy(projectors.at[rows], slots.at[rows], sems.at[at]))
        copies[-1].start(priority=at % 2)
    for at, copy in enumerate(copies):
        copy.wait()
        rows = slice(at * block, (at + 1) * block)
        for side, group in enumerate((core, 1 - core)):
            start = pl.multiple_of(group * PCAP, PCAP)
            flipped[side * PCAP : (side + 1) * PCAP, rows] = slots[rows, pl.ds(start, PCAP)].T


def load(projectors):
    depth, slots = projectors.shape
    return pl.pallas_call(
        load_kernel,
        in_specs=[HBM],
        out_specs=VMEM,
        out_shape=jax.ShapeDtypeStruct((slots, depth), jnp.bfloat16),
        scratch_shapes=[pltpu.VMEM((depth, slots), jnp.bfloat16), pltpu.SemaphoreType.DMA((4,))],
        compiler_params=PARAMS,
        name="load",
    )(pltpu.with_memory_space_constraint(projectors, pltpu.HBM))


def project_kernel(parts, flipped, columns, theirs, ours):
    rows = slice(0, columns.shape[0])
    for at, part in enumerate(parts):
        sums = jnp.dot(flipped[...], pair_at(columns, rows, part), preferred_element_type=jnp.float32)
        keep_sums(ours, theirs, at, sums)


def project(flipped, band_coeffs, parts):
    slots, depth = flipped.shape
    shape = (2 * len(parts), PCAP, LANES)

    def kernel(*refs):
        project_kernel(parts, *refs)

    return pl.pallas_call(
        kernel,
        in_specs=[VMEM, VMEM],
        out_specs=[VMEM, VMEM],
        out_shape=[jax.ShapeDtypeStruct(shape, jnp.bfloat16), jax.ShapeDtypeStruct(shape, jnp.float32)],
        compiler_params=PARAMS,
        cost_estimate=pl.CostEstimate(
            flops=4 * depth * slots * len(parts) * LANES, bytes_accessed=2 * depth * slots, transcendentals=0
        ),
        name="project",
    )(flipped, pltpu.with_memory_space_constraint(band_coeffs, pltpu.VMEM))


def project_plain(projectors, band_coeffs, parts):
    depth, bands = band_coeffs.shape
    chips = lax.axis_size("pw") // 2
    blocks = jnp.stack([block_of(place()[1], q, r) for q in parts for r in range(chips // SQUARE)])
    columns = jnp.take(band_coeffs.reshape(depth, chips, bands // chips), blocks, axis=1)
    outs = []
    core = place()[0]
    for group, dtype in ((1 - core, jnp.bfloat16), (core, jnp.float32)):
        slots = lax.dynamic_slice_in_dim(projectors, group * PCAP, PCAP, 1)
        sums = jnp.einsum("ds,dhw->hsw", slots, columns, preferred_element_type=jnp.float32)
        outs.append(sums.astype(dtype))
    return outs


def choose_kernel(owners, own, sibling, after, out):
    del after
    core, chip = place()
    me = 2 * chip + core
    owner = jnp.where(core == 0, owners[0:1, :], owners[1:2, :])
    width = out.shape[2]
    for part in range(SQUARE):
        rows = pl.ds(pl.multiple_of(((chip & 3) ^ part) * QUARTER, QUARTER), QUARTER)
        piece = jnp.where(owner == me, own[rows], jnp.where(owner == (me ^ 1), sibling[rows], 0.0))
        for cut in range(PCAP // width):
            out[part, cut * QUARTER : (cut + 1) * QUARTER] = piece[:, cut * width : (cut + 1) * width].astype(
                out.dtype
            )


def choose(owners, own, sibling, width, after):
    return pl.pallas_call(
        choose_kernel,
        in_specs=[VMEM, VMEM, VMEM, ANY],
        out_specs=VMEM,
        out_shape=jax.ShapeDtypeStruct((SQUARE, QUARTER * PCAP // width, width), jnp.bfloat16),
        compiler_params=PARAMS,
        name="choose",
    )(jnp.broadcast_to(owners[:, None], (owners.shape[0], PCAP)), own, sibling, after)


def send_kernel(first, second, ours, theirs, quarters, message):
    entries = ours.shape[0] // (1 if first == second else 2)
    core = place()[0]
    start, part = (0, first) if first == second else ((1 - core) * entries, 2 - core)
    for entry in range(entries):
        total = ours[start + entry] + theirs[start + entry].astype(jnp.float32)
        message[entry * PCAP : (entry + 1) * PCAP] = total.astype(message.dtype)
    message[entries * PCAP :] = quarters[part]


def send(ours, theirs, quarters, parts):
    count, _, width = ours.shape
    rows = count // len(parts) * PCAP + quarters.shape[1]

    def kernel(*refs):
        send_kernel(parts[0], parts[-1], *refs)

    return pl.pallas_call(
        kernel,
        in_specs=[VMEM] * 3,
        out_specs=VMEM,
        out_shape=jax.ShapeDtypeStruct((rows, width), jnp.bfloat16),
        compiler_params=PARAMS,
        name="send",
    )(ours, theirs, quarters)


def forward_kernel(ours, theirs, quarters, got, *messages):
    core = place()[0]
    entries = ours.shape[0] // 2
    half = entries // 2
    start = core * entries
    for entry in range(entries):
        rows = slice(entry * PCAP, (entry + 1) * PCAP)
        total = ours[start + entry] + theirs[start + entry].astype(jnp.float32)
        total = (total + got[rows].astype(jnp.float32)).astype(got.dtype)
        at = entry % half
        messages[entry // half][at * PCAP : (at + 1) * PCAP] = total
    messages[1][half * PCAP :] = quarters[1 + core] + got[entries * PCAP :]


def forward(ours, theirs, quarters, got):
    rows, width = got.shape
    half = ours.shape[0] // 4 * PCAP
    return pl.pallas_call(
        forward_kernel,
        in_specs=[VMEM] * 4,
        out_specs=[VMEM] * 2,
        out_shape=[
            jax.ShapeDtypeStruct((half, width), got.dtype),
            jax.ShapeDtypeStruct((rows - half, width), got.dtype),
        ],
        compiler_params=PARAMS,
        name="forward",
    )(ours, theirs, quarters, got)


def fold_kernel(ours, theirs, quarters, first, second, third, kept, message):
    entries = ours.shape[0]
    half = entries // 2
    for entry in range(entries):
        rows = slice(entry * PCAP, (entry + 1) * PCAP)
        total = ours[entry] + theirs[entry].astype(jnp.float32) + first[rows].astype(jnp.float32)
        at = entry % half
        got = (second, third)[entry // half][at * PCAP : (at + 1) * PCAP]
        total = total + got.astype(jnp.float32)
        kept[rows] = total
        away = entry ^ 1
        message[away * PCAP : (away + 1) * PCAP] = total.astype(message.dtype)
    table = quarters[0] + first[entries * PCAP :] + third[half * PCAP :]
    kept[entries * PCAP :] = table.astype(kept.dtype)
    message[entries * PCAP :] = table


def fold(ours, theirs, quarters, gots):
    shape = gots[0].shape
    return pl.pallas_call(
        fold_kernel,
        in_specs=[VMEM] * (3 + len(gots)),
        out_specs=[VMEM, VMEM],
        out_shape=[jax.ShapeDtypeStruct(shape, jnp.float32), jax.ShapeDtypeStruct(shape, jnp.bfloat16)],
        compiler_params=PARAMS,
        name="fold",
    )(ours, theirs, quarters, *gots)


def add_kernel(left, right, out):
    out[...] = (left[...] + right[...].astype(jnp.float32)).astype(out.dtype)


def add(left, right):
    return pl.pallas_call(
        add_kernel,
        in_specs=[VMEM, VMEM],
        out_specs=VMEM,
        out_shape=jax.ShapeDtypeStruct(left.shape, jnp.bfloat16),
        compiler_params=PARAMS,
        name="add",
    )(left, right)


def mask_kernel(counts, atom_of, after, out):
    del after
    core = place()[0]
    slot = lax.broadcasted_iota(jnp.int32, (1, PCAP), 1)
    limit = jnp.zeros((1, PCAP), jnp.int32)
    for channel in range(CHANNELS):
        limit = jnp.where(slot >= channel * CH_CAP, channel * CH_CAP + counts[core, channel], limit)
    atoms = jnp.where(core == 0, atom_of[0:1], atom_of[1:2])
    code = jnp.broadcast_to(jnp.where(slot < limit, atoms, -1), (PCAP, PCAP))
    out[...] = jnp.where((code == code.T) & (code >= 0), 1.0, 0.0).astype(out.dtype)


def mask(counts, atom_of, after):
    return pl.pallas_call(
        mask_kernel,
        in_specs=[SMEM, VMEM, ANY],
        out_specs=VMEM,
        out_shape=jax.ShapeDtypeStruct((PCAP, PCAP), jnp.bfloat16),
        compiler_params=PARAMS,
        name="mask",
    )(counts, atom_of, after)


def couple_kernel(allowed, *refs):
    *messages, out, coupling = refs
    width = out.shape[2]
    entries = out.shape[0] // SQUARE
    core, chip = place()
    corner = chip & 3
    parts = (0, 2 - core, 1 + core, 3)
    for part, message in zip(parts, messages):
        start = pl.multiple_of((corner ^ part) * QUARTER, QUARTER)
        for cut in range(PCAP // width):
            lanes = slice(cut * width, (cut + 1) * width)
            first = entries * PCAP + cut * QUARTER
            coupling[pl.ds(start, QUARTER), lanes] = (
                message[first : first + QUARTER] * allowed[pl.ds(start, QUARTER), lanes]
            )
    for part, message in zip(parts, messages):
        wide = jnp.concatenate([message[e * PCAP : (e + 1) * PCAP] for e in range(entries)], axis=1)
        scaled = jnp.dot(coupling[...], wide, preferred_element_type=jnp.float32).astype(out.dtype)
        for entry in range(entries):
            out[part * entries + entry] = scaled[:, entry * width : (entry + 1) * width]


def couple(allowed, messages):
    rows, width = messages[0].shape
    entries = (rows - QUARTER * PCAP // width) // PCAP
    return pl.pallas_call(
        couple_kernel,
        in_specs=[VMEM] * (1 + SQUARE),
        out_specs=VMEM,
        out_shape=jax.ShapeDtypeStruct((SQUARE * entries, PCAP, width), jnp.bfloat16),
        scratch_shapes=[pltpu.VMEM((PCAP, PCAP), jnp.bfloat16)],
        compiler_params=PARAMS,
        name="couple",
    )(allowed, *messages)


def group_slots(group):
    return pl.ds(pl.multiple_of(group * PCAP, PCAP), PCAP)


def wide_pair(scaled, part):
    return jnp.concatenate([scaled[2 * part], scaled[2 * part + 1]], axis=1)


def begin_kernel(projectors, scaled, out):
    slots = group_slots(place()[0])
    for part in range(SQUARE):
        for block in range(projectors.shape[0] // ROW_BLOCK):
            rows = slice(block * ROW_BLOCK, (block + 1) * ROW_BLOCK)
            out[part, rows] = jnp.dot(
                projectors[rows, slots], wide_pair(scaled, part), preferred_element_type=jnp.float32
            )


def begin(projectors, scaled):
    depth, slots = projectors.shape
    return pl.pallas_call(
        begin_kernel,
        in_specs=[VMEM, VMEM],
        out_specs=VMEM,
        out_shape=jax.ShapeDtypeStruct((SQUARE, depth, 2 * LANES), jnp.float32),
        compiler_params=PARAMS,
        cost_estimate=pl.CostEstimate(
            flops=2 * depth * slots * LANES * SQUARE, bytes_accessed=2 * depth * slots, transcendentals=0
        ),
        name="begin",
    )(projectors, scaled)


def finish_kernel(projectors, begun, other, out, blocks, sems):
    core, chip = place()
    slots = group_slots(1 - core)
    copies = []
    first = 0
    for size in ROW_BLOCKS:
        rows = slice(first, first + size)
        first += size
        for part in range(SQUARE):
            sums = begun[part, rows] + jnp.dot(
                projectors[rows, slots], wide_pair(other, part), preferred_element_type=jnp.float32
            )
            for entry in range(2):
                start = pl.multiple_of(block_of(chip, part, entry) * LANES, LANES)
                lanes = slice(entry * LANES, (entry + 1) * LANES)
                blocks[rows, pl.ds(start, LANES)] = sums[:, lanes].astype(blocks.dtype)
        for start in range(rows.start, rows.stop, COPY_ROWS):
            written = slice(start, start + COPY_ROWS)
            copies.append(pltpu.make_async_copy(blocks.at[written], out.at[written], sems.at[len(copies)]))
            copies[-1].start(priority=len(copies) % 2)
    for copy in copies:
        copy.wait()


def finish(projectors, begun, other):
    depth, slots = projectors.shape
    bands = other.shape[0] * LANES
    return pl.pallas_call(
        finish_kernel,
        in_specs=[VMEM] * 3,
        out_specs=HBM,
        out_shape=jax.ShapeDtypeStruct((depth, bands), jnp.bfloat16),
        scratch_shapes=[
            pltpu.VMEM((depth, bands), jnp.bfloat16),
            pltpu.SemaphoreType.DMA((depth // COPY_ROWS,)),
        ],
        compiler_params=PARAMS,
        cost_estimate=pl.CostEstimate(
            flops=depth * slots * bands, bytes_accessed=2 * depth * (slots + bands), transcendentals=0
        ),
        name="finish",
    )(projectors, begun, other)


def apply_plain(projectors, mine, other):
    chips, _, width = mine.shape
    blocks = jnp.stack([block_of(place()[1], q, r) for q in range(SQUARE) for r in range(chips // SQUARE)])
    rows = []
    for group in range(2):
        part = jnp.where(place()[0] == group, mine, other)
        part = jnp.zeros_like(part).at[blocks].set(part)
        rows.append(part.transpose(1, 0, 2).reshape(PCAP, chips * width))
    return jnp.dot(projectors, jnp.concatenate(rows), preferred_element_type=jnp.float32).astype(jnp.bfloat16)


def local(band_coeffs, projectors, counts, atom_of, owners, couplings):
    chips = lax.axis_size("pw") // 2
    entries = chips // SQUARE
    width = band_coeffs.shape[1] // chips
    fast = width == LANES and entries == 2
    own_table = couplings[0]
    sibling_table = swap_cores(own_table)
    if fast:
        flipped = load(projectors)

        def partial(parts):
            return project(flipped, band_coeffs, parts)
    else:

        def partial(parts):
            return project_plain(projectors, band_coeffs, parts)

    theirs, ours = partial((3,))
    theirs, sibling_table = lax.optimization_barrier((theirs, sibling_table))
    theirs = swap_cores(theirs)
    pair_theirs, pair_ours = partial((1, 2))
    quarters = choose(owners, own_table, sibling_table, width, ours)
    got = swap_first(send(ours, theirs, quarters, (3,)))
    pair_theirs = swap_cores(pair_theirs)
    low_theirs, low_ours = partial((0,))
    low_theirs = swap_cores(low_theirs)
    got_first = swap_first(send(pair_ours, pair_theirs, quarters, (1, 2)))
    messages = forward(pair_ours, pair_theirs, quarters, got)
    got_second = [swap_second(message) for message in messages]
    allowed = mask(counts, atom_of, messages[0])

    total, message = fold(low_ours, low_theirs, quarters, [got_first] + got_second)
    mine = add(total, swap_chips(message, SQUARE))
    distance = 2 * SQUARE
    while distance < chips:
        body = mine[: entries * PCAP].reshape(entries, PCAP, width)
        order = [entry ^ (distance // SQUARE) for entry in range(entries)]
        message = jnp.concatenate([body[jnp.array(order)].reshape(-1, width), mine[entries * PCAP :]])
        mine = add(mine.astype(jnp.float32), swap_chips(message, distance))
        distance *= 2

    scaled = couple(allowed, [mine, swap_first(mine), swap_second(mine), swap_chips(mine, 3)])
    other = swap_cores(scaled)
    if not fast:
        return apply_plain(projectors, scaled, other)
    return finish(projectors, begin(projectors, scaled), other)


def solution(mesh):
    placed = (
        P("pw", "group"),
        P("pw", "group"),
        P("group", None),
        P("group", None),
        P("group"),
        P("pw", "group", None),
    )
    return jax.shard_map(
        local, mesh=mesh, in_specs=placed, out_specs=P("pw", "group"), check_vma=False
    )
```

```python
import jax
import jax.numpy as jnp
from jax import lax
from jax.experimental import pallas as pl
from jax.experimental.pallas import tpu as pltpu
from jax.sharding import PartitionSpec as P

CHANNELS = 4
CH_CAP = 64
PCAP = 256
LANES = 128
SQUARE = 4
QUARTER = PCAP // SQUARE
ROW_BLOCK = 1024
ROW_BLOCKS = (512, 1024, 256, 256)
COPY_ROWS = 128
PARAMS = pltpu.CompilerParams(vmem_limit_bytes=40 * 1024 * 1024)
VMEM = pl.BlockSpec(memory_space=pltpu.VMEM)
SMEM = pl.BlockSpec(memory_space=pltpu.SMEM)
HBM = pl.BlockSpec(memory_space=pltpu.HBM)
ANY = pl.BlockSpec(memory_space=pl.ANY)


def place():
    me = lax.axis_index("pw")
    return lax.rem(me, 2), lax.div(me, 2)


def block_of(chip, part, entry):
    return chip ^ (part + SQUARE * entry)


def swap(x, distance):
    count = lax.axis_size("pw")
    return lax.ppermute(x, "pw", [(i, i ^ distance) for i in range(count)])


def swap_cores(x):
    return swap(x, 1)


def swap_chips(x, distance):
    return swap(x, 2 * distance)


def swap_first(x):
    count = lax.axis_size("pw")
    return lax.ppermute(x, "pw", [(i, i ^ (4, 2)[i % 2]) for i in range(count)])


def swap_second(x):
    count = lax.axis_size("pw")
    return lax.ppermute(x, "pw", [(i, i ^ (2, 4)[i % 2]) for i in range(count)])


def pair_at(columns, rows, part):
    chip = place()[1]
    starts = [pl.multiple_of(block_of(chip, part, entry) * LANES, LANES) for entry in range(2)]
    return jnp.concatenate([columns[rows, pl.ds(start, LANES)] for start in starts], axis=1)


def keep_sums(ours, theirs, at, sums):
    for entry in range(2):
        lanes = slice(entry * LANES, (entry + 1) * LANES)
        ours[2 * at + entry] = sums[:PCAP, lanes]
        theirs[2 * at + entry] = sums[PCAP:, lanes].astype(theirs.dtype)


def load_kernel(projectors, flipped, slots, sems):
    core = place()[0]
    count = sems.shape[0]
    block = slots.shape[0] // count
    copies = []
    for at in range(count):
        rows = slice(at * block, (at + 1) * block)
        copies.append(pltpu.make_async_copy(projectors.at[rows], slots.at[rows], sems.at[at]))
        copies[-1].start(priority=at % 2)
    for at, copy in enumerate(copies):
        copy.wait()
        rows = slice(at * block, (at + 1) * block)
        for side, group in enumerate((core, 1 - core)):
            start = pl.multiple_of(group * PCAP, PCAP)
            flipped[side * PCAP : (side + 1) * PCAP, rows] = slots[rows, pl.ds(start, PCAP)].T


def load(projectors):
    depth, slots = projectors.shape
    return pl.pallas_call(
        load_kernel,
        in_specs=[HBM],
        out_specs=VMEM,
        out_shape=jax.ShapeDtypeStruct((slots, depth), jnp.bfloat16),
        scratch_shapes=[pltpu.VMEM((depth, slots), jnp.bfloat16), pltpu.SemaphoreType.DMA((4,))],
        compiler_params=PARAMS,
        name="load",
    )(pltpu.with_memory_space_constraint(projectors, pltpu.HBM))


def project_kernel(parts, flipped, columns, theirs, ours):
    rows = slice(0, columns.shape[0])
    for at, part in enumerate(parts):
        sums = jnp.dot(flipped[...], pair_at(columns, rows, part), preferred_element_type=jnp.float32)
        keep_sums(ours, theirs, at, sums)


def project(flipped, band_coeffs, parts):
    slots, depth = flipped.shape
    shape = (2 * len(parts), PCAP, LANES)

    def kernel(*refs):
        project_kernel(parts, *refs)

    return pl.pallas_call(
        kernel,
        in_specs=[VMEM, VMEM],
        out_specs=[VMEM, VMEM],
        out_shape=[jax.ShapeDtypeStruct(shape, jnp.bfloat16), jax.ShapeDtypeStruct(shape, jnp.float32)],
        compiler_params=PARAMS,
        cost_estimate=pl.CostEstimate(
            flops=4 * depth * slots * len(parts) * LANES, bytes_accessed=2 * depth * slots, transcendentals=0
        ),
        name="project",
    )(flipped, pltpu.with_memory_space_constraint(band_coeffs, pltpu.VMEM))


def project_plain(projectors, band_coeffs, parts):
    depth, bands = band_coeffs.shape
    chips = lax.axis_size("pw") // 2
    blocks = jnp.stack([block_of(place()[1], q, r) for q in parts for r in range(chips // SQUARE)])
    columns = jnp.take(band_coeffs.reshape(depth, chips, bands // chips), blocks, axis=1)
    outs = []
    core = place()[0]
    for group, dtype in ((1 - core, jnp.bfloat16), (core, jnp.float32)):
        slots = lax.dynamic_slice_in_dim(projectors, group * PCAP, PCAP, 1)
        sums = jnp.einsum("ds,dhw->hsw", slots, columns, preferred_element_type=jnp.float32)
        outs.append(sums.astype(dtype))
    return outs


def choose_kernel(owners, own, sibling, after, out):
    del after
    core, chip = place()
    me = 2 * chip + core
    owner = jnp.where(core == 0, owners[0:1, :], owners[1:2, :])
    width = out.shape[2]
    for part in range(SQUARE):
        rows = pl.ds(pl.multiple_of(((chip & 3) ^ part) * QUARTER, QUARTER), QUARTER)
        piece = jnp.where(owner == me, own[rows], jnp.where(owner == (me ^ 1), sibling[rows], 0.0))
        for cut in range(PCAP // width):
            out[part, cut * QUARTER : (cut + 1) * QUARTER] = piece[:, cut * width : (cut + 1) * width].astype(
                out.dtype
            )


def choose(owners, own, sibling, width, after):
    return pl.pallas_call(
        choose_kernel,
        in_specs=[VMEM, VMEM, VMEM, ANY],
        out_specs=VMEM,
        out_shape=jax.ShapeDtypeStruct((SQUARE, QUARTER * PCAP // width, width), jnp.bfloat16),
        compiler_params=PARAMS,
        name="choose",
    )(jnp.broadcast_to(owners[:, None], (owners.shape[0], PCAP)), own, sibling, after)


def send_kernel(first, second, ours, theirs, quarters, message):
    entries = ours.shape[0] // (1 if first == second else 2)
    core = place()[0]
    start, part = (0, first) if first == second else ((1 - core) * entries, 2 - core)
    for entry in range(entries):
        total = ours[start + entry] + theirs[start + entry].astype(jnp.float32)
        message[entry * PCAP : (entry + 1) * PCAP] = total.astype(message.dtype)
    message[entries * PCAP :] = quarters[part]


def send(ours, theirs, quarters, parts):
    count, _, width = ours.shape
    rows = count // len(parts) * PCAP + quarters.shape[1]

    def kernel(*refs):
        send_kernel(parts[0], parts[-1], *refs)

    return pl.pallas_call(
        kernel,
        in_specs=[VMEM] * 3,
        out_specs=VMEM,
        out_shape=jax.ShapeDtypeStruct((rows, width), jnp.bfloat16),
        compiler_params=PARAMS,
        name="send",
    )(ours, theirs, quarters)


def forward_kernel(ours, theirs, quarters, got, message):
    core = place()[0]
    entries = ours.shape[0] // 2
    start = core * entries
    for entry in range(entries):
        rows = slice(entry * PCAP, (entry + 1) * PCAP)
        total = ours[start + entry] + theirs[start + entry].astype(jnp.float32)
        message[rows] = (total + got[rows].astype(jnp.float32)).astype(message.dtype)
    message[entries * PCAP :] = quarters[1 + core] + got[entries * PCAP :]


def forward(ours, theirs, quarters, got):
    return pl.pallas_call(
        forward_kernel,
        in_specs=[VMEM] * 4,
        out_specs=VMEM,
        out_shape=jax.ShapeDtypeStruct(got.shape, got.dtype),
        compiler_params=PARAMS,
        name="forward",
    )(ours, theirs, quarters, got)


def fold_kernel(ours, theirs, quarters, *refs):
    *gots, kept, message = refs
    entries = ours.shape[0]
    for entry in range(entries):
        rows = slice(entry * PCAP, (entry + 1) * PCAP)
        total = ours[entry] + theirs[entry].astype(jnp.float32)
        for got in gots:
            total = total + got[rows].astype(jnp.float32)
        kept[rows] = total
        away = entry ^ 1
        message[away * PCAP : (away + 1) * PCAP] = total.astype(message.dtype)
    table = quarters[0]
    for got in gots:
        table = table + got[entries * PCAP :]
    kept[entries * PCAP :] = table.astype(kept.dtype)
    message[entries * PCAP :] = table


def fold(ours, theirs, quarters, gots):
    shape = gots[0].shape
    return pl.pallas_call(
        fold_kernel,
        in_specs=[VMEM] * (3 + len(gots)),
        out_specs=[VMEM, VMEM],
        out_shape=[jax.ShapeDtypeStruct(shape, jnp.float32), jax.ShapeDtypeStruct(shape, jnp.bfloat16)],
        compiler_params=PARAMS,
        name="fold",
    )(ours, theirs, quarters, *gots)


def add_kernel(left, right, out):
    out[...] = (left[...] + right[...].astype(jnp.float32)).astype(out.dtype)


def add(left, right):
    return pl.pallas_call(
        add_kernel,
        in_specs=[VMEM, VMEM],
        out_specs=VMEM,
        out_shape=jax.ShapeDtypeStruct(left.shape, jnp.bfloat16),
        compiler_params=PARAMS,
        name="add",
    )(left, right)


def mask_kernel(counts, atom_of, after, out):
    del after
    core = place()[0]
    slot = lax.broadcasted_iota(jnp.int32, (1, PCAP), 1)
    limit = jnp.zeros((1, PCAP), jnp.int32)
    for channel in range(CHANNELS):
        limit = jnp.where(slot >= channel * CH_CAP, channel * CH_CAP + counts[core, channel], limit)
    atoms = jnp.where(core == 0, atom_of[0:1], atom_of[1:2])
    code = jnp.broadcast_to(jnp.where(slot < limit, atoms, -1), (PCAP, PCAP))
    out[...] = jnp.where((code == code.T) & (code >= 0), 1.0, 0.0).astype(out.dtype)


def mask(counts, atom_of, after):
    return pl.pallas_call(
        mask_kernel,
        in_specs=[SMEM, VMEM, ANY],
        out_specs=VMEM,
        out_shape=jax.ShapeDtypeStruct((PCAP, PCAP), jnp.bfloat16),
        compiler_params=PARAMS,
        name="mask",
    )(counts, atom_of, after)


def couple_kernel(allowed, *refs):
    *messages, out, coupling = refs
    width = out.shape[2]
    entries = out.shape[0] // SQUARE
    core, chip = place()
    corner = chip & 3
    parts = (0, 2 - core, 1 + core, 3)
    for part, message in zip(parts, messages):
        start = pl.multiple_of((corner ^ part) * QUARTER, QUARTER)
        for cut in range(PCAP // width):
            lanes = slice(cut * width, (cut + 1) * width)
            first = entries * PCAP + cut * QUARTER
            coupling[pl.ds(start, QUARTER), lanes] = (
                message[first : first + QUARTER] * allowed[pl.ds(start, QUARTER), lanes]
            )
    for part, message in zip(parts, messages):
        wide = jnp.concatenate([message[e * PCAP : (e + 1) * PCAP] for e in range(entries)], axis=1)
        scaled = jnp.dot(coupling[...], wide, preferred_element_type=jnp.float32).astype(out.dtype)
        for entry in range(entries):
            out[part * entries + entry] = scaled[:, entry * width : (entry + 1) * width]


def couple(allowed, messages):
    rows, width = messages[0].shape
    entries = (rows - QUARTER * PCAP // width) // PCAP
    return pl.pallas_call(
        couple_kernel,
        in_specs=[VMEM] * (1 + SQUARE),
        out_specs=VMEM,
        out_shape=jax.ShapeDtypeStruct((SQUARE * entries, PCAP, width), jnp.bfloat16),
        scratch_shapes=[pltpu.VMEM((PCAP, PCAP), jnp.bfloat16)],
        compiler_params=PARAMS,
        name="couple",
    )(allowed, *messages)


def group_slots(group):
    return pl.ds(pl.multiple_of(group * PCAP, PCAP), PCAP)


def wide_pair(scaled, part):
    return jnp.concatenate([scaled[2 * part], scaled[2 * part + 1]], axis=1)


def begin_kernel(projectors, scaled, out):
    slots = group_slots(place()[0])
    for part in range(SQUARE):
        for block in range(projectors.shape[0] // ROW_BLOCK):
            rows = slice(block * ROW_BLOCK, (block + 1) * ROW_BLOCK)
            out[part, rows] = jnp.dot(
                projectors[rows, slots], wide_pair(scaled, part), preferred_element_type=jnp.float32
            )


def begin(projectors, scaled):
    depth, slots = projectors.shape
    return pl.pallas_call(
        begin_kernel,
        in_specs=[VMEM, VMEM],
        out_specs=VMEM,
        out_shape=jax.ShapeDtypeStruct((SQUARE, depth, 2 * LANES), jnp.float32),
        compiler_params=PARAMS,
        cost_estimate=pl.CostEstimate(
            flops=2 * depth * slots * LANES * SQUARE, bytes_accessed=2 * depth * slots, transcendentals=0
        ),
        name="begin",
    )(projectors, scaled)


def finish_kernel(projectors, begun, other, out, blocks, sems):
    core, chip = place()
    slots = group_slots(1 - core)
    copies = []
    first = 0
    for size in ROW_BLOCKS:
        rows = slice(first, first + size)
        first += size
        for part in range(SQUARE):
            sums = begun[part, rows] + jnp.dot(
                projectors[rows, slots], wide_pair(other, part), preferred_element_type=jnp.float32
            )
            for entry in range(2):
                start = pl.multiple_of(block_of(chip, part, entry) * LANES, LANES)
                lanes = slice(entry * LANES, (entry + 1) * LANES)
                blocks[rows, pl.ds(start, LANES)] = sums[:, lanes].astype(blocks.dtype)
        for start in range(rows.start, rows.stop, COPY_ROWS):
            written = slice(start, start + COPY_ROWS)
            copies.append(pltpu.make_async_copy(blocks.at[written], out.at[written], sems.at[len(copies)]))
            copies[-1].start(priority=len(copies) % 2)
    for copy in copies:
        copy.wait()


def finish(projectors, begun, other):
    depth, slots = projectors.shape
    bands = other.shape[0] * LANES
    return pl.pallas_call(
        finish_kernel,
        in_specs=[VMEM] * 3,
        out_specs=HBM,
        out_shape=jax.ShapeDtypeStruct((depth, bands), jnp.bfloat16),
        scratch_shapes=[
            pltpu.VMEM((depth, bands), jnp.bfloat16),
            pltpu.SemaphoreType.DMA((depth // COPY_ROWS,)),
        ],
        compiler_params=PARAMS,
        cost_estimate=pl.CostEstimate(
            flops=depth * slots * bands, bytes_accessed=2 * depth * (slots + bands), transcendentals=0
        ),
        name="finish",
    )(projectors, begun, other)


def apply_plain(projectors, mine, other):
    chips, _, width = mine.shape
    blocks = jnp.stack([block_of(place()[1], q, r) for q in range(SQUARE) for r in range(chips // SQUARE)])
    rows = []
    for group in range(2):
        part = jnp.where(place()[0] == group, mine, other)
        part = jnp.zeros_like(part).at[blocks].set(part)
        rows.append(part.transpose(1, 0, 2).reshape(PCAP, chips * width))
    return jnp.dot(projectors, jnp.concatenate(rows), preferred_element_type=jnp.float32).astype(jnp.bfloat16)


def local(band_coeffs, projectors, counts, atom_of, owners, couplings):
    chips = lax.axis_size("pw") // 2
    entries = chips // SQUARE
    width = band_coeffs.shape[1] // chips
    fast = width == LANES and entries == 2
    own_table = couplings[0]
    sibling_table = swap_cores(own_table)
    if fast:
        flipped = load(projectors)

        def partial(parts):
            return project(flipped, band_coeffs, parts)
    else:

        def partial(parts):
            return project_plain(projectors, band_coeffs, parts)

    theirs, ours = partial((3,))
    theirs, sibling_table = lax.optimization_barrier((theirs, sibling_table))
    theirs = swap_cores(theirs)
    pair_theirs, pair_ours = partial((1, 2))
    quarters = choose(owners, own_table, sibling_table, width, ours)
    got = swap_first(send(ours, theirs, quarters, (3,)))
    pair_theirs = swap_cores(pair_theirs)
    low_theirs, low_ours = partial((0,))
    low_theirs = swap_cores(low_theirs)
    got_first = swap_first(send(pair_ours, pair_theirs, quarters, (1, 2)))
    message = forward(pair_ours, pair_theirs, quarters, got)
    got_second = swap_second(message)
    allowed = mask(counts, atom_of, message)

    total, message = fold(low_ours, low_theirs, quarters, [got_first, got_second])
    mine = add(total, swap_chips(message, SQUARE))
    distance = 2 * SQUARE
    while distance < chips:
        body = mine[: entries * PCAP].reshape(entries, PCAP, width)
        order = [entry ^ (distance // SQUARE) for entry in range(entries)]
        message = jnp.concatenate([body[jnp.array(order)].reshape(-1, width), mine[entries * PCAP :]])
        mine = add(mine.astype(jnp.float32), swap_chips(message, distance))
        distance *= 2

    scaled = couple(allowed, [mine, swap_first(mine), swap_second(mine), swap_chips(mine, 3)])
    other = swap_cores(scaled)
    if not fast:
        return apply_plain(projectors, scaled, other)
    return finish(projectors, begin(projectors, scaled), other)


def solution(mesh):
    placed = (
        P("pw", "group"),
        P("pw", "group"),
        P("group", None),
        P("group", None),
        P("group"),
        P("pw", "group", None),
    )
    return jax.shard_map(
        local, mesh=mesh, in_specs=placed, out_specs=P("pw", "group"), check_vma=False
    )
```

```python
import jax
import jax.numpy as jnp
from jax import lax
from jax.experimental import pallas as pl
from jax.experimental.pallas import tpu as pltpu
from jax.sharding import PartitionSpec as P

CHANNELS = 4
CH_CAP = 64
PCAP = 256
LANES = 128
SQUARE = 4
QUARTER = PCAP // SQUARE
ROW_BLOCK = 512
ROW_BLOCKS = (256,) * 8
COPY_ROWS = 128
PARAMS = pltpu.CompilerParams(vmem_limit_bytes=40 * 1024 * 1024)
VMEM = pl.BlockSpec(memory_space=pltpu.VMEM)
SMEM = pl.BlockSpec(memory_space=pltpu.SMEM)
HBM = pl.BlockSpec(memory_space=pltpu.HBM)
ANY = pl.BlockSpec(memory_space=pl.ANY)


def place():
    me = lax.axis_index("pw")
    return lax.rem(me, 2), lax.div(me, 2)


def block_of(chip, part, entry):
    return chip ^ (part + SQUARE * entry)


def swap(x, distance):
    count = lax.axis_size("pw")
    return lax.ppermute(x, "pw", [(i, i ^ distance) for i in range(count)])


def swap_cores(x):
    return swap(x, 1)


def swap_chips(x, distance):
    return swap(x, 2 * distance)


def swap_first(x):
    count = lax.axis_size("pw")
    return lax.ppermute(x, "pw", [(i, i ^ (4, 2)[i % 2]) for i in range(count)])


def swap_second(x):
    count = lax.axis_size("pw")
    return lax.ppermute(x, "pw", [(i, i ^ (2, 4)[i % 2]) for i in range(count)])


def pair_at(columns, rows, part):
    chip = place()[1]
    starts = [pl.multiple_of(block_of(chip, part, entry) * LANES, LANES) for entry in range(2)]
    return jnp.concatenate([columns[rows, pl.ds(start, LANES)] for start in starts], axis=1)


def keep_sums(ours, theirs, at, sums):
    for entry in range(2):
        lanes = slice(entry * LANES, (entry + 1) * LANES)
        ours[2 * at + entry] = sums[:PCAP, lanes]
        theirs[2 * at + entry] = sums[PCAP:, lanes].astype(theirs.dtype)


def load_kernel(projectors, flipped, slots, sems):
    core = place()[0]
    count = sems.shape[0]
    block = slots.shape[0] // count
    copies = []
    for at in range(count):
        rows = slice(at * block, (at + 1) * block)
        copies.append(pltpu.make_async_copy(projectors.at[rows], slots.at[rows], sems.at[at]))
        copies[-1].start(priority=at % 2)
    for at, copy in enumerate(copies):
        copy.wait()
        rows = slice(at * block, (at + 1) * block)
        for side, group in enumerate((core, 1 - core)):
            start = pl.multiple_of(group * PCAP, PCAP)
            flipped[side * PCAP : (side + 1) * PCAP, rows] = slots[rows, pl.ds(start, PCAP)].T


def load(projectors):
    depth, slots = projectors.shape
    return pl.pallas_call(
        load_kernel,
        in_specs=[HBM],
        out_specs=VMEM,
        out_shape=jax.ShapeDtypeStruct((slots, depth), jnp.bfloat16),
        scratch_shapes=[pltpu.VMEM((depth, slots), jnp.bfloat16), pltpu.SemaphoreType.DMA((4,))],
        compiler_params=PARAMS,
        name="load",
    )(pltpu.with_memory_space_constraint(projectors, pltpu.HBM))


def project_kernel(parts, flipped, columns, theirs, ours):
    rows = slice(0, columns.shape[0])
    for at, part in enumerate(parts):
        sums = jnp.dot(flipped[...], pair_at(columns, rows, part), preferred_element_type=jnp.float32)
        keep_sums(ours, theirs, at, sums)


def project(flipped, band_coeffs, parts):
    slots, depth = flipped.shape
    shape = (2 * len(parts), PCAP, LANES)

    def kernel(*refs):
        project_kernel(parts, *refs)

    return pl.pallas_call(
        kernel,
        in_specs=[VMEM, VMEM],
        out_specs=[VMEM, VMEM],
        out_shape=[jax.ShapeDtypeStruct(shape, jnp.bfloat16), jax.ShapeDtypeStruct(shape, jnp.float32)],
        compiler_params=PARAMS,
        cost_estimate=pl.CostEstimate(
            flops=4 * depth * slots * len(parts) * LANES, bytes_accessed=2 * depth * slots, transcendentals=0
        ),
        name="project",
    )(flipped, pltpu.with_memory_space_constraint(band_coeffs, pltpu.VMEM))


def project_plain(projectors, band_coeffs, parts):
    depth, bands = band_coeffs.shape
    chips = lax.axis_size("pw") // 2
    blocks = jnp.stack([block_of(place()[1], q, r) for q in parts for r in range(chips // SQUARE)])
    columns = jnp.take(band_coeffs.reshape(depth, chips, bands // chips), blocks, axis=1)
    outs = []
    core = place()[0]
    for group, dtype in ((1 - core, jnp.bfloat16), (core, jnp.float32)):
        slots = lax.dynamic_slice_in_dim(projectors, group * PCAP, PCAP, 1)
        sums = jnp.einsum("ds,dhw->hsw", slots, columns, preferred_element_type=jnp.float32)
        outs.append(sums.astype(dtype))
    return outs


def choose_kernel(owners, own, sibling, after, out):
    del after
    core, chip = place()
    me = 2 * chip + core
    owner = jnp.where(core == 0, owners[0:1, :], owners[1:2, :])
    width = out.shape[2]
    for part in range(SQUARE):
        rows = pl.ds(pl.multiple_of(((chip & 3) ^ part) * QUARTER, QUARTER), QUARTER)
        piece = jnp.where(owner == me, own[rows], jnp.where(owner == (me ^ 1), sibling[rows], 0.0))
        for cut in range(PCAP // width):
            out[part, cut * QUARTER : (cut + 1) * QUARTER] = piece[:, cut * width : (cut + 1) * width].astype(
                out.dtype
            )


def choose(owners, own, sibling, width, after):
    return pl.pallas_call(
        choose_kernel,
        in_specs=[VMEM, VMEM, VMEM, ANY],
        out_specs=VMEM,
        out_shape=jax.ShapeDtypeStruct((SQUARE, QUARTER * PCAP // width, width), jnp.bfloat16),
        compiler_params=PARAMS,
        name="choose",
    )(jnp.broadcast_to(owners[:, None], (owners.shape[0], PCAP)), own, sibling, after)


def send_kernel(first, second, ours, theirs, quarters, message):
    entries = ours.shape[0] // (1 if first == second else 2)
    core = place()[0]
    start, part = (0, first) if first == second else ((1 - core) * entries, 2 - core)
    for entry in range(entries):
        total = ours[start + entry] + theirs[start + entry].astype(jnp.float32)
        message[entry * PCAP : (entry + 1) * PCAP] = total.astype(message.dtype)
    message[entries * PCAP :] = quarters[part]


def send(ours, theirs, quarters, parts):
    count, _, width = ours.shape
    rows = count // len(parts) * PCAP + quarters.shape[1]

    def kernel(*refs):
        send_kernel(parts[0], parts[-1], *refs)

    return pl.pallas_call(
        kernel,
        in_specs=[VMEM] * 3,
        out_specs=VMEM,
        out_shape=jax.ShapeDtypeStruct((rows, width), jnp.bfloat16),
        compiler_params=PARAMS,
        name="send",
    )(ours, theirs, quarters)


def forward_kernel(ours, theirs, quarters, got, message):
    core = place()[0]
    entries = ours.shape[0] // 2
    start = core * entries
    for entry in range(entries):
        rows = slice(entry * PCAP, (entry + 1) * PCAP)
        total = ours[start + entry] + theirs[start + entry].astype(jnp.float32)
        message[rows] = (total + got[rows].astype(jnp.float32)).astype(message.dtype)
    message[entries * PCAP :] = quarters[1 + core] + got[entries * PCAP :]


def forward(ours, theirs, quarters, got):
    return pl.pallas_call(
        forward_kernel,
        in_specs=[VMEM] * 4,
        out_specs=VMEM,
        out_shape=jax.ShapeDtypeStruct(got.shape, got.dtype),
        compiler_params=PARAMS,
        name="forward",
    )(ours, theirs, quarters, got)


def fold_kernel(ours, theirs, quarters, *refs):
    *gots, kept, message = refs
    entries = ours.shape[0]
    for entry in range(entries):
        rows = slice(entry * PCAP, (entry + 1) * PCAP)
        total = ours[entry] + theirs[entry].astype(jnp.float32)
        for got in gots:
            total = total + got[rows].astype(jnp.float32)
        kept[rows] = total
        away = entry ^ 1
        message[away * PCAP : (away + 1) * PCAP] = total.astype(message.dtype)
    table = quarters[0]
    for got in gots:
        table = table + got[entries * PCAP :]
    kept[entries * PCAP :] = table.astype(kept.dtype)
    message[entries * PCAP :] = table


def fold(ours, theirs, quarters, gots):
    shape = gots[0].shape
    return pl.pallas_call(
        fold_kernel,
        in_specs=[VMEM] * (3 + len(gots)),
        out_specs=[VMEM, VMEM],
        out_shape=[jax.ShapeDtypeStruct(shape, jnp.float32), jax.ShapeDtypeStruct(shape, jnp.bfloat16)],
        compiler_params=PARAMS,
        name="fold",
    )(ours, theirs, quarters, *gots)


def add_kernel(left, right, out):
    out[...] = (left[...] + right[...].astype(jnp.float32)).astype(out.dtype)


def add(left, right):
    return pl.pallas_call(
        add_kernel,
        in_specs=[VMEM, VMEM],
        out_specs=VMEM,
        out_shape=jax.ShapeDtypeStruct(left.shape, jnp.bfloat16),
        compiler_params=PARAMS,
        name="add",
    )(left, right)


def mask_kernel(counts, atom_of, after, out):
    del after
    core = place()[0]
    slot = lax.broadcasted_iota(jnp.int32, (1, PCAP), 1)
    limit = jnp.zeros((1, PCAP), jnp.int32)
    for channel in range(CHANNELS):
        limit = jnp.where(slot >= channel * CH_CAP, channel * CH_CAP + counts[core, channel], limit)
    atoms = jnp.where(core == 0, atom_of[0:1], atom_of[1:2])
    code = jnp.broadcast_to(jnp.where(slot < limit, atoms, -1), (PCAP, PCAP))
    out[...] = jnp.where((code == code.T) & (code >= 0), 1.0, 0.0).astype(out.dtype)


def mask(counts, atom_of, after):
    return pl.pallas_call(
        mask_kernel,
        in_specs=[SMEM, VMEM, ANY],
        out_specs=VMEM,
        out_shape=jax.ShapeDtypeStruct((PCAP, PCAP), jnp.bfloat16),
        compiler_params=PARAMS,
        name="mask",
    )(counts, atom_of, after)


def couple_kernel(allowed, *refs):
    *messages, out, coupling = refs
    width = out.shape[2]
    entries = out.shape[0] // SQUARE
    core, chip = place()
    corner = chip & 3
    parts = (0, 2 - core, 1 + core, 3)
    for part, message in zip(parts, messages):
        start = pl.multiple_of((corner ^ part) * QUARTER, QUARTER)
        for cut in range(PCAP // width):
            lanes = slice(cut * width, (cut + 1) * width)
            first = entries * PCAP + cut * QUARTER
            coupling[pl.ds(start, QUARTER), lanes] = (
                message[first : first + QUARTER] * allowed[pl.ds(start, QUARTER), lanes]
            )
    for part, message in zip(parts, messages):
        wide = jnp.concatenate([message[e * PCAP : (e + 1) * PCAP] for e in range(entries)], axis=1)
        scaled = jnp.dot(coupling[...], wide, preferred_element_type=jnp.float32).astype(out.dtype)
        for entry in range(entries):
            out[part * entries + entry] = scaled[:, entry * width : (entry + 1) * width]


def couple(allowed, messages):
    rows, width = messages[0].shape
    entries = (rows - QUARTER * PCAP // width) // PCAP
    return pl.pallas_call(
        couple_kernel,
        in_specs=[VMEM] * (1 + SQUARE),
        out_specs=VMEM,
        out_shape=jax.ShapeDtypeStruct((SQUARE * entries, PCAP, width), jnp.bfloat16),
        scratch_shapes=[pltpu.VMEM((PCAP, PCAP), jnp.bfloat16)],
        compiler_params=PARAMS,
        name="couple",
    )(allowed, *messages)


def group_slots(group):
    return pl.ds(pl.multiple_of(group * PCAP, PCAP), PCAP)


def wide_pair(scaled, part):
    return jnp.concatenate([scaled[2 * part], scaled[2 * part + 1]], axis=1)


def begin_kernel(projectors, scaled, out):
    slots = group_slots(place()[0])
    for part in range(SQUARE):
        for block in range(projectors.shape[0] // ROW_BLOCK):
            rows = slice(block * ROW_BLOCK, (block + 1) * ROW_BLOCK)
            out[part, rows] = jnp.dot(
                projectors[rows, slots], wide_pair(scaled, part), preferred_element_type=jnp.float32
            )


def begin(projectors, scaled):
    depth, slots = projectors.shape
    return pl.pallas_call(
        begin_kernel,
        in_specs=[VMEM, VMEM],
        out_specs=VMEM,
        out_shape=jax.ShapeDtypeStruct((SQUARE, depth, 2 * LANES), jnp.float32),
        compiler_params=PARAMS,
        cost_estimate=pl.CostEstimate(
            flops=2 * depth * slots * LANES * SQUARE, bytes_accessed=2 * depth * slots, transcendentals=0
        ),
        name="begin",
    )(projectors, scaled)


def finish_kernel(projectors, begun, other, out, blocks, sems):
    core, chip = place()
    slots = group_slots(1 - core)
    copies = []
    first = 0
    for size in ROW_BLOCKS:
        rows = slice(first, first + size)
        first += size
        for part in range(SQUARE):
            sums = begun[part, rows] + jnp.dot(
                projectors[rows, slots], wide_pair(other, part), preferred_element_type=jnp.float32
            )
            for entry in range(2):
                start = pl.multiple_of(block_of(chip, part, entry) * LANES, LANES)
                lanes = slice(entry * LANES, (entry + 1) * LANES)
                blocks[rows, pl.ds(start, LANES)] = sums[:, lanes].astype(blocks.dtype)
        for start in range(rows.start, rows.stop, COPY_ROWS):
            written = slice(start, start + COPY_ROWS)
            copies.append(pltpu.make_async_copy(blocks.at[written], out.at[written], sems.at[len(copies)]))
            copies[-1].start(priority=len(copies) % 2)
    for copy in copies:
        copy.wait()


def finish(projectors, begun, other):
    depth, slots = projectors.shape
    bands = other.shape[0] * LANES
    return pl.pallas_call(
        finish_kernel,
        in_specs=[VMEM] * 3,
        out_specs=HBM,
        out_shape=jax.ShapeDtypeStruct((depth, bands), jnp.bfloat16),
        scratch_shapes=[
            pltpu.VMEM((depth, bands), jnp.bfloat16),
            pltpu.SemaphoreType.DMA((depth // COPY_ROWS,)),
        ],
        compiler_params=PARAMS,
        cost_estimate=pl.CostEstimate(
            flops=depth * slots * bands, bytes_accessed=2 * depth * (slots + bands), transcendentals=0
        ),
        name="finish",
    )(projectors, begun, other)


def apply_plain(projectors, mine, other):
    chips, _, width = mine.shape
    blocks = jnp.stack([block_of(place()[1], q, r) for q in range(SQUARE) for r in range(chips // SQUARE)])
    rows = []
    for group in range(2):
        part = jnp.where(place()[0] == group, mine, other)
        part = jnp.zeros_like(part).at[blocks].set(part)
        rows.append(part.transpose(1, 0, 2).reshape(PCAP, chips * width))
    return jnp.dot(projectors, jnp.concatenate(rows), preferred_element_type=jnp.float32).astype(jnp.bfloat16)


def local(band_coeffs, projectors, counts, atom_of, owners, couplings):
    chips = lax.axis_size("pw") // 2
    entries = chips // SQUARE
    width = band_coeffs.shape[1] // chips
    fast = width == LANES and entries == 2
    own_table = couplings[0]
    sibling_table = swap_cores(own_table)
    if fast:
        flipped = load(projectors)

        def partial(parts):
            return project(flipped, band_coeffs, parts)
    else:

        def partial(parts):
            return project_plain(projectors, band_coeffs, parts)

    theirs, ours = partial((3,))
    theirs, sibling_table = lax.optimization_barrier((theirs, sibling_table))
    theirs = swap_cores(theirs)
    pair_theirs, pair_ours = partial((1, 2))
    quarters = choose(owners, own_table, sibling_table, width, ours)
    got = swap_first(send(ours, theirs, quarters, (3,)))
    pair_theirs = swap_cores(pair_theirs)
    low_theirs, low_ours = partial((0,))
    low_theirs = swap_cores(low_theirs)
    got_first = swap_first(send(pair_ours, pair_theirs, quarters, (1, 2)))
    message = forward(pair_ours, pair_theirs, quarters, got)
    got_second = swap_second(message)
    allowed = mask(counts, atom_of, message)

    total, message = fold(low_ours, low_theirs, quarters, [got_first, got_second])
    mine = add(total, swap_chips(message, SQUARE))
    distance = 2 * SQUARE
    while distance < chips:
        body = mine[: entries * PCAP].reshape(entries, PCAP, width)
        order = [entry ^ (distance // SQUARE) for entry in range(entries)]
        message = jnp.concatenate([body[jnp.array(order)].reshape(-1, width), mine[entries * PCAP :]])
        mine = add(mine.astype(jnp.float32), swap_chips(message, distance))
        distance *= 2

    scaled = couple(allowed, [mine, swap_first(mine), swap_second(mine), swap_chips(mine, 3)])
    other = swap_cores(scaled)
    if not fast:
        return apply_plain(projectors, scaled, other)
    return finish(projectors, begin(projectors, scaled), other)


def solution(mesh):
    placed = (
        P("pw", "group"),
        P("pw", "group"),
        P("group", None),
        P("group", None),
        P("group"),
        P("pw", "group", None),
    )
    return jax.shard_map(
        local, mesh=mesh, in_specs=placed, out_specs=P("pw", "group"), check_vma=False
    )
```

```python
import jax
import jax.numpy as jnp
from jax import lax
from jax.experimental import pallas as pl
from jax.experimental.pallas import tpu as pltpu
from jax.sharding import PartitionSpec as P

CHANNELS = 4
CH_CAP = 64
PCAP = 256
LANES = 128
SQUARE = 4
QUARTER = PCAP // SQUARE
ROW_BLOCK = 512
ROW_BLOCKS = (256,) * 8
COPY_ROWS = 128
PARAMS = pltpu.CompilerParams(vmem_limit_bytes=40 * 1024 * 1024)
VMEM = pl.BlockSpec(memory_space=pltpu.VMEM)
SMEM = pl.BlockSpec(memory_space=pltpu.SMEM)
HBM = pl.BlockSpec(memory_space=pltpu.HBM)
ANY = pl.BlockSpec(memory_space=pl.ANY)


def place():
    me = lax.axis_index("pw")
    return lax.rem(me, 2), lax.div(me, 2)


def block_of(chip, part, entry):
    return chip ^ (part + SQUARE * entry)


def swap(x, distance):
    count = lax.axis_size("pw")
    return lax.ppermute(x, "pw", [(i, i ^ distance) for i in range(count)])


def swap_cores(x):
    return swap(x, 1)


def swap_chips(x, distance):
    return swap(x, 2 * distance)


def swap_first(x):
    count = lax.axis_size("pw")
    return lax.ppermute(x, "pw", [(i, i ^ (4, 2)[i % 2]) for i in range(count)])


def swap_second(x):
    count = lax.axis_size("pw")
    return lax.ppermute(x, "pw", [(i, i ^ (2, 4)[i % 2]) for i in range(count)])


def pair_at(columns, rows, part):
    chip = place()[1]
    starts = [pl.multiple_of(block_of(chip, part, entry) * LANES, LANES) for entry in range(2)]
    return jnp.concatenate([columns[rows, pl.ds(start, LANES)] for start in starts], axis=1)


def keep_sums(ours, theirs, at, sums):
    for entry in range(2):
        lanes = slice(entry * LANES, (entry + 1) * LANES)
        ours[2 * at + entry] = sums[:PCAP, lanes]
        theirs[2 * at + entry] = sums[PCAP:, lanes].astype(theirs.dtype)


def load_kernel(projectors, flipped, slots, sems):
    core = place()[0]
    count = sems.shape[0]
    block = slots.shape[0] // count
    copies = []
    for at in range(count):
        rows = slice(at * block, (at + 1) * block)
        copies.append(pltpu.make_async_copy(projectors.at[rows], slots.at[rows], sems.at[at]))
        copies[-1].start(priority=at % 2)
    for at, copy in enumerate(copies):
        copy.wait()
        rows = slice(at * block, (at + 1) * block)
        for side, group in enumerate((core, 1 - core)):
            start = pl.multiple_of(group * PCAP, PCAP)
            flipped[side * PCAP : (side + 1) * PCAP, rows] = slots[rows, pl.ds(start, PCAP)].T


def load(projectors):
    depth, slots = projectors.shape
    return pl.pallas_call(
        load_kernel,
        in_specs=[HBM],
        out_specs=VMEM,
        out_shape=jax.ShapeDtypeStruct((slots, depth), jnp.bfloat16),
        scratch_shapes=[pltpu.VMEM((depth, slots), jnp.bfloat16), pltpu.SemaphoreType.DMA((4,))],
        compiler_params=PARAMS,
        name="load",
    )(pltpu.with_memory_space_constraint(projectors, pltpu.HBM))


def project_kernel(parts, flipped, columns, theirs, ours):
    rows = slice(0, columns.shape[0])
    for at, part in enumerate(parts):
        sums = jnp.dot(flipped[...], pair_at(columns, rows, part), preferred_element_type=jnp.float32)
        keep_sums(ours, theirs, at, sums)


def project(flipped, band_coeffs, parts):
    slots, depth = flipped.shape
    shape = (2 * len(parts), PCAP, LANES)

    def kernel(*refs):
        project_kernel(parts, *refs)

    return pl.pallas_call(
        kernel,
        in_specs=[VMEM, VMEM],
        out_specs=[VMEM, VMEM],
        out_shape=[jax.ShapeDtypeStruct(shape, jnp.bfloat16), jax.ShapeDtypeStruct(shape, jnp.float32)],
        compiler_params=PARAMS,
        cost_estimate=pl.CostEstimate(
            flops=4 * depth * slots * len(parts) * LANES, bytes_accessed=2 * depth * slots, transcendentals=0
        ),
        name="project",
    )(flipped, pltpu.with_memory_space_constraint(band_coeffs, pltpu.VMEM))


def project_plain(projectors, band_coeffs, parts):
    depth, bands = band_coeffs.shape
    chips = lax.axis_size("pw") // 2
    blocks = jnp.stack([block_of(place()[1], q, r) for q in parts for r in range(chips // SQUARE)])
    columns = jnp.take(band_coeffs.reshape(depth, chips, bands // chips), blocks, axis=1)
    outs = []
    core = place()[0]
    for group, dtype in ((1 - core, jnp.bfloat16), (core, jnp.float32)):
        slots = lax.dynamic_slice_in_dim(projectors, group * PCAP, PCAP, 1)
        sums = jnp.einsum("ds,dhw->hsw", slots, columns, preferred_element_type=jnp.float32)
        outs.append(sums.astype(dtype))
    return outs


def choose_kernel(owners, own, sibling, after, out):
    del after
    core, chip = place()
    me = 2 * chip + core
    owner = jnp.where(core == 0, owners[0:1, :], owners[1:2, :])
    width = out.shape[2]
    for part in range(SQUARE):
        rows = pl.ds(pl.multiple_of(((chip & 3) ^ part) * QUARTER, QUARTER), QUARTER)
        piece = jnp.where(owner == me, own[rows], jnp.where(owner == (me ^ 1), sibling[rows], 0.0))
        for cut in range(PCAP // width):
            out[part, cut * QUARTER : (cut + 1) * QUARTER] = piece[:, cut * width : (cut + 1) * width].astype(
                out.dtype
            )


def choose(owners, own, sibling, width, after):
    return pl.pallas_call(
        choose_kernel,
        in_specs=[VMEM, VMEM, VMEM, ANY],
        out_specs=VMEM,
        out_shape=jax.ShapeDtypeStruct((SQUARE, QUARTER * PCAP // width, width), jnp.bfloat16),
        compiler_params=PARAMS,
        name="choose",
    )(jnp.broadcast_to(owners[:, None], (owners.shape[0], PCAP)), own, sibling, after)


def send_kernel(first, second, ours, theirs, quarters, message):
    entries = ours.shape[0] // (1 if first == second else 2)
    core = place()[0]
    start, part = (0, first) if first == second else ((1 - core) * entries, 2 - core)
    for entry in range(entries):
        total = ours[start + entry] + theirs[start + entry].astype(jnp.float32)
        message[entry * PCAP : (entry + 1) * PCAP] = total.astype(message.dtype)
    message[entries * PCAP :] = quarters[part]


def send(ours, theirs, quarters, parts):
    count, _, width = ours.shape
    rows = count // len(parts) * PCAP + quarters.shape[1]

    def kernel(*refs):
        send_kernel(parts[0], parts[-1], *refs)

    return pl.pallas_call(
        kernel,
        in_specs=[VMEM] * 3,
        out_specs=VMEM,
        out_shape=jax.ShapeDtypeStruct((rows, width), jnp.bfloat16),
        compiler_params=PARAMS,
        name="send",
    )(ours, theirs, quarters)


def forward_kernel(ours, theirs, quarters, got, message):
    core = place()[0]
    entries = ours.shape[0] // 2
    start = core * entries
    for entry in range(entries):
        rows = slice(entry * PCAP, (entry + 1) * PCAP)
        total = ours[start + entry] + theirs[start + entry].astype(jnp.float32)
        message[rows] = (total + got[rows].astype(jnp.float32)).astype(message.dtype)
    message[entries * PCAP :] = quarters[1 + core] + got[entries * PCAP :]


def forward(ours, theirs, quarters, got):
    return pl.pallas_call(
        forward_kernel,
        in_specs=[VMEM] * 4,
        out_specs=VMEM,
        out_shape=jax.ShapeDtypeStruct(got.shape, got.dtype),
        compiler_params=PARAMS,
        name="forward",
    )(ours, theirs, quarters, got)


def fold_kernel(ours, theirs, quarters, *refs):
    *gots, kept, message = refs
    entries = ours.shape[0]
    for entry in range(entries):
        rows = slice(entry * PCAP, (entry + 1) * PCAP)
        total = ours[entry] + theirs[entry].astype(jnp.float32)
        for got in gots:
            total = total + got[rows].astype(jnp.float32)
        kept[rows] = total
        away = entry ^ 1
        message[away * PCAP : (away + 1) * PCAP] = total.astype(message.dtype)
    table = quarters[0]
    for got in gots:
        table = table + got[entries * PCAP :]
    kept[entries * PCAP :] = table.astype(kept.dtype)
    message[entries * PCAP :] = table


def fold(ours, theirs, quarters, gots):
    shape = gots[0].shape
    return pl.pallas_call(
        fold_kernel,
        in_specs=[VMEM] * (3 + len(gots)),
        out_specs=[VMEM, VMEM],
        out_shape=[jax.ShapeDtypeStruct(shape, jnp.float32), jax.ShapeDtypeStruct(shape, jnp.bfloat16)],
        compiler_params=PARAMS,
        name="fold",
    )(ours, theirs, quarters, *gots)


def add_kernel(left, right, out):
    out[...] = (left[...] + right[...].astype(jnp.float32)).astype(out.dtype)


def add(left, right):
    return pl.pallas_call(
        add_kernel,
        in_specs=[VMEM, VMEM],
        out_specs=VMEM,
        out_shape=jax.ShapeDtypeStruct(left.shape, jnp.bfloat16),
        compiler_params=PARAMS,
        name="add",
    )(left, right)


def mask_kernel(counts, atom_of, after, out):
    del after
    core = place()[0]
    slot = lax.broadcasted_iota(jnp.int32, (1, PCAP), 1)
    limit = jnp.zeros((1, PCAP), jnp.int32)
    for channel in range(CHANNELS):
        limit = jnp.where(slot >= channel * CH_CAP, channel * CH_CAP + counts[core, channel], limit)
    atoms = jnp.where(core == 0, atom_of[0:1], atom_of[1:2])
    code = jnp.broadcast_to(jnp.where(slot < limit, atoms, -1), (PCAP, PCAP))
    out[...] = jnp.where((code == code.T) & (code >= 0), 1.0, 0.0).astype(out.dtype)


def mask(counts, atom_of, after):
    return pl.pallas_call(
        mask_kernel,
        in_specs=[SMEM, VMEM, ANY],
        out_specs=VMEM,
        out_shape=jax.ShapeDtypeStruct((PCAP, PCAP), jnp.bfloat16),
        compiler_params=PARAMS,
        name="mask",
    )(counts, atom_of, after)


def couple_kernel(allowed, *refs):
    *messages, out, coupling = refs
    width = out.shape[2]
    entries = out.shape[0] // SQUARE
    core, chip = place()
    corner = chip & 3
    parts = (0, 3, 1 + core, 2 - core)
    for part, message in zip(parts, messages):
        start = pl.multiple_of((corner ^ part) * QUARTER, QUARTER)
        for cut in range(PCAP // width):
            lanes = slice(cut * width, (cut + 1) * width)
            first = entries * PCAP + cut * QUARTER
            coupling[pl.ds(start, QUARTER), lanes] = (
                message[first : first + QUARTER] * allowed[pl.ds(start, QUARTER), lanes]
            )
    for part, message in zip(parts, messages):
        wide = jnp.concatenate([message[e * PCAP : (e + 1) * PCAP] for e in range(entries)], axis=1)
        scaled = jnp.dot(coupling[...], wide, preferred_element_type=jnp.float32).astype(out.dtype)
        for entry in range(entries):
            out[part * entries + entry] = scaled[:, entry * width : (entry + 1) * width]


def couple(allowed, messages):
    rows, width = messages[0].shape
    entries = (rows - QUARTER * PCAP // width) // PCAP
    return pl.pallas_call(
        couple_kernel,
        in_specs=[VMEM] * (1 + SQUARE),
        out_specs=VMEM,
        out_shape=jax.ShapeDtypeStruct((SQUARE * entries, PCAP, width), jnp.bfloat16),
        scratch_shapes=[pltpu.VMEM((PCAP, PCAP), jnp.bfloat16)],
        compiler_params=PARAMS,
        name="couple",
    )(allowed, *messages)


def group_slots(group):
    return pl.ds(pl.multiple_of(group * PCAP, PCAP), PCAP)


def wide_pair(scaled, part):
    return jnp.concatenate([scaled[2 * part], scaled[2 * part + 1]], axis=1)


def begin_kernel(projectors, scaled, out):
    slots = group_slots(place()[0])
    for part in range(SQUARE):
        for block in range(projectors.shape[0] // ROW_BLOCK):
            rows = slice(block * ROW_BLOCK, (block + 1) * ROW_BLOCK)
            out[part, rows] = jnp.dot(
                projectors[rows, slots], wide_pair(scaled, part), preferred_element_type=jnp.float32
            )


def begin(projectors, scaled):
    depth, slots = projectors.shape
    return pl.pallas_call(
        begin_kernel,
        in_specs=[VMEM, VMEM],
        out_specs=VMEM,
        out_shape=jax.ShapeDtypeStruct((SQUARE, depth, 2 * LANES), jnp.float32),
        compiler_params=PARAMS,
        cost_estimate=pl.CostEstimate(
            flops=2 * depth * slots * LANES * SQUARE, bytes_accessed=2 * depth * slots, transcendentals=0
        ),
        name="begin",
    )(projectors, scaled)


def finish_kernel(projectors, begun, other, out, blocks, sems):
    core, chip = place()
    slots = group_slots(1 - core)
    copies = []
    first = 0
    for size in ROW_BLOCKS:
        rows = slice(first, first + size)
        first += size
        for part in range(SQUARE):
            sums = begun[part, rows] + jnp.dot(
                projectors[rows, slots], wide_pair(other, part), preferred_element_type=jnp.float32
            )
            for entry in range(2):
                start = pl.multiple_of(block_of(chip, part, entry) * LANES, LANES)
                lanes = slice(entry * LANES, (entry + 1) * LANES)
                blocks[rows, pl.ds(start, LANES)] = sums[:, lanes].astype(blocks.dtype)
        for start in range(rows.start, rows.stop, COPY_ROWS):
            written = slice(start, start + COPY_ROWS)
            copies.append(pltpu.make_async_copy(blocks.at[written], out.at[written], sems.at[len(copies)]))
            copies[-1].start(priority=len(copies) % 2)
    for copy in copies:
        copy.wait()


def finish(projectors, begun, other):
    depth, slots = projectors.shape
    bands = other.shape[0] * LANES
    return pl.pallas_call(
        finish_kernel,
        in_specs=[VMEM] * 3,
        out_specs=HBM,
        out_shape=jax.ShapeDtypeStruct((depth, bands), jnp.bfloat16),
        scratch_shapes=[
            pltpu.VMEM((depth, bands), jnp.bfloat16),
            pltpu.SemaphoreType.DMA((depth // COPY_ROWS,)),
        ],
        compiler_params=PARAMS,
        cost_estimate=pl.CostEstimate(
            flops=depth * slots * bands, bytes_accessed=2 * depth * (slots + bands), transcendentals=0
        ),
        name="finish",
    )(projectors, begun, other)


def apply_plain(projectors, mine, other):
    chips, _, width = mine.shape
    blocks = jnp.stack([block_of(place()[1], q, r) for q in range(SQUARE) for r in range(chips // SQUARE)])
    rows = []
    for group in range(2):
        part = jnp.where(place()[0] == group, mine, other)
        part = jnp.zeros_like(part).at[blocks].set(part)
        rows.append(part.transpose(1, 0, 2).reshape(PCAP, chips * width))
    return jnp.dot(projectors, jnp.concatenate(rows), preferred_element_type=jnp.float32).astype(jnp.bfloat16)


def local(band_coeffs, projectors, counts, atom_of, owners, couplings):
    chips = lax.axis_size("pw") // 2
    entries = chips // SQUARE
    width = band_coeffs.shape[1] // chips
    fast = width == LANES and entries == 2
    own_table = couplings[0]
    sibling_table = swap_cores(own_table)
    if fast:
        flipped = load(projectors)

        def partial(parts):
            return project(flipped, band_coeffs, parts)
    else:

        def partial(parts):
            return project_plain(projectors, band_coeffs, parts)

    theirs, ours = partial((3,))
    theirs, sibling_table = lax.optimization_barrier((theirs, sibling_table))
    theirs = swap_cores(theirs)
    pair_theirs, pair_ours = partial((1, 2))
    quarters = choose(owners, own_table, sibling_table, width, ours)
    got = swap_first(send(ours, theirs, quarters, (3,)))
    pair_theirs = swap_cores(pair_theirs)
    low_theirs, low_ours = partial((0,))
    low_theirs = swap_cores(low_theirs)
    got_first = swap_first(send(pair_ours, pair_theirs, quarters, (1, 2)))
    message = forward(pair_ours, pair_theirs, quarters, got)
    got_second = swap_second(message)
    allowed = mask(counts, atom_of, message)

    total, message = fold(low_ours, low_theirs, quarters, [got_first, got_second])
    mine = add(total, swap_chips(message, SQUARE))
    distance = 2 * SQUARE
    while distance < chips:
        body = mine[: entries * PCAP].reshape(entries, PCAP, width)
        order = [entry ^ (distance // SQUARE) for entry in range(entries)]
        message = jnp.concatenate([body[jnp.array(order)].reshape(-1, width), mine[entries * PCAP :]])
        mine = add(mine.astype(jnp.float32), swap_chips(message, distance))
        distance *= 2

    scaled = couple(allowed, [mine, swap_chips(mine, 3), swap_second(mine), swap_first(mine)])
    other = swap_cores(scaled)
    if not fast:
        return apply_plain(projectors, scaled, other)
    return finish(projectors, begin(projectors, scaled), other)


def solution(mesh):
    placed = (
        P("pw", "group"),
        P("pw", "group"),
        P("group", None),
        P("group", None),
        P("group"),
        P("pw", "group", None),
    )
    return jax.shard_map(
        local, mesh=mesh, in_specs=placed, out_specs=P("pw", "group"), check_vma=False
    )
```

```python
import jax
import jax.numpy as jnp
from jax import lax
from jax.experimental import pallas as pl
from jax.experimental.pallas import tpu as pltpu
from jax.sharding import PartitionSpec as P

CHANNELS = 4
CH_CAP = 64
PCAP = 256
LANES = 128
SQUARE = 4
QUARTER = PCAP // SQUARE
ROW_BLOCK = 512
ROW_BLOCKS = (256,) * 8
COPY_ROWS = 128
PARAMS = pltpu.CompilerParams(vmem_limit_bytes=40 * 1024 * 1024)
VMEM = pl.BlockSpec(memory_space=pltpu.VMEM)
SMEM = pl.BlockSpec(memory_space=pltpu.SMEM)
HBM = pl.BlockSpec(memory_space=pltpu.HBM)
ANY = pl.BlockSpec(memory_space=pl.ANY)


def place():
    me = lax.axis_index("pw")
    return lax.rem(me, 2), lax.div(me, 2)


def block_of(chip, part, entry):
    return chip ^ (part + SQUARE * entry)


def swap(x, distance):
    count = lax.axis_size("pw")
    return lax.ppermute(x, "pw", [(i, i ^ distance) for i in range(count)])


def swap_cores(x):
    return swap(x, 1)


def swap_chips(x, distance):
    return swap(x, 2 * distance)


def swap_first(x):
    count = lax.axis_size("pw")
    return lax.ppermute(x, "pw", [(i, i ^ (4, 2)[i % 2]) for i in range(count)])


def swap_second(x):
    count = lax.axis_size("pw")
    return lax.ppermute(x, "pw", [(i, i ^ (2, 4)[i % 2]) for i in range(count)])


def pair_at(columns, rows, part):
    chip = place()[1]
    starts = [pl.multiple_of(block_of(chip, part, entry) * LANES, LANES) for entry in range(2)]
    return jnp.concatenate([columns[rows, pl.ds(start, LANES)] for start in starts], axis=1)


def keep_sums(ours, theirs, at, sums):
    for entry in range(2):
        lanes = slice(entry * LANES, (entry + 1) * LANES)
        ours[2 * at + entry] = sums[:PCAP, lanes]
        theirs[2 * at + entry] = sums[PCAP:, lanes].astype(theirs.dtype)


def load_kernel(projectors, bands, theirs, ours, flipped, columns, slots, totals, slot_sems, column_sems):
    core = place()[0]
    count = slot_sems.shape[0]
    depth = slots.shape[0] // count
    copies = []
    for at in range(count):
        rows = slice(at * depth, (at + 1) * depth)
        copies.append(
            (
                pltpu.make_async_copy(projectors.at[rows], slots.at[rows], slot_sems.at[at]),
                pltpu.make_async_copy(bands.at[rows], columns.at[rows], column_sems.at[at]),
            )
        )
    for pair in copies[:2]:
        for copy in pair:
            copy.start()
    for at in range(count):
        rows = slice(at * depth, (at + 1) * depth)
        copies[at][0].wait()
        if at + 2 < count:
            copies[at + 2][0].start()
        for side, group in enumerate((core, 1 - core)):
            start = pl.multiple_of(group * PCAP, PCAP)
            flipped[side * PCAP : (side + 1) * PCAP, rows] = slots[rows, pl.ds(start, PCAP)].T
        copies[at][1].wait()
        if at + 2 < count:
            copies[at + 2][1].start()
        sums = jnp.dot(flipped[:, rows], pair_at(columns, rows, 3), preferred_element_type=jnp.float32)
        if at:
            sums = totals[...] + sums
        if at < count - 1:
            totals[...] = sums
        else:
            keep_sums(ours, theirs, 0, sums)


def load(projectors, band_coeffs):
    depth, slots = projectors.shape
    shape = (2, PCAP, LANES)
    return pl.pallas_call(
        load_kernel,
        in_specs=[HBM, HBM],
        out_specs=[VMEM] * 4,
        out_shape=[
            jax.ShapeDtypeStruct(shape, jnp.bfloat16),
            jax.ShapeDtypeStruct(shape, jnp.float32),
            jax.ShapeDtypeStruct((slots, depth), jnp.bfloat16),
            jax.ShapeDtypeStruct(band_coeffs.shape, jnp.bfloat16),
        ],
        scratch_shapes=[
            pltpu.VMEM((depth, slots), jnp.bfloat16),
            pltpu.VMEM((slots, 2 * LANES), jnp.float32),
            pltpu.SemaphoreType.DMA((4,)),
            pltpu.SemaphoreType.DMA((4,)),
        ],
        compiler_params=PARAMS,
        name="load",
    )(
        pltpu.with_memory_space_constraint(projectors, pltpu.HBM),
        pltpu.with_memory_space_constraint(band_coeffs, pltpu.HBM),
    )


def project_kernel(parts, flipped, columns, theirs, ours):
    rows = slice(0, columns.shape[0])
    for at, part in enumerate(parts):
        sums = jnp.dot(flipped[...], pair_at(columns, rows, part), preferred_element_type=jnp.float32)
        keep_sums(ours, theirs, at, sums)


def project(flipped, band_coeffs, parts):
    slots, depth = flipped.shape
    shape = (2 * len(parts), PCAP, LANES)

    def kernel(*refs):
        project_kernel(parts, *refs)

    return pl.pallas_call(
        kernel,
        in_specs=[VMEM, VMEM],
        out_specs=[VMEM, VMEM],
        out_shape=[jax.ShapeDtypeStruct(shape, jnp.bfloat16), jax.ShapeDtypeStruct(shape, jnp.float32)],
        compiler_params=PARAMS,
        cost_estimate=pl.CostEstimate(
            flops=4 * depth * slots * len(parts) * LANES, bytes_accessed=2 * depth * slots, transcendentals=0
        ),
        name="project",
    )(flipped, band_coeffs)


def project_plain(projectors, band_coeffs, parts):
    depth, bands = band_coeffs.shape
    chips = lax.axis_size("pw") // 2
    blocks = jnp.stack([block_of(place()[1], q, r) for q in parts for r in range(chips // SQUARE)])
    columns = jnp.take(band_coeffs.reshape(depth, chips, bands // chips), blocks, axis=1)
    outs = []
    core = place()[0]
    for group, dtype in ((1 - core, jnp.bfloat16), (core, jnp.float32)):
        slots = lax.dynamic_slice_in_dim(projectors, group * PCAP, PCAP, 1)
        sums = jnp.einsum("ds,dhw->hsw", slots, columns, preferred_element_type=jnp.float32)
        outs.append(sums.astype(dtype))
    return outs


def choose_kernel(owners, own, sibling, after, out):
    del after
    core, chip = place()
    me = 2 * chip + core
    owner = jnp.where(core == 0, owners[0:1, :], owners[1:2, :])
    width = out.shape[2]
    for part in range(SQUARE):
        rows = pl.ds(pl.multiple_of(((chip & 3) ^ part) * QUARTER, QUARTER), QUARTER)
        piece = jnp.where(owner == me, own[rows], jnp.where(owner == (me ^ 1), sibling[rows], 0.0))
        for cut in range(PCAP // width):
            out[part, cut * QUARTER : (cut + 1) * QUARTER] = piece[:, cut * width : (cut + 1) * width].astype(
                out.dtype
            )


def choose(owners, own, sibling, width, after):
    return pl.pallas_call(
        choose_kernel,
        in_specs=[VMEM, VMEM, VMEM, ANY],
        out_specs=VMEM,
        out_shape=jax.ShapeDtypeStruct((SQUARE, QUARTER * PCAP // width, width), jnp.bfloat16),
        compiler_params=PARAMS,
        name="choose",
    )(jnp.broadcast_to(owners[:, None], (owners.shape[0], PCAP)), own, sibling, after)


def send_kernel(first, second, ours, theirs, quarters, message):
    entries = ours.shape[0] // (1 if first == second else 2)
    core = place()[0]
    start, part = (0, first) if first == second else ((1 - core) * entries, 2 - core)
    for entry in range(entries):
        total = ours[start + entry] + theirs[start + entry].astype(jnp.float32)
        message[entry * PCAP : (entry + 1) * PCAP] = total.astype(message.dtype)
    message[entries * PCAP :] = quarters[part]


def send(ours, theirs, quarters, parts):
    count, _, width = ours.shape
    rows = count // len(parts) * PCAP + quarters.shape[1]

    def kernel(*refs):
        send_kernel(parts[0], parts[-1], *refs)

    return pl.pallas_call(
        kernel,
        in_specs=[VMEM] * 3,
        out_specs=VMEM,
        out_shape=jax.ShapeDtypeStruct((rows, width), jnp.bfloat16),
        compiler_params=PARAMS,
        name="send",
    )(ours, theirs, quarters)


def forward_kernel(ours, theirs, quarters, got, message):
    core = place()[0]
    entries = ours.shape[0] // 2
    start = core * entries
    for entry in range(entries):
        rows = slice(entry * PCAP, (entry + 1) * PCAP)
        total = ours[start + entry] + theirs[start + entry].astype(jnp.float32)
        message[rows] = (total + got[rows].astype(jnp.float32)).astype(message.dtype)
    message[entries * PCAP :] = quarters[1 + core] + got[entries * PCAP :]


def forward(ours, theirs, quarters, got):
    return pl.pallas_call(
        forward_kernel,
        in_specs=[VMEM] * 4,
        out_specs=VMEM,
        out_shape=jax.ShapeDtypeStruct(got.shape, got.dtype),
        compiler_params=PARAMS,
        name="forward",
    )(ours, theirs, quarters, got)


def fold_kernel(ours, theirs, quarters, *refs):
    *gots, kept, message = refs
    entries = ours.shape[0]
    for entry in range(entries):
        rows = slice(entry * PCAP, (entry + 1) * PCAP)
        total = ours[entry] + theirs[entry].astype(jnp.float32)
        for got in gots:
            total = total + got[rows].astype(jnp.float32)
        kept[rows] = total
        away = entry ^ 1
        message[away * PCAP : (away + 1) * PCAP] = total.astype(message.dtype)
    table = quarters[0]
    for got in gots:
        table = table + got[entries * PCAP :]
    kept[entries * PCAP :] = table.astype(kept.dtype)
    message[entries * PCAP :] = table


def fold(ours, theirs, quarters, gots):
    shape = gots[0].shape
    return pl.pallas_call(
        fold_kernel,
        in_specs=[VMEM] * (3 + len(gots)),
        out_specs=[VMEM, VMEM],
        out_shape=[jax.ShapeDtypeStruct(shape, jnp.float32), jax.ShapeDtypeStruct(shape, jnp.bfloat16)],
        compiler_params=PARAMS,
        name="fold",
    )(ours, theirs, quarters, *gots)


def add_kernel(left, right, out):
    out[...] = (left[...] + right[...].astype(jnp.float32)).astype(out.dtype)


def add(left, right):
    return pl.pallas_call(
        add_kernel,
        in_specs=[VMEM, VMEM],
        out_specs=VMEM,
        out_shape=jax.ShapeDtypeStruct(left.shape, jnp.bfloat16),
        compiler_params=PARAMS,
        name="add",
    )(left, right)


def mask_kernel(counts, atom_of, after, out):
    del after
    core = place()[0]
    slot = lax.broadcasted_iota(jnp.int32, (1, PCAP), 1)
    limit = jnp.zeros((1, PCAP), jnp.int32)
    for channel in range(CHANNELS):
        limit = jnp.where(slot >= channel * CH_CAP, channel * CH_CAP + counts[core, channel], limit)
    atoms = jnp.where(core == 0, atom_of[0:1], atom_of[1:2])
    code = jnp.broadcast_to(jnp.where(slot < limit, atoms, -1), (PCAP, PCAP))
    out[...] = jnp.where((code == code.T) & (code >= 0), 1.0, 0.0).astype(out.dtype)


def mask(counts, atom_of, after):
    return pl.pallas_call(
        mask_kernel,
        in_specs=[SMEM, VMEM, ANY],
        out_specs=VMEM,
        out_shape=jax.ShapeDtypeStruct((PCAP, PCAP), jnp.bfloat16),
        compiler_params=PARAMS,
        name="mask",
    )(counts, atom_of, after)


def couple_kernel(allowed, *refs):
    *messages, out, coupling = refs
    width = out.shape[2]
    entries = out.shape[0] // SQUARE
    core, chip = place()
    corner = chip & 3
    parts = (0, 2 - core, 1 + core, 3)
    for part, message in zip(parts, messages):
        start = pl.multiple_of((corner ^ part) * QUARTER, QUARTER)
        for cut in range(PCAP // width):
            lanes = slice(cut * width, (cut + 1) * width)
            first = entries * PCAP + cut * QUARTER
            coupling[pl.ds(start, QUARTER), lanes] = (
                message[first : first + QUARTER] * allowed[pl.ds(start, QUARTER), lanes]
            )
    for part, message in zip(parts, messages):
        wide = jnp.concatenate([message[e * PCAP : (e + 1) * PCAP] for e in range(entries)], axis=1)
        scaled = jnp.dot(coupling[...], wide, preferred_element_type=jnp.float32).astype(out.dtype)
        for entry in range(entries):
            out[part * entries + entry] = scaled[:, entry * width : (entry + 1) * width]


def couple(allowed, messages):
    rows, width = messages[0].shape
    entries = (rows - QUARTER * PCAP // width) // PCAP
    return pl.pallas_call(
        couple_kernel,
        in_specs=[VMEM] * (1 + SQUARE),
        out_specs=VMEM,
        out_shape=jax.ShapeDtypeStruct((SQUARE * entries, PCAP, width), jnp.bfloat16),
        scratch_shapes=[pltpu.VMEM((PCAP, PCAP), jnp.bfloat16)],
        compiler_params=PARAMS,
        name="couple",
    )(allowed, *messages)


def group_slots(group):
    return pl.ds(pl.multiple_of(group * PCAP, PCAP), PCAP)


def wide_pair(scaled, part):
    return jnp.concatenate([scaled[2 * part], scaled[2 * part + 1]], axis=1)


def begin_kernel(projectors, scaled, out):
    slots = group_slots(place()[0])
    for part in range(SQUARE):
        for block in range(projectors.shape[0] // ROW_BLOCK):
            rows = slice(block * ROW_BLOCK, (block + 1) * ROW_BLOCK)
            out[part, rows] = jnp.dot(
                projectors[rows, slots], wide_pair(scaled, part), preferred_element_type=jnp.float32
            )


def begin(projectors, scaled):
    depth, slots = projectors.shape
    return pl.pallas_call(
        begin_kernel,
        in_specs=[VMEM, VMEM],
        out_specs=VMEM,
        out_shape=jax.ShapeDtypeStruct((SQUARE, depth, 2 * LANES), jnp.float32),
        compiler_params=PARAMS,
        cost_estimate=pl.CostEstimate(
            flops=2 * depth * slots * LANES * SQUARE, bytes_accessed=2 * depth * slots, transcendentals=0
        ),
        name="begin",
    )(projectors, scaled)


def finish_kernel(projectors, begun, other, out, blocks, sems):
    core, chip = place()
    slots = group_slots(1 - core)
    copies = []
    first = 0
    for size in ROW_BLOCKS:
        rows = slice(first, first + size)
        first += size
        for part in range(SQUARE):
            sums = begun[part, rows] + jnp.dot(
                projectors[rows, slots], wide_pair(other, part), preferred_element_type=jnp.float32
            )
            for entry in range(2):
                start = pl.multiple_of(block_of(chip, part, entry) * LANES, LANES)
                lanes = slice(entry * LANES, (entry + 1) * LANES)
                blocks[rows, pl.ds(start, LANES)] = sums[:, lanes].astype(blocks.dtype)
        for start in range(rows.start, rows.stop, COPY_ROWS):
            written = slice(start, start + COPY_ROWS)
            copies.append(pltpu.make_async_copy(blocks.at[written], out.at[written], sems.at[len(copies)]))
            copies[-1].start(priority=len(copies) % 2)
    for copy in copies:
        copy.wait()


def finish(projectors, begun, other):
    depth, slots = projectors.shape
    bands = other.shape[0] * LANES
    return pl.pallas_call(
        finish_kernel,
        in_specs=[VMEM] * 3,
        out_specs=HBM,
        out_shape=jax.ShapeDtypeStruct((depth, bands), jnp.bfloat16),
        scratch_shapes=[
            pltpu.VMEM((depth, bands), jnp.bfloat16),
            pltpu.SemaphoreType.DMA((depth // COPY_ROWS,)),
        ],
        compiler_params=PARAMS,
        cost_estimate=pl.CostEstimate(
            flops=depth * slots * bands, bytes_accessed=2 * depth * (slots + bands), transcendentals=0
        ),
        name="finish",
    )(projectors, begun, other)


def apply_plain(projectors, mine, other):
    chips, _, width = mine.shape
    blocks = jnp.stack([block_of(place()[1], q, r) for q in range(SQUARE) for r in range(chips // SQUARE)])
    rows = []
    for group in range(2):
        part = jnp.where(place()[0] == group, mine, other)
        part = jnp.zeros_like(part).at[blocks].set(part)
        rows.append(part.transpose(1, 0, 2).reshape(PCAP, chips * width))
    return jnp.dot(projectors, jnp.concatenate(rows), preferred_element_type=jnp.float32).astype(jnp.bfloat16)


def local(band_coeffs, projectors, counts, atom_of, owners, couplings):
    chips = lax.axis_size("pw") // 2
    entries = chips // SQUARE
    width = band_coeffs.shape[1] // chips
    fast = width == LANES and entries == 2
    own_table = couplings[0]
    sibling_table = swap_cores(own_table)
    if fast:
        theirs, ours, flipped, columns = load(projectors, band_coeffs)

        def partial(parts):
            return project(flipped, columns, parts)
    else:

        def partial(parts):
            return project_plain(projectors, band_coeffs, parts)

        theirs, ours = partial((3,))

    theirs, sibling_table = lax.optimization_barrier((theirs, sibling_table))
    theirs = swap_cores(theirs)
    pair_theirs, pair_ours = partial((1, 2))
    quarters = choose(owners, own_table, sibling_table, width, ours)
    got = swap_first(send(ours, theirs, quarters, (3,)))
    pair_theirs = swap_cores(pair_theirs)
    low_theirs, low_ours = partial((0,))
    low_theirs = swap_cores(low_theirs)
    got_first = swap_first(send(pair_ours, pair_theirs, quarters, (1, 2)))
    message = forward(pair_ours, pair_theirs, quarters, got)
    got_second = swap_second(message)
    allowed = mask(counts, atom_of, message)

    total, message = fold(low_ours, low_theirs, quarters, [got_first, got_second])
    mine = add(total, swap_chips(message, SQUARE))
    distance = 2 * SQUARE
    while distance < chips:
        body = mine[: entries * PCAP].reshape(entries, PCAP, width)
        order = [entry ^ (distance // SQUARE) for entry in range(entries)]
        message = jnp.concatenate([body[jnp.array(order)].reshape(-1, width), mine[entries * PCAP :]])
        mine = add(mine.astype(jnp.float32), swap_chips(message, distance))
        distance *= 2

    scaled = couple(allowed, [mine, swap_first(mine), swap_second(mine), swap_chips(mine, 3)])
    other = swap_cores(scaled)
    if not fast:
        return apply_plain(projectors, scaled, other)
    return finish(projectors, begin(projectors, scaled), other)


def solution(mesh):
    placed = (
        P("pw", "group"),
        P("pw", "group"),
        P("group", None),
        P("group", None),
        P("group"),
        P("pw", "group", None),
    )
    return jax.shard_map(
        local, mesh=mesh, in_specs=placed, out_specs=P("pw", "group"), check_vma=False
    )
```

```python
import jax
import jax.numpy as jnp
from jax import lax
from jax.experimental import pallas as pl
from jax.experimental.pallas import tpu as pltpu
from jax.sharding import PartitionSpec as P

CHANNELS = 4
CH_CAP = 64
PCAP = 256
LANES = 128
SQUARE = 4
QUARTER = PCAP // SQUARE
ROW_BLOCK = 512
ROW_BLOCKS = (128, 128) + (256,) * 6 + (128, 128)
COPY_ROWS = 128
PARAMS = pltpu.CompilerParams(vmem_limit_bytes=40 * 1024 * 1024)
VMEM = pl.BlockSpec(memory_space=pltpu.VMEM)
SMEM = pl.BlockSpec(memory_space=pltpu.SMEM)
HBM = pl.BlockSpec(memory_space=pltpu.HBM)
ANY = pl.BlockSpec(memory_space=pl.ANY)


def place():
    me = lax.axis_index("pw")
    return lax.rem(me, 2), lax.div(me, 2)


def block_of(chip, part, entry):
    return chip ^ (part + SQUARE * entry)


def swap(x, distance):
    count = lax.axis_size("pw")
    return lax.ppermute(x, "pw", [(i, i ^ distance) for i in range(count)])


def swap_cores(x):
    return swap(x, 1)


def swap_chips(x, distance):
    return swap(x, 2 * distance)


def swap_first(x):
    count = lax.axis_size("pw")
    return lax.ppermute(x, "pw", [(i, i ^ (4, 2)[i % 2]) for i in range(count)])


def swap_second(x):
    count = lax.axis_size("pw")
    return lax.ppermute(x, "pw", [(i, i ^ (2, 4)[i % 2]) for i in range(count)])


def pair_at(columns, rows, part):
    chip = place()[1]
    starts = [pl.multiple_of(block_of(chip, part, entry) * LANES, LANES) for entry in range(2)]
    return jnp.concatenate([columns[rows, pl.ds(start, LANES)] for start in starts], axis=1)


def keep_sums(ours, theirs, at, sums):
    for entry in range(2):
        lanes = slice(entry * LANES, (entry + 1) * LANES)
        ours[2 * at + entry] = sums[:PCAP, lanes]
        theirs[2 * at + entry] = sums[PCAP:, lanes].astype(theirs.dtype)


def load_kernel(projectors, flipped, slots, sems):
    core = place()[0]
    count = sems.shape[0]
    block = slots.shape[0] // count
    copies = []
    for at in range(count):
        rows = slice(at * block, (at + 1) * block)
        copies.append(pltpu.make_async_copy(projectors.at[rows], slots.at[rows], sems.at[at]))
        copies[-1].start(priority=at % 2)
    for at, copy in enumerate(copies):
        copy.wait()
        rows = slice(at * block, (at + 1) * block)
        for side, group in enumerate((core, 1 - core)):
            start = pl.multiple_of(group * PCAP, PCAP)
            flipped[side * PCAP : (side + 1) * PCAP, rows] = slots[rows, pl.ds(start, PCAP)].T


def load(projectors):
    depth, slots = projectors.shape
    return pl.pallas_call(
        load_kernel,
        in_specs=[HBM],
        out_specs=VMEM,
        out_shape=jax.ShapeDtypeStruct((slots, depth), jnp.bfloat16),
        scratch_shapes=[pltpu.VMEM((depth, slots), jnp.bfloat16), pltpu.SemaphoreType.DMA((4,))],
        compiler_params=PARAMS,
        name="load",
    )(pltpu.with_memory_space_constraint(projectors, pltpu.HBM))


def project_kernel(parts, flipped, columns, theirs, ours):
    rows = slice(0, columns.shape[0])
    for at, part in enumerate(parts):
        sums = jnp.dot(flipped[...], pair_at(columns, rows, part), preferred_element_type=jnp.float32)
        keep_sums(ours, theirs, at, sums)


def project(flipped, band_coeffs, parts):
    slots, depth = flipped.shape
    shape = (2 * len(parts), PCAP, LANES)

    def kernel(*refs):
        project_kernel(parts, *refs)

    return pl.pallas_call(
        kernel,
        in_specs=[VMEM, VMEM],
        out_specs=[VMEM, VMEM],
        out_shape=[jax.ShapeDtypeStruct(shape, jnp.bfloat16), jax.ShapeDtypeStruct(shape, jnp.float32)],
        compiler_params=PARAMS,
        cost_estimate=pl.CostEstimate(
            flops=4 * depth * slots * len(parts) * LANES, bytes_accessed=2 * depth * slots, transcendentals=0
        ),
        name="project",
    )(flipped, pltpu.with_memory_space_constraint(band_coeffs, pltpu.VMEM))


def project_plain(projectors, band_coeffs, parts):
    depth, bands = band_coeffs.shape
    chips = lax.axis_size("pw") // 2
    blocks = jnp.stack([block_of(place()[1], q, r) for q in parts for r in range(chips // SQUARE)])
    columns = jnp.take(band_coeffs.reshape(depth, chips, bands // chips), blocks, axis=1)
    outs = []
    core = place()[0]
    for group, dtype in ((1 - core, jnp.bfloat16), (core, jnp.float32)):
        slots = lax.dynamic_slice_in_dim(projectors, group * PCAP, PCAP, 1)
        sums = jnp.einsum("ds,dhw->hsw", slots, columns, preferred_element_type=jnp.float32)
        outs.append(sums.astype(dtype))
    return outs


def choose_kernel(owners, own, sibling, after, out):
    del after
    core, chip = place()
    me = 2 * chip + core
    owner = jnp.where(core == 0, owners[0:1, :], owners[1:2, :])
    width = out.shape[2]
    for part in range(SQUARE):
        rows = pl.ds(pl.multiple_of(((chip & 3) ^ part) * QUARTER, QUARTER), QUARTER)
        piece = jnp.where(owner == me, own[rows], jnp.where(owner == (me ^ 1), sibling[rows], 0.0))
        for cut in range(PCAP // width):
            out[part, cut * QUARTER : (cut + 1) * QUARTER] = piece[:, cut * width : (cut + 1) * width].astype(
                out.dtype
            )


def choose(owners, own, sibling, width, after):
    return pl.pallas_call(
        choose_kernel,
        in_specs=[VMEM, VMEM, VMEM, ANY],
        out_specs=VMEM,
        out_shape=jax.ShapeDtypeStruct((SQUARE, QUARTER * PCAP // width, width), jnp.bfloat16),
        compiler_params=PARAMS,
        name="choose",
    )(jnp.broadcast_to(owners[:, None], (owners.shape[0], PCAP)), own, sibling, after)


def send_kernel(first, second, ours, theirs, quarters, message):
    entries = ours.shape[0] // (1 if first == second else 2)
    core = place()[0]
    start, part = (0, first) if first == second else ((1 - core) * entries, 2 - core)
    for entry in range(entries):
        total = ours[start + entry] + theirs[start + entry].astype(jnp.float32)
        message[entry * PCAP : (entry + 1) * PCAP] = total.astype(message.dtype)
    message[entries * PCAP :] = quarters[part]


def send(ours, theirs, quarters, parts):
    count, _, width = ours.shape
    rows = count // len(parts) * PCAP + quarters.shape[1]

    def kernel(*refs):
        send_kernel(parts[0], parts[-1], *refs)

    return pl.pallas_call(
        kernel,
        in_specs=[VMEM] * 3,
        out_specs=VMEM,
        out_shape=jax.ShapeDtypeStruct((rows, width), jnp.bfloat16),
        compiler_params=PARAMS,
        name="send",
    )(ours, theirs, quarters)


def forward_kernel(ours, theirs, quarters, got, message):
    core = place()[0]
    entries = ours.shape[0] // 2
    start = core * entries
    for entry in range(entries):
        rows = slice(entry * PCAP, (entry + 1) * PCAP)
        total = ours[start + entry] + theirs[start + entry].astype(jnp.float32)
        message[rows] = (total + got[rows].astype(jnp.float32)).astype(message.dtype)
    message[entries * PCAP :] = quarters[1 + core] + got[entries * PCAP :]


def forward(ours, theirs, quarters, got):
    return pl.pallas_call(
        forward_kernel,
        in_specs=[VMEM] * 4,
        out_specs=VMEM,
        out_shape=jax.ShapeDtypeStruct(got.shape, got.dtype),
        compiler_params=PARAMS,
        name="forward",
    )(ours, theirs, quarters, got)


def fold_kernel(ours, theirs, quarters, *refs):
    *gots, kept, message = refs
    entries = ours.shape[0]
    for entry in range(entries):
        rows = slice(entry * PCAP, (entry + 1) * PCAP)
        total = ours[entry] + theirs[entry].astype(jnp.float32)
        for got in gots:
            total = total + got[rows].astype(jnp.float32)
        kept[rows] = total
        away = entry ^ 1
        message[away * PCAP : (away + 1) * PCAP] = total.astype(message.dtype)
    table = quarters[0]
    for got in gots:
        table = table + got[entries * PCAP :]
    kept[entries * PCAP :] = table.astype(kept.dtype)
    message[entries * PCAP :] = table


def fold(ours, theirs, quarters, gots):
    shape = gots[0].shape
    return pl.pallas_call(
        fold_kernel,
        in_specs=[VMEM] * (3 + len(gots)),
        out_specs=[VMEM, VMEM],
        out_shape=[jax.ShapeDtypeStruct(shape, jnp.float32), jax.ShapeDtypeStruct(shape, jnp.bfloat16)],
        compiler_params=PARAMS,
        name="fold",
    )(ours, theirs, quarters, *gots)


def add_kernel(left, right, out):
    out[...] = (left[...] + right[...].astype(jnp.float32)).astype(out.dtype)


def add(left, right):
    return pl.pallas_call(
        add_kernel,
        in_specs=[VMEM, VMEM],
        out_specs=VMEM,
        out_shape=jax.ShapeDtypeStruct(left.shape, jnp.bfloat16),
        compiler_params=PARAMS,
        name="add",
    )(left, right)


def mask_kernel(counts, atom_of, after, out):
    del after
    core = place()[0]
    slot = lax.broadcasted_iota(jnp.int32, (1, PCAP), 1)
    limit = jnp.zeros((1, PCAP), jnp.int32)
    for channel in range(CHANNELS):
        limit = jnp.where(slot >= channel * CH_CAP, channel * CH_CAP + counts[core, channel], limit)
    atoms = jnp.where(core == 0, atom_of[0:1], atom_of[1:2])
    code = jnp.broadcast_to(jnp.where(slot < limit, atoms, -1), (PCAP, PCAP))
    out[...] = jnp.where((code == code.T) & (code >= 0), 1.0, 0.0).astype(out.dtype)


def mask(counts, atom_of, after):
    return pl.pallas_call(
        mask_kernel,
        in_specs=[SMEM, VMEM, ANY],
        out_specs=VMEM,
        out_shape=jax.ShapeDtypeStruct((PCAP, PCAP), jnp.bfloat16),
        compiler_params=PARAMS,
        name="mask",
    )(counts, atom_of, after)


def couple_kernel(allowed, *refs):
    *messages, out, coupling = refs
    width = out.shape[2]
    entries = out.shape[0] // SQUARE
    core, chip = place()
    corner = chip & 3
    parts = (0, 2 - core, 1 + core, 3)
    for part, message in zip(parts, messages):
        start = pl.multiple_of((corner ^ part) * QUARTER, QUARTER)
        for cut in range(PCAP // width):
            lanes = slice(cut * width, (cut + 1) * width)
            first = entries * PCAP + cut * QUARTER
            coupling[pl.ds(start, QUARTER), lanes] = (
                message[first : first + QUARTER] * allowed[pl.ds(start, QUARTER), lanes]
            )
    for part, message in zip(parts, messages):
        wide = jnp.concatenate([message[e * PCAP : (e + 1) * PCAP] for e in range(entries)], axis=1)
        scaled = jnp.dot(coupling[...], wide, preferred_element_type=jnp.float32).astype(out.dtype)
        for entry in range(entries):
            out[part * entries + entry] = scaled[:, entry * width : (entry + 1) * width]


def couple(allowed, messages):
    rows, width = messages[0].shape
    entries = (rows - QUARTER * PCAP // width) // PCAP
    return pl.pallas_call(
        couple_kernel,
        in_specs=[VMEM] * (1 + SQUARE),
        out_specs=VMEM,
        out_shape=jax.ShapeDtypeStruct((SQUARE * entries, PCAP, width), jnp.bfloat16),
        scratch_shapes=[pltpu.VMEM((PCAP, PCAP), jnp.bfloat16)],
        compiler_params=PARAMS,
        name="couple",
    )(allowed, *messages)


def group_slots(group):
    return pl.ds(pl.multiple_of(group * PCAP, PCAP), PCAP)


def wide_pair(scaled, part):
    return jnp.concatenate([scaled[2 * part], scaled[2 * part + 1]], axis=1)


def begin_kernel(projectors, scaled, out):
    slots = group_slots(place()[0])
    for part in range(SQUARE):
        for block in range(projectors.shape[0] // ROW_BLOCK):
            rows = slice(block * ROW_BLOCK, (block + 1) * ROW_BLOCK)
            out[part, rows] = jnp.dot(
                projectors[rows, slots], wide_pair(scaled, part), preferred_element_type=jnp.float32
            )


def begin(projectors, scaled):
    depth, slots = projectors.shape
    return pl.pallas_call(
        begin_kernel,
        in_specs=[VMEM, VMEM],
        out_specs=VMEM,
        out_shape=jax.ShapeDtypeStruct((SQUARE, depth, 2 * LANES), jnp.float32),
        compiler_params=PARAMS,
        cost_estimate=pl.CostEstimate(
            flops=2 * depth * slots * LANES * SQUARE, bytes_accessed=2 * depth * slots, transcendentals=0
        ),
        name="begin",
    )(projectors, scaled)


def finish_kernel(projectors, begun, other, out, blocks, sems):
    core, chip = place()
    slots = group_slots(1 - core)
    copies = []
    first = 0
    for size in ROW_BLOCKS:
        rows = slice(first, first + size)
        first += size
        for part in range(SQUARE):
            sums = begun[part, rows] + jnp.dot(
                projectors[rows, slots], wide_pair(other, part), preferred_element_type=jnp.float32
            )
            for entry in range(2):
                start = pl.multiple_of(block_of(chip, part, entry) * LANES, LANES)
                lanes = slice(entry * LANES, (entry + 1) * LANES)
                blocks[rows, pl.ds(start, LANES)] = sums[:, lanes].astype(blocks.dtype)
        for start in range(rows.start, rows.stop, COPY_ROWS):
            written = slice(start, start + COPY_ROWS)
            copies.append(pltpu.make_async_copy(blocks.at[written], out.at[written], sems.at[len(copies)]))
            copies[-1].start(priority=len(copies) % 2)
    for copy in copies:
        copy.wait()


def finish(projectors, begun, other):
    depth, slots = projectors.shape
    bands = other.shape[0] * LANES
    return pl.pallas_call(
        finish_kernel,
        in_specs=[VMEM] * 3,
        out_specs=HBM,
        out_shape=jax.ShapeDtypeStruct((depth, bands), jnp.bfloat16),
        scratch_shapes=[
            pltpu.VMEM((depth, bands), jnp.bfloat16),
            pltpu.SemaphoreType.DMA((depth // COPY_ROWS,)),
        ],
        compiler_params=PARAMS,
        cost_estimate=pl.CostEstimate(
            flops=depth * slots * bands, bytes_accessed=2 * depth * (slots + bands), transcendentals=0
        ),
        name="finish",
    )(projectors, begun, other)


def apply_plain(projectors, mine, other):
    chips, _, width = mine.shape
    blocks = jnp.stack([block_of(place()[1], q, r) for q in range(SQUARE) for r in range(chips // SQUARE)])
    rows = []
    for group in range(2):
        part = jnp.where(place()[0] == group, mine, other)
        part = jnp.zeros_like(part).at[blocks].set(part)
        rows.append(part.transpose(1, 0, 2).reshape(PCAP, chips * width))
    return jnp.dot(projectors, jnp.concatenate(rows), preferred_element_type=jnp.float32).astype(jnp.bfloat16)


def local(band_coeffs, projectors, counts, atom_of, owners, couplings):
    chips = lax.axis_size("pw") // 2
    entries = chips // SQUARE
    width = band_coeffs.shape[1] // chips
    fast = width == LANES and entries == 2
    own_table = couplings[0]
    sibling_table = swap_cores(own_table)
    if fast:
        flipped = load(projectors)

        def partial(parts):
            return project(flipped, band_coeffs, parts)
    else:

        def partial(parts):
            return project_plain(projectors, band_coeffs, parts)

    theirs, ours = partial((3,))
    theirs, sibling_table = lax.optimization_barrier((theirs, sibling_table))
    theirs = swap_cores(theirs)
    pair_theirs, pair_ours = partial((1, 2))
    quarters = choose(owners, own_table, sibling_table, width, ours)
    got = swap_first(send(ours, theirs, quarters, (3,)))
    pair_theirs = swap_cores(pair_theirs)
    low_theirs, low_ours = partial((0,))
    low_theirs = swap_cores(low_theirs)
    got_first = swap_first(send(pair_ours, pair_theirs, quarters, (1, 2)))
    message = forward(pair_ours, pair_theirs, quarters, got)
    got_second = swap_second(message)
    allowed = mask(counts, atom_of, message)

    total, message = fold(low_ours, low_theirs, quarters, [got_first, got_second])
    mine = add(total, swap_chips(message, SQUARE))
    distance = 2 * SQUARE
    while distance < chips:
        body = mine[: entries * PCAP].reshape(entries, PCAP, width)
        order = [entry ^ (distance // SQUARE) for entry in range(entries)]
        message = jnp.concatenate([body[jnp.array(order)].reshape(-1, width), mine[entries * PCAP :]])
        mine = add(mine.astype(jnp.float32), swap_chips(message, distance))
        distance *= 2

    scaled = couple(allowed, [mine, swap_first(mine), swap_second(mine), swap_chips(mine, 3)])
    other = swap_cores(scaled)
    if not fast:
        return apply_plain(projectors, scaled, other)
    return finish(projectors, begin(projectors, scaled), other)


def solution(mesh):
    placed = (
        P("pw", "group"),
        P("pw", "group"),
        P("group", None),
        P("group", None),
        P("group"),
        P("pw", "group", None),
    )
    return jax.shard_map(
        local, mesh=mesh, in_specs=placed, out_specs=P("pw", "group"), check_vma=False
    )
```
